32 devices in a mesh: dp: 8 (over z, x), tensor: 4 (over y, core).
Axes of the slice: x: 2, y: 2, z: 4, core: 2. Of those that a mesh axis runs over, the one named last changes fastest.
Arguments:
- hidden_pre: bfloat16 [8256, 6144], P('dp', 'tensor'), may hold values from -6 to 6
- cotangent: bfloat16 [8256, 1536], P('dp', 'tensor'), may hold values from -6 to 6
- down_weight: bfloat16 [1536, 6144], P(None, 'tensor'), may hold values from -0.078125 to 0.078125
- layer_scale: float32 [1536], replicated, may hold values from 0.3 to 3
- crop_lengths: int32 [8, 4], replicated, may hold values from 0 to 257, as said below
- crop_moves: int32 [8, 4], replicated, may hold values from 0 to 1, as said below
Outputs:
- hidden_grad: bfloat16 [5760, 6144], P('dp', 'tensor')
- down_grad: float32 [1536, 6144], P('dp', 'tensor')
The draws below stay inside these ranges and needn't reach their ends.
Inputs may be any that keep to these rules, and one draw needn't show every extreme that they name: `crop_lengths`: devices d and d + 4 form a pair: in each pair one device holds crops of 257 or 50 tokens in every slot, the other crops of 50 tokens or empty slots (0). Some device holds 1028 tokens. `crop_moves`: only the first kind of device of a pair moves crops, exactly 2 of its slots, to its partner; a device holds at most 714 tokens after the moves and sends at most 514, and both are reached.
All inputs are finite; a program needn't handle non-finite values.
Results may differ from the reference program's by a relative error of at most 0.005.
Values may be sent and summed in bfloat16 or wider, within the bound.
No kernel may reach another device: no remote copies, remote signals or barrier semaphores. Data moves between devices by JAX's collectives and lax.ppermute only.
A program may use at most 64 MiB of HBM per device.

```python
import math
import jax
import jax.numpy as jnp
from jax import lax

D = 1536
FF = 6144
SLOTS = 4
GLOBAL_LEN = 257
LOCAL_LEN = 50
HOME = 1032
BAL = 720
HOME_ALL = 8256
N_DP = 8


def pair_layout(key):
    half_axis = N_DP // 2
    loaded_key, full_key = jax.random.split(key)
    first_loaded = jax.random.randint(loaded_key, (half_axis,), 0, 2)
    full_pair = jax.random.randint(full_key, (), 0, half_axis)
    loaded = jnp.concatenate([first_loaded, 1 - first_loaded])
    pair_index = jnp.arange(N_DP) % half_axis
    full_mark = pair_index == full_pair
    return (loaded, full_mark)


def slot_order(row_key):
    return jax.random.permutation(row_key, SLOTS)


def draw_crop_lengths(key, part):
    loaded, full_mark = pair_layout(key)
    key = jax.random.fold_in(key, 3)
    big_key, live_key = jax.random.split(key)
    big_crop = jax.random.randint(big_key, (N_DP, SLOTS), 0, 2)
    live_crop = jax.random.randint(live_key, (N_DP, SLOTS), 0, 2)
    big_crop = jnp.where(full_mark[:, None], 1, big_crop)
    live_crop = jnp.where(full_mark[:, None], 1, live_crop)
    heavy_sizes = jnp.where(big_crop == 1, GLOBAL_LEN, LOCAL_LEN)
    sizes = jnp.where(loaded[:, None] == 1, heavy_sizes, live_crop * LOCAL_LEN)
    return sizes.astype(jnp.int32)


def draw_crop_moves(key, part):
    loaded, full_mark = pair_layout(key)
    key = jax.random.fold_in(key, 5)
    ranks = jax.vmap(slot_order)(jax.random.split(key, N_DP))
    moving = (ranks < SLOTS // 2) & (loaded[:, None] == 1)
    return moving.astype(jnp.int32)


def with_spikes(values, own_key, source, target, parts, factor):
    def block_of(axis_at):
        return (jnp.arange(values.shape[axis_at]) // (values.shape[axis_at] // parts)).reshape((-1,) + (1,) * (values.ndim - 1 - axis_at))

    one_side = jax.random.permutation(own_key, parts)[block_of(target)]
    second = (block_of(target) + parts // 2) % parts
    return jnp.where((block_of(source) == one_side) | (block_of(source) == second), factor * values, values)


def block_levels(rng, dims, pieces, low, high):
    loudness = 1.0
    for axis_at, blocks in pieces:
        heights = jax.random.uniform(jax.random.fold_in(jax.random.fold_in(rng, 6), axis_at), (blocks,), jnp.float32, low / len(pieces), high / len(pieces))
        loudness = loudness * jnp.repeat(jnp.exp(heights), dims[axis_at] // blocks).reshape((-1,) + (1,) * (len(dims) - 1 - axis_at))
    return loudness


def scatter_about(key, shape, scale, bound, shards=(), held_as=jnp.bfloat16):
    array = scale * jax.random.normal(key, shape, jnp.float32)
    if shards:
        array = array * block_levels(key, shape, shards, -0.22, 0.18)
    return jnp.clip(array, -bound, bound).astype(held_as)


def gaussian_with(own_key, shape, deviation, most, cuts, heavy, held_as=jnp.bfloat16):
    values = deviation * jax.random.normal(own_key, shape, jnp.float32)
    if cuts:
        values = values * block_levels(own_key, shape, cuts, -0.22, 0.18)
    return jnp.clip(with_spikes(values, jax.random.fold_in(own_key, 3), *heavy), -most, most).astype(held_as)


def setup_inputs(seed: int = 0) -> dict:
    keys = jax.random.split(jax.random.key(seed), 7)
    return {
        "hidden_pre": scatter_about(keys[0], (N_DP * HOME, FF), 1.0, 6.0, ((0, 8), (1, 4))),
        "cotangent": gaussian_with(keys[1], (N_DP * HOME, D), 1.0, 6.0, ((0, 8), (1, 4)), (0, 1, 8, 2.0)),
        "down_weight": scatter_about(keys[2], (D, FF), FF ** -0.5, 0.078125, ((1, 4),)),
        "layer_scale": jnp.clip(jnp.exp(jax.random.uniform(keys[3], (D,), jnp.float32, math.log(0.3), math.log(3.0))), 0.3, 3.0),
        "crop_lengths": draw_crop_lengths(jax.random.fold_in(keys[6], 71), 0),
        "crop_moves": draw_crop_moves(jax.random.fold_in(keys[6], 71), 0),
    }


inv_root_two = 0.7071067811865476
inv_root_tau = 0.3989422804014327

def gelu_parts(pre_act):
    cumulative = 0.5 * (1.0 + jax.scipy.special.erf(pre_act * inv_root_two))
    activated = pre_act * cumulative
    derivative = cumulative + pre_act * jnp.exp(-0.5 * pre_act * pre_act) * inv_root_tau
    return (activated, derivative)

def crop_rows(row_total, crop_sizes, crop_starts):
    crop_ends = jnp.cumsum(crop_sizes).astype(jnp.int32)
    crop_begins = crop_ends - crop_sizes
    target_rows = jnp.arange(row_total, dtype=jnp.int32)[:, None]
    inside_crop = (target_rows >= crop_begins[None, :]) & (target_rows < crop_ends[None, :])
    source_rows = lax.optimization_barrier(jnp.sum(jnp.where(inside_crop, crop_starts[None, :] + target_rows - crop_begins[None, :], 0), axis=1)).astype(jnp.int32)
    return (source_rows, jnp.any(inside_crop, axis=1))

def reference(hidden_pre, cotangent, down_weight, layer_scale, crop_lengths, crop_moves):
    half_axis = N_DP // 2

    def one_device(grad_total, device_index):
        partner_index = (device_index + half_axis) % N_DP
        own_lengths = crop_lengths[device_index]
        own_moves = crop_moves[device_index]
        partner_lengths = crop_lengths[partner_index]
        partner_moves = crop_moves[partner_index]
        own_starts = (device_index * HOME + jnp.cumsum(own_lengths) - own_lengths).astype(jnp.int32)
        partner_starts = (partner_index * HOME + jnp.cumsum(partner_lengths) - partner_lengths).astype(jnp.int32)
        crop_sizes = jnp.concatenate([own_lengths * (1 - own_moves), partner_lengths * partner_moves]).astype(jnp.int32)
        crop_starts = jnp.concatenate([own_starts, partner_starts]).astype(jnp.int32)
        source_rows, valid_rows = crop_rows(BAL, crop_sizes, crop_starts)
        pre_act = jnp.take(hidden_pre, source_rows, axis=0).astype(jnp.float32)
        cot_rows = jnp.take(cotangent, source_rows, axis=0).astype(jnp.float32)
        scaled = (cot_rows * layer_scale[None, :]).astype(jnp.bfloat16)
        activated, derivative = gelu_parts(pre_act)
        activation = jnp.where(valid_rows[:, None], activated, 0.0).astype(jnp.bfloat16)
        backward = jnp.dot(scaled, down_weight, preferred_element_type=jnp.float32) * derivative
        gradient_rows = jnp.where(valid_rows[:, None], backward, 0.0).astype(jnp.bfloat16)
        grad_total = grad_total + lax.dot_general(scaled, activation, (((0,), (0,)), ((), ())), preferred_element_type=jnp.float32)
        return (grad_total, gradient_rows)
    grad_total, gradient_blocks = lax.scan(one_device, jnp.zeros((D, FF), jnp.float32), jnp.arange(N_DP, dtype=jnp.int32))
    hidden_grad = gradient_blocks.reshape(N_DP * BAL, FF)
    down_grad = grad_total / math.sqrt(HOME_ALL)
    return (hidden_grad, down_grad)
```

```python
import functools
import math

import jax
import jax.numpy as jnp
from jax import lax
from jax.experimental import pallas as pl
from jax.experimental.pallas import tpu as pltpu
from jax.sharding import PartitionSpec as P

SEND = 528
KEEP = 528
TILE = 16
BAL = 720
BF = jnp.bfloat16
F32 = jnp.float32

inv_root_two = 0.7071067811865476
inv_root_tau = 0.3989422804014327


def call(kernel, grid, scalars, in_specs, out_specs, out_shape, scratch, flops, nbytes, trans=0):
    return pl.pallas_call(
        kernel,
        grid_spec=pltpu.PrefetchScalarGridSpec(
            num_scalar_prefetch=scalars,
            grid=grid,
            in_specs=in_specs,
            out_specs=out_specs,
            scratch_shapes=scratch,
        ),
        out_shape=out_shape,
        cost_estimate=pl.CostEstimate(flops=flops, bytes_accessed=nbytes, transcendentals=trans),
        compiler_params=pltpu.CompilerParams(vmem_limit_bytes=48 * 1024 * 1024),
    )


def whole(shape):
    return pl.BlockSpec(shape, lambda *_: (0,) * len(shape))


def kept_total(lens, moves, d):
    return sum(lens[d, j] * (1 - moves[d, j]) for j in range(lens.shape[1]))


def picks(lens, moves, d, moved, first, rows, home):
    at = lax.broadcasted_iota(jnp.int32, (rows, 1), 0) - first
    source = jnp.full((rows, 1), -1, jnp.int32)
    begin = jnp.int32(0)
    start = jnp.int32(0)
    for j in range(lens.shape[1]):
        length = lens[d, j]
        size = length * (moves[d, j] if moved else 1 - moves[d, j])
        inside = (at >= begin) & (at < begin + size)
        source = jnp.where(inside, at + (start - begin), source)
        begin = begin + size
        start = start + length
    columns = lax.broadcasted_iota(jnp.int32, (rows, home), 1)
    return jnp.where(columns == source, 1.0, 0.0).astype(BF)


def both_picks(place, lens, moves, home):
    d = place[0]
    n = lens.shape[0]
    partner = lax.rem(d + n // 2, n)
    first = lax.rem(kept_total(lens, moves, partner), TILE)
    sent = picks(lens, moves, d, True, first, SEND, home)
    kept = picks(lens, moves, d, False, 0, KEEP, home)
    return sent, kept


def scaled_kernel(place, lens, moves, cot, scale, sent_out, kept_out):
    sent, kept = both_picks(place, lens, moves, cot.shape[0])
    for pick, out in ((sent, sent_out), (kept, kept_out)):
        rows = jnp.dot(pick, cot[...], preferred_element_type=F32)
        out[...] = (rows * scale[...]).astype(BF)


def gelu_kernel(place, lens, moves, pre, act_out, der_out, pick, rows_f32):
    home = pre.shape[0]

    @pl.when(pl.program_id(0) == 0)
    def _():
        sent, kept = both_picks(place, lens, moves, home)
        pick[0:SEND, :] = sent
        pick[SEND : SEND + KEEP, :] = kept

    rows_f32[...] = jnp.dot(pick[...], pre[...], preferred_element_type=F32)
    step = 3 * TILE

    def body(i, _):
        at = pl.ds(pl.multiple_of(i * step, step), step)
        x = rows_f32[at, :]
        cumulative = 0.5 * (1.0 + lax.erf(x * inv_root_two))
        act_out[at, :] = (x * cumulative).astype(BF)
        der_out[at, :] = cumulative + x * jnp.exp(-0.5 * x * x) * inv_root_tau
        return 0

    lax.fori_loop(0, (SEND + KEEP) // step, body, 0)


def assemble(place, pieces, lhs):
    t = place[1]
    width = pieces[0].shape[1]
    for j, piece in enumerate(pieces):
        at = pl.ds(pl.multiple_of((t ^ j) * width, 128), width)
        lhs[:, at] = piece[...]


def grad_kernel(chunks, place, p0, p1, p2, p3, weight, der, *rest):
    outs, lhs = rest[:chunks], rest[chunks]
    step = pl.program_id(0)

    @pl.when(step == 0)
    def _():
        assemble(place, (p0, p1, p2, p3), lhs)

    value = (jnp.dot(lhs[...], weight[...], preferred_element_type=F32) * der[...]).astype(BF)
    for c in range(chunks):

        @pl.when(step == c)
        def _():
            outs[c][...] = value


def weight_kernel(place, sent, kept, act, send_out, keep_out, lhs):
    @pl.when(pl.program_id(0) == 0)
    def _():
        both = jnp.concatenate([sent[...], kept[...]], axis=0).astype(F32).T.astype(BF)
        half = both.shape[0] // 2
        mine = place[0] % 2 == 0
        lo, hi = both[:half], both[half:]
        lhs[0:half, :] = jnp.where(mine, hi, lo)
        lhs[half : 2 * half, :] = jnp.where(mine, lo, hi)

    half = lhs.shape[0] // 2
    value = jnp.dot(lhs[...], act[...], preferred_element_type=F32)
    send_out[...] = value[:half].astype(BF)
    keep_out[...] = value[half:]


def place_kernel(place, lens, moves, kept, *rest):
    incoming, out = rest[:-1], rest[-1]
    d = place[0]
    count = kept_total(lens, moves, d)
    first = jnp.minimum(count - lax.rem(count, TILE), BAL - SEND)
    first = pl.multiple_of(first, TILE)
    out[0:KEEP, :] = kept[...]
    out[KEEP:, :] = jnp.zeros((out.shape[0] - KEEP, out.shape[1]), BF)
    rows = lax.broadcasted_iota(jnp.int32, (SEND, 1), 0) + first
    step = pl.program_id(0)
    window = pl.ds(first, SEND)
    for c, block in enumerate(incoming):

        @pl.when(step == c)
        def _():
            out[window, :] = jnp.where(rows < count, out[window, :], block[...])


def swapped(block, axis, distance):
    n = lax.axis_size(axis)
    return lax.ppermute(block, axis, [(i, i ^ distance) for i in range(n)])


def shards(hidden_pre, cotangent, down_weight, layer_scale, crop_lengths, crop_moves):
    home, ff = hidden_pre.shape
    width = cotangent.shape[1]
    features = down_weight.shape[0]
    n = lax.axis_size("dp")
    d = lax.axis_index("dp").astype(jnp.int32)
    t = lax.axis_index("tensor").astype(jnp.int32)
    place = jnp.stack([d, t])
    rows = SEND + KEEP
    scale = layer_scale.reshape(1, features)

    sent, kept = call(
        scaled_kernel, (1,), 3,
        [whole((home, width)), pl.BlockSpec((1, width), lambda i, place, *_: (0, place[1]))],
        [whole((SEND, width)), whole((KEEP, width))],
        [jax.ShapeDtypeStruct((SEND, width), BF), jax.ShapeDtypeStruct((KEEP, width), BF)],
        [], 2 * rows * home * width, 2 * (rows + home) * width,
    )(place, crop_lengths, crop_moves, cotangent, scale)

    sent_y, sent_c = swapped(sent, "tensor", 2), swapped(sent, "tensor", 1)
    kept_y, kept_c = swapped(kept, "tensor", 2), swapped(kept, "tensor", 1)
    sent_yc, kept_yc = swapped(sent_y, "tensor", 1), swapped(kept_y, "tensor", 1)
    sents = (sent, sent_c, sent_y, sent_yc)
    kepts = (kept, kept_c, kept_y, kept_yc)

    cols = 256
    act, der = call(
        gelu_kernel, (ff // cols,), 3,
        [pl.BlockSpec((home, cols), lambda i, *_: (0, i))],
        [pl.BlockSpec((rows, cols), lambda i, *_: (0, i))] * 2,
        [jax.ShapeDtypeStruct((rows, ff), BF), jax.ShapeDtypeStruct((rows, ff), F32)],
        [pltpu.VMEM((rows, home), BF), pltpu.VMEM((rows, cols), F32)],
        2 * rows * home * ff, 2 * home * ff + 6 * rows * ff, 2 * rows * ff,
    )(place, crop_lengths, crop_moves, hidden_pre)

    def grads(pieces, half, chunks):
        cols = ff // 4
        count = pieces[0].shape[0]
        if chunks == 1:
            out_specs = [pl.BlockSpec((count, cols), lambda i, *_: (0, i))]
            out_shape = [jax.ShapeDtypeStruct((count, ff), BF)]
            kernel = functools.partial(grad_one_kernel)
        else:
            out_specs = [whole((count, cols))] * chunks
            out_shape = [jax.ShapeDtypeStruct((count, cols), BF)] * chunks
            kernel = functools.partial(grad_kernel, chunks)
        return call(
            kernel, (4,), 1,
            [whole((count, width))] * 4
            + [
                pl.BlockSpec((features, cols), lambda i, *_: (0, i)),
                pl.BlockSpec((count, cols), lambda i, *_: (half, i)),
            ],
            out_specs, out_shape, [pltpu.VMEM((count, features), BF)],
            2 * count * features * ff, 2 * features * ff + 6 * count * ff,
        )(place, *pieces, down_weight, der)

    def weight_piece(j):
        block = 512 if ff % 512 == 0 else ff
        half = width // 2
        return call(
            weight_kernel, (ff // block,), 1,
            [whole((SEND, width)), whole((KEEP, width)), pl.BlockSpec((rows, block), lambda i, *_: (0, i))],
            [pl.BlockSpec((half, block), lambda i, *_: (0, i))] * 2,
            [jax.ShapeDtypeStruct((half, ff), BF), jax.ShapeDtypeStruct((half, ff), F32)],
            [pltpu.VMEM((width, rows), BF)],
            2 * rows * width * ff, 2 * rows * ff + 3 * width * ff,
        )(place, sents[j], kepts[j], act)

    moving = grads(sents, 0, 4)
    arrived = [swapped(block, "dp", n // 2) for block in moving]

    held = []
    for j in range(4):
        out, keep = weight_piece(j)
        held.append(keep + swapped(out, "dp", 1).astype(F32))
    near = ((d // 2) ^ t) % 2 == 0
    held_near = []
    for a, b in ((held[0], held[1]), (held[2], held[3])):
        out = jnp.where(near, b, a).astype(BF)
        held_near.append(jnp.where(near, a, b) + swapped(out, "dp", 2).astype(F32))
    far = ((d // 4) ^ (t // 2)) % 2 == 0
    a, b = held_near
    out = jnp.where(far, b, a).astype(BF)
    total = jnp.where(far, a, b) + swapped(out, "dp", 4).astype(F32)
    down_grad = total / math.sqrt(n * home)

    kept_grad = grads(kepts, 1, 1)[0]
    quarter = ff // 4
    hidden_grad = call(
        place_kernel, (4,), 3,
        [pl.BlockSpec((KEEP, quarter), lambda i, *_: (0, i))] + [whole((SEND, quarter))] * 4,
        pl.BlockSpec((BAL, quarter), lambda i, *_: (0, i)),
        jax.ShapeDtypeStruct((BAL, ff), BF),
        [], 0, 2 * ff * (BAL + KEEP + SEND),
    )(place, crop_lengths, crop_moves, kept_grad, *arrived)
    return (hidden_grad, down_grad)


def grad_one_kernel(place, p0, p1, p2, p3, weight, der, out, lhs):
    @pl.when(pl.program_id(0) == 0)
    def _():
        assemble(place, (p0, p1, p2, p3), lhs)

    out[...] = (jnp.dot(lhs[...], weight[...], preferred_element_type=F32) * der[...]).astype(BF)


def solution(mesh):
    from_start = (mesh.shape["dp"], mesh.shape["tensor"]) != (8, 4)
    return jax.shard_map(
        general_shards if from_start else shards,
        mesh=mesh,
        in_specs=(P("dp", "tensor"), P("dp", "tensor"), P(None, "tensor"), P(), P(), P()),
        out_specs=(P("dp", "tensor"), P("dp", "tensor")),
        check_vma=False,
    )


def shifted(block, axis, distance):
    devices = range(lax.axis_size(axis))
    route = [((i - distance) % len(devices), i) for i in devices]
    return lax.ppermute(block, axis, route)


def crop_rows(row_total, crop_sizes, crop_starts):
    crop_ends = jnp.cumsum(crop_sizes)
    crop_begins = crop_ends - crop_sizes
    target_rows = jnp.arange(row_total, dtype=jnp.int32)[:, None]
    inside_crop = (target_rows >= crop_begins[None, :]) & (target_rows < crop_ends[None, :])
    source_rows = jnp.sum(
        jnp.where(inside_crop, crop_starts[None, :] + target_rows - crop_begins[None, :], 0), axis=1
    )
    return (source_rows, jnp.any(inside_crop, axis=1))


def select_rows(row_block, source_rows, valid_rows):
    taken = jnp.take(row_block, source_rows, axis=0)
    return jnp.where(valid_rows[:, None], taken, jnp.zeros((), row_block.dtype))


def gelu_parts(pre_act):
    cumulative = 0.5 * (1.0 + jax.scipy.special.erf(pre_act * inv_root_two))
    activated = pre_act * cumulative
    derivative = cumulative + pre_act * jnp.exp(-0.5 * pre_act * pre_act) * inv_root_tau
    return (activated, derivative)


def local_grads(pre_rows, cot_part, live_rows, layer_scale, down_weight, home_rows):
    cot_full = lax.all_gather(cot_part, "tensor", axis=1, tiled=True)
    scaled = (cot_full.astype(F32) * layer_scale[None, :]).astype(BF)
    activated, derivative = gelu_parts(pre_rows.astype(F32))
    activation = jnp.where(live_rows[:, None], activated, 0.0).astype(BF)
    backward = jnp.dot(scaled, down_weight, preferred_element_type=F32) * derivative
    gradient_rows = jnp.where(live_rows[:, None], backward, 0.0).astype(BF)
    weight_grad = lax.psum_scatter(
        lax.dot_general(scaled, activation, (((0,), (0,)), ((), ())), preferred_element_type=F32),
        "dp",
        scatter_dimension=0,
        tiled=True,
    )
    return (gradient_rows, weight_grad / math.sqrt(lax.axis_size("dp") * home_rows))


def general_shards(hidden_pre, cotangent, down_weight, layer_scale, crop_lengths, crop_moves):
    devices = lax.axis_size("dp")
    half_axis = devices // 2
    device_index = lax.axis_index("dp")
    partner_index = (device_index + half_axis) % devices
    own_lengths = lax.dynamic_index_in_dim(crop_lengths, device_index, 0, keepdims=False)
    own_moves = lax.dynamic_index_in_dim(crop_moves, device_index, 0, keepdims=False)
    partner_lengths = lax.dynamic_index_in_dim(crop_lengths, partner_index, 0, keepdims=False)
    partner_moves = lax.dynamic_index_in_dim(crop_moves, partner_index, 0, keepdims=False)
    home_rows = hidden_pre.shape[0]
    own_starts = jnp.cumsum(own_lengths) - own_lengths
    sent_sizes = own_lengths * own_moves
    kept_sizes = own_lengths * (1 - own_moves)
    arrived = jnp.sum(partner_lengths * partner_moves)
    send_source, send_valid = crop_rows(SEND, sent_sizes, own_starts)
    keep_sizes = jnp.concatenate([kept_sizes, arrived[None]])
    keep_starts = jnp.concatenate([own_starts, jnp.full((1,), home_rows, jnp.int32)])
    keep_source, keep_valid = crop_rows(BAL, keep_sizes, keep_starts)
    live_home = jnp.arange(home_rows, dtype=jnp.int32) < jnp.sum(own_lengths)
    gradient_rows, weight_grad = local_grads(
        hidden_pre, cotangent, live_home, layer_scale, down_weight, home_rows
    )
    outgoing = select_rows(gradient_rows, send_source, send_valid)
    incoming = shifted(outgoing, "dp", half_axis)
    balanced = select_rows(jnp.concatenate([gradient_rows, incoming], 0), keep_source, keep_valid)
    return (balanced, weight_grad)
```

```python
import functools
import math

import jax
import jax.numpy as jnp
from jax import lax
from jax.experimental import pallas as pl
from jax.experimental.pallas import tpu as pltpu
from jax.sharding import PartitionSpec as P

SEND = 528
KEEP = 528
TILE = 16
EARLY = 128
LATE = SEND - EARLY
SLOTS = 4
BAL = 720
BF = jnp.bfloat16
F32 = jnp.float32

inv_root_two = 0.7071067811865476
inv_root_tau = 0.3989422804014327


def call(kernel, grid, scalars, in_specs, out_specs, out_shape, scratch, flops, nbytes, trans=0):
    return pl.pallas_call(
        kernel,
        grid_spec=pltpu.PrefetchScalarGridSpec(
            num_scalar_prefetch=scalars,
            grid=grid,
            in_specs=in_specs,
            out_specs=out_specs,
            scratch_shapes=scratch,
        ),
        out_shape=out_shape,
        cost_estimate=pl.CostEstimate(flops=1, bytes_accessed=1, transcendentals=0),
        compiler_params=pltpu.CompilerParams(vmem_limit_bytes=48 * 1024 * 1024),
    )


def whole(shape):
    return pl.BlockSpec(shape, lambda *_: (0,) * len(shape))


def lengths_of(meta, d):
    return [meta[2 + d * SLOTS + j] for j in range(SLOTS)]


def moves_of(meta, n, d):
    return [meta[2 + (n + d) * SLOTS + j] for j in range(SLOTS)]


def kept_total(meta, n, d):
    return sum(a * (1 - b) for a, b in zip(lengths_of(meta, d), moves_of(meta, n, d)))


def picks(meta, n, moved, first, rows, home):
    d = meta[0]
    at = lax.broadcasted_iota(jnp.int32, (rows, 1), 0) - first
    source = jnp.full((rows, 1), -1, jnp.int32)
    begin = jnp.int32(0)
    start = jnp.int32(0)
    for length, move in zip(lengths_of(meta, d), moves_of(meta, n, d)):
        size = length * (move if moved else 1 - move)
        inside = (at >= begin) & (at < begin + size)
        source = jnp.where(inside, at + (start - begin), source)
        begin = begin + size
        start = start + length
    columns = lax.broadcasted_iota(jnp.int32, (rows, home), 1)
    return jnp.where(columns == source, 1.0, 0.0).astype(BF)


def sent_first(meta, n):
    partner = lax.rem(meta[0] + n // 2, n)
    return lax.rem(kept_total(meta, n, partner), TILE)


def early_picks(meta, n, home):
    return picks(meta, n, True, sent_first(meta, n), EARLY, home)


def late_picks(meta, n, home):
    return picks(meta, n, True, sent_first(meta, n) - EARLY, LATE, home)


def kept_picks(meta, n, home):
    return picks(meta, n, False, 0, KEEP, home)


def scaled_rows(pick, cot, scale):
    rows = jnp.dot(pick, cot[...], preferred_element_type=F32)
    return (rows * scale[...]).astype(BF)


def first_kernel(n, meta, cot, scale, pre, late_out, early_out, pre_a, pre_b):
    home = cot.shape[0]
    late_out[...] = scaled_rows(late_picks(meta, n, home), cot, scale)
    early = early_picks(meta, n, home)
    early_out[...] = scaled_rows(early, cot, scale)
    rows = jnp.dot(early, pre[...], preferred_element_type=F32).astype(BF)
    cut = pre_a.shape[1]
    pre_a[...] = rows[:, :cut]
    pre_b[...] = rows[:, cut:]


def rest_kernel(n, meta, cot, scale, rest_out):
    home = cot.shape[0]
    rest_out[0:EARLY, :] = scaled_rows(early_picks(meta, n, home), cot, scale)
    rest_out[EARLY:, :] = scaled_rows(kept_picks(meta, n, home), cot, scale)


def gelu_kernel(n, meta, pre, act_out, der_out, pick, rows_f32):
    home = pre.shape[0]

    @pl.when(pl.program_id(0) == 0)
    def _():
        pick[0:LATE, :] = late_picks(meta, n, home)
        pick[LATE:SEND, :] = early_picks(meta, n, home)
        pick[SEND:, :] = kept_picks(meta, n, home)

    rows_f32[...] = jnp.dot(pick[...], pre[...], preferred_element_type=F32)
    step = 3 * TILE

    def body(i, _):
        at = pl.ds(pl.multiple_of(i * step, step), step)
        x = rows_f32[at, :]
        cumulative = 0.5 * (1.0 + lax.erf(x * inv_root_two))
        act_out[at, :] = (x * cumulative).astype(BF)
        der_out[at, :] = cumulative + x * jnp.exp(-0.5 * x * x) * inv_root_tau
        return 0

    lax.fori_loop(0, (SEND + KEEP) // step, body, 0)


def assemble(meta, pieces, lhs):
    width = pieces[0].shape[1]
    for j, piece in enumerate(pieces):
        at = pl.ds(pl.multiple_of((meta[1] ^ j) * width, 128), width)
        lhs[:, at] = piece[...]


def late_kernel(meta, p0, p1, p2, p3, weight, der, *rest):
    outs, lhs = rest[:-1], rest[-1]
    step = pl.program_id(0)

    @pl.when(step == 0)
    def _():
        assemble(meta, (p0, p1, p2, p3), lhs)

    value = (jnp.dot(lhs[...], weight[...], preferred_element_type=F32) * der[...]).astype(BF)
    for c, out in enumerate(outs):

        @pl.when(step == c)
        def _():
            out[...] = value


def kept_kernel(meta, r0, r1, r2, r3, weight, der, out, lhs):
    @pl.when(pl.program_id(0) == 0)
    def _():
        assemble(meta, [r.at[pl.ds(EARLY, KEEP), :] for r in (r0, r1, r2, r3)], lhs)

    out[...] = (jnp.dot(lhs[...], weight[...], preferred_element_type=F32) * der[...]).astype(BF)


def early_kernel(meta, p0, p1, p2, p3, weight, pre_a, pre_b, out, lhs, acc, pre):
    step = pl.program_id(0)

    @pl.when(step == 0)
    def _():
        assemble(meta, (p0, p1, p2, p3), lhs)
        pre[...] = pre_a[...]

    @pl.when(step > 0)
    def _():
        pre[...] = pre_b[...]

    acc[...] = jnp.dot(lhs[...], weight[...], preferred_element_type=F32)
    for r in range(0, EARLY, TILE):
        at = slice(r, r + TILE)
        x = pre[at, :].astype(F32)
        cumulative = 0.5 * (1.0 + lax.erf(x * inv_root_two))
        derivative = cumulative + x * jnp.exp(-0.5 * x * x) * inv_root_tau
        out[at, :] = (acc[at, :] * derivative).astype(BF)


def transposed(meta, late, rest):
    both = jnp.concatenate([late[...], rest[...]], axis=0).T
    half = both.shape[0] // 2
    mine = meta[0] % 2 == 0
    lo, hi = both[:half], both[half:]
    return jnp.where(mine, hi, lo), jnp.where(mine, lo, hi)


def weight_kernel(meta, late, rest, act, send_out, keep_out, lhs):
    half = lhs.shape[0] // 2

    @pl.when(pl.program_id(0) == 0)
    def _():
        lhs[0:half, :], lhs[half:, :] = transposed(meta, late, rest)

    value = jnp.dot(lhs[...], act[...], preferred_element_type=F32)
    send_out[...] = value[:half].astype(BF)
    keep_out[...] = value[half:]


def weight_pair_kernel(meta, late_a, rest_a, late_b, rest_b, act, *rest):
    outs, lhs = rest[:-1], rest[-1]
    half = lhs.shape[0] // 4
    keeps_a = (meta[0] // 2 + meta[1]) % 2 == 0

    @pl.when(pl.program_id(0) == 0)
    def _():
        a = transposed(meta, late_a, rest_a)
        b = transposed(meta, late_b, rest_b)
        for i in range(2):
            lhs[i * half : (i + 1) * half, :] = jnp.where(keeps_a, b[i], a[i])
            lhs[(i + 2) * half : (i + 3) * half, :] = jnp.where(keeps_a, a[i], b[i])

    value = jnp.dot(lhs[...], act[...], preferred_element_type=F32)
    for i, out in enumerate(outs):
        out[...] = value[i * half : (i + 1) * half].astype(out.dtype)


def place_kernel(n, meta, kept, early, *rest):
    late, out = rest[:-1], rest[-1]
    count = kept_total(meta, n, meta[0])
    first = jnp.minimum(count - lax.rem(count, TILE), BAL - SEND)
    first = pl.multiple_of(first, TILE)
    out[0:KEEP, :] = kept[...]
    out[KEEP:, :] = jnp.zeros((out.shape[0] - KEEP, out.shape[1]), BF)
    step = pl.program_id(0)

    def put(block, at):
        rows = lax.broadcasted_iota(jnp.int32, (block.shape[0], 1), 0) + at
        window = pl.ds(at, block.shape[0])
        out[window, :] = jnp.where(rows < count, out[window, :], block[...])

    put(early, first)
    for c, block in enumerate(late):

        @pl.when(step == c)
        def _():
            put(block, pl.multiple_of(first + EARLY, TILE))


def swapped(block, axis, distance):
    n = lax.axis_size(axis)
    return lax.ppermute(block, axis, [(i, i ^ distance) for i in range(n)])


def after(value, *others):
    return lax.optimization_barrier((value, *others))[0]


def gathered(block, *others):
    far = after(swapped(block, "tensor", 2), *others)
    return (block, swapped(block, "tensor", 1), far, swapped(far, "tensor", 1))


def shards(hidden_pre, cotangent, down_weight, layer_scale, crop_lengths, crop_moves):
    home, ff = hidden_pre.shape
    width = cotangent.shape[1]
    features = down_weight.shape[0]
    half = width // 2
    n = lax.axis_size("dp")
    d = lax.axis_index("dp").astype(jnp.int32)
    t = lax.axis_index("tensor").astype(jnp.int32)
    meta = jnp.concatenate([jnp.stack([d, t]), crop_lengths.reshape(-1), crop_moves.reshape(-1)])
    rows = SEND + KEEP
    scale = layer_scale.reshape(1, features)
    scale_spec = pl.BlockSpec((1, width), lambda i, meta: (0, meta[1]))

    def shape(a, b, dtype=BF):
        return jax.ShapeDtypeStruct((a, b), dtype)

    block = 512
    steps = ff // block
    late, early, pre_a, pre_b = call(
        functools.partial(first_kernel, n), (1,), 1,
        [whole((home, width)), scale_spec, whole((home, ff))],
        [whole((LATE, width)), whole((EARLY, width)), whole((EARLY, block)), whole((EARLY, ff - block))],
        [shape(LATE, width), shape(EARLY, width), shape(EARLY, block), shape(EARLY, ff - block)],
        [], 2 * home * (SEND * width + EARLY * ff), 2 * home * (ff + width),
    )(meta, cotangent, scale, hidden_pre)

    arrived_early = swapped(early, "dp", n // 2)
    arrived_a = swapped(pre_a, "dp", n // 2)
    arrived_b = swapped(pre_b, "dp", n // 2)
    lates = gathered(late, arrived_early, arrived_a)

    rest = call(
        functools.partial(rest_kernel, n), (1,), 1,
        [whole((home, width)), scale_spec], whole((EARLY + KEEP, width)), shape(EARLY + KEEP, width),
        [], 2 * home * (EARLY + KEEP) * width, 4 * home * width,
    )(after(meta, late), cotangent, scale)
    rests = gathered(rest)

    cols = 256
    act, der = call(
        functools.partial(gelu_kernel, n), (ff // cols,), 1,
        [pl.BlockSpec((home, cols), lambda i, *_: (0, i))],
        [pl.BlockSpec((rows, cols), lambda i, *_: (0, i))] * 2,
        [shape(rows, ff), shape(rows, ff, F32)],
        [pltpu.VMEM((rows, home), BF), pltpu.VMEM((rows, cols), F32)],
        2 * rows * home * ff, 2 * home * ff + 6 * rows * ff, 2 * rows * ff,
    )(after(meta, rest), hidden_pre)

    act_spec = pl.BlockSpec((rows, block), lambda i, *_: (0, i))
    half_spec = pl.BlockSpec((half, block), lambda i, *_: (0, i))
    weight_spec = pl.BlockSpec((features, block), lambda i, *_: (0, i))

    def weight_piece(meta, j):
        return call(
            weight_kernel, (steps,), 1,
            [whole((LATE, width)), whole((EARLY + KEEP, width)), act_spec],
            [half_spec] * 2, [shape(half, ff), shape(half, ff, F32)],
            [pltpu.VMEM((width, rows), BF)],
            2 * rows * width * ff, 2 * rows * ff + 3 * width * ff,
        )(meta, lates[j], rests[j], act)

    out_0, keep_0 = weight_piece(meta, 0)
    got_0 = swapped(out_0, "dp", 1)

    wide = ff // 2
    moving = call(
        late_kernel, (2,), 1,
        [whole((LATE, width))] * 4
        + [pl.BlockSpec((features, wide), lambda i, *_: (0, i)), pl.BlockSpec((LATE, wide), lambda i, *_: (0, i))],
        [whole((LATE, wide))] * 2, [shape(LATE, wide)] * 2,
        [pltpu.VMEM((LATE, features), BF)],
        2 * LATE * features * ff, 2 * features * ff + 6 * LATE * ff,
    )(after(meta, out_0), *lates, down_weight, der)
    arrived = [swapped(block, "dp", n // 2) for block in moving]

    out_1, keep_1 = weight_piece(after(meta, *moving, arrived_b), 1)
    got_1 = swapped(out_1, "dp", 1)

    send_a, send_b, keep_a, keep_b = call(
        weight_pair_kernel, (steps,), 1,
        [whole((LATE, width)), whole((EARLY + KEEP, width))] * 2 + [act_spec],
        [half_spec] * 4, [shape(half, ff)] * 2 + [shape(half, ff, F32)] * 2,
        [pltpu.VMEM((2 * width, rows), BF)],
        4 * rows * width * ff, 2 * rows * ff + 6 * width * ff,
    )(after(meta, out_1), lates[2], rests[2], lates[3], rests[3], act)
    got_a = swapped(send_a, "dp", 2)
    got_b = swapped(send_b, "dp", 2)

    arrived_earlies = gathered(arrived_early)
    early_grad = call(
        early_kernel, (steps,), 1,
        [whole((EARLY, width))] * 4
        + [weight_spec, whole((EARLY, block)), pl.BlockSpec((EARLY, block), lambda i, *_: (0, jnp.maximum(i - 1, 0)))],
        pl.BlockSpec((EARLY, block), lambda i, *_: (0, i)), shape(EARLY, ff),
        [pltpu.VMEM((EARLY, features), BF), pltpu.VMEM((EARLY, block), F32), pltpu.VMEM((EARLY, block), BF)],
        2 * EARLY * features * ff, 2 * features * ff + 4 * EARLY * ff, EARLY * ff,
    )(after(meta, send_a), *arrived_earlies, down_weight, arrived_a, arrived_b)

    kept_grad = call(
        kept_kernel, (steps,), 1,
        [whole((EARLY + KEEP, width))] * 4 + [weight_spec, pl.BlockSpec((KEEP, block), lambda i, *_: (1, i))],
        pl.BlockSpec((KEEP, block), lambda i, *_: (0, i)), shape(KEEP, ff),
        [pltpu.VMEM((KEEP, features), BF)],
        2 * KEEP * features * ff, 2 * features * ff + 6 * KEEP * ff,
    )(after(meta, early_grad), *rests, down_weight, der)

    near = ((d // 2) ^ t) % 2 == 0
    got_0 = after(got_0, arrived[0])
    got_a = after(got_a, arrived[0])
    held_0 = keep_0 + got_0.astype(F32)
    held_1 = keep_1 + got_1.astype(F32)
    out_n = jnp.where(near, held_1, held_0).astype(BF)
    first = jnp.where(near, held_0, held_1) + swapped(out_n, "dp", 2).astype(F32)
    out_x = (keep_a + got_a.astype(F32)).astype(BF)
    second = keep_b + got_b.astype(F32) + swapped(out_x, "dp", 1).astype(F32)
    far = ((d // 4) ^ (t // 2)) % 2 == 0
    first = after(first, arrived[1])
    out_f = jnp.where(far, second, first).astype(BF)
    total = jnp.where(far, first, second) + swapped(out_f, "dp", 4).astype(F32)
    down_grad = total / math.sqrt(n * home)

    hidden_grad = call(
        functools.partial(place_kernel, n), (2,), 1,
        [pl.BlockSpec((KEEP, wide), lambda i, *_: (0, i)), pl.BlockSpec((EARLY, wide), lambda i, *_: (0, i))]
        + [whole((LATE, wide))] * 2,
        pl.BlockSpec((BAL, wide), lambda i, *_: (0, i)), shape(BAL, ff),
        [], 0, 2 * ff * (BAL + KEEP + SEND),
    )(meta, kept_grad, early_grad, *arrived)
    return (hidden_grad, down_grad)


def solution(mesh):
    pairs_and_fours = (mesh.shape["dp"], mesh.shape["tensor"]) == (8, 4)
    return jax.shard_map(
        shards if pairs_and_fours else general_shards,
        mesh=mesh,
        in_specs=(P("dp", "tensor"), P("dp", "tensor"), P(None, "tensor"), P(), P(), P()),
        out_specs=(P("dp", "tensor"), P("dp", "tensor")),
        check_vma=False,
    )


def shifted(block, axis, distance):
    devices = range(lax.axis_size(axis))
    route = [((i - distance) % len(devices), i) for i in devices]
    return lax.ppermute(block, axis, route)


def crop_rows(row_total, crop_sizes, crop_starts):
    crop_ends = jnp.cumsum(crop_sizes)
    crop_begins = crop_ends - crop_sizes
    target_rows = jnp.arange(row_total, dtype=jnp.int32)[:, None]
    inside_crop = (target_rows >= crop_begins[None, :]) & (target_rows < crop_ends[None, :])
    source_rows = jnp.sum(
        jnp.where(inside_crop, crop_starts[None, :] + target_rows - crop_begins[None, :], 0), axis=1
    )
    return (source_rows, jnp.any(inside_crop, axis=1))


def select_rows(row_block, source_rows, valid_rows):
    taken = jnp.take(row_block, source_rows, axis=0)
    return jnp.where(valid_rows[:, None], taken, jnp.zeros((), row_block.dtype))


def gelu_parts(pre_act):
    cumulative = 0.5 * (1.0 + jax.scipy.special.erf(pre_act * inv_root_two))
    activated = pre_act * cumulative
    derivative = cumulative + pre_act * jnp.exp(-0.5 * pre_act * pre_act) * inv_root_tau
    return (activated, derivative)


def local_grads(pre_rows, cot_part, live_rows, layer_scale, down_weight, home_rows):
    cot_full = lax.all_gather(cot_part, "tensor", axis=1, tiled=True)
    scaled = (cot_full.astype(F32) * layer_scale[None, :]).astype(BF)
    activated, derivative = gelu_parts(pre_rows.astype(F32))
    activation = jnp.where(live_rows[:, None], activated, 0.0).astype(BF)
    backward = jnp.dot(scaled, down_weight, preferred_element_type=F32) * derivative
    gradient_rows = jnp.where(live_rows[:, None], backward, 0.0).astype(BF)
    weight_grad = lax.psum_scatter(
        lax.dot_general(scaled, activation, (((0,), (0,)), ((), ())), preferred_element_type=F32),
        "dp",
        scatter_dimension=0,
        tiled=True,
    )
    return (gradient_rows, weight_grad / math.sqrt(lax.axis_size("dp") * home_rows))


def general_shards(hidden_pre, cotangent, down_weight, layer_scale, crop_lengths, crop_moves):
    devices = lax.axis_size("dp")
    half_axis = devices // 2
    device_index = lax.axis_index("dp")
    partner_index = (device_index + half_axis) % devices
    own_lengths = lax.dynamic_index_in_dim(crop_lengths, device_index, 0, keepdims=False)
    own_moves = lax.dynamic_index_in_dim(crop_moves, device_index, 0, keepdims=False)
    partner_lengths = lax.dynamic_index_in_dim(crop_lengths, partner_index, 0, keepdims=False)
    partner_moves = lax.dynamic_index_in_dim(crop_moves, partner_index, 0, keepdims=False)
    home_rows = hidden_pre.shape[0]
    own_starts = jnp.cumsum(own_lengths) - own_lengths
    sent_sizes = own_lengths * own_moves
    kept_sizes = own_lengths * (1 - own_moves)
    arrived = jnp.sum(partner_lengths * partner_moves)
    send_source, send_valid = crop_rows(SEND, sent_sizes, own_starts)
    keep_sizes = jnp.concatenate([kept_sizes, arrived[None]])
    keep_starts = jnp.concatenate([own_starts, jnp.full((1,), home_rows, jnp.int32)])
    keep_source, keep_valid = crop_rows(BAL, keep_sizes, keep_starts)
    live_home = jnp.arange(home_rows, dtype=jnp.int32) < jnp.sum(own_lengths)
    gradient_rows, weight_grad = local_grads(
        hidden_pre, cotangent, live_home, layer_scale, down_weight, home_rows
    )
    outgoing = select_rows(gradient_rows, send_source, send_valid)
    incoming = shifted(outgoing, "dp", half_axis)
    balanced = select_rows(jnp.concatenate([gradient_rows, incoming], 0), keep_source, keep_valid)
    return (balanced, weight_grad)
```

```python
import functools
import math

import jax
import jax.numpy as jnp
from jax import lax
from jax.experimental import pallas as pl
from jax.experimental.pallas import tpu as pltpu
from jax.sharding import PartitionSpec as P

SEND = 528
KEEP = 528
TILE = 16
EARLY = 128
LATE = SEND - EARLY
SLOTS = 4
BAL = 720
BF = jnp.bfloat16
F32 = jnp.float32

inv_root_two = 0.7071067811865476
inv_root_tau = 0.3989422804014327


def kernel_call(kernel, out_shape, in_specs, out_specs, scratch=(), grid=(1,)):
    return pl.pallas_call(
        kernel,
        grid_spec=pltpu.PrefetchScalarGridSpec(
            num_scalar_prefetch=1,
            grid=grid,
            in_specs=in_specs,
            out_specs=out_specs,
            scratch_shapes=list(scratch),
        ),
        out_shape=out_shape,
        cost_estimate=pl.CostEstimate(flops=1, bytes_accessed=1, transcendentals=0),
        compiler_params=pltpu.CompilerParams(vmem_limit_bytes=16 * 1024 * 1024),
    )


IN_VMEM = pl.BlockSpec(memory_space=pltpu.VMEM)
IN_HBM = pl.BlockSpec(memory_space=pltpu.HBM)


def shape(a, b, dtype=BF):
    return jax.ShapeDtypeStruct((a, b), dtype)


def lengths_of(meta, d):
    return [meta[j, d] for j in range(SLOTS)]


def moves_of(meta, d):
    return [meta[SLOTS + j, d] for j in range(SLOTS)]


def dp_at(meta):
    return meta[2 * SLOTS, 0]


def tensor_at(meta):
    return meta[2 * SLOTS, 1]


def kept_total(meta, d):
    return sum(a * (1 - b) for a, b in zip(lengths_of(meta, d), moves_of(meta, d)))


def picks(meta, moved, first, rows, home):
    d = dp_at(meta)
    at = lax.broadcasted_iota(jnp.int32, (rows, 1), 0) - first
    source = jnp.full((rows, 1), -1, jnp.int32)
    begin = jnp.int32(0)
    start = jnp.int32(0)
    for length, move in zip(lengths_of(meta, d), moves_of(meta, d)):
        size = length * (move if moved else 1 - move)
        inside = (at >= begin) & (at < begin + size)
        source = jnp.where(inside, at + (start - begin), source)
        begin = begin + size
        start = start + length
    columns = lax.broadcasted_iota(jnp.int32, (rows, home), 1)
    return jnp.where(columns == source, 1.0, 0.0).astype(BF)


def sent_first(meta):
    n = meta.shape[1]
    partner = lax.rem(dp_at(meta) + n // 2, n)
    return lax.rem(kept_total(meta, partner), TILE)


def early_picks(meta, home):
    return picks(meta, True, sent_first(meta), EARLY, home)


def late_picks(meta, home):
    return picks(meta, True, sent_first(meta) - EARLY, LATE, home)


def kept_picks(meta, home):
    return picks(meta, False, 0, KEEP, home)


def scaled_rows(meta, pick, cot, scale):
    width = cot.shape[1]
    rows = jnp.dot(pick, cot[...], preferred_element_type=F32)
    own = scale[pl.ds(pl.multiple_of(tensor_at(meta) * width, 128), width)]
    return (rows * own[None, :]).astype(BF)


def first_kernel(meta, cot_hbm, scale_hbm, pre_hbm, late_out, early_out, *rest):
    pre_outs, (cot, scale, pre, sems) = rest[:-4], rest[-4:]
    home = cot.shape[0]
    pairs = ((cot_hbm, cot), (scale_hbm, scale), (pre_hbm, pre))
    copies = [pltpu.make_async_copy(a, b, sems.at[i]) for i, (a, b) in enumerate(pairs)]
    for copy in copies:
        copy.start()
    early = early_picks(meta, home)
    late = late_picks(meta, home)
    copies[0].wait()
    copies[1].wait()
    early_out[...] = scaled_rows(meta, early, cot, scale)
    late_out[...] = scaled_rows(meta, late, cot, scale)
    copies[2].wait()
    at = 0
    for out in pre_outs:
        columns = slice(at, at + out.shape[1])
        out[...] = jnp.dot(early, pre[:, columns], preferred_element_type=F32).astype(BF)
        at = columns.stop


def rest_kernel(meta, cot_hbm, scale_hbm, rest_out, cot, scale, sems):
    home = cot.shape[0]
    pairs = ((cot_hbm, cot), (scale_hbm, scale))
    copies = [pltpu.make_async_copy(a, b, sems.at[i]) for i, (a, b) in enumerate(pairs)]
    for copy in copies:
        copy.start()
    early = early_picks(meta, home)
    kept = kept_picks(meta, home)
    for copy in copies:
        copy.wait()
    rest_out[0:EARLY, :] = scaled_rows(meta, early, cot, scale)
    rest_out[EARLY:, :] = scaled_rows(meta, kept, cot, scale)


def gelu_and_slope(x):
    cumulative = 0.5 * (1.0 + lax.erf(x * inv_root_two))
    return x * cumulative, cumulative + x * jnp.exp(-0.5 * x * x) * inv_root_tau


def gelu_kernel(base, block, meta, pre_hbm, act_out, der_out, pick, rows_f32, pre, sems):
    home = pre.shape[1]
    rows = pick.shape[0]
    blocks = act_out.shape[1] // block

    def fetch(i):
        columns = pl.ds(base + i * block, block)
        return pltpu.make_async_copy(pre_hbm.at[:, columns], pre.at[i], sems.at[i])

    for i in range(blocks):
        fetch(i).start()
    pick[0:LATE, :] = late_picks(meta, home)
    pick[LATE:SEND, :] = early_picks(meta, home)
    pick[SEND:, :] = kept_picks(meta, home)
    step = 3 * TILE
    for i in range(blocks):
        fetch(i).wait()
        rows_f32[...] = jnp.dot(pick[...], pre[i], preferred_element_type=F32)
        columns = slice(i * block, (i + 1) * block)

        def body(k, _):
            at = pl.ds(pl.multiple_of(k * step, step), step)
            value, slope = gelu_and_slope(rows_f32[at, :])
            act_out[at, columns] = value.astype(BF)
            der_out[at, columns] = slope
            return 0

        lax.fori_loop(0, rows // step, body, 0)


def assemble(meta, pieces, lhs):
    width = pieces[0].shape[1]
    for j, piece in enumerate(pieces):
        at = pl.ds(pl.multiple_of((tensor_at(meta) ^ j) * width, 128), width)
        lhs[:, at] = piece[...]


def grad_kernel(first_piece_row, first_row, block, meta, p0, p1, p2, p3, weight, der_a, der_b, out, lhs):
    rows = out.shape[0]
    assemble(meta, [p.at[pl.ds(first_piece_row, rows), :] for p in (p0, p1, p2, p3)], lhs)
    half = der_a.shape[1]
    for at in range(0, out.shape[1], block):
        columns = slice(at, at + block)
        der = der_a if at < half else der_b
        slope = der[first_row : first_row + rows, at % half : at % half + block]
        value = jnp.dot(lhs[...], weight[:, columns], preferred_element_type=F32)
        out[:, columns] = (value * slope).astype(BF)


def early_kernel(block, meta, p0, p1, p2, p3, weight, *rest):
    pres, (out, lhs, acc) = rest[:-3], rest[-3:]
    assemble(meta, (p0, p1, p2, p3), lhs)
    at = 0
    for pre in pres:
        for c in range(0, pre.shape[1], block):
            columns = slice(at + c, at + c + block)
            acc[...] = jnp.dot(lhs[...], weight[:, columns], preferred_element_type=F32)

            def body(k, _):
                rows = pl.ds(pl.multiple_of(k * TILE, TILE), TILE)
                _, slope = gelu_and_slope(pre[rows, c : c + block].astype(F32))
                out[rows, columns] = (acc[rows, :] * slope).astype(BF)
                return 0

            lax.fori_loop(0, EARLY // TILE, body, 0)
        at += pre.shape[1]


def weight_kernel(count, block, meta, *refs):
    pieces, (act, send, keep, lhs) = refs[: 2 * count], refs[2 * count :]
    half = pieces[0].shape[1] // 2
    mine = dp_at(meta) % 2 == 0
    for i in range(count):
        both = jnp.concatenate([pieces[2 * i][...], pieces[2 * i + 1][...]], axis=0).T
        lo, hi = both[:half], both[half:]
        lhs[i * half : (i + 1) * half, :] = jnp.where(mine, hi, lo)
        lhs[(count + i) * half : (count + i + 1) * half, :] = jnp.where(mine, lo, hi)
    for at in range(0, act.shape[1], block):
        columns = slice(at, at + block)
        value = jnp.dot(lhs[...], act[:, columns], preferred_element_type=F32)
        send[:, columns] = value[: count * half].astype(BF)
        keep[:, columns] = value[count * half :]


def near_kernel(count, meta, *refs):
    keeps, gots, (out, mine) = refs[:count], refs[count : 2 * count], refs[2 * count :]
    half = out.shape[0] // 2
    parts = [(k, g, at) for k, g in zip(keeps, gots) for at in range(0, k.shape[0], half)]
    keeps_even = (dp_at(meta) // 2 + tensor_at(meta)) % 2 == 0
    step = 2 * TILE

    for pair in range(2):
        (k0, g0, a0), (k1, g1, a1) = parts[2 * pair], parts[2 * pair + 1]

        def body(i, _):
            def rows(at):
                return pl.ds(pl.multiple_of(at + i * step, TILE), step)

            even = k0[rows(a0), :] + g0[rows(a0), :].astype(F32)
            odd = k1[rows(a1), :] + g1[rows(a1), :].astype(F32)
            out[rows(pair * half), :] = jnp.where(keeps_even, odd, even).astype(BF)
            mine[rows(pair * half), :] = jnp.where(keeps_even, even, odd)
            return 0

        lax.fori_loop(0, half // step, body, 0)


def far_kernel(meta, held, got, out, mine):
    half = out.shape[0]
    keeps_first = (dp_at(meta) // 4 + tensor_at(meta) // 2) % 2 == 0
    step = 2 * TILE

    def body(i, _):
        first = pl.ds(pl.multiple_of(i * step, TILE), step)
        second = pl.ds(pl.multiple_of(half + i * step, TILE), step)
        a = held[first, :] + got[first, :].astype(F32)
        b = held[second, :] + got[second, :].astype(F32)
        out[first, :] = jnp.where(keeps_first, b, a).astype(BF)
        mine[first, :] = jnp.where(keeps_first, a, b)
        return 0

    lax.fori_loop(0, half // step, body, 0)


def place_kernel(meta, kept, early, late, out):
    count = kept_total(meta, dp_at(meta))
    first = jnp.minimum(count - lax.rem(count, TILE), BAL - SEND)
    first = pl.multiple_of(first, TILE)
    out[0:KEEP, :] = kept[...]
    out[KEEP:, :] = jnp.zeros((out.shape[0] - KEEP, out.shape[1]), BF)
    for block, at in ((early, first), (late, pl.multiple_of(first + EARLY, TILE))):
        rows = lax.broadcasted_iota(jnp.int32, (block.shape[0], 1), 0) + at
        window = pl.ds(at, block.shape[0])
        out[window, :] = jnp.where(rows < count, out[window, :], block[...])


def swapped(block, axis, distance):
    n = lax.axis_size(axis)
    return lax.ppermute(block, axis, [(i, i ^ distance) for i in range(n)])


def after(value, *others):
    return lax.optimization_barrier((value, *others))[0]


def shards(hidden_pre, cotangent, down_weight, layer_scale, crop_lengths, crop_moves):
    home, ff = hidden_pre.shape
    width = cotangent.shape[1]
    features = down_weight.shape[0]
    half, wide = width // 2, ff // 2
    rows = SEND + KEEP
    n = lax.axis_size("dp")
    d = lax.axis_index("dp").astype(jnp.int32)
    t = lax.axis_index("tensor").astype(jnp.int32)
    column = lax.broadcasted_iota(jnp.int32, (1, n), 1)
    own = jnp.where(column == 0, d, jnp.where(column == 1, t, 0))
    meta = jnp.concatenate([crop_lengths.T, crop_moves.T, own])
    vmem = pltpu.VMEM
    hidden_pre, cotangent, layer_scale = (
        pltpu.with_memory_space_constraint(x, pltpu.HBM) for x in (hidden_pre, cotangent, layer_scale)
    )
    sems = pltpu.SemaphoreType.DMA

    cuts = (256, 768, ff - 1024)
    late, early, *pres = kernel_call(
        first_kernel,
        [shape(LATE, width), shape(EARLY, width)] + [shape(EARLY, c) for c in cuts],
        [IN_HBM] * 3, [IN_VMEM] * 5,
        [vmem((home, width), BF), vmem((features,), F32), vmem((home, ff), BF), sems((3,))],
    )(meta, cotangent, layer_scale, hidden_pre)
    arrived_early = swapped(early, "dp", n // 2)
    arrived_pres = [swapped(pre, "dp", n // 2) for pre in pres]

    rest = kernel_call(
        rest_kernel, shape(EARLY + KEEP, width), [IN_HBM] * 2, IN_VMEM,
        [vmem((home, width), BF), vmem((features,), F32), sems((2,))],
    )(after(meta, late), cotangent, layer_scale)

    def gelu(meta, base):
        block = 256
        return kernel_call(
            functools.partial(gelu_kernel, base, block),
            [shape(rows, wide), shape(rows, wide, F32)],
            [IN_HBM], [IN_VMEM] * 2,
            [vmem((rows, home), BF), vmem((rows, block), F32), vmem((wide // block, home, block), BF),
             sems((wide // block,))],
        )(meta, hidden_pre)

    def weight_part(meta, pieces, act):
        count = len(pieces)
        return kernel_call(
            functools.partial(weight_kernel, count, 256),
            [shape(count * half, wide), shape(count * half, wide, F32)],
            [IN_VMEM] * (2 * count + 1), [IN_VMEM] * 2,
            [vmem((count * width, rows), BF)],
        )(meta, *[lates[j] if k == 0 else rests[j] for j in pieces for k in range(2)], act)

    def grads(meta, pieces, first_piece_row, first_row, count):
        return kernel_call(
            functools.partial(grad_kernel, first_piece_row, first_row, 256),
            shape(count, ff), [IN_VMEM] * 7, IN_VMEM, [vmem((count, features), BF)],
        )(meta, *pieces, down_weight, der_a, der_b)

    act_a, der_a = gelu(after(meta, rest), 0)
    late_c, late_y = swapped(late, "tensor", 1), swapped(late, "tensor", 2)
    late_y = after(late_y, act_a, late_c, arrived_early, arrived_pres[0])
    late_yc = swapped(late_y, "tensor", 1)
    lates, rests = (late,), (rest,)
    send_0, keep_0 = weight_part(after(meta, late_y), (0,), act_a)
    got_0 = swapped(send_0, "dp", 1)

    rest_sent = after(rest, late_y)
    rest_c, rest_y = swapped(rest_sent, "tensor", 1), swapped(rest_sent, "tensor", 2)
    act_b, der_b = gelu(after(meta, send_0), wide)
    lates, rests = (late, late_c, late_y, late_yc), (rest, rest_c)
    send_1, keep_1 = weight_part(after(meta, act_b, got_0, arrived_pres[1]), (1,), act_a)
    got_1 = swapped(send_1, "dp", 1)

    rest_y = after(rest_y, send_1)
    rest_yc = swapped(rest_y, "tensor", 1)
    rests = (rest, rest_c, rest_y, rest_yc)
    early_sent = after(arrived_early, rest_y)
    early_c, early_y = swapped(early_sent, "tensor", 1), swapped(early_sent, "tensor", 2)
    moving = grads(after(meta, rest_y), lates, 0, 0, LATE)
    arrived = swapped(moving, "dp", n // 2)

    early_y = after(early_y, moving, early_c)
    early_yc = swapped(early_y, "tensor", 1)
    send_23, keep_23 = weight_part(after(meta, early_y, arrived_pres[2], got_1), (2, 3), act_a)
    got_23 = swapped(send_23, "dp", 1)
    send_b, keep_b = weight_part(after(meta, send_23), (0, 1, 2, 3), act_b)
    kept_grad = grads(after(meta, send_b), rests, EARLY, SEND, KEEP)

    def near_step(meta, keeps, gots):
        count = len(keeps)
        return kernel_call(
            functools.partial(near_kernel, count),
            [shape(width, wide), shape(width, wide, F32)], [IN_VMEM] * (2 * count), [IN_VMEM] * 2,
        )(meta, *keeps, *gots)

    def far_step(meta, mine, got):
        return kernel_call(
            far_kernel, [shape(half, wide), shape(half, wide, F32)], [IN_VMEM] * 2, [IN_VMEM] * 2
        )(meta, mine, got)

    out_na, mine_a = near_step(after(meta, kept_grad), (keep_0, keep_1, keep_23), (got_0, got_1, got_23))
    got_na = swapped(out_na, "dp", 2)
    got_b = swapped(after(send_b, out_na), "dp", 1)

    early_grad = kernel_call(
        functools.partial(early_kernel, 256), shape(EARLY, ff), [IN_VMEM] * (5 + len(cuts)), IN_VMEM,
        [vmem((EARLY, features), BF), vmem((EARLY, 256), F32)],
    )(after(meta, out_na), arrived_early, early_c, early_y, early_yc, down_weight, *arrived_pres)

    out_fa, own_a = far_step(after(meta, arrived, early_grad), mine_a, got_na)
    got_fa = swapped(out_fa, "dp", 4)
    out_nb, mine_b = near_step(after(meta, out_fa), (keep_b,), (got_b,))
    got_nb = swapped(out_nb, "dp", 2)
    out_fb, own_b = far_step(meta, mine_b, got_nb)
    got_fb = swapped(out_fb, "dp", 4)
    total = jnp.concatenate([own_a + got_fa.astype(F32), own_b + got_fb.astype(F32)], axis=1)
    down_grad = total / math.sqrt(n * home)

    def columns(rows):
        return pl.BlockSpec((rows, 512), lambda i, *_: (0, i))

    hidden_grad = kernel_call(
        place_kernel, shape(BAL, ff), [columns(KEEP), columns(EARLY), columns(LATE)], columns(BAL),
        grid=(ff // 512,),
    )(meta, kept_grad, early_grad, arrived)
    return (hidden_grad, down_grad)


def solution(mesh):
    pairs_and_fours = (mesh.shape["dp"], mesh.shape["tensor"]) == (8, 4)
    return jax.shard_map(
        shards if pairs_and_fours else general_shards,
        mesh=mesh,
        in_specs=(P("dp", "tensor"), P("dp", "tensor"), P(None, "tensor"), P(), P(), P()),
        out_specs=(P("dp", "tensor"), P("dp", "tensor")),
        check_vma=False,
    )


def shifted(block, axis, distance):
    devices = range(lax.axis_size(axis))
    route = [((i - distance) % len(devices), i) for i in devices]
    return lax.ppermute(block, axis, route)


def crop_rows(row_total, crop_sizes, crop_starts):
    crop_ends = jnp.cumsum(crop_sizes)
    crop_begins = crop_ends - crop_sizes
    target_rows = jnp.arange(row_total, dtype=jnp.int32)[:, None]
    inside_crop = (target_rows >= crop_begins[None, :]) & (target_rows < crop_ends[None, :])
    source_rows = jnp.sum(
        jnp.where(inside_crop, crop_starts[None, :] + target_rows - crop_begins[None, :], 0), axis=1
    )
    return (source_rows, jnp.any(inside_crop, axis=1))


def select_rows(row_block, source_rows, valid_rows):
    taken = jnp.take(row_block, source_rows, axis=0)
    return jnp.where(valid_rows[:, None], taken, jnp.zeros((), row_block.dtype))


def gelu_parts(pre_act):
    cumulative = 0.5 * (1.0 + jax.scipy.special.erf(pre_act * inv_root_two))
    activated = pre_act * cumulative
    derivative = cumulative + pre_act * jnp.exp(-0.5 * pre_act * pre_act) * inv_root_tau
    return (activated, derivative)


def local_grads(pre_rows, cot_part, live_rows, layer_scale, down_weight, home_rows):
    cot_full = lax.all_gather(cot_part, "tensor", axis=1, tiled=True)
    scaled = (cot_full.astype(F32) * layer_scale[None, :]).astype(BF)
    activated, derivative = gelu_parts(pre_rows.astype(F32))
    activation = jnp.where(live_rows[:, None], activated, 0.0).astype(BF)
    backward = jnp.dot(scaled, down_weight, preferred_element_type=F32) * derivative
    gradient_rows = jnp.where(live_rows[:, None], backward, 0.0).astype(BF)
    weight_grad = lax.psum_scatter(
        lax.dot_general(scaled, activation, (((0,), (0,)), ((), ())), preferred_element_type=F32),
        "dp",
        scatter_dimension=0,
        tiled=True,
    )
    return (gradient_rows, weight_grad / math.sqrt(lax.axis_size("dp") * home_rows))


def general_shards(hidden_pre, cotangent, down_weight, layer_scale, crop_lengths, crop_moves):
    devices = lax.axis_size("dp")
    half_axis = devices // 2
    device_index = lax.axis_index("dp")
    partner_index = (device_index + half_axis) % devices
    own_lengths = lax.dynamic_index_in_dim(crop_lengths, device_index, 0, keepdims=False)
    own_moves = lax.dynamic_index_in_dim(crop_moves, device_index, 0, keepdims=False)
    partner_lengths = lax.dynamic_index_in_dim(crop_lengths, partner_index, 0, keepdims=False)
    partner_moves = lax.dynamic_index_in_dim(crop_moves, partner_index, 0, keepdims=False)
    home_rows = hidden_pre.shape[0]
    own_starts = jnp.cumsum(own_lengths) - own_lengths
    sent_sizes = own_lengths * own_moves
    kept_sizes = own_lengths * (1 - own_moves)
    arrived = jnp.sum(partner_lengths * partner_moves)
    send_source, send_valid = crop_rows(SEND, sent_sizes, own_starts)
    keep_sizes = jnp.concatenate([kept_sizes, arrived[None]])
    keep_starts = jnp.concatenate([own_starts, jnp.full((1,), home_rows, jnp.int32)])
    keep_source, keep_valid = crop_rows(BAL, keep_sizes, keep_starts)
    live_home = jnp.arange(home_rows, dtype=jnp.int32) < jnp.sum(own_lengths)
    gradient_rows, weight_grad = local_grads(
        hidden_pre, cotangent, live_home, layer_scale, down_weight, home_rows
    )
    outgoing = select_rows(gradient_rows, send_source, send_valid)
    incoming = shifted(outgoing, "dp", half_axis)
    balanced = select_rows(jnp.concatenate([gradient_rows, incoming], 0), keep_source, keep_valid)
    return (balanced, weight_grad)
```

```python
import functools
import math

import jax
import jax.numpy as jnp
from jax import lax
from jax.experimental import pallas as pl
from jax.experimental.pallas import tpu as pltpu
from jax.sharding import PartitionSpec as P

SEND = 528
KEEP = 528
TILE = 16
EARLY = 96
LATE = SEND - EARLY
SLOTS = 4
BAL = 720
BF = jnp.bfloat16
F32 = jnp.float32

inv_root_two = 0.7071067811865476
inv_root_tau = 0.3989422804014327


def kernel_call(kernel, out_shape, in_specs, out_specs, scratch=(), grid=(1,)):
    return pl.pallas_call(
        kernel,
        grid_spec=pltpu.PrefetchScalarGridSpec(
            num_scalar_prefetch=1,
            grid=grid,
            in_specs=in_specs,
            out_specs=out_specs,
            scratch_shapes=list(scratch),
        ),
        out_shape=out_shape,
        cost_estimate=pl.CostEstimate(flops=1, bytes_accessed=1, transcendentals=0),
        compiler_params=pltpu.CompilerParams(vmem_limit_bytes=16 * 1024 * 1024),
    )


IN_VMEM = pl.BlockSpec(memory_space=pltpu.VMEM)
IN_HBM = pl.BlockSpec(memory_space=pltpu.HBM)


def shape(a, b, dtype=BF):
    return jax.ShapeDtypeStruct((a, b), dtype)


def lengths_of(meta, d):
    return [meta[j, d] for j in range(SLOTS)]


def moves_of(meta, d):
    return [meta[SLOTS + j, d] for j in range(SLOTS)]


def dp_at(meta):
    return meta[2 * SLOTS, 0]


def tensor_at(meta):
    return meta[2 * SLOTS, 1]


def kept_total(meta, d):
    return sum(a * (1 - b) for a, b in zip(lengths_of(meta, d), moves_of(meta, d)))


def picks(meta, moved, first, rows, home):
    d = dp_at(meta)
    at = lax.broadcasted_iota(jnp.int32, (rows, 1), 0) - first
    source = jnp.full((rows, 1), -1, jnp.int32)
    begin = jnp.int32(0)
    start = jnp.int32(0)
    for length, move in zip(lengths_of(meta, d), moves_of(meta, d)):
        size = length * (move if moved else 1 - move)
        inside = (at >= begin) & (at < begin + size)
        source = jnp.where(inside, at + (start - begin), source)
        begin = begin + size
        start = start + length
    columns = lax.broadcasted_iota(jnp.int32, (rows, home), 1)
    return jnp.where(columns == source, 1.0, 0.0).astype(BF)


def sent_first(meta):
    n = meta.shape[1]
    partner = lax.rem(dp_at(meta) + n // 2, n)
    return lax.rem(kept_total(meta, partner), TILE)


def early_picks(meta, home):
    return picks(meta, True, sent_first(meta), EARLY, home)


def late_picks(meta, home):
    return picks(meta, True, sent_first(meta) - EARLY, LATE, home)


def kept_picks(meta, home):
    return picks(meta, False, 0, KEEP, home)


def scaled_rows(meta, pick, cot, scale):
    width = cot.shape[1]
    rows = jnp.dot(pick, cot[...], preferred_element_type=F32)
    own = scale[pl.ds(pl.multiple_of(tensor_at(meta) * width, 128), width)]
    return (rows * own[None, :]).astype(BF)


def first_kernel(meta, cot_hbm, scale_hbm, pre_hbm, late_out, early_out, rest_out, *rest):
    pre_outs, (cot, scale, pre, sems) = rest[:-4], rest[-4:]
    home = cot.shape[0]
    pairs = ((cot_hbm, cot), (scale_hbm, scale), (pre_hbm, pre))
    copies = [pltpu.make_async_copy(a, b, sems.at[i]) for i, (a, b) in enumerate(pairs)]
    for copy in copies:
        copy.start()
    early = early_picks(meta, home)
    copies[0].wait()
    copies[1].wait()
    early_rows = scaled_rows(meta, early, cot, scale)
    early_out[...] = early_rows
    rest_out[0:EARLY, :] = early_rows
    rest_out[EARLY:, :] = scaled_rows(meta, kept_picks(meta, home), cot, scale)
    late_out[...] = scaled_rows(meta, late_picks(meta, home), cot, scale)
    copies[2].wait()
    at = 0
    for out in pre_outs:
        columns = slice(at, at + out.shape[1])
        out[...] = jnp.dot(early, pre[:, columns], preferred_element_type=F32).astype(BF)
        at = columns.stop


def gelu_and_slope(x):
    cumulative = 0.5 * (1.0 + lax.erf(x * inv_root_two))
    return x * cumulative, cumulative + x * jnp.exp(-0.5 * x * x) * inv_root_tau


def gelu_kernel(late, base, block, meta, pre_hbm, act_out, der_out, pick, rows_f32, pre, sems):
    home = pre.shape[1]
    rows = pick.shape[0]
    blocks = act_out.shape[1] // block

    def fetch(i):
        columns = pl.ds(base + i * block, block)
        return pltpu.make_async_copy(pre_hbm.at[:, columns], pre.at[i], sems.at[i])

    for i in range(blocks):
        fetch(i).start()
    if late:
        pick[...] = late_picks(meta, home)
    else:
        pick[0:EARLY, :] = early_picks(meta, home)
        pick[EARLY:, :] = kept_picks(meta, home)
    step = 3 * TILE
    for i in range(blocks):
        fetch(i).wait()
        rows_f32[...] = jnp.dot(pick[...], pre[i], preferred_element_type=F32)
        columns = slice(i * block, (i + 1) * block)

        def body(k, _):
            at = pl.ds(pl.multiple_of(k * step, step), step)
            value, slope = gelu_and_slope(rows_f32[at, :])
            act_out[at, columns] = value.astype(BF)
            der_out[at, columns] = slope
            return 0

        lax.fori_loop(0, rows // step, body, 0)


def assemble(meta, pieces, lhs):
    width = pieces[0].shape[1]
    for j, piece in enumerate(pieces):
        at = pl.ds(pl.multiple_of((tensor_at(meta) ^ j) * width, 128), width)
        lhs[:, at] = piece[...]


def grad_kernel(first_row, slope_count, block, meta, p0, p1, p2, p3, weight, *rest):
    slopes, outs, lhs = rest[:slope_count], rest[slope_count:-1], rest[-1]
    rows = lhs.shape[0]
    assemble(meta, [p.at[pl.ds(first_row, rows), :] for p in (p0, p1, p2, p3)], lhs)
    part = slopes[0].shape[1]
    at = 0
    for out in outs:
        for c in range(0, out.shape[1], block):
            slope = slopes[at // part][first_row : first_row + rows, at % part : at % part + block]
            value = jnp.dot(lhs[...], weight[:, at : at + block], preferred_element_type=F32)
            out[:, c : c + block] = (value * slope).astype(BF)
            at += block


def early_kernel(block, meta, p0, p1, p2, p3, weight, *rest):
    pres, (out, lhs, acc) = rest[:-3], rest[-3:]
    assemble(meta, (p0, p1, p2, p3), lhs)
    at = 0
    for pre in pres:
        for c in range(0, pre.shape[1], block):
            columns = slice(at + c, at + c + block)
            acc[...] = jnp.dot(lhs[...], weight[:, columns], preferred_element_type=F32)

            def body(k, _):
                rows = pl.ds(pl.multiple_of(k * TILE, TILE), TILE)
                _, slope = gelu_and_slope(pre[rows, c : c + block].astype(F32))
                out[rows, columns] = (acc[rows, :] * slope).astype(BF)
                return 0

            lax.fori_loop(0, EARLY // TILE, body, 0)
        at += pre.shape[1]


def product(lhs_late, lhs_rest, act_late, act_rest, base):
    columns = slice(base, base + act_rest.shape[1])
    return jnp.dot(lhs_late[...], act_late[:, columns], preferred_element_type=F32) + jnp.dot(
        lhs_rest[...], act_rest[...], preferred_element_type=F32
    )


def weight_kernel(count, base, meta, *refs):
    pieces, (act_late, act_rest, send, keep, lhs_late, lhs_rest) = refs[: 2 * count], refs[2 * count :]
    half = pieces[0].shape[1] // 2
    mine = dp_at(meta) % 2 == 0
    for i in range(count):
        for piece, lhs in ((pieces[2 * i], lhs_late), (pieces[2 * i + 1], lhs_rest)):
            both = piece[...].T
            lo, hi = both[:half], both[half:]
            lhs[i * half : (i + 1) * half, :] = jnp.where(mine, hi, lo)
            lhs[(count + i) * half : (count + i + 1) * half, :] = jnp.where(mine, lo, hi)
    value = product(lhs_late, lhs_rest, act_late, act_rest, base)
    send[...] = value[: count * half].astype(BF)
    keep[...] = value[count * half :]


def weight_again_kernel(base, meta, late_01, rest_01, late_23, rest_23, act_late, act_rest, *outs):
    rows = late_01.shape[0] // 2
    sends, keeps = outs[:2], outs[2:]
    for i, (late, rest) in enumerate(((late_01, rest_01), (late_23, rest_23))):
        value = product(late, rest, act_late, act_rest, base)
        sends[i][...] = value[:rows].astype(BF)
        keeps[i][...] = value[rows:]


def near_kernel(count, meta, *refs):
    keeps, gots, (out, mine) = refs[:count], refs[count : 2 * count], refs[2 * count :]
    half = out.shape[0] // 2
    parts = [(k, g, at) for k, g in zip(keeps, gots) for at in range(0, k.shape[0], half)]
    keeps_even = (dp_at(meta) // 2 + tensor_at(meta)) % 2 == 0
    step = 2 * TILE

    for pair in range(2):
        (k0, g0, a0), (k1, g1, a1) = parts[2 * pair], parts[2 * pair + 1]

        def body(i, _):
            def rows(at):
                return pl.ds(pl.multiple_of(at + i * step, TILE), step)

            even = k0[rows(a0), :] + g0[rows(a0), :].astype(F32)
            odd = k1[rows(a1), :] + g1[rows(a1), :].astype(F32)
            out[rows(pair * half), :] = jnp.where(keeps_even, odd, even).astype(BF)
            mine[rows(pair * half), :] = jnp.where(keeps_even, even, odd)
            return 0

        lax.fori_loop(0, half // step, body, 0)


def far_kernel(meta, held, got, out, mine):
    half = out.shape[0]
    keeps_first = (dp_at(meta) // 4 + tensor_at(meta) // 2) % 2 == 0
    step = 2 * TILE

    def body(i, _):
        first = pl.ds(pl.multiple_of(i * step, TILE), step)
        second = pl.ds(pl.multiple_of(half + i * step, TILE), step)
        a = held[first, :] + got[first, :].astype(F32)
        b = held[second, :] + got[second, :].astype(F32)
        out[first, :] = jnp.where(keeps_first, b, a).astype(BF)
        mine[first, :] = jnp.where(keeps_first, a, b)
        return 0

    lax.fori_loop(0, half // step, body, 0)


def place_kernel(cuts, meta, kept, early, *rest):
    lates, out = rest[:-1], rest[-1]
    count = kept_total(meta, dp_at(meta))
    first = jnp.minimum(count - lax.rem(count, TILE), BAL - SEND)
    first = pl.multiple_of(first, TILE)
    wide = out.shape[1]
    step = pl.program_id(0)
    columns = pl.ds(pl.multiple_of(step * wide, wide), wide)
    out[0:KEEP, :] = kept[:, columns]
    out[KEEP:, :] = jnp.zeros((out.shape[0] - KEEP, wide), BF)

    def put(block, at):
        rows = lax.broadcasted_iota(jnp.int32, (block.shape[0], 1), 0) + at
        window = pl.ds(at, block.shape[0])
        out[window, :] = jnp.where(rows < count, out[window, :], block)

    put(early[:, columns], first)
    sources = [(late, c) for late, cut in zip(lates, cuts) for c in range(0, cut, wide)]
    for i, (late, c) in enumerate(sources):

        @pl.when(step == i)
        def _():
            put(late[:, c : c + wide], pl.multiple_of(first + EARLY, TILE))


def swapped(block, axis, distance):
    n = lax.axis_size(axis)
    return lax.ppermute(block, axis, [(i, i ^ distance) for i in range(n)])


def after(value, *others):
    return lax.optimization_barrier((value, *others))[0]


def shards(hidden_pre, cotangent, down_weight, layer_scale, crop_lengths, crop_moves):
    hidden_pre, cotangent, layer_scale = (
        pltpu.with_memory_space_constraint(x, pltpu.HBM) for x in (hidden_pre, cotangent, layer_scale)
    )
    home, ff = hidden_pre.shape
    width = cotangent.shape[1]
    features = down_weight.shape[0]
    half, part = width // 2, ff // 3
    others = EARLY + KEEP
    n = lax.axis_size("dp")
    d = lax.axis_index("dp").astype(jnp.int32)
    t = lax.axis_index("tensor").astype(jnp.int32)
    column = lax.broadcasted_iota(jnp.int32, (1, n), 1)
    own = jnp.where(column == 0, d, jnp.where(column == 1, t, 0))
    meta = jnp.concatenate([crop_lengths.T, crop_moves.T, own])
    vmem = pltpu.VMEM
    sems = pltpu.SemaphoreType.DMA

    def gelu(meta, late, base, columns):
        block = 256
        rows = LATE if late else others
        return kernel_call(
            functools.partial(gelu_kernel, late, base, block),
            [shape(rows, columns), shape(rows, columns, F32)],
            [IN_HBM], [IN_VMEM] * 2,
            [vmem((rows, home), BF), vmem((rows, block), F32), vmem((columns // block, home, block), BF),
             sems((columns // block,))],
        )(meta, hidden_pre)

    def weight_part(meta, pieces, act):
        count = len(pieces)
        return kernel_call(
            functools.partial(weight_kernel, count, 0),
            [shape(count * half, part), shape(count * half, part, F32),
             shape(count * width, LATE), shape(count * width, others)],
            [IN_VMEM] * (2 * count + 2), [IN_VMEM] * 4,
        )(meta, *[x for j in pieces for x in (lates[j], rests[j])], act_late, act)

    def weight_again(meta, base, act):
        return kernel_call(
            functools.partial(weight_again_kernel, base),
            [shape(width, part)] * 2 + [shape(width, part, F32)] * 2, [IN_VMEM] * 6, [IN_VMEM] * 4,
        )(meta, *lhs_01, *lhs_23, act_late, act)

    def grads(meta, pieces, first_row, rows, slopes, cuts):
        return kernel_call(
            functools.partial(grad_kernel, first_row, len(slopes), 256),
            [shape(rows, c) for c in cuts], [IN_VMEM] * (5 + len(slopes)), [IN_VMEM] * len(cuts),
            [vmem((rows, features), BF)],
        )(meta, *pieces, down_weight, *slopes)

    def near_step(meta, keeps, gots):
        count = len(keeps)
        return kernel_call(
            functools.partial(near_kernel, count),
            [shape(width, part), shape(width, part, F32)], [IN_VMEM] * (2 * count), [IN_VMEM] * 2,
        )(meta, *keeps, *gots)

    def far_step(meta, mine, got):
        return kernel_call(
            far_kernel, [shape(half, part), shape(half, part, F32)], [IN_VMEM] * 2, [IN_VMEM] * 2
        )(meta, mine, got)

    cuts = (ff // 2, ff // 2)
    late, early, rest, *pres = kernel_call(
        first_kernel,
        [shape(LATE, width), shape(EARLY, width), shape(others, width)] + [shape(EARLY, c) for c in cuts],
        [IN_HBM] * 3, [IN_VMEM] * (3 + len(cuts)),
        [vmem((home, width), BF), vmem((features,), F32), vmem((home, ff), BF), sems((3,))],
    )(meta, cotangent, layer_scale, hidden_pre)
    arrived_early = swapped(early, "dp", n // 2)
    arrived_pres = [swapped(pre, "dp", n // 2) for pre in pres]
    late_c, late_y = swapped(late, "tensor", 1), swapped(late, "tensor", 2)
    act_late, der_late = gelu(after(meta, late), True, 0, ff)

    late_y = after(late_y, act_late, late_c, arrived_early, arrived_pres[0])
    late_yc = swapped(late_y, "tensor", 1)
    rest_sent = after(rest, late_y)
    rest_c, rest_y = swapped(rest_sent, "tensor", 1), swapped(rest_sent, "tensor", 2)

    lates = (late, late_c, late_y, late_yc)
    moves = (256, ff - 256)
    moving = grads(after(meta, late_y), lates, 0, LATE, (der_late,), moves)
    arrived = [swapped(block, "dp", n // 2) for block in moving]

    act_a, der_a = gelu(after(meta, *moving, arrived_pres[1]), False, 0, part)
    rests = (rest, rest_c)
    send_01, keep_01, *lhs_01 = weight_part(after(meta, act_a), (0, 1), act_a)
    got_01 = swapped(send_01, "dp", 1)
    rest_y = after(rest_y, send_01, arrived[0])
    rest_yc = swapped(rest_y, "tensor", 1)
    rests = (rest, rest_c, rest_y, rest_yc)
    early_sent = after(arrived_early, rest_y)
    early_c, early_y = swapped(early_sent, "tensor", 1), swapped(early_sent, "tensor", 2)

    act_b, der_b = gelu(after(meta, rest_y), False, part, part)
    early_y = after(early_y, act_b, early_c)
    early_yc = swapped(early_y, "tensor", 1)
    send_23, keep_23, *lhs_23 = weight_part(after(meta, early_y), (2, 3), act_a)
    got_23 = swapped(send_23, "dp", 1)
    *sends_b, keep_b01, keep_b23 = weight_again(after(meta, send_23), part, act_b)
    act_c, der_c = gelu(after(meta, keep_b23), False, 2 * part, part)
    *sends_c, keep_c01, keep_c23 = weight_again(after(meta, act_c), 2 * part, act_c)
    (kept_grad,) = grads(after(meta, keep_c23), rests, EARLY, KEEP, (der_a, der_b, der_c), (ff,))

    out_na, mine_a = near_step(after(meta, kept_grad), (keep_01, keep_23), (got_01, got_23))
    got_na = swapped(out_na, "dp", 2)
    gots_b = [swapped(after(send, out_na), "dp", 1) for send in sends_b]

    early_grad = kernel_call(
        functools.partial(early_kernel, 256), shape(EARLY, ff), [IN_VMEM] * (5 + len(cuts)), IN_VMEM,
        [vmem((EARLY, features), BF), vmem((EARLY, 256), F32)],
    )(after(meta, out_na), arrived_early, early_c, early_y, early_yc, down_weight, *arrived_pres)

    out_nb, mine_b = near_step(after(meta, early_grad, got_na), (keep_b01, keep_b23), gots_b)
    got_nb = swapped(out_nb, "dp", 2)
    gots_c = [swapped(after(send, out_nb), "dp", 1) for send in sends_c]
    out_fa, own_a = far_step(after(meta, out_nb, arrived[1]), mine_a, got_na)
    got_fa = swapped(out_fa, "dp", 4)
    out_nc, mine_c = near_step(after(meta, out_fa), (keep_c01, keep_c23), gots_c)
    got_nc = swapped(out_nc, "dp", 2)
    out_fb, own_b = far_step(after(meta, out_nc), mine_b, got_nb)
    got_fb = swapped(out_fb, "dp", 4)
    out_fc, own_c = far_step(after(meta, out_fb), mine_c, got_nc)
    got_fc = swapped(out_fc, "dp", 4)
    total = [a + b.astype(F32) for a, b in ((own_a, got_fa), (own_b, got_fb), (own_c, got_fc))]
    down_grad = jnp.concatenate(total, axis=1) / math.sqrt(n * home)

    hidden_grad = kernel_call(
        functools.partial(place_kernel, moves), shape(BAL, ff), [IN_VMEM] * (2 + len(moves)),
        pl.BlockSpec((BAL, 256), lambda i, *_: (0, i)), grid=(ff // 256,),
    )(after(meta, out_fb), kept_grad, early_grad, *arrived)
    return (hidden_grad, down_grad)


def solution(mesh):
    pairs_and_fours = (mesh.shape["dp"], mesh.shape["tensor"]) == (8, 4)
    return jax.shard_map(
        shards if pairs_and_fours else general_shards,
        mesh=mesh,
        in_specs=(P("dp", "tensor"), P("dp", "tensor"), P(None, "tensor"), P(), P(), P()),
        out_specs=(P("dp", "tensor"), P("dp", "tensor")),
        check_vma=False,
    )


def shifted(block, axis, distance):
    devices = range(lax.axis_size(axis))
    route = [((i - distance) % len(devices), i) for i in devices]
    return lax.ppermute(block, axis, route)


def crop_rows(row_total, crop_sizes, crop_starts):
    crop_ends = jnp.cumsum(crop_sizes)
    crop_begins = crop_ends - crop_sizes
    target_rows = jnp.arange(row_total, dtype=jnp.int32)[:, None]
    inside_crop = (target_rows >= crop_begins[None, :]) & (target_rows < crop_ends[None, :])
    source_rows = jnp.sum(
        jnp.where(inside_crop, crop_starts[None, :] + target_rows - crop_begins[None, :], 0), axis=1
    )
    return (source_rows, jnp.any(inside_crop, axis=1))


def select_rows(row_block, source_rows, valid_rows):
    taken = jnp.take(row_block, source_rows, axis=0)
    return jnp.where(valid_rows[:, None], taken, jnp.zeros((), row_block.dtype))


def gelu_parts(pre_act):
    cumulative = 0.5 * (1.0 + jax.scipy.special.erf(pre_act * inv_root_two))
    activated = pre_act * cumulative
    derivative = cumulative + pre_act * jnp.exp(-0.5 * pre_act * pre_act) * inv_root_tau
    return (activated, derivative)


def local_grads(pre_rows, cot_part, live_rows, layer_scale, down_weight, home_rows):
    cot_full = lax.all_gather(cot_part, "tensor", axis=1, tiled=True)
    scaled = (cot_full.astype(F32) * layer_scale[None, :]).astype(BF)
    activated, derivative = gelu_parts(pre_rows.astype(F32))
    activation = jnp.where(live_rows[:, None], activated, 0.0).astype(BF)
    backward = jnp.dot(scaled, down_weight, preferred_element_type=F32) * derivative
    gradient_rows = jnp.where(live_rows[:, None], backward, 0.0).astype(BF)
    weight_grad = lax.psum_scatter(
        lax.dot_general(scaled, activation, (((0,), (0,)), ((), ())), preferred_element_type=F32),
        "dp",
        scatter_dimension=0,
        tiled=True,
    )
    return (gradient_rows, weight_grad / math.sqrt(lax.axis_size("dp") * home_rows))


def general_shards(hidden_pre, cotangent, down_weight, layer_scale, crop_lengths, crop_moves):
    devices = lax.axis_size("dp")
    half_axis = devices // 2
    device_index = lax.axis_index("dp")
    partner_index = (device_index + half_axis) % devices
    own_lengths = lax.dynamic_index_in_dim(crop_lengths, device_index, 0, keepdims=False)
    own_moves = lax.dynamic_index_in_dim(crop_moves, device_index, 0, keepdims=False)
    partner_lengths = lax.dynamic_index_in_dim(crop_lengths, partner_index, 0, keepdims=False)
    partner_moves = lax.dynamic_index_in_dim(crop_moves, partner_index, 0, keepdims=False)
    home_rows = hidden_pre.shape[0]
    own_starts = jnp.cumsum(own_lengths) - own_lengths
    sent_sizes = own_lengths * own_moves
    kept_sizes = own_lengths * (1 - own_moves)
    arrived = jnp.sum(partner_lengths * partner_moves)
    send_source, send_valid = crop_rows(SEND, sent_sizes, own_starts)
    keep_sizes = jnp.concatenate([kept_sizes, arrived[None]])
    keep_starts = jnp.concatenate([own_starts, jnp.full((1,), home_rows, jnp.int32)])
    keep_source, keep_valid = crop_rows(BAL, keep_sizes, keep_starts)
    live_home = jnp.arange(home_rows, dtype=jnp.int32) < jnp.sum(own_lengths)
    gradient_rows, weight_grad = local_grads(
        hidden_pre, cotangent, live_home, layer_scale, down_weight, home_rows
    )
    outgoing = select_rows(gradient_rows, send_source, send_valid)
    incoming = shifted(outgoing, "dp", half_axis)
    balanced = select_rows(jnp.concatenate([gradient_rows, incoming], 0), keep_source, keep_valid)
    return (balanced, weight_grad)
```

```python
import functools
import math

import jax
import jax.numpy as jnp
from jax import lax
from jax.experimental import pallas as pl
from jax.experimental.pallas import tpu as pltpu
from jax.sharding import PartitionSpec as P

SEND = 528
KEEP = 528
TILE = 16
EARLY = 112
LATE = SEND - EARLY
SLOTS = 4
BAL = 720
BF = jnp.bfloat16
F32 = jnp.float32

inv_root_two = 0.7071067811865476
inv_root_tau = 0.3989422804014327


def kernel_call(kernel, out_shape, in_specs, out_specs, scratch=(), grid=(1,)):
    return pl.pallas_call(
        kernel,
        grid_spec=pltpu.PrefetchScalarGridSpec(
            num_scalar_prefetch=1,
            grid=grid,
            in_specs=in_specs,
            out_specs=out_specs,
            scratch_shapes=list(scratch),
        ),
        out_shape=out_shape,
        cost_estimate=pl.CostEstimate(flops=1, bytes_accessed=1, transcendentals=0),
        compiler_params=pltpu.CompilerParams(vmem_limit_bytes=16 * 1024 * 1024),
    )


IN_VMEM = pl.BlockSpec(memory_space=pltpu.VMEM)
IN_HBM = pl.BlockSpec(memory_space=pltpu.HBM)


def shape(a, b, dtype=BF):
    return jax.ShapeDtypeStruct((a, b), dtype)


def lengths_of(meta, d):
    return [meta[j, d] for j in range(SLOTS)]


def moves_of(meta, d):
    return [meta[SLOTS + j, d] for j in range(SLOTS)]


def dp_at(meta):
    return meta[2 * SLOTS, 0]


def tensor_at(meta):
    return meta[2 * SLOTS, 1]


def kept_total(meta, d):
    return sum(a * (1 - b) for a, b in zip(lengths_of(meta, d), moves_of(meta, d)))


def picks(meta, moved, first, rows, home):
    d = dp_at(meta)
    at = lax.broadcasted_iota(jnp.int32, (rows, 1), 0) - first
    source = jnp.full((rows, 1), -1, jnp.int32)
    begin = jnp.int32(0)
    start = jnp.int32(0)
    for length, move in zip(lengths_of(meta, d), moves_of(meta, d)):
        size = length * (move if moved else 1 - move)
        inside = (at >= begin) & (at < begin + size)
        source = jnp.where(inside, at + (start - begin), source)
        begin = begin + size
        start = start + length
    columns = lax.broadcasted_iota(jnp.int32, (rows, home), 1)
    return jnp.where(columns == source, 1.0, 0.0).astype(BF)


def sent_first(meta):
    n = meta.shape[1]
    partner = lax.rem(dp_at(meta) + n // 2, n)
    return lax.rem(kept_total(meta, partner), TILE)


def early_picks(meta, home):
    return picks(meta, True, sent_first(meta), EARLY, home)


def late_picks(meta, home):
    return picks(meta, True, sent_first(meta) - EARLY, LATE, home)


def kept_picks(meta, home):
    return picks(meta, False, 0, KEEP, home)


def scaled_rows(meta, pick, cot, scale):
    width = cot.shape[1]
    rows = jnp.dot(pick, cot[...], preferred_element_type=F32)
    own = scale[pl.ds(pl.multiple_of(tensor_at(meta) * width, 128), width)]
    return (rows * own[None, :]).astype(BF)


def first_kernel(meta, cot_hbm, scale_hbm, pre_hbm, late_out, early_out, rest_a, rest_b, cot, scale, pre, sems):
    width = cot.shape[1]
    home = cot.shape[0]
    pairs = ((cot_hbm, cot), (scale_hbm, scale), (pre_hbm, pre))
    copies = [pltpu.make_async_copy(a, b, sems.at[i]) for i, (a, b) in enumerate(pairs)]
    for copy in copies:
        copy.start()
    early = early_picks(meta, home)
    copies[0].wait()
    copies[1].wait()
    early_rows = scaled_rows(meta, early, cot, scale)
    early_out[:, :width] = early_rows
    kept_rows = scaled_rows(meta, kept_picks(meta, home), cot, scale)
    cut = rest_a.shape[0] - EARLY
    rest_a[0:EARLY, :] = early_rows
    rest_a[EARLY:, :] = kept_rows[:cut]
    rest_b[...] = kept_rows[cut:]
    late_out[...] = scaled_rows(meta, late_picks(meta, home), cot, scale)
    copies[2].wait()
    early_out[:, width:] = jnp.dot(early, pre[...], preferred_element_type=F32).astype(BF)


def gelu_and_slope(x):
    cumulative = 0.5 * (1.0 + lax.erf(x * inv_root_two))
    return x * cumulative, cumulative + x * jnp.exp(-0.5 * x * x) * inv_root_tau


def gelu_kernel(late, base, block, meta, pre_hbm, act_out, der_out, pick, rows_f32, pre, sems):
    home = pre.shape[1]
    rows = pick.shape[0]
    blocks = act_out.shape[1] // block

    def fetch(i):
        columns = pl.ds(base + i * block, block)
        return pltpu.make_async_copy(pre_hbm.at[:, columns], pre.at[i], sems.at[i])

    for i in range(blocks):
        fetch(i).start()
    if late:
        pick[...] = late_picks(meta, home)
    else:
        pick[0:EARLY, :] = early_picks(meta, home)
        pick[EARLY:, :] = kept_picks(meta, home)
    step = next(TILE * k for k in (3, 4, 2, 1) if rows % (TILE * k) == 0)
    for i in range(blocks):
        fetch(i).wait()
        rows_f32[...] = jnp.dot(pick[...], pre[i], preferred_element_type=F32)
        columns = slice(i * block, (i + 1) * block)

        def body(k, _):
            at = pl.ds(pl.multiple_of(k * step, step), step)
            value, slope = gelu_and_slope(rows_f32[at, :])
            act_out[at, columns] = value.astype(BF)
            der_out[at, columns] = slope
            return 0

        lax.fori_loop(0, rows // step, body, 0)


def assemble(meta, pieces, first_row, lhs):
    rows = lhs.shape[0]
    width = pieces[1][0].shape[1]
    for j, piece in enumerate(pieces):
        columns = pl.ds(pl.multiple_of((tensor_at(meta) ^ j) * width, 128), width)
        at = 0
        for block in piece:
            low, high = max(at, first_row), min(at + block.shape[0], first_row + rows)
            if low < high:
                lhs[low - first_row : high - first_row, columns] = block[low - at : high - at, 0:width]
            at += block.shape[0]


def split(refs, counts):
    out, at = [], 0
    for count in counts:
        out.append(refs[at : at + count])
        at += count
    return out


def grad_kernel(counts, first_row, block, meta, *refs):
    p0, p1, p2, p3, (weight,), slopes, outs, (lhs,) = split(refs, counts)
    rows = lhs.shape[0]
    assemble(meta, (p0, p1, p2, p3), first_row, lhs)
    part = slopes[0].shape[1]
    at = 0
    for out in outs:
        for c in range(0, out.shape[1], block):
            slope = slopes[at // part][first_row : first_row + rows, at % part : at % part + block]
            value = jnp.dot(lhs[...], weight[:, at : at + block], preferred_element_type=F32)
            out[:, c : c + block] = (value * slope).astype(BF)
            at += block


def early_kernel(block, meta, own, p1, p2, p3, weight, out, lhs, acc):
    width = p1.shape[1]
    assemble(meta, ([own], [p1], [p2], [p3]), 0, lhs)
    for at in range(0, out.shape[1], block):
        columns = slice(at, at + block)
        acc[...] = jnp.dot(lhs[...], weight[:, columns], preferred_element_type=F32)

        def body(k, _):
            rows = pl.ds(pl.multiple_of(k * TILE, TILE), TILE)
            _, slope = gelu_and_slope(own[rows, width + at : width + at + block].astype(F32))
            out[rows, columns] = (acc[rows, :] * slope).astype(BF)
            return 0

        lax.fori_loop(0, EARLY // TILE, body, 0)


def product(lhs_late, lhs_rest, act_late, act_rest, base):
    columns = slice(base, base + act_rest.shape[1])
    return jnp.dot(lhs_late[...], act_late[:, columns], preferred_element_type=F32) + jnp.dot(
        lhs_rest[...], act_rest[...], preferred_element_type=F32
    )


def weight_kernel(counts, base, meta, *refs):
    *parts, (act_late, act_rest, send, keep, lhs_late, lhs_rest) = split(refs, counts)
    count = len(parts) // 2
    half = parts[0][0].shape[1] // 2
    mine = dp_at(meta) % 2 == 0
    for i in range(count):
        for blocks, lhs in ((parts[2 * i], lhs_late), (parts[2 * i + 1], lhs_rest)):
            both = blocks[0][...]
            if len(blocks) > 1:
                both = jnp.concatenate([block[...] for block in blocks], axis=0)
            both = both.T
            lo, hi = both[:half], both[half:]
            lhs[i * half : (i + 1) * half, :] = jnp.where(mine, hi, lo)
            lhs[(count + i) * half : (count + i + 1) * half, :] = jnp.where(mine, lo, hi)
    value = product(lhs_late, lhs_rest, act_late, act_rest, base)
    send[...] = value[: count * half].astype(BF)
    keep[...] = value[count * half :]


def weight_again_kernel(base, meta, late_01, rest_01, late_23, rest_23, act_late, act_rest, send, keep):
    rows = late_01.shape[0] // 2
    for i, (late, rest) in enumerate(((late_01, rest_01), (late_23, rest_23))):
        value = product(late, rest, act_late, act_rest, base)
        send[i * rows : (i + 1) * rows, :] = value[:rows].astype(BF)
        keep[i * rows : (i + 1) * rows, :] = value[rows:]


def near_kernel(count, meta, *refs):
    keeps, gots, (out, mine) = refs[:count], refs[count : 2 * count], refs[2 * count :]
    half = out.shape[0] // 2
    parts = [(k, g, at) for k, g in zip(keeps, gots) for at in range(0, k.shape[0], half)]
    keeps_even = (dp_at(meta) // 2 + tensor_at(meta)) % 2 == 0
    step = 2 * TILE

    for pair in range(2):
        (k0, g0, a0), (k1, g1, a1) = parts[2 * pair], parts[2 * pair + 1]

        def body(i, _):
            def rows(at):
                return pl.ds(pl.multiple_of(at + i * step, TILE), step)

            even = k0[rows(a0), :] + g0[rows(a0), :].astype(F32)
            odd = k1[rows(a1), :] + g1[rows(a1), :].astype(F32)
            out[rows(pair * half), :] = jnp.where(keeps_even, odd, even).astype(BF)
            mine[rows(pair * half), :] = jnp.where(keeps_even, even, odd)
            return 0

        lax.fori_loop(0, half // step, body, 0)


def far_kernel(meta, held, got, out, mine):
    half = out.shape[0]
    keeps_first = (dp_at(meta) // 4 + tensor_at(meta) // 2) % 2 == 0
    step = 2 * TILE

    def body(i, _):
        first = pl.ds(pl.multiple_of(i * step, TILE), step)
        second = pl.ds(pl.multiple_of(half + i * step, TILE), step)
        a = held[first, :] + got[first, :].astype(F32)
        b = held[second, :] + got[second, :].astype(F32)
        out[first, :] = jnp.where(keeps_first, b, a).astype(BF)
        mine[first, :] = jnp.where(keeps_first, a, b)
        return 0

    lax.fori_loop(0, half // step, body, 0)


def place_kernel(cuts, meta, kept, early, *rest):
    lates, out = rest[:-1], rest[-1]
    count = kept_total(meta, dp_at(meta))
    first = jnp.minimum(count - lax.rem(count, TILE), BAL - SEND)
    first = pl.multiple_of(first, TILE)
    wide = out.shape[1]
    step = pl.program_id(0)
    columns = pl.ds(pl.multiple_of(step * wide, wide), wide)
    out[0:KEEP, :] = kept[:, columns]
    out[KEEP:, :] = jnp.zeros((out.shape[0] - KEEP, wide), BF)

    def put(block, at):
        rows = lax.broadcasted_iota(jnp.int32, (block.shape[0], 1), 0) + at
        window = pl.ds(at, block.shape[0])
        out[window, :] = jnp.where(rows < count, out[window, :], block)

    put(early[:, columns], first)
    sources = [(late, c) for late, cut in zip(lates, cuts) for c in range(0, cut, wide)]
    for i, (late, c) in enumerate(sources):

        @pl.when(step == i)
        def _():
            put(late[:, c : c + wide], pl.multiple_of(first + EARLY, TILE))


def swapped(block, axis, distance):
    n = lax.axis_size(axis)
    return lax.ppermute(block, axis, [(i, i ^ distance) for i in range(n)])


def after(value, *others):
    return lax.optimization_barrier((value, *others))[0]


def shards(hidden_pre, cotangent, down_weight, layer_scale, crop_lengths, crop_moves):
    hidden_pre, cotangent, layer_scale = (
        pltpu.with_memory_space_constraint(x, pltpu.HBM) for x in (hidden_pre, cotangent, layer_scale)
    )
    home, ff = hidden_pre.shape
    width = cotangent.shape[1]
    features = down_weight.shape[0]
    half, part = width // 2, ff // 3
    others = EARLY + KEEP
    n = lax.axis_size("dp")
    d = lax.axis_index("dp").astype(jnp.int32)
    t = lax.axis_index("tensor").astype(jnp.int32)
    column = lax.broadcasted_iota(jnp.int32, (1, n), 1)
    own = jnp.where(column == 0, d, jnp.where(column == 1, t, 0))
    meta = jnp.concatenate([crop_lengths.T, crop_moves.T, own])
    vmem = pltpu.VMEM
    sems = pltpu.SemaphoreType.DMA

    def gelu(meta, late, base, columns):
        block = 256
        rows = LATE if late else others
        return kernel_call(
            functools.partial(gelu_kernel, late, base, block),
            [shape(rows, columns), shape(rows, columns, F32)],
            [IN_HBM], [IN_VMEM] * 2,
            [vmem((rows, home), BF), vmem((rows, block), F32), vmem((columns // block, home, block), BF),
             sems((columns // block,))],
        )(meta, hidden_pre)

    def weight_part(meta, pieces, act):
        count = len(pieces)
        parts = [x for j in pieces for x in (lates[j], rests[j])]
        counts = [len(x) for x in parts] + [6]
        blocks = [block for x in parts for block in x]
        return kernel_call(
            functools.partial(weight_kernel, counts, 0),
            [shape(count * half, part), shape(count * half, part, F32),
             shape(count * width, LATE), shape(count * width, others)],
            [IN_VMEM] * (len(blocks) + 2), [IN_VMEM] * 4,
        )(meta, *blocks, act_late, act)

    def weight_again(meta, base, act):
        return kernel_call(
            functools.partial(weight_again_kernel, base),
            [shape(4 * half, part), shape(4 * half, part, F32)], [IN_VMEM] * 6, [IN_VMEM] * 2,
        )(meta, *lhs_01, *lhs_23, act_late, act)

    def grads(meta, pieces, first_row, rows, slopes, cuts):
        counts = [len(x) for x in pieces] + [1, len(slopes), len(cuts), 1]
        blocks = [block for x in pieces for block in x]
        return kernel_call(
            functools.partial(grad_kernel, counts, first_row, 256),
            [shape(rows, c) for c in cuts], [IN_VMEM] * (len(blocks) + 1 + len(slopes)), [IN_VMEM] * len(cuts),
            [vmem((rows, features), BF)],
        )(meta, *blocks, down_weight, *slopes)

    def near_step(meta, keeps, gots):
        count = len(keeps)
        return kernel_call(
            functools.partial(near_kernel, count),
            [shape(width, part), shape(width, part, F32)], [IN_VMEM] * (2 * count), [IN_VMEM] * 2,
        )(meta, *keeps, *gots)

    def far_step(meta, mine, got):
        return kernel_call(
            far_kernel, [shape(half, part), shape(half, part, F32)], [IN_VMEM] * 2, [IN_VMEM] * 2
        )(meta, mine, got)

    cut = others // 2
    late, early, *rest = kernel_call(
        first_kernel,
        [shape(LATE, width), shape(EARLY, width + ff), shape(cut, width), shape(others - cut, width)],
        [IN_HBM] * 3, [IN_VMEM] * 4,
        [vmem((home, width), BF), vmem((features,), F32), vmem((home, ff), BF), sems((3,))],
    )(meta, cotangent, layer_scale, hidden_pre)
    arrived_early = swapped(early, "dp", n // 2)
    late_c, late_y = swapped(late, "tensor", 1), swapped(late, "tensor", 2)
    act_late, der_late = gelu(after(meta, late), True, 0, ff)

    late_y = after(late_y, act_late, late_c)
    late_yc = swapped(late_y, "tensor", 1)
    rest_sent = [after(block, late_y) for block in rest]
    rest_y = [swapped(block, "tensor", 2) for block in rest_sent]
    rest_c = [swapped(block, "tensor", 1) for block in rest_sent]

    lates = ([late], [late_c], [late_y], [late_yc])
    moves = (512, ff - 512)
    moving = grads(after(meta, late_y), lates, 0, LATE, (der_late,), moves)
    arrived = [swapped(block, "dp", n // 2) for block in moving]

    act_a, der_a = gelu(after(meta, *moving, arrived_early), False, 0, part)
    rests = (rest, rest_c)
    send_01, keep_01, *lhs_01 = weight_part(after(meta, act_a), (0, 1), act_a)
    got_01 = swapped(send_01, "dp", 1)
    rest_y = [after(block, send_01) for block in rest_y]
    rest_yc = [swapped(block, "tensor", 1) for block in rest_y]
    rests = (rest, rest_c, rest_y, rest_yc)

    act_b, der_b = gelu(after(meta, *rest_y), False, part, part)
    send_23, keep_23, *lhs_23 = weight_part(after(meta, act_b, arrived[0]), (2, 3), act_a)
    got_23 = swapped(send_23, "dp", 1)
    early_sent = after(arrived_early[:, :width], send_23)
    early_c, early_y = swapped(early_sent, "tensor", 1), swapped(early_sent, "tensor", 2)
    send_b, keep_b = weight_again(after(meta, send_23), part, act_b)
    got_b = swapped(send_b, "dp", 1)
    act_c, der_c = gelu(after(meta, send_b), False, 2 * part, part)
    early_y = after(early_y, act_c, early_c)
    early_yc = swapped(early_y, "tensor", 1)
    send_c, keep_c = weight_again(after(meta, early_y), 2 * part, act_c)

    out_na, mine_a = near_step(after(meta, send_c), (keep_01, keep_23), (got_01, got_23))
    got_na = swapped(out_na, "dp", 2)
    (kept_grad,) = grads(after(meta, out_na), rests, EARLY, KEEP, (der_a, der_b, der_c), (ff,))

    early_grad = kernel_call(
        functools.partial(early_kernel, 256), shape(EARLY, ff), [IN_VMEM] * 5, IN_VMEM,
        [vmem((EARLY, features), BF), vmem((EARLY, 256), F32)],
    )(after(meta, kept_grad), arrived_early, early_c, early_y, early_yc, down_weight)

    out_nb, mine_b = near_step(after(meta, early_grad, got_na), (keep_b,), (got_b,))
    got_nb = swapped(out_nb, "dp", 2)
    got_c = swapped(after(send_c, early_grad), "dp", 1)
    out_fa, own_a = far_step(after(meta, out_nb, arrived[1]), mine_a, got_na)
    got_fa = swapped(out_fa, "dp", 4)
    out_nc, mine_c = near_step(after(meta, out_fa), (keep_c,), (got_c,))
    got_nc = swapped(out_nc, "dp", 2)
    out_fb, own_b = far_step(after(meta, out_nc), mine_b, got_nb)
    got_fb = swapped(out_fb, "dp", 4)
    out_fc, own_c = far_step(after(meta, out_fb), mine_c, got_nc)
    got_fc = swapped(out_fc, "dp", 4)
    total = [a + b.astype(F32) for a, b in ((own_a, got_fa), (own_b, got_fb), (own_c, got_fc))]
    down_grad = jnp.concatenate(total, axis=1) / math.sqrt(n * home)

    hidden_grad = kernel_call(
        functools.partial(place_kernel, moves), shape(BAL, ff), [IN_VMEM] * (2 + len(moves)),
        pl.BlockSpec((BAL, 256), lambda i, *_: (0, i)), grid=(ff // 256,),
    )(after(meta, out_fb), kept_grad, early_grad, *arrived)
    return (hidden_grad, down_grad)


def solution(mesh):
    pairs_and_fours = (mesh.shape["dp"], mesh.shape["tensor"]) == (8, 4)
    return jax.shard_map(
        shards if pairs_and_fours else general_shards,
        mesh=mesh,
        in_specs=(P("dp", "tensor"), P("dp", "tensor"), P(None, "tensor"), P(), P(), P()),
        out_specs=(P("dp", "tensor"), P("dp", "tensor")),
        check_vma=False,
    )


def shifted(block, axis, distance):
    devices = range(lax.axis_size(axis))
    route = [((i - distance) % len(devices), i) for i in devices]
    return lax.ppermute(block, axis, route)


def crop_rows(row_total, crop_sizes, crop_starts):
    crop_ends = jnp.cumsum(crop_sizes)
    crop_begins = crop_ends - crop_sizes
    target_rows = jnp.arange(row_total, dtype=jnp.int32)[:, None]
    inside_crop = (target_rows >= crop_begins[None, :]) & (target_rows < crop_ends[None, :])
    source_rows = jnp.sum(
        jnp.where(inside_crop, crop_starts[None, :] + target_rows - crop_begins[None, :], 0), axis=1
    )
    return (source_rows, jnp.any(inside_crop, axis=1))


def select_rows(row_block, source_rows, valid_rows):
    taken = jnp.take(row_block, source_rows, axis=0)
    return jnp.where(valid_rows[:, None], taken, jnp.zeros((), row_block.dtype))


def gelu_parts(pre_act):
    cumulative = 0.5 * (1.0 + jax.scipy.special.erf(pre_act * inv_root_two))
    activated = pre_act * cumulative
    derivative = cumulative + pre_act * jnp.exp(-0.5 * pre_act * pre_act) * inv_root_tau
    return (activated, derivative)


def local_grads(pre_rows, cot_part, live_rows, layer_scale, down_weight, home_rows):
    cot_full = lax.all_gather(cot_part, "tensor", axis=1, tiled=True)
    scaled = (cot_full.astype(F32) * layer_scale[None, :]).astype(BF)
    activated, derivative = gelu_parts(pre_rows.astype(F32))
    activation = jnp.where(live_rows[:, None], activated, 0.0).astype(BF)
    backward = jnp.dot(scaled, down_weight, preferred_element_type=F32) * derivative
    gradient_rows = jnp.where(live_rows[:, None], backward, 0.0).astype(BF)
    weight_grad = lax.psum_scatter(
        lax.dot_general(scaled, activation, (((0,), (0,)), ((), ())), preferred_element_type=F32),
        "dp",
        scatter_dimension=0,
        tiled=True,
    )
    return (gradient_rows, weight_grad / math.sqrt(lax.axis_size("dp") * home_rows))


def general_shards(hidden_pre, cotangent, down_weight, layer_scale, crop_lengths, crop_moves):
    devices = lax.axis_size("dp")
    half_axis = devices // 2
    device_index = lax.axis_index("dp")
    partner_index = (device_index + half_axis) % devices
    own_lengths = lax.dynamic_index_in_dim(crop_lengths, device_index, 0, keepdims=False)
    own_moves = lax.dynamic_index_in_dim(crop_moves, device_index, 0, keepdims=False)
    partner_lengths = lax.dynamic_index_in_dim(crop_lengths, partner_index, 0, keepdims=False)
    partner_moves = lax.dynamic_index_in_dim(crop_moves, partner_index, 0, keepdims=False)
    home_rows = hidden_pre.shape[0]
    own_starts = jnp.cumsum(own_lengths) - own_lengths
    sent_sizes = own_lengths * own_moves
    kept_sizes = own_lengths * (1 - own_moves)
    arrived = jnp.sum(partner_lengths * partner_moves)
    send_source, send_valid = crop_rows(SEND, sent_sizes, own_starts)
    keep_sizes = jnp.concatenate([kept_sizes, arrived[None]])
    keep_starts = jnp.concatenate([own_starts, jnp.full((1,), home_rows, jnp.int32)])
    keep_source, keep_valid = crop_rows(BAL, keep_sizes, keep_starts)
    live_home = jnp.arange(home_rows, dtype=jnp.int32) < jnp.sum(own_lengths)
    gradient_rows, weight_grad = local_grads(
        hidden_pre, cotangent, live_home, layer_scale, down_weight, home_rows
    )
    outgoing = select_rows(gradient_rows, send_source, send_valid)
    incoming = shifted(outgoing, "dp", half_axis)
    balanced = select_rows(jnp.concatenate([gradient_rows, incoming], 0), keep_source, keep_valid)
    return (balanced, weight_grad)
```

```python
import functools
import math

import jax
import jax.numpy as jnp
from jax import lax
from jax.experimental import pallas as pl
from jax.experimental.pallas import tpu as pltpu
from jax.sharding import PartitionSpec as P

SEND = 528
KEEP = 528
TILE = 16
EARLY = 80
LATE = SEND - EARLY
SLOTS = 4
BAL = 720
BF = jnp.bfloat16
F32 = jnp.float32

inv_root_two = 0.7071067811865476
inv_root_tau = 0.3989422804014327


def kernel_call(kernel, out_shape, in_specs, out_specs, scratch=(), grid=(1,)):
    return pl.pallas_call(
        kernel,
        grid_spec=pltpu.PrefetchScalarGridSpec(
            num_scalar_prefetch=1,
            grid=grid,
            in_specs=in_specs,
            out_specs=out_specs,
            scratch_shapes=list(scratch),
        ),
        out_shape=out_shape,
        cost_estimate=pl.CostEstimate(flops=1, bytes_accessed=1, transcendentals=0),
        compiler_params=pltpu.CompilerParams(vmem_limit_bytes=16 * 1024 * 1024),
    )


IN_VMEM = pl.BlockSpec(memory_space=pltpu.VMEM)
IN_HBM = pl.BlockSpec(memory_space=pltpu.HBM)


def shape(a, b, dtype=BF):
    return jax.ShapeDtypeStruct((a, b), dtype)


def lengths_of(meta, d):
    return [meta[j, d] for j in range(SLOTS)]


def moves_of(meta, d):
    return [meta[SLOTS + j, d] for j in range(SLOTS)]


def dp_at(meta):
    return meta[2 * SLOTS, 0]


def tensor_at(meta):
    return meta[2 * SLOTS, 1]


def kept_total(meta, d):
    return sum(a * (1 - b) for a, b in zip(lengths_of(meta, d), moves_of(meta, d)))


def picks(meta, moved, first, rows, home):
    d = dp_at(meta)
    at = lax.broadcasted_iota(jnp.int32, (rows, 1), 0) - first
    source = jnp.full((rows, 1), -1, jnp.int32)
    begin = jnp.int32(0)
    start = jnp.int32(0)
    for length, move in zip(lengths_of(meta, d), moves_of(meta, d)):
        size = length * (move if moved else 1 - move)
        inside = (at >= begin) & (at < begin + size)
        source = jnp.where(inside, at + (start - begin), source)
        begin = begin + size
        start = start + length
    columns = lax.broadcasted_iota(jnp.int32, (rows, home), 1)
    return jnp.where(columns == source, 1.0, 0.0).astype(BF)


def sent_first(meta):
    n = meta.shape[1]
    partner = lax.rem(dp_at(meta) + n // 2, n)
    return lax.rem(kept_total(meta, partner), TILE)


def early_picks(meta, home):
    return picks(meta, True, sent_first(meta), EARLY, home)


def late_picks(meta, home):
    return picks(meta, True, sent_first(meta) - EARLY, LATE, home)


def kept_picks(meta, home):
    return picks(meta, False, 0, KEEP, home)


def scaled_rows(meta, pick, cot, scale):
    width = cot.shape[1]
    rows = jnp.dot(pick, cot[...], preferred_element_type=F32)
    own = scale[pl.ds(pl.multiple_of(tensor_at(meta) * width, 128), width)]
    return (rows * own[None, :]).astype(BF)


def first_kernel(meta, cot_hbm, scale_hbm, pre_hbm, late_out, early_out, rest_out, rest_a, rest_b, cot, scale, pre, sems):
    width = cot.shape[1]
    home = cot.shape[0]
    pairs = ((cot_hbm, cot), (scale_hbm, scale), (pre_hbm, pre))
    copies = [pltpu.make_async_copy(a, b, sems.at[i]) for i, (a, b) in enumerate(pairs)]
    for copy in copies:
        copy.start()
    early = early_picks(meta, home)
    copies[0].wait()
    copies[1].wait()
    early_rows = scaled_rows(meta, early, cot, scale)
    early_out[:, :width] = early_rows
    kept_rows = scaled_rows(meta, kept_picks(meta, home), cot, scale)
    rest_out[0:EARLY, :] = early_rows
    rest_out[EARLY:, :] = kept_rows
    cut = rest_a.shape[0] - EARLY
    rest_a[0:EARLY, :] = early_rows
    rest_a[EARLY:, :] = kept_rows[:cut]
    rest_b[...] = kept_rows[cut:]
    late_out[...] = scaled_rows(meta, late_picks(meta, home), cot, scale)
    copies[2].wait()
    early_out[:, width:] = jnp.dot(early, pre[...], preferred_element_type=F32).astype(BF)


def gelu_and_slope(x):
    cumulative = 0.5 * (1.0 + lax.erf(x * inv_root_two))
    return x * cumulative, cumulative + x * jnp.exp(-0.5 * x * x) * inv_root_tau


def gelu_kernel(late, base, block, meta, pre_hbm, act_out, der_out, pick, rows_f32, pre, sems):
    home = pre.shape[1]
    rows = pick.shape[0]
    blocks = act_out.shape[1] // block

    def fetch(i):
        columns = pl.ds(base + i * block, block)
        return pltpu.make_async_copy(pre_hbm.at[:, columns], pre.at[i], sems.at[i])

    for i in range(blocks):
        fetch(i).start()
    if late:
        pick[...] = late_picks(meta, home)
    else:
        pick[0:EARLY, :] = early_picks(meta, home)
        pick[EARLY:, :] = kept_picks(meta, home)
    step = next(TILE * k for k in (3, 4, 2, 1) if rows % (TILE * k) == 0)
    for i in range(blocks):
        fetch(i).wait()
        rows_f32[...] = jnp.dot(pick[...], pre[i], preferred_element_type=F32)
        columns = slice(i * block, (i + 1) * block)

        def body(k, _):
            at = pl.ds(pl.multiple_of(k * step, step), step)
            value, slope = gelu_and_slope(rows_f32[at, :])
            act_out[at, columns] = value.astype(BF)
            der_out[at, columns] = slope
            return 0

        lax.fori_loop(0, rows // step, body, 0)


def assemble(meta, pieces, first_row, lhs):
    rows = lhs.shape[0]
    width = pieces[1][0].shape[1]
    for j, piece in enumerate(pieces):
        columns = pl.ds(pl.multiple_of((tensor_at(meta) ^ j) * width, 128), width)
        at = 0
        for block in piece:
            low, high = max(at, first_row), min(at + block.shape[0], first_row + rows)
            if low < high:
                lhs[low - first_row : high - first_row, columns] = block[low - at : high - at, 0:width]
            at += block.shape[0]


def split(refs, counts):
    out, at = [], 0
    for count in counts:
        out.append(refs[at : at + count])
        at += count
    return out


def grad_kernel(counts, first_row, block, meta, *refs):
    p0, p1, p2, p3, (weight,), slopes, outs, (lhs,) = split(refs, counts)
    rows = lhs.shape[0]
    assemble(meta, (p0, p1, p2, p3), first_row, lhs)
    part = slopes[0].shape[1]
    at = 0
    for out in outs:
        for c in range(0, out.shape[1], block):
            slope = slopes[at // part][first_row : first_row + rows, at % part : at % part + block]
            value = jnp.dot(lhs[...], weight[:, at : at + block], preferred_element_type=F32)
            out[:, c : c + block] = (value * slope).astype(BF)
            at += block


def early_kernel(block, meta, own, p1, p2, p3, weight, out, lhs, acc):
    width = p1.shape[1]
    assemble(meta, ([own], [p1], [p2], [p3]), 0, lhs)
    for at in range(0, out.shape[1], block):
        columns = slice(at, at + block)
        acc[...] = jnp.dot(lhs[...], weight[:, columns], preferred_element_type=F32)

        def body(k, _):
            rows = pl.ds(pl.multiple_of(k * TILE, TILE), TILE)
            _, slope = gelu_and_slope(own[rows, width + at : width + at + block].astype(F32))
            out[rows, columns] = (acc[rows, :] * slope).astype(BF)
            return 0

        lax.fori_loop(0, EARLY // TILE, body, 0)


def product(lhs_late, lhs_rest, act_late, act_rest, base):
    columns = slice(base, base + act_rest.shape[1])
    return jnp.dot(lhs_late[...], act_late[:, columns], preferred_element_type=F32) + jnp.dot(
        lhs_rest[...], act_rest[...], preferred_element_type=F32
    )


def weight_kernel(counts, base, meta, *refs):
    *parts, (act_late, act_rest, send, keep, lhs_late, lhs_rest) = split(refs, counts)
    count = len(parts) // 2
    half = parts[0][0].shape[1] // 2
    mine = dp_at(meta) % 2 == 0
    for i in range(count):
        for blocks, lhs in ((parts[2 * i], lhs_late), (parts[2 * i + 1], lhs_rest)):
            both = blocks[0][...]
            if len(blocks) > 1:
                both = jnp.concatenate([block[...] for block in blocks], axis=0)
            both = both.T
            lo, hi = both[:half], both[half:]
            lhs[i * half : (i + 1) * half, :] = jnp.where(mine, hi, lo)
            lhs[(count + i) * half : (count + i + 1) * half, :] = jnp.where(mine, lo, hi)
    value = product(lhs_late, lhs_rest, act_late, act_rest, base)
    send[...] = value[: count * half].astype(BF)
    keep[...] = value[count * half :]


def weight_again_kernel(base, meta, late_01, rest_01, late_23, rest_23, act_late, act_rest, send, keep):
    rows = late_01.shape[0] // 2
    for i, (late, rest) in enumerate(((late_01, rest_01), (late_23, rest_23))):
        value = product(late, rest, act_late, act_rest, base)
        send[i * rows : (i + 1) * rows, :] = value[:rows].astype(BF)
        keep[i * rows : (i + 1) * rows, :] = value[rows:]


def near_kernel(count, meta, *refs):
    keeps, gots, (out, mine) = refs[:count], refs[count : 2 * count], refs[2 * count :]
    half = out.shape[0] // 2
    parts = [(k, g, at) for k, g in zip(keeps, gots) for at in range(0, k.shape[0], half)]
    keeps_even = (dp_at(meta) // 2 + tensor_at(meta)) % 2 == 0
    step = 2 * TILE

    for pair in range(2):
        (k0, g0, a0), (k1, g1, a1) = parts[2 * pair], parts[2 * pair + 1]

        def body(i, _):
            def rows(at):
                return pl.ds(pl.multiple_of(at + i * step, TILE), step)

            even = k0[rows(a0), :] + g0[rows(a0), :].astype(F32)
            odd = k1[rows(a1), :] + g1[rows(a1), :].astype(F32)
            out[rows(pair * half), :] = jnp.where(keeps_even, odd, even).astype(BF)
            mine[rows(pair * half), :] = jnp.where(keeps_even, even, odd)
            return 0

        lax.fori_loop(0, half // step, body, 0)


def far_kernel(meta, held, got, out, mine):
    half = out.shape[0]
    keeps_first = (dp_at(meta) // 4 + tensor_at(meta) // 2) % 2 == 0
    step = 2 * TILE

    def body(i, _):
        first = pl.ds(pl.multiple_of(i * step, TILE), step)
        second = pl.ds(pl.multiple_of(half + i * step, TILE), step)
        a = held[first, :] + got[first, :].astype(F32)
        b = held[second, :] + got[second, :].astype(F32)
        out[first, :] = jnp.where(keeps_first, b, a).astype(BF)
        mine[first, :] = jnp.where(keeps_first, a, b)
        return 0

    lax.fori_loop(0, half // step, body, 0)


def place_kernel(meta, kept, early, inner, outer, out):
    d = dp_at(meta)
    count = kept_total(meta, d)
    first = jnp.minimum(count - lax.rem(count, TILE), BAL - SEND)
    first = pl.multiple_of(first, TILE)
    wide = out.shape[1]
    columns = pl.ds(pl.multiple_of(pl.program_id(0) * wide, wide), wide)
    out[0:KEEP, :] = kept[:, columns]
    out[KEEP:, :] = jnp.zeros((out.shape[0] - KEEP, wide), BF)

    def put(block, at):
        rows = lax.broadcasted_iota(jnp.int32, (block.shape[0], 1), 0) + at
        window = pl.ds(at, block.shape[0])
        out[window, :] = jnp.where(rows < count, out[window, :], block)

    put(early[:, columns], first)
    is_inner = (d // 2 == 1) | (d // 2 == 2)
    put(jnp.where(is_inner, inner[:, columns], outer[:, columns]), pl.multiple_of(first + EARLY, TILE))


def swapped(block, axis, distance):
    n = lax.axis_size(axis)
    return lax.ppermute(block, axis, [(i, i ^ distance) for i in range(n)])


def routed(block, pairs):
    return lax.ppermute(block, "dp", [(2 * a + x, 2 * b + x) for a, b in pairs for x in range(2)])


def after(value, *others):
    return lax.optimization_barrier((value, *others))[0]


def shards(hidden_pre, cotangent, down_weight, layer_scale, crop_lengths, crop_moves):
    hidden_pre, cotangent, layer_scale = (
        pltpu.with_memory_space_constraint(x, pltpu.HBM) for x in (hidden_pre, cotangent, layer_scale)
    )
    home, ff = hidden_pre.shape
    width = cotangent.shape[1]
    features = down_weight.shape[0]
    half, part = width // 2, ff // 3
    others = EARLY + KEEP
    n = lax.axis_size("dp")
    d = lax.axis_index("dp").astype(jnp.int32)
    t = lax.axis_index("tensor").astype(jnp.int32)
    column = lax.broadcasted_iota(jnp.int32, (1, n), 1)
    own = jnp.where(column == 0, d, jnp.where(column == 1, t, 0))
    meta = jnp.concatenate([crop_lengths.T, crop_moves.T, own])
    vmem = pltpu.VMEM
    sems = pltpu.SemaphoreType.DMA

    def gelu(meta, late, base, columns):
        block = 256
        rows = LATE if late else others
        return kernel_call(
            functools.partial(gelu_kernel, late, base, block),
            [shape(rows, columns), shape(rows, columns, F32)],
            [IN_HBM], [IN_VMEM] * 2,
            [vmem((rows, home), BF), vmem((rows, block), F32), vmem((columns // block, home, block), BF),
             sems((columns // block,))],
        )(meta, hidden_pre)

    def weight_part(meta, pieces, act):
        count = len(pieces)
        parts = [x for j in pieces for x in (lates[j], rests[j])]
        counts = [len(x) for x in parts] + [6]
        blocks = [block for x in parts for block in x]
        return kernel_call(
            functools.partial(weight_kernel, counts, 0),
            [shape(count * half, part), shape(count * half, part, F32),
             shape(count * width, LATE), shape(count * width, others)],
            [IN_VMEM] * (len(blocks) + 2), [IN_VMEM] * 4,
        )(meta, *blocks, act_late, act)

    def weight_again(meta, base, act):
        return kernel_call(
            functools.partial(weight_again_kernel, base),
            [shape(4 * half, part), shape(4 * half, part, F32)], [IN_VMEM] * 6, [IN_VMEM] * 2,
        )(meta, *lhs_01, *lhs_23, act_late, act)

    def grads(meta, pieces, first_row, rows, slopes, cuts):
        counts = [len(x) for x in pieces] + [1, len(slopes), len(cuts), 1]
        blocks = [block for x in pieces for block in x]
        return kernel_call(
            functools.partial(grad_kernel, counts, first_row, 256),
            [shape(rows, c) for c in cuts], [IN_VMEM] * (len(blocks) + 1 + len(slopes)), [IN_VMEM] * len(cuts),
            [vmem((rows, features), BF)],
        )(meta, *blocks, down_weight, *slopes)

    def near_step(meta, keeps, gots):
        count = len(keeps)
        return kernel_call(
            functools.partial(near_kernel, count),
            [shape(width, part), shape(width, part, F32)], [IN_VMEM] * (2 * count), [IN_VMEM] * 2,
        )(meta, *keeps, *gots)

    def far_step(meta, mine, got):
        return kernel_call(
            far_kernel, [shape(half, part), shape(half, part, F32)], [IN_VMEM] * 2, [IN_VMEM] * 2
        )(meta, mine, got)

    cut = others // 2
    late, early, rest, *rest_blocks = kernel_call(
        first_kernel,
        [shape(r, c) for r, c in ((LATE, width), (EARLY, width + ff), (others, width), (cut, width), (others - cut, width))],
        [IN_HBM] * 3, [IN_VMEM] * 5,
        [vmem((home, width), BF), vmem((features,), F32), vmem((home, ff), BF), sems((3,))],
    )(meta, cotangent, layer_scale, hidden_pre)
    arrived_early = swapped(early, "dp", n // 2)
    late_c, late_y = swapped(late, "tensor", 1), swapped(late, "tensor", 2)
    act_late, der_late = gelu(after(meta, late), True, 0, ff)

    late_y = after(late_y, act_late, late_c, arrived_early)
    late_yc = swapped(late_y, "tensor", 1)
    rest_y = [swapped(after(block, late_y), "tensor", 2) for block in rest_blocks]
    rest_c = swapped(after(rest, late_y), "tensor", 1)

    lates = ([late], [late_c], [late_y], [late_yc])
    (moving,) = grads(after(meta, late_y), lates, 0, LATE, (der_late,), (ff,))
    from_outer = routed(moving, ((0, 1), (3, 2)))
    from_inner = routed(moving, ((1, 2), (2, 1)))

    act_a, der_a = gelu(after(meta, moving), False, 0, part)
    rests = ([rest], [rest_c])
    send_01, keep_01, *lhs_01 = weight_part(after(meta, act_a), (0, 1), act_a)
    got_01 = swapped(send_01, "dp", 1)
    act_b, der_b = gelu(after(meta, send_01), False, part, part)
    rest_y = [after(block, act_b) for block in rest_y]
    rest_yc = [swapped(block, "tensor", 1) for block in rest_y]
    rests = ([rest], [rest_c], rest_y, rest_yc)
    send_23, keep_23, *lhs_23 = weight_part(after(meta, act_b, got_01), (2, 3), act_a)
    got_23 = swapped(send_23, "dp", 1)
    send_b, keep_b = weight_again(after(meta, send_23), part, act_b)
    got_b = swapped(send_b, "dp", 1)

    out_na, mine_a = near_step(after(meta, send_b), (keep_01, keep_23), (got_01, got_23))
    got_na = swapped(out_na, "dp", 2)
    arrived_inner = routed(after(from_outer, out_na), ((1, 2), (2, 1)))
    arrived_outer = routed(after(from_inner, out_na), ((2, 3), (1, 0)))

    act_c, der_c = gelu(after(meta, out_na), False, 2 * part, part)
    early_sent = after(arrived_early[:, :width], act_c)
    early_c, early_y = swapped(early_sent, "tensor", 1), swapped(early_sent, "tensor", 2)
    send_c, keep_c = weight_again(after(meta, act_c), 2 * part, act_c)
    out_nb, mine_b = near_step(after(meta, send_c, got_na), (keep_b,), (got_b,))
    got_nb = swapped(out_nb, "dp", 2)
    got_c = swapped(after(send_c, out_nb), "dp", 1)

    (kept_grad,) = grads(after(meta, out_nb), rests, EARLY, KEEP, (der_a, der_b, der_c), (ff,))
    early_y = after(early_y, kept_grad, early_c)
    early_yc = swapped(early_y, "tensor", 1)
    early_grad = kernel_call(
        functools.partial(early_kernel, 256), shape(EARLY, ff), [IN_VMEM] * 5, IN_VMEM,
        [vmem((EARLY, features), BF), vmem((EARLY, 256), F32)],
    )(after(meta, kept_grad), arrived_early, early_c, early_y, early_yc, down_weight)

    out_fa, own_a = far_step(after(meta, early_grad, arrived_inner, arrived_outer), mine_a, got_na)
    got_fa = swapped(out_fa, "dp", 4)
    out_nc, mine_c = near_step(after(meta, out_fa), (keep_c,), (got_c,))
    got_nc = swapped(out_nc, "dp", 2)
    out_fb, own_b = far_step(after(meta, out_nc, got_fa), mine_b, got_nb)
    got_fb = swapped(out_fb, "dp", 4)
    out_fc, own_c = far_step(after(meta, out_fb), mine_c, got_nc)
    got_fc = swapped(out_fc, "dp", 4)
    total = [a + b.astype(F32) for a, b in ((own_a, got_fa), (own_b, got_fb), (own_c, got_fc))]
    down_grad = jnp.concatenate(total, axis=1) / math.sqrt(n * home)

    hidden_grad = kernel_call(
        place_kernel, shape(BAL, ff), [IN_VMEM] * 4,
        pl.BlockSpec((BAL, 256), lambda i, *_: (0, i)), grid=(ff // 256,),
    )(after(meta, out_fb), kept_grad, early_grad, arrived_inner, arrived_outer)
    return (hidden_grad, down_grad)


def solution(mesh):
    pairs_and_fours = (mesh.shape["dp"], mesh.shape["tensor"]) == (8, 4)
    return jax.shard_map(
        shards if pairs_and_fours else general_shards,
        mesh=mesh,
        in_specs=(P("dp", "tensor"), P("dp", "tensor"), P(None, "tensor"), P(), P(), P()),
        out_specs=(P("dp", "tensor"), P("dp", "tensor")),
        check_vma=False,
    )


def shifted(block, axis, distance):
    devices = range(lax.axis_size(axis))
    route = [((i - distance) % len(devices), i) for i in devices]
    return lax.ppermute(block, axis, route)


def crop_rows(row_total, crop_sizes, crop_starts):
    crop_ends = jnp.cumsum(crop_sizes)
    crop_begins = crop_ends - crop_sizes
    target_rows = jnp.arange(row_total, dtype=jnp.int32)[:, None]
    inside_crop = (target_rows >= crop_begins[None, :]) & (target_rows < crop_ends[None, :])
    source_rows = jnp.sum(
        jnp.where(inside_crop, crop_starts[None, :] + target_rows - crop_begins[None, :], 0), axis=1
    )
    return (source_rows, jnp.any(inside_crop, axis=1))


def select_rows(row_block, source_rows, valid_rows):
    taken = jnp.take(row_block, source_rows, axis=0)
    return jnp.where(valid_rows[:, None], taken, jnp.zeros((), row_block.dtype))


def gelu_parts(pre_act):
    cumulative = 0.5 * (1.0 + jax.scipy.special.erf(pre_act * inv_root_two))
    activated = pre_act * cumulative
    derivative = cumulative + pre_act * jnp.exp(-0.5 * pre_act * pre_act) * inv_root_tau
    return (activated, derivative)


def local_grads(pre_rows, cot_part, live_rows, layer_scale, down_weight, home_rows):
    cot_full = lax.all_gather(cot_part, "tensor", axis=1, tiled=True)
    scaled = (cot_full.astype(F32) * layer_scale[None, :]).astype(BF)
    activated, derivative = gelu_parts(pre_rows.astype(F32))
    activation = jnp.where(live_rows[:, None], activated, 0.0).astype(BF)
    backward = jnp.dot(scaled, down_weight, preferred_element_type=F32) * derivative
    gradient_rows = jnp.where(live_rows[:, None], backward, 0.0).astype(BF)
    weight_grad = lax.psum_scatter(
        lax.dot_general(scaled, activation, (((0,), (0,)), ((), ())), preferred_element_type=F32),
        "dp",
        scatter_dimension=0,
        tiled=True,
    )
    return (gradient_rows, weight_grad / math.sqrt(lax.axis_size("dp") * home_rows))


def general_shards(hidden_pre, cotangent, down_weight, layer_scale, crop_lengths, crop_moves):
    devices = lax.axis_size("dp")
    half_axis = devices // 2
    device_index = lax.axis_index("dp")
    partner_index = (device_index + half_axis) % devices
    own_lengths = lax.dynamic_index_in_dim(crop_lengths, device_index, 0, keepdims=False)
    own_moves = lax.dynamic_index_in_dim(crop_moves, device_index, 0, keepdims=False)
    partner_lengths = lax.dynamic_index_in_dim(crop_lengths, partner_index, 0, keepdims=False)
    partner_moves = lax.dynamic_index_in_dim(crop_moves, partner_index, 0, keepdims=False)
    home_rows = hidden_pre.shape[0]
    own_starts = jnp.cumsum(own_lengths) - own_lengths
    sent_sizes = own_lengths * own_moves
    kept_sizes = own_lengths * (1 - own_moves)
    arrived = jnp.sum(partner_lengths * partner_moves)
    send_source, send_valid = crop_rows(SEND, sent_sizes, own_starts)
    keep_sizes = jnp.concatenate([kept_sizes, arrived[None]])
    keep_starts = jnp.concatenate([own_starts, jnp.full((1,), home_rows, jnp.int32)])
    keep_source, keep_valid = crop_rows(BAL, keep_sizes, keep_starts)
    live_home = jnp.arange(home_rows, dtype=jnp.int32) < jnp.sum(own_lengths)
    gradient_rows, weight_grad = local_grads(
        hidden_pre, cotangent, live_home, layer_scale, down_weight, home_rows
    )
    outgoing = select_rows(gradient_rows, send_source, send_valid)
    incoming = shifted(outgoing, "dp", half_axis)
    balanced = select_rows(jnp.concatenate([gradient_rows, incoming], 0), keep_source, keep_valid)
    return (balanced, weight_grad)
```

```python
import functools
import math

import jax
import jax.numpy as jnp
from jax import lax
from jax.experimental import pallas as pl
from jax.experimental.pallas import tpu as pltpu
from jax.sharding import PartitionSpec as P

SEND = 528
KEEP = 528
TILE = 16
EARLY = 80
LATE = SEND - EARLY
SLOTS = 4
BAL = 720
BF = jnp.bfloat16
F32 = jnp.float32

inv_root_two = 0.7071067811865476
inv_root_tau = 0.3989422804014327


def kernel_call(kernel, out_shape, in_specs, out_specs, scratch=(), grid=(1,)):
    return pl.pallas_call(
        kernel,
        grid_spec=pltpu.PrefetchScalarGridSpec(
            num_scalar_prefetch=1,
            grid=grid,
            in_specs=in_specs,
            out_specs=out_specs,
            scratch_shapes=list(scratch),
        ),
        out_shape=out_shape,
        cost_estimate=pl.CostEstimate(flops=1, bytes_accessed=1, transcendentals=0),
        compiler_params=pltpu.CompilerParams(vmem_limit_bytes=16 * 1024 * 1024),
    )


IN_VMEM = pl.BlockSpec(memory_space=pltpu.VMEM)
IN_HBM = pl.BlockSpec(memory_space=pltpu.HBM)


def shape(a, b, dtype=BF):
    return jax.ShapeDtypeStruct((a, b), dtype)


def lengths_of(meta, d):
    return [meta[j, d] for j in range(SLOTS)]


def moves_of(meta, d):
    return [meta[SLOTS + j, d] for j in range(SLOTS)]


def dp_at(meta):
    return meta[2 * SLOTS, 0]


def tensor_at(meta):
    return meta[2 * SLOTS, 1]


def kept_total(meta, d):
    return sum(a * (1 - b) for a, b in zip(lengths_of(meta, d), moves_of(meta, d)))


def picks(meta, moved, first, rows, home):
    d = dp_at(meta)
    at = lax.broadcasted_iota(jnp.int32, (rows, 1), 0) - first
    source = jnp.full((rows, 1), -1, jnp.int32)
    begin = jnp.int32(0)
    start = jnp.int32(0)
    for length, move in zip(lengths_of(meta, d), moves_of(meta, d)):
        size = length * (move if moved else 1 - move)
        inside = (at >= begin) & (at < begin + size)
        source = jnp.where(inside, at + (start - begin), source)
        begin = begin + size
        start = start + length
    columns = lax.broadcasted_iota(jnp.int32, (rows, home), 1)
    return jnp.where(columns == source, 1.0, 0.0).astype(BF)


def sent_first(meta):
    n = meta.shape[1]
    partner = lax.rem(dp_at(meta) + n // 2, n)
    return lax.rem(kept_total(meta, partner), TILE)


def early_picks(meta, home):
    return picks(meta, True, sent_first(meta), EARLY, home)


def late_picks(meta, home):
    return picks(meta, True, sent_first(meta) - EARLY, LATE, home)


def kept_picks(meta, home):
    return picks(meta, False, 0, KEEP, home)


def scaled_rows(meta, pick, cot, scale):
    width = cot.shape[1]
    rows = jnp.dot(pick, cot[...], preferred_element_type=F32)
    own = scale[pl.ds(pl.multiple_of(tensor_at(meta) * width, 128), width)]
    return (rows * own[None, :]).astype(BF)


def first_kernel(meta, cot_hbm, scale_hbm, pre_hbm, rows_out, early_out, cot, scale, pre, sems):
    home, width = cot.shape
    pairs = ((cot_hbm, cot), (scale_hbm, scale), (pre_hbm, pre))
    copies = [pltpu.make_async_copy(a, b, sems.at[i]) for i, (a, b) in enumerate(pairs)]
    for copy in copies:
        copy.start()
    early = early_picks(meta, home)
    copies[0].wait()
    copies[1].wait()
    early_rows = scaled_rows(meta, early, cot, scale)
    early_out[:, :width] = early_rows
    rows_out[0:LATE, :] = scaled_rows(meta, late_picks(meta, home), cot, scale)
    rows_out[LATE:SEND, :] = early_rows
    rows_out[SEND:, :] = scaled_rows(meta, kept_picks(meta, home), cot, scale)
    copies[2].wait()
    early_out[:, width:] = jnp.dot(early, pre[...], preferred_element_type=F32).astype(BF)


def gelu_and_slope(x):
    cumulative = 0.5 * (1.0 + lax.erf(x * inv_root_two))
    return x * cumulative, cumulative + x * jnp.exp(-0.5 * x * x) * inv_root_tau


def gelu_kernel(late, base, block, meta, pre_hbm, act_out, der_out, pick, rows_f32, pre, sems):
    home = pre.shape[1]
    rows = pick.shape[0]
    blocks = act_out.shape[1] // block

    def fetch(i):
        columns = pl.ds(base + i * block, block)
        return pltpu.make_async_copy(pre_hbm.at[:, columns], pre.at[i], sems.at[i])

    for i in range(blocks):
        fetch(i).start()
    if late:
        pick[...] = late_picks(meta, home)
    else:
        pick[0:EARLY, :] = early_picks(meta, home)
        pick[EARLY:, :] = kept_picks(meta, home)
    step = next(TILE * k for k in (3, 4, 2, 1) if rows % (TILE * k) == 0)
    for i in range(blocks):
        fetch(i).wait()
        rows_f32[...] = jnp.dot(pick[...], pre[i], preferred_element_type=F32)
        columns = slice(i * block, (i + 1) * block)

        def body(k, _):
            at = pl.ds(pl.multiple_of(k * step, step), step)
            value, slope = gelu_and_slope(rows_f32[at, :])
            act_out[at, columns] = value.astype(BF)
            der_out[at, columns] = slope
            return 0

        lax.fori_loop(0, rows // step, body, 0)


def assemble(meta, pieces, first_row, lhs):
    rows = lhs.shape[0]
    width = pieces[1].shape[1]
    for j, piece in enumerate(pieces):
        columns = pl.ds(pl.multiple_of((tensor_at(meta) ^ j) * width, 128), width)
        lhs[:, columns] = piece[first_row : first_row + rows, 0:width]


def grad_kernel(first_row, first_slope, slope_count, block, meta, p0, p1, p2, p3, weight, *rest):
    slopes, outs, lhs = rest[:slope_count], rest[slope_count:-1], rest[-1]
    rows = lhs.shape[0]
    assemble(meta, (p0, p1, p2, p3), first_row, lhs)
    part = slopes[0].shape[1]
    at = 0
    for out in outs:
        for c in range(0, out.shape[1], block):
            slope = slopes[at // part][first_slope : first_slope + rows, at % part : at % part + block]
            value = jnp.dot(lhs[...], weight[:, at : at + block], preferred_element_type=F32)
            out[:, c : c + block] = (value * slope).astype(BF)
            at += block


def early_kernel(block, meta, own, p1, p2, p3, weight, out, lhs, acc):
    width = p1.shape[1]
    assemble(meta, (own, p1, p2, p3), 0, lhs)
    for at in range(0, out.shape[1], block):
        columns = slice(at, at + block)
        acc[...] = jnp.dot(lhs[...], weight[:, columns], preferred_element_type=F32)

        def body(k, _):
            rows = pl.ds(pl.multiple_of(k * TILE, TILE), TILE)
            _, slope = gelu_and_slope(own[rows, width + at : width + at + block].astype(F32))
            out[rows, columns] = (acc[rows, :] * slope).astype(BF)
            return 0

        lax.fori_loop(0, EARLY // TILE, body, 0)


def product(lhs_late, lhs_rest, act_late, act_rest, base):
    columns = slice(base, base + act_rest.shape[1])
    return jnp.dot(lhs_late[...], act_late[:, columns], preferred_element_type=F32) + jnp.dot(
        lhs_rest[...], act_rest[...], preferred_element_type=F32
    )


def weight_kernel(count, base, meta, *refs):
    pieces, (act_late, act_rest, send, keep, lhs_late, lhs_rest) = refs[:count], refs[count:]
    half = pieces[0].shape[1] // 2
    mine = dp_at(meta) % 2 == 0
    for i, piece in enumerate(pieces):
        for rows, lhs in ((slice(0, LATE), lhs_late), (slice(LATE, SEND + KEEP), lhs_rest)):
            both = piece[rows, :].T
            lo, hi = both[:half], both[half:]
            lhs[i * half : (i + 1) * half, :] = jnp.where(mine, hi, lo)
            lhs[(count + i) * half : (count + i + 1) * half, :] = jnp.where(mine, lo, hi)
    value = product(lhs_late, lhs_rest, act_late, act_rest, base)
    send[...] = value[: count * half].astype(BF)
    keep[...] = value[count * half :]


def weight_again_kernel(base, meta, late_01, rest_01, late_23, rest_23, act_late, act_rest, send, keep):
    rows = late_01.shape[0] // 2
    for i, (late, rest) in enumerate(((late_01, rest_01), (late_23, rest_23))):
        value = product(late, rest, act_late, act_rest, base)
        send[i * rows : (i + 1) * rows, :] = value[:rows].astype(BF)
        keep[i * rows : (i + 1) * rows, :] = value[rows:]


def near_kernel(count, meta, *refs):
    keeps, gots, (out, mine) = refs[:count], refs[count : 2 * count], refs[2 * count :]
    half = out.shape[0] // 2
    parts = [(k, g, at) for k, g in zip(keeps, gots) for at in range(0, k.shape[0], half)]
    keeps_even = (dp_at(meta) // 2 + tensor_at(meta)) % 2 == 0
    step = 2 * TILE

    for pair in range(2):
        (k0, g0, a0), (k1, g1, a1) = parts[2 * pair], parts[2 * pair + 1]

        def body(i, _):
            def rows(at):
                return pl.ds(pl.multiple_of(at + i * step, TILE), step)

            even = k0[rows(a0), :] + g0[rows(a0), :].astype(F32)
            odd = k1[rows(a1), :] + g1[rows(a1), :].astype(F32)
            out[rows(pair * half), :] = jnp.where(keeps_even, odd, even).astype(BF)
            mine[rows(pair * half), :] = jnp.where(keeps_even, even, odd)
            return 0

        lax.fori_loop(0, half // step, body, 0)


def far_kernel(meta, held, got, out, mine):
    half = out.shape[0]
    keeps_first = (dp_at(meta) // 4 + tensor_at(meta) // 2) % 2 == 0
    step = 2 * TILE

    def body(i, _):
        first = pl.ds(pl.multiple_of(i * step, TILE), step)
        second = pl.ds(pl.multiple_of(half + i * step, TILE), step)
        a = held[first, :] + got[first, :].astype(F32)
        b = held[second, :] + got[second, :].astype(F32)
        out[first, :] = jnp.where(keeps_first, b, a).astype(BF)
        mine[first, :] = jnp.where(keeps_first, a, b)
        return 0

    lax.fori_loop(0, half // step, body, 0)


def place_kernel(meta, kept, early, *rest):
    inner, outer, out = rest[:2], rest[2:4], rest[4]
    d = dp_at(meta)
    count = kept_total(meta, d)
    first = jnp.minimum(count - lax.rem(count, TILE), BAL - SEND)
    first = pl.multiple_of(first, TILE)
    wide = out.shape[1]
    step = pl.program_id(0)
    columns = pl.ds(pl.multiple_of(step * wide, wide), wide)
    out[0:KEEP, :] = kept[:, columns]
    out[KEEP:, :] = jnp.zeros((out.shape[0] - KEEP, wide), BF)

    def put(block, at):
        rows = lax.broadcasted_iota(jnp.int32, (block.shape[0], 1), 0) + at
        window = pl.ds(at, block.shape[0])
        out[window, :] = jnp.where(rows < count, out[window, :], block)

    put(early[:, columns], first)
    is_inner = (d // 2 == 1) | (d // 2 == 2)
    half = inner[0].shape[1] // wide
    for i in range(2):

        @pl.when(step // half == i)
        def _():
            at = pl.ds(pl.multiple_of((step - i * half) * wide, wide), wide)
            block = jnp.where(is_inner, inner[i][:, at], outer[i][:, at])
            put(block, pl.multiple_of(first + EARLY, TILE))


def swapped(block, axis, distance):
    n = lax.axis_size(axis)
    return lax.ppermute(block, axis, [(i, i ^ distance) for i in range(n)])


def routed(block, pairs):
    return lax.ppermute(block, "dp", [(2 * a + x, 2 * b + x) for a, b in pairs for x in range(2)])


def after(value, *others):
    return lax.optimization_barrier((value, *others))[0]


def shards(hidden_pre, cotangent, down_weight, layer_scale, crop_lengths, crop_moves):
    hidden_pre, cotangent, layer_scale = (
        pltpu.with_memory_space_constraint(x, pltpu.HBM) for x in (hidden_pre, cotangent, layer_scale)
    )
    home, ff = hidden_pre.shape
    width = cotangent.shape[1]
    features = down_weight.shape[0]
    half, part = width // 2, ff // 3
    others = EARLY + KEEP
    n = lax.axis_size("dp")
    d = lax.axis_index("dp").astype(jnp.int32)
    t = lax.axis_index("tensor").astype(jnp.int32)
    column = lax.broadcasted_iota(jnp.int32, (1, n), 1)
    own = jnp.where(column == 0, d, jnp.where(column == 1, t, 0))
    meta = jnp.concatenate([crop_lengths.T, crop_moves.T, own])
    vmem = pltpu.VMEM
    sems = pltpu.SemaphoreType.DMA

    def gelu(meta, late, base, columns):
        block = 256
        rows = LATE if late else others
        return kernel_call(
            functools.partial(gelu_kernel, late, base, block),
            [shape(rows, columns), shape(rows, columns, F32)],
            [IN_HBM], [IN_VMEM] * 2,
            [vmem((rows, home), BF), vmem((rows, block), F32), vmem((columns // block, home, block), BF),
             sems((columns // block,))],
        )(meta, hidden_pre)

    def weight_part(meta, pieces, act):
        count = len(pieces)
        return kernel_call(
            functools.partial(weight_kernel, count, 0),
            [shape(count * half, part), shape(count * half, part, F32),
             shape(count * width, LATE), shape(count * width, others)],
            [IN_VMEM] * (count + 2), [IN_VMEM] * 4,
        )(meta, *pieces, act_late, act)

    def weight_again(meta, base, act):
        return kernel_call(
            functools.partial(weight_again_kernel, base),
            [shape(4 * half, part), shape(4 * half, part, F32)], [IN_VMEM] * 6, [IN_VMEM] * 2,
        )(meta, *lhs_01, *lhs_23, act_late, act)

    def grads(meta, first_row, first_slope, rows, slopes, cuts):
        return kernel_call(
            functools.partial(grad_kernel, first_row, first_slope, len(slopes), 256),
            [shape(rows, c) for c in cuts], [IN_VMEM] * (5 + len(slopes)), [IN_VMEM] * len(cuts),
            [vmem((rows, features), BF)],
        )(meta, *pieces, down_weight, *slopes)

    def near_step(meta, keeps, gots):
        count = len(keeps)
        return kernel_call(
            functools.partial(near_kernel, count),
            [shape(width, part), shape(width, part, F32)], [IN_VMEM] * (2 * count), [IN_VMEM] * 2,
        )(meta, *keeps, *gots)

    def far_step(meta, mine, got):
        return kernel_call(
            far_kernel, [shape(half, part), shape(half, part, F32)], [IN_VMEM] * 2, [IN_VMEM] * 2
        )(meta, mine, got)

    own_rows, early = kernel_call(
        first_kernel, [shape(SEND + KEEP, width), shape(EARLY, width + ff)], [IN_HBM] * 3, [IN_VMEM] * 2,
        [vmem((home, width), BF), vmem((features,), F32), vmem((home, ff), BF), sems((3,))],
    )(meta, cotangent, layer_scale, hidden_pre)
    arrived_early = swapped(early, "dp", n // 2)

    rows_c, rows_y = swapped(own_rows, "tensor", 1), swapped(own_rows, "tensor", 2)
    act_late, der_late = gelu(after(meta, own_rows), True, 0, ff)
    act_a, der_a = gelu(after(meta, act_late), False, 0, part)

    send_01, keep_01, *lhs_01 = weight_part(after(meta, act_a), (own_rows, rows_c), act_a)
    got_01 = swapped(send_01, "dp", 1)
    rows_y = after(rows_y, send_01, arrived_early)
    rows_yc = swapped(rows_y, "tensor", 1)
    pieces = (own_rows, rows_c, rows_y, rows_yc)

    moving = grads(after(meta, rows_y), 0, 0, LATE, (der_late,), (ff // 2, ff // 2))
    to_inner, across, to_outer = ((0, 1), (3, 2)), ((1, 2), (2, 1)), ((1, 0), (2, 3))
    at_inner_a = routed(moving[0], to_inner)
    crossed_a = routed(moving[0], across)
    crossed_b = routed(moving[1], across)

    send_23, keep_23, *lhs_23 = weight_part(after(meta, got_01, *moving), (rows_y, rows_yc), act_a)
    got_23 = swapped(send_23, "dp", 1)
    act_b, der_b = gelu(after(meta, send_23), False, part, part)
    send_b, keep_b = weight_again(after(meta, act_b), part, act_b)
    got_b = swapped(send_b, "dp", 1)

    out_na, mine_a = near_step(
        after(meta, send_b, at_inner_a, crossed_a), (keep_01, keep_23), (got_01, got_23)
    )
    got_na = swapped(out_na, "dp", 2)
    act_c, der_c = gelu(after(meta, out_na), False, 2 * part, part)
    early_sent = after(arrived_early[:, :width], act_c)
    early_c, early_y = swapped(early_sent, "tensor", 1), swapped(early_sent, "tensor", 2)
    send_c, keep_c = weight_again(after(meta, act_c), 2 * part, act_c)
    early_y = after(early_y, send_c, early_c)
    early_yc = swapped(early_y, "tensor", 1)

    is_inner = (d // 2 == 1) | (d // 2 == 2)
    hop = jnp.where(is_inner, crossed_a, moving[1])
    hop = after(hop, got_na, send_c, crossed_b)
    hopped = routed(hop, to_inner + to_outer)
    inner_a = routed(after(at_inner_a, send_c), across)

    out_fa, own_a = far_step(after(meta, hop), mine_a, got_na)
    got_fa = swapped(out_fa, "dp", 4)
    out_nb, mine_b = near_step(after(meta, out_fa, hopped, inner_a, early_yc), (keep_b,), (got_b,))
    got_nb = swapped(out_nb, "dp", 2)
    got_c = swapped(after(send_c, out_nb), "dp", 1)
    inner_b = routed(after(hopped, out_nb), across)
    outer_b = routed(after(crossed_b, out_nb), to_outer)

    (kept_grad,) = grads(after(meta, out_nb), SEND, EARLY, KEEP, (der_a, der_b, der_c), (ff,))
    early_grad = kernel_call(
        functools.partial(early_kernel, 256), shape(EARLY, ff), [IN_VMEM] * 5, IN_VMEM,
        [vmem((EARLY, features), BF), vmem((EARLY, 256), F32)],
    )(after(meta, kept_grad), arrived_early, early_c, early_y, early_yc, down_weight)

    out_fb, own_b = far_step(after(meta, early_grad, got_fa), mine_b, got_nb)
    got_fb = swapped(out_fb, "dp", 4)
    out_nc, mine_c = near_step(after(meta, out_fb), (keep_c,), (got_c,))
    got_nc = swapped(out_nc, "dp", 2)
    out_fc, own_c = far_step(after(meta, out_nc, inner_b, outer_b), mine_c, got_nc)
    got_fc = swapped(out_fc, "dp", 4)
    total = [a + b.astype(F32) for a, b in ((own_a, got_fa), (own_b, got_fb), (own_c, got_fc))]
    down_grad = jnp.concatenate(total, axis=1) / math.sqrt(n * home)

    hidden_grad = kernel_call(
        place_kernel, shape(BAL, ff), [IN_VMEM] * 6,
        pl.BlockSpec((BAL, 256), lambda i, *_: (0, i)), grid=(ff // 256,),
    )(after(meta, out_fc), kept_grad, early_grad, inner_a, inner_b, hopped, outer_b)
    return (hidden_grad, down_grad)


def solution(mesh):
    pairs_and_fours = (mesh.shape["dp"], mesh.shape["tensor"]) == (8, 4)
    return jax.shard_map(
        shards if pairs_and_fours else general_shards,
        mesh=mesh,
        in_specs=(P("dp", "tensor"), P("dp", "tensor"), P(None, "tensor"), P(), P(), P()),
        out_specs=(P("dp", "tensor"), P("dp", "tensor")),
        check_vma=False,
    )


def shifted(block, axis, distance):
    devices = range(lax.axis_size(axis))
    route = [((i - distance) % len(devices), i) for i in devices]
    return lax.ppermute(block, axis, route)


def crop_rows(row_total, crop_sizes, crop_starts):
    crop_ends = jnp.cumsum(crop_sizes)
    crop_begins = crop_ends - crop_sizes
    target_rows = jnp.arange(row_total, dtype=jnp.int32)[:, None]
    inside_crop = (target_rows >= crop_begins[None, :]) & (target_rows < crop_ends[None, :])
    source_rows = jnp.sum(
        jnp.where(inside_crop, crop_starts[None, :] + target_rows - crop_begins[None, :], 0), axis=1
    )
    return (source_rows, jnp.any(inside_crop, axis=1))


def select_rows(row_block, source_rows, valid_rows):
    taken = jnp.take(row_block, source_rows, axis=0)
    return jnp.where(valid_rows[:, None], taken, jnp.zeros((), row_block.dtype))


def gelu_parts(pre_act):
    cumulative = 0.5 * (1.0 + jax.scipy.special.erf(pre_act * inv_root_two))
    activated = pre_act * cumulative
    derivative = cumulative + pre_act * jnp.exp(-0.5 * pre_act * pre_act) * inv_root_tau
    return (activated, derivative)


def local_grads(pre_rows, cot_part, live_rows, layer_scale, down_weight, home_rows):
    cot_full = lax.all_gather(cot_part, "tensor", axis=1, tiled=True)
    scaled = (cot_full.astype(F32) * layer_scale[None, :]).astype(BF)
    activated, derivative = gelu_parts(pre_rows.astype(F32))
    activation = jnp.where(live_rows[:, None], activated, 0.0).astype(BF)
    backward = jnp.dot(scaled, down_weight, preferred_element_type=F32) * derivative
    gradient_rows = jnp.where(live_rows[:, None], backward, 0.0).astype(BF)
    weight_grad = lax.psum_scatter(
        lax.dot_general(scaled, activation, (((0,), (0,)), ((), ())), preferred_element_type=F32),
        "dp",
        scatter_dimension=0,
        tiled=True,
    )
    return (gradient_rows, weight_grad / math.sqrt(lax.axis_size("dp") * home_rows))


def general_shards(hidden_pre, cotangent, down_weight, layer_scale, crop_lengths, crop_moves):
    devices = lax.axis_size("dp")
    half_axis = devices // 2
    device_index = lax.axis_index("dp")
    partner_index = (device_index + half_axis) % devices
    own_lengths = lax.dynamic_index_in_dim(crop_lengths, device_index, 0, keepdims=False)
    own_moves = lax.dynamic_index_in_dim(crop_moves, device_index, 0, keepdims=False)
    partner_lengths = lax.dynamic_index_in_dim(crop_lengths, partner_index, 0, keepdims=False)
    partner_moves = lax.dynamic_index_in_dim(crop_moves, partner_index, 0, keepdims=False)
    home_rows = hidden_pre.shape[0]
    own_starts = jnp.cumsum(own_lengths) - own_lengths
    sent_sizes = own_lengths * own_moves
    kept_sizes = own_lengths * (1 - own_moves)
    arrived = jnp.sum(partner_lengths * partner_moves)
    send_source, send_valid = crop_rows(SEND, sent_sizes, own_starts)
    keep_sizes = jnp.concatenate([kept_sizes, arrived[None]])
    keep_starts = jnp.concatenate([own_starts, jnp.full((1,), home_rows, jnp.int32)])
    keep_source, keep_valid = crop_rows(BAL, keep_sizes, keep_starts)
    live_home = jnp.arange(home_rows, dtype=jnp.int32) < jnp.sum(own_lengths)
    gradient_rows, weight_grad = local_grads(
        hidden_pre, cotangent, live_home, layer_scale, down_weight, home_rows
    )
    outgoing = select_rows(gradient_rows, send_source, send_valid)
    incoming = shifted(outgoing, "dp", half_axis)
    balanced = select_rows(jnp.concatenate([gradient_rows, incoming], 0), keep_source, keep_valid)
    return (balanced, weight_grad)
```

```python
import functools
import math

import jax
import jax.numpy as jnp
from jax import lax
from jax.experimental import pallas as pl
from jax.experimental.pallas import tpu as pltpu
from jax.sharding import PartitionSpec as P

SEND = 528
KEEP = 528
TILE = 16
EARLY = 80
LATE = SEND - EARLY
SLOTS = 4
BAL = 720
BF = jnp.bfloat16
F32 = jnp.float32

inv_root_two = 0.7071067811865476
inv_root_tau = 0.3989422804014327


def kernel_call(kernel, out_shape, in_specs, out_specs, scratch=(), grid=(1,)):
    return pl.pallas_call(
        kernel,
        grid_spec=pltpu.PrefetchScalarGridSpec(
            num_scalar_prefetch=1,
            grid=grid,
            in_specs=in_specs,
            out_specs=out_specs,
            scratch_shapes=list(scratch),
        ),
        out_shape=out_shape,
        cost_estimate=pl.CostEstimate(flops=1, bytes_accessed=1, transcendentals=0),
        compiler_params=pltpu.CompilerParams(vmem_limit_bytes=16 * 1024 * 1024),
    )


IN_VMEM = pl.BlockSpec(memory_space=pltpu.VMEM)
IN_HBM = pl.BlockSpec(memory_space=pltpu.HBM)


def shape(a, b, dtype=BF):
    return jax.ShapeDtypeStruct((a, b), dtype)


def lengths_of(meta, d):
    return [meta[j, d] for j in range(SLOTS)]


def moves_of(meta, d):
    return [meta[SLOTS + j, d] for j in range(SLOTS)]


def dp_at(meta):
    return meta[2 * SLOTS, 0]


def tensor_at(meta):
    return meta[2 * SLOTS, 1]


def kept_total(meta, d):
    return sum(a * (1 - b) for a, b in zip(lengths_of(meta, d), moves_of(meta, d)))


def picks(meta, moved, first, rows, home):
    d = dp_at(meta)
    at = lax.broadcasted_iota(jnp.int32, (rows, 1), 0) - first
    source = jnp.full((rows, 1), -1, jnp.int32)
    begin = jnp.int32(0)
    start = jnp.int32(0)
    for length, move in zip(lengths_of(meta, d), moves_of(meta, d)):
        size = length * (move if moved else 1 - move)
        inside = (at >= begin) & (at < begin + size)
        source = jnp.where(inside, at + (start - begin), source)
        begin = begin + size
        start = start + length
    columns = lax.broadcasted_iota(jnp.int32, (rows, home), 1)
    return jnp.where(columns == source, 1.0, 0.0).astype(BF)


def sent_first(meta):
    n = meta.shape[1]
    partner = lax.rem(dp_at(meta) + n // 2, n)
    return lax.rem(kept_total(meta, partner), TILE)


def early_picks(meta, home):
    return picks(meta, True, sent_first(meta), EARLY, home)


def late_picks(meta, home):
    return picks(meta, True, sent_first(meta) - EARLY, LATE, home)


def kept_picks(meta, home):
    return picks(meta, False, 0, KEEP, home)


def scaled_rows(meta, pick, cot, scale):
    width = cot.shape[1]
    rows = jnp.dot(pick, cot[...], preferred_element_type=F32)
    own = scale[pl.ds(pl.multiple_of(tensor_at(meta) * width, 128), width)]
    return (rows * own[None, :]).astype(BF)


def first_kernel(meta, cot_hbm, scale_hbm, pre_hbm, rows_out, early_out, cot, scale, pre, sems):
    home, width = cot.shape
    pairs = ((cot_hbm, cot), (scale_hbm, scale), (pre_hbm, pre))
    copies = [pltpu.make_async_copy(a, b, sems.at[i]) for i, (a, b) in enumerate(pairs)]
    for copy in copies:
        copy.start()
    early = early_picks(meta, home)
    copies[0].wait()
    copies[1].wait()
    early_rows = scaled_rows(meta, early, cot, scale)
    early_out[:, :width] = early_rows
    rows_out[0:LATE, :] = scaled_rows(meta, late_picks(meta, home), cot, scale)
    rows_out[LATE:SEND, :] = early_rows
    rows_out[SEND:, :] = scaled_rows(meta, kept_picks(meta, home), cot, scale)
    copies[2].wait()
    early_out[:, width:] = jnp.dot(early, pre[...], preferred_element_type=F32).astype(BF)


def gelu_and_slope(x):
    cumulative = 0.5 * (1.0 + lax.erf(x * inv_root_two))
    return x * cumulative, cumulative + x * jnp.exp(-0.5 * x * x) * inv_root_tau


def gelu_kernel(late, base, block, meta, pre_hbm, act_out, der_out, pick, rows_f32, pre, sems):
    home = pre.shape[1]
    rows = pick.shape[0]
    blocks = act_out.shape[1] // block

    def fetch(i):
        columns = pl.ds(base + i * block, block)
        return pltpu.make_async_copy(pre_hbm.at[:, columns], pre.at[i], sems.at[i])

    for i in range(blocks):
        fetch(i).start()
    if late:
        pick[...] = late_picks(meta, home)
    else:
        pick[0:EARLY, :] = early_picks(meta, home)
        pick[EARLY:, :] = kept_picks(meta, home)
    step = next(TILE * k for k in (3, 4, 2, 1) if rows % (TILE * k) == 0)
    for i in range(blocks):
        fetch(i).wait()
        rows_f32[...] = jnp.dot(pick[...], pre[i], preferred_element_type=F32)
        columns = slice(i * block, (i + 1) * block)

        def body(k, _):
            at = pl.ds(pl.multiple_of(k * step, step), step)
            value, slope = gelu_and_slope(rows_f32[at, :])
            act_out[at, columns] = value.astype(BF)
            der_out[at, columns] = slope
            return 0

        lax.fori_loop(0, rows // step, body, 0)


def assemble(meta, pieces, first_row, lhs):
    rows = lhs.shape[0]
    width = pieces[1].shape[1]
    for j, piece in enumerate(pieces):
        columns = pl.ds(pl.multiple_of((tensor_at(meta) ^ j) * width, 128), width)
        lhs[:, columns] = piece[first_row : first_row + rows, 0:width]


def grad_kernel(first_row, first_slope, slope_count, block, meta, p0, p1, p2, p3, weight, *rest):
    slopes, outs, lhs = rest[:slope_count], rest[slope_count:-1], rest[-1]
    rows = lhs.shape[0]
    assemble(meta, (p0, p1, p2, p3), first_row, lhs)
    part = slopes[0].shape[1]
    at = 0
    for out in outs:
        for c in range(0, out.shape[1], block):
            slope = slopes[at // part][first_slope : first_slope + rows, at % part : at % part + block]
            value = jnp.dot(lhs[...], weight[:, at : at + block], preferred_element_type=F32)
            out[:, c : c + block] = (value * slope).astype(BF)
            at += block


def early_kernel(block, meta, own, p1, p2, p3, weight, out, lhs, acc):
    width = p1.shape[1]
    assemble(meta, (own, p1, p2, p3), 0, lhs)
    for at in range(0, out.shape[1], block):
        columns = slice(at, at + block)
        acc[...] = jnp.dot(lhs[...], weight[:, columns], preferred_element_type=F32)

        def body(k, _):
            rows = pl.ds(pl.multiple_of(k * TILE, TILE), TILE)
            _, slope = gelu_and_slope(own[rows, width + at : width + at + block].astype(F32))
            out[rows, columns] = (acc[rows, :] * slope).astype(BF)
            return 0

        lax.fori_loop(0, EARLY // TILE, body, 0)


def product(lhs_late, lhs_rest, act_late, act_rest, base):
    columns = slice(base, base + act_rest.shape[1])
    return jnp.dot(lhs_late[...], act_late[:, columns], preferred_element_type=F32) + jnp.dot(
        lhs_rest[...], act_rest[...], preferred_element_type=F32
    )


def weight_kernel(count, base, meta, *refs):
    pieces, (act_late, act_rest, send, keep, lhs_late, lhs_rest) = refs[:count], refs[count:]
    half = pieces[0].shape[1] // 2
    mine = dp_at(meta) % 2 == 0
    for i, piece in enumerate(pieces):
        for rows, lhs in ((slice(0, LATE), lhs_late), (slice(LATE, SEND + KEEP), lhs_rest)):
            both = piece[rows, :].T
            lo, hi = both[:half], both[half:]
            lhs[i * half : (i + 1) * half, :] = jnp.where(mine, hi, lo)
            lhs[(count + i) * half : (count + i + 1) * half, :] = jnp.where(mine, lo, hi)
    value = product(lhs_late, lhs_rest, act_late, act_rest, base)
    send[...] = value[: count * half].astype(BF)
    keep[...] = value[count * half :]


def weight_again_kernel(base, meta, late_01, rest_01, late_23, rest_23, act_late, act_rest, send, keep):
    rows = late_01.shape[0] // 2
    for i, (late, rest) in enumerate(((late_01, rest_01), (late_23, rest_23))):
        value = product(late, rest, act_late, act_rest, base)
        send[i * rows : (i + 1) * rows, :] = value[:rows].astype(BF)
        keep[i * rows : (i + 1) * rows, :] = value[rows:]


def near_kernel(count, meta, *refs):
    keeps, gots, (out, mine) = refs[:count], refs[count : 2 * count], refs[2 * count :]
    half = out.shape[0] // 2
    parts = [(k, g, at) for k, g in zip(keeps, gots) for at in range(0, k.shape[0], half)]
    keeps_even = (dp_at(meta) // 2 + tensor_at(meta)) % 2 == 0
    step = 2 * TILE

    for pair in range(2):
        (k0, g0, a0), (k1, g1, a1) = parts[2 * pair], parts[2 * pair + 1]

        def body(i, _):
            def rows(at):
                return pl.ds(pl.multiple_of(at + i * step, TILE), step)

            even = k0[rows(a0), :] + g0[rows(a0), :].astype(F32)
            odd = k1[rows(a1), :] + g1[rows(a1), :].astype(F32)
            out[rows(pair * half), :] = jnp.where(keeps_even, odd, even).astype(BF)
            mine[rows(pair * half), :] = jnp.where(keeps_even, even, odd)
            return 0

        lax.fori_loop(0, half // step, body, 0)


def far_kernel(meta, held, got, out, mine):
    half = out.shape[0]
    keeps_first = (dp_at(meta) // 4 + tensor_at(meta) // 2) % 2 == 0
    step = 2 * TILE

    def body(i, _):
        first = pl.ds(pl.multiple_of(i * step, TILE), step)
        second = pl.ds(pl.multiple_of(half + i * step, TILE), step)
        a = held[first, :] + got[first, :].astype(F32)
        b = held[second, :] + got[second, :].astype(F32)
        out[first, :] = jnp.where(keeps_first, b, a).astype(BF)
        mine[first, :] = jnp.where(keeps_first, a, b)
        return 0

    lax.fori_loop(0, half // step, body, 0)


def place_kernel(meta, kept, early, *rest):
    inner, outer, out = rest[:2], rest[2:4], rest[4]
    d = dp_at(meta)
    count = kept_total(meta, d)
    first = jnp.minimum(count - lax.rem(count, TILE), BAL - SEND)
    first = pl.multiple_of(first, TILE)
    wide = out.shape[1]
    step = pl.program_id(0)
    columns = pl.ds(pl.multiple_of(step * wide, wide), wide)
    out[0:KEEP, :] = kept[:, columns]
    out[KEEP:, :] = jnp.zeros((out.shape[0] - KEEP, wide), BF)

    def put(block, at):
        rows = lax.broadcasted_iota(jnp.int32, (block.shape[0], 1), 0) + at
        window = pl.ds(at, block.shape[0])
        out[window, :] = jnp.where(rows < count, out[window, :], block)

    put(early[:, columns], first)
    is_inner = (d // 2 == 1) | (d // 2 == 2)
    half = inner[0].shape[1] // wide
    for i in range(2):

        @pl.when(step // half == i)
        def _():
            at = pl.ds(pl.multiple_of((step - i * half) * wide, wide), wide)
            block = jnp.where(is_inner, inner[i][:, at], outer[i][:, at])
            put(block, pl.multiple_of(first + EARLY, TILE))


def swapped(block, axis, distance):
    n = lax.axis_size(axis)
    return lax.ppermute(block, axis, [(i, i ^ distance) for i in range(n)])


def routed(block, pairs):
    return lax.ppermute(block, "dp", [(2 * a + x, 2 * b + x) for a, b in pairs for x in range(2)])


def after(value, *others):
    return lax.optimization_barrier((value, *others))[0]


def shards(hidden_pre, cotangent, down_weight, layer_scale, crop_lengths, crop_moves):
    hidden_pre, cotangent, layer_scale = (
        pltpu.with_memory_space_constraint(x, pltpu.HBM) for x in (hidden_pre, cotangent, layer_scale)
    )
    home, ff = hidden_pre.shape
    width = cotangent.shape[1]
    features = down_weight.shape[0]
    half, part = width // 2, ff // 3
    others = EARLY + KEEP
    n = lax.axis_size("dp")
    d = lax.axis_index("dp").astype(jnp.int32)
    t = lax.axis_index("tensor").astype(jnp.int32)
    column = lax.broadcasted_iota(jnp.int32, (1, n), 1)
    own = jnp.where(column == 0, d, jnp.where(column == 1, t, 0))
    meta = jnp.concatenate([crop_lengths.T, crop_moves.T, own])
    vmem = pltpu.VMEM
    sems = pltpu.SemaphoreType.DMA

    def gelu(meta, late, base, columns):
        block = 256
        rows = LATE if late else others
        return kernel_call(
            functools.partial(gelu_kernel, late, base, block),
            [shape(rows, columns), shape(rows, columns, F32)],
            [IN_HBM], [IN_VMEM] * 2,
            [vmem((rows, home), BF), vmem((rows, block), F32), vmem((columns // block, home, block), BF),
             sems((columns // block,))],
        )(meta, hidden_pre)

    def weight_part(meta, pieces, act):
        count = len(pieces)
        return kernel_call(
            functools.partial(weight_kernel, count, 0),
            [shape(count * half, part), shape(count * half, part, F32),
             shape(count * width, LATE), shape(count * width, others)],
            [IN_VMEM] * (count + 2), [IN_VMEM] * 4,
        )(meta, *pieces, act_late, act)

    def weight_again(meta, base, act):
        return kernel_call(
            functools.partial(weight_again_kernel, base),
            [shape(4 * half, part), shape(4 * half, part, F32)], [IN_VMEM] * 6, [IN_VMEM] * 2,
        )(meta, *lhs_01, *lhs_23, act_late, act)

    def grads(meta, first_row, first_slope, rows, slopes, cuts):
        return kernel_call(
            functools.partial(grad_kernel, first_row, first_slope, len(slopes), 256),
            [shape(rows, c) for c in cuts], [IN_VMEM] * (5 + len(slopes)), [IN_VMEM] * len(cuts),
            [vmem((rows, features), BF)],
        )(meta, *pieces, down_weight, *slopes)

    def near_step(meta, keeps, gots):
        count = len(keeps)
        return kernel_call(
            functools.partial(near_kernel, count),
            [shape(width, part), shape(width, part, F32)], [IN_VMEM] * (2 * count), [IN_VMEM] * 2,
        )(meta, *keeps, *gots)

    def far_step(meta, mine, got):
        return kernel_call(
            far_kernel, [shape(half, part), shape(half, part, F32)], [IN_VMEM] * 2, [IN_VMEM] * 2
        )(meta, mine, got)

    own_rows, early = kernel_call(
        first_kernel, [shape(SEND + KEEP, width), shape(EARLY, width + ff)], [IN_HBM] * 3, [IN_VMEM] * 2,
        [vmem((home, width), BF), vmem((features,), F32), vmem((home, ff), BF), sems((3,))],
    )(meta, cotangent, layer_scale, hidden_pre)
    arrived_early = swapped(early, "dp", n // 2)

    rows_c, rows_y = swapped(own_rows, "tensor", 1), swapped(own_rows, "tensor", 2)
    act_late, der_late = gelu(after(meta, own_rows), True, 0, ff)
    act_a, der_a = gelu(after(meta, act_late), False, 0, part)

    send_01, keep_01, *lhs_01 = weight_part(after(meta, act_a), (own_rows, rows_c), act_a)
    got_01 = swapped(send_01, "dp", 1)
    rows_y = after(rows_y, send_01, arrived_early)
    rows_yc = swapped(rows_y, "tensor", 1)
    pieces = (own_rows, rows_c, rows_y, rows_yc)

    moving = grads(after(meta, rows_y), 0, 0, LATE, (der_late,), (ff // 2, ff // 2))
    to_inner, across, to_outer = ((0, 1), (3, 2)), ((1, 2), (2, 1)), ((1, 0), (2, 3))
    at_inner_a = routed(moving[0], to_inner)
    crossed_a = routed(moving[0], across)
    crossed_b = routed(moving[1], across)

    early_sent = after(arrived_early[:, :width], *moving)
    early_c, early_y = swapped(early_sent, "tensor", 1), swapped(early_sent, "tensor", 2)

    send_23, keep_23, *lhs_23 = weight_part(
        after(meta, got_01, early_y, early_c, *moving), (rows_y, rows_yc), act_a
    )
    got_23 = swapped(send_23, "dp", 1)
    early_y = after(early_y, send_23)
    early_yc = swapped(early_y, "tensor", 1)
    act_b, der_b = gelu(after(meta, send_23), False, part, part)
    send_b, keep_b = weight_again(after(meta, act_b, early_yc), part, act_b)
    got_b = swapped(send_b, "dp", 1)

    is_inner = (d // 2 == 1) | (d // 2 == 2)
    hop = after(jnp.where(is_inner, crossed_a, moving[1]), send_b, got_23, at_inner_a)
    hopped = routed(hop, to_inner + to_outer)
    inner_a = routed(after(at_inner_a, hop), across)
    act_c, der_c = gelu(after(meta, hop), False, 2 * part, part)
    send_c, keep_c = weight_again(after(meta, act_c), 2 * part, act_c)
    got_c = swapped(send_c, "dp", 1)

    out_na, mine_a = near_step(
        after(meta, send_c, hopped, crossed_b), (keep_01, keep_23), (got_01, got_23)
    )
    got_na = swapped(out_na, "dp", 2)
    inner_b = routed(after(hopped, out_na), across)
    (kept_grad,) = grads(after(meta, out_na), SEND, EARLY, KEEP, (der_a, der_b, der_c), (ff,))
    out_nb, mine_b = near_step(after(meta, kept_grad, inner_a), (keep_b,), (got_b,))
    got_nb = swapped(out_nb, "dp", 2)
    outer_b = routed(after(crossed_b, out_nb), to_outer)

    early_grad = kernel_call(
        functools.partial(early_kernel, 256), shape(EARLY, ff), [IN_VMEM] * 5, IN_VMEM,
        [vmem((EARLY, features), BF), vmem((EARLY, 256), F32)],
    )(after(meta, out_nb), arrived_early, early_c, early_y, early_yc, down_weight)

    out_fa, own_a = far_step(after(meta, early_grad), mine_a, got_na)
    got_fa = swapped(out_fa, "dp", 4)
    out_nc, mine_c = near_step(after(meta, out_fa, inner_b), (keep_c,), (got_c,))
    got_nc = swapped(out_nc, "dp", 2)
    out_fb, own_b = far_step(after(meta, out_nc), mine_b, got_nb)
    got_fb = swapped(out_fb, "dp", 4)
    out_fc, own_c = far_step(after(meta, out_fb, outer_b, got_fa), mine_c, got_nc)
    got_fc = swapped(out_fc, "dp", 4)
    total = [a + b.astype(F32) for a, b in ((own_a, got_fa), (own_b, got_fb), (own_c, got_fc))]
    down_grad = jnp.concatenate(total, axis=1) / math.sqrt(n * home)

    hidden_grad = kernel_call(
        place_kernel, shape(BAL, ff), [IN_VMEM] * 6,
        pl.BlockSpec((BAL, 256), lambda i, *_: (0, i)), grid=(ff // 256,),
    )(after(meta, out_fc), kept_grad, early_grad, inner_a, inner_b, hopped, outer_b)
    return (hidden_grad, down_grad)


def solution(mesh):
    pairs_and_fours = (mesh.shape["dp"], mesh.shape["tensor"]) == (8, 4)
    return jax.shard_map(
        shards if pairs_and_fours else general_shards,
        mesh=mesh,
        in_specs=(P("dp", "tensor"), P("dp", "tensor"), P(None, "tensor"), P(), P(), P()),
        out_specs=(P("dp", "tensor"), P("dp", "tensor")),
        check_vma=False,
    )


def shifted(block, axis, distance):
    devices = range(lax.axis_size(axis))
    route = [((i - distance) % len(devices), i) for i in devices]
    return lax.ppermute(block, axis, route)


def crop_rows(row_total, crop_sizes, crop_starts):
    crop_ends = jnp.cumsum(crop_sizes)
    crop_begins = crop_ends - crop_sizes
    target_rows = jnp.arange(row_total, dtype=jnp.int32)[:, None]
    inside_crop = (target_rows >= crop_begins[None, :]) & (target_rows < crop_ends[None, :])
    source_rows = jnp.sum(
        jnp.where(inside_crop, crop_starts[None, :] + target_rows - crop_begins[None, :], 0), axis=1
    )
    return (source_rows, jnp.any(inside_crop, axis=1))


def select_rows(row_block, source_rows, valid_rows):
    taken = jnp.take(row_block, source_rows, axis=0)
    return jnp.where(valid_rows[:, None], taken, jnp.zeros((), row_block.dtype))


def gelu_parts(pre_act):
    cumulative = 0.5 * (1.0 + jax.scipy.special.erf(pre_act * inv_root_two))
    activated = pre_act * cumulative
    derivative = cumulative + pre_act * jnp.exp(-0.5 * pre_act * pre_act) * inv_root_tau
    return (activated, derivative)


def local_grads(pre_rows, cot_part, live_rows, layer_scale, down_weight, home_rows):
    cot_full = lax.all_gather(cot_part, "tensor", axis=1, tiled=True)
    scaled = (cot_full.astype(F32) * layer_scale[None, :]).astype(BF)
    activated, derivative = gelu_parts(pre_rows.astype(F32))
    activation = jnp.where(live_rows[:, None], activated, 0.0).astype(BF)
    backward = jnp.dot(scaled, down_weight, preferred_element_type=F32) * derivative
    gradient_rows = jnp.where(live_rows[:, None], backward, 0.0).astype(BF)
    weight_grad = lax.psum_scatter(
        lax.dot_general(scaled, activation, (((0,), (0,)), ((), ())), preferred_element_type=F32),
        "dp",
        scatter_dimension=0,
        tiled=True,
    )
    return (gradient_rows, weight_grad / math.sqrt(lax.axis_size("dp") * home_rows))


def general_shards(hidden_pre, cotangent, down_weight, layer_scale, crop_lengths, crop_moves):
    devices = lax.axis_size("dp")
    half_axis = devices // 2
    device_index = lax.axis_index("dp")
    partner_index = (device_index + half_axis) % devices
    own_lengths = lax.dynamic_index_in_dim(crop_lengths, device_index, 0, keepdims=False)
    own_moves = lax.dynamic_index_in_dim(crop_moves, device_index, 0, keepdims=False)
    partner_lengths = lax.dynamic_index_in_dim(crop_lengths, partner_index, 0, keepdims=False)
    partner_moves = lax.dynamic_index_in_dim(crop_moves, partner_index, 0, keepdims=False)
    home_rows = hidden_pre.shape[0]
    own_starts = jnp.cumsum(own_lengths) - own_lengths
    sent_sizes = own_lengths * own_moves
    kept_sizes = own_lengths * (1 - own_moves)
    arrived = jnp.sum(partner_lengths * partner_moves)
    send_source, send_valid = crop_rows(SEND, sent_sizes, own_starts)
    keep_sizes = jnp.concatenate([kept_sizes, arrived[None]])
    keep_starts = jnp.concatenate([own_starts, jnp.full((1,), home_rows, jnp.int32)])
    keep_source, keep_valid = crop_rows(BAL, keep_sizes, keep_starts)
    live_home = jnp.arange(home_rows, dtype=jnp.int32) < jnp.sum(own_lengths)
    gradient_rows, weight_grad = local_grads(
        hidden_pre, cotangent, live_home, layer_scale, down_weight, home_rows
    )
    outgoing = select_rows(gradient_rows, send_source, send_valid)
    incoming = shifted(outgoing, "dp", half_axis)
    balanced = select_rows(jnp.concatenate([gradient_rows, incoming], 0), keep_source, keep_valid)
    return (balanced, weight_grad)
```

```python
import functools
import math

import jax
import jax.numpy as jnp
from jax import lax
from jax.experimental import pallas as pl
from jax.experimental.pallas import tpu as pltpu
from jax.sharding import PartitionSpec as P

SEND = 528
KEEP = 528
TILE = 16
EARLY = 48
LATE = SEND - EARLY
SLOTS = 4
BAL = 720
BF = jnp.bfloat16
F32 = jnp.float32

inv_root_two = 0.7071067811865476
inv_root_tau = 0.3989422804014327


def kernel_call(kernel, out_shape, in_specs, out_specs, scratch=(), grid=(1,)):
    return pl.pallas_call(
        kernel,
        grid_spec=pltpu.PrefetchScalarGridSpec(
            num_scalar_prefetch=1,
            grid=grid,
            in_specs=in_specs,
            out_specs=out_specs,
            scratch_shapes=list(scratch),
        ),
        out_shape=out_shape,
        cost_estimate=pl.CostEstimate(flops=1, bytes_accessed=1, transcendentals=0),
        compiler_params=pltpu.CompilerParams(vmem_limit_bytes=16 * 1024 * 1024),
    )


IN_VMEM = pl.BlockSpec(memory_space=pltpu.VMEM)
IN_HBM = pl.BlockSpec(memory_space=pltpu.HBM)


def shape(a, b, dtype=BF):
    return jax.ShapeDtypeStruct((a, b), dtype)


def lengths_of(meta, d):
    return [meta[j, d] for j in range(SLOTS)]


def moves_of(meta, d):
    return [meta[SLOTS + j, d] for j in range(SLOTS)]


def dp_at(meta):
    return meta[2 * SLOTS, 0]


def tensor_at(meta):
    return meta[2 * SLOTS, 1]


def kept_total(meta, d):
    return sum(a * (1 - b) for a, b in zip(lengths_of(meta, d), moves_of(meta, d)))


def picks(meta, moved, first, rows, home):
    d = dp_at(meta)
    at = lax.broadcasted_iota(jnp.int32, (rows, 1), 0) - first
    source = jnp.full((rows, 1), -1, jnp.int32)
    begin = jnp.int32(0)
    start = jnp.int32(0)
    for length, move in zip(lengths_of(meta, d), moves_of(meta, d)):
        size = length * (move if moved else 1 - move)
        inside = (at >= begin) & (at < begin + size)
        source = jnp.where(inside, at + (start - begin), source)
        begin = begin + size
        start = start + length
    columns = lax.broadcasted_iota(jnp.int32, (rows, home), 1)
    return jnp.where(columns == source, 1.0, 0.0).astype(BF)


def sent_first(meta):
    n = meta.shape[1]
    partner = lax.rem(dp_at(meta) + n // 2, n)
    return lax.rem(kept_total(meta, partner), TILE)


def early_picks(meta, home):
    return picks(meta, True, sent_first(meta), EARLY, home)


def late_picks(meta, home):
    return picks(meta, True, sent_first(meta) - EARLY, LATE, home)


def kept_picks(meta, home):
    return picks(meta, False, 0, KEEP, home)


def scaled_rows(meta, pick, cot, scale):
    width = cot.shape[1]
    rows = jnp.dot(pick, cot[...], preferred_element_type=F32)
    own = scale[pl.ds(pl.multiple_of(tensor_at(meta) * width, 128), width)]
    return (rows * own[None, :]).astype(BF)


def first_kernel(meta, cot_hbm, scale_hbm, pre_hbm, late_out, rest_out, early_out, cot, scale, pre, sems):
    home, width = cot.shape
    pairs = ((cot_hbm, cot), (scale_hbm, scale), (pre_hbm, pre))
    copies = [pltpu.make_async_copy(a, b, sems.at[i]) for i, (a, b) in enumerate(pairs)]
    for copy in copies:
        copy.start()
    early = early_picks(meta, home)
    copies[0].wait()
    copies[1].wait()
    early_rows = scaled_rows(meta, early, cot, scale)
    early_out[:, :width] = early_rows
    late_out[...] = scaled_rows(meta, late_picks(meta, home), cot, scale)
    rest_out[0:EARLY, :] = early_rows
    rest_out[EARLY:, :] = scaled_rows(meta, kept_picks(meta, home), cot, scale)
    copies[2].wait()
    early_out[:, width:] = jnp.dot(early, pre[...], preferred_element_type=F32).astype(BF)


def gelu_and_slope(x):
    cumulative = 0.5 * (1.0 + lax.erf(x * inv_root_two))
    return x * cumulative, cumulative + x * jnp.exp(-0.5 * x * x) * inv_root_tau


def gelu_kernel(late, base, block, meta, pre_hbm, act_out, der_out, pick, rows_f32, pre, sems):
    home = pre.shape[1]
    rows = pick.shape[0]
    blocks = act_out.shape[1] // block

    def fetch(i):
        columns = pl.ds(base + i * block, block)
        return pltpu.make_async_copy(pre_hbm.at[:, columns], pre.at[i], sems.at[i])

    for i in range(blocks):
        fetch(i).start()
    if late:
        pick[...] = late_picks(meta, home)
    else:
        pick[0:EARLY, :] = early_picks(meta, home)
        pick[EARLY:, :] = kept_picks(meta, home)
    step = next(TILE * k for k in (3, 4, 2, 1) if rows % (TILE * k) == 0)
    for i in range(blocks):
        fetch(i).wait()
        rows_f32[...] = jnp.dot(pick[...], pre[i], preferred_element_type=F32)
        columns = slice(i * block, (i + 1) * block)

        def body(k, _):
            at = pl.ds(pl.multiple_of(k * step, step), step)
            value, slope = gelu_and_slope(rows_f32[at, :])
            act_out[at, columns] = value.astype(BF)
            der_out[at, columns] = slope
            return 0

        lax.fori_loop(0, rows // step, body, 0)


def assemble(meta, pieces, first_row, lhs):
    rows = lhs.shape[0]
    width = pieces[1].shape[1]
    for j, piece in enumerate(pieces):
        columns = pl.ds(pl.multiple_of((tensor_at(meta) ^ j) * width, 128), width)
        lhs[:, columns] = piece[first_row : first_row + rows, 0:width]


def grad_kernel(first_row, first_slope, slope_count, block, meta, p0, p1, p2, p3, weight, *rest):
    slopes, outs, lhs = rest[:slope_count], rest[slope_count:-1], rest[-1]
    rows = lhs.shape[0]
    assemble(meta, (p0, p1, p2, p3), first_row, lhs)
    part = slopes[0].shape[1]
    at = 0
    for out in outs:
        for c in range(0, out.shape[1], block):
            slope = slopes[at // part][first_slope : first_slope + rows, at % part : at % part + block]
            value = jnp.dot(lhs[...], weight[:, at : at + block], preferred_element_type=F32)
            out[:, c : c + block] = (value * slope).astype(BF)
            at += block


def early_kernel(block, meta, own, p1, p2, p3, weight, out, lhs, acc):
    width = p1.shape[1]
    assemble(meta, (own, p1, p2, p3), 0, lhs)
    for at in range(0, out.shape[1], block):
        columns = slice(at, at + block)
        acc[...] = jnp.dot(lhs[...], weight[:, columns], preferred_element_type=F32)

        def body(k, _):
            rows = pl.ds(pl.multiple_of(k * TILE, TILE), TILE)
            _, slope = gelu_and_slope(own[rows, width + at : width + at + block].astype(F32))
            out[rows, columns] = (acc[rows, :] * slope).astype(BF)
            return 0

        lax.fori_loop(0, EARLY // TILE, body, 0)


def weight_kernel(count, base, meta, *refs):
    lates, rests = refs[:count], refs[count : 2 * count]
    act_late, act_rest, send, keep, lhs_late, lhs_rest = refs[2 * count :]
    half = lates[0].shape[1] // 2
    mine = dp_at(meta) % 2 == 0
    for i in range(count):
        for piece, lhs in ((lates[i], lhs_late), (rests[i], lhs_rest)):
            both = piece[...].T
            lo, hi = both[:half], both[half:]
            lhs[i * half : (i + 1) * half, :] = jnp.where(mine, hi, lo)
            lhs[(count + i) * half : (count + i + 1) * half, :] = jnp.where(mine, lo, hi)
    again_kernel(base, meta, lhs_late, lhs_rest, act_late, act_rest, send, keep)


def again_kernel(base, meta, lhs_late, lhs_rest, act_late, act_rest, send, keep):
    rows = send.shape[0]
    for out, at in ((send, 0), (keep, rows)):
        for i in range(0, rows, rows // 2):
            part = slice(at + i, at + i + rows // 2)
            columns = slice(base, base + act_rest.shape[1])
            value = jnp.dot(lhs_late[part, :], act_late[:, columns], preferred_element_type=F32)
            value += jnp.dot(lhs_rest[part, :], act_rest[...], preferred_element_type=F32)
            out[i : i + rows // 2, :] = value.astype(out.dtype)


def near_kernel(count, meta, *refs):
    keeps, gots, (out, mine) = refs[:count], refs[count : 2 * count], refs[2 * count :]
    half = out.shape[0] // 2
    parts = [(k, g, at) for k, g in zip(keeps, gots) for at in range(0, k.shape[0], half)]
    keeps_even = (dp_at(meta) // 2 + tensor_at(meta)) % 2 == 0
    step = 2 * TILE

    for pair in range(2):
        (k0, g0, a0), (k1, g1, a1) = parts[2 * pair], parts[2 * pair + 1]

        def body(i, _):
            def rows(at):
                return pl.ds(pl.multiple_of(at + i * step, TILE), step)

            even = k0[rows(a0), :] + g0[rows(a0), :].astype(F32)
            odd = k1[rows(a1), :] + g1[rows(a1), :].astype(F32)
            out[rows(pair * half), :] = jnp.where(keeps_even, odd, even).astype(BF)
            mine[rows(pair * half), :] = jnp.where(keeps_even, even, odd)
            return 0

        lax.fori_loop(0, half // step, body, 0)


def far_kernel(meta, held, got, out, mine):
    half = out.shape[0]
    keeps_first = (dp_at(meta) // 4 + tensor_at(meta) // 2) % 2 == 0
    step = 2 * TILE

    def body(i, _):
        first = pl.ds(pl.multiple_of(i * step, TILE), step)
        second = pl.ds(pl.multiple_of(half + i * step, TILE), step)
        a = held[first, :] + got[first, :].astype(F32)
        b = held[second, :] + got[second, :].astype(F32)
        out[first, :] = jnp.where(keeps_first, b, a).astype(BF)
        mine[first, :] = jnp.where(keeps_first, a, b)
        return 0

    lax.fori_loop(0, half // step, body, 0)


def place_kernel(cuts, meta, kept, early, *rest):
    lates, out = rest[:-1], rest[-1]
    count = kept_total(meta, dp_at(meta))
    first = jnp.minimum(count - lax.rem(count, TILE), BAL - SEND)
    first = pl.multiple_of(first, TILE)
    wide = out.shape[1]
    step = pl.program_id(0)
    columns = pl.ds(pl.multiple_of(step * wide, wide), wide)
    out[0:KEEP, :] = kept[:, columns]
    out[KEEP:, :] = jnp.zeros((out.shape[0] - KEEP, wide), BF)

    def put(block, at):
        rows = lax.broadcasted_iota(jnp.int32, (block.shape[0], 1), 0) + at
        window = pl.ds(at, block.shape[0])
        out[window, :] = jnp.where(rows < count, out[window, :], block)

    put(early[:, columns], first)
    sources = [(late, c) for late, cut in zip(lates, cuts) for c in range(0, cut, wide)]
    for i, (late, c) in enumerate(sources):

        @pl.when(step == i)
        def _():
            put(late[:, c : c + wide], pl.multiple_of(first + EARLY, TILE))


def swapped(block, axis, distance):
    n = lax.axis_size(axis)
    return lax.ppermute(block, axis, [(i, i ^ distance) for i in range(n)])


def after(value, *others):
    return lax.optimization_barrier((value, *others))[0]


def shards(hidden_pre, cotangent, down_weight, layer_scale, crop_lengths, crop_moves):
    hidden_pre, cotangent, layer_scale = (
        pltpu.with_memory_space_constraint(x, pltpu.HBM) for x in (hidden_pre, cotangent, layer_scale)
    )
    home, ff = hidden_pre.shape
    width = cotangent.shape[1]
    features = down_weight.shape[0]
    half, part = width // 2, ff // 3
    others = EARLY + KEEP
    n = lax.axis_size("dp")
    d = lax.axis_index("dp").astype(jnp.int32)
    t = lax.axis_index("tensor").astype(jnp.int32)
    column = lax.broadcasted_iota(jnp.int32, (1, n), 1)
    own = jnp.where(column == 0, d, jnp.where(column == 1, t, 0))
    meta = jnp.concatenate([crop_lengths.T, crop_moves.T, own])
    vmem = pltpu.VMEM
    sems = pltpu.SemaphoreType.DMA

    def gelu(meta, late, base, columns):
        block = 256
        rows = LATE if late else others
        return kernel_call(
            functools.partial(gelu_kernel, late, base, block),
            [shape(rows, columns), shape(rows, columns, F32)],
            [IN_HBM], [IN_VMEM] * 2,
            [vmem((rows, home), BF), vmem((rows, block), F32), vmem((columns // block, home, block), BF),
             sems((columns // block,))],
        )(meta, hidden_pre)

    def weight_first(meta, act):
        count = len(lates)
        return kernel_call(
            functools.partial(weight_kernel, count, 0),
            [shape(count * half, part), shape(count * half, part, F32),
             shape(count * width, LATE), shape(count * width, others)],
            [IN_VMEM] * (2 * count + 2), [IN_VMEM] * 4,
        )(meta, *lates, *rests, act_late, act)

    def weight_again(meta, base, act):
        return kernel_call(
            functools.partial(again_kernel, base),
            [shape(4 * half, part), shape(4 * half, part, F32)], [IN_VMEM] * 4, [IN_VMEM] * 2,
        )(meta, *lhs, act_late, act)

    def grads(meta, pieces, first_row, first_slope, rows, slopes, cuts):
        return kernel_call(
            functools.partial(grad_kernel, first_row, first_slope, len(slopes), 256),
            [shape(rows, c) for c in cuts], [IN_VMEM] * (5 + len(slopes)), [IN_VMEM] * len(cuts),
            [vmem((rows, features), BF)],
        )(meta, *pieces, down_weight, *slopes)

    def near_step(meta, keeps, gots):
        count = len(keeps)
        return kernel_call(
            functools.partial(near_kernel, count),
            [shape(width, part), shape(width, part, F32)], [IN_VMEM] * (2 * count), [IN_VMEM] * 2,
        )(meta, *keeps, *gots)

    def far_step(meta, mine, got):
        return kernel_call(
            far_kernel, [shape(half, part), shape(half, part, F32)], [IN_VMEM] * 2, [IN_VMEM] * 2
        )(meta, mine, got)

    late, rest, early = kernel_call(
        first_kernel, [shape(LATE, width), shape(others, width), shape(EARLY, width + ff)],
        [IN_HBM] * 3, [IN_VMEM] * 3,
        [vmem((home, width), BF), vmem((features,), F32), vmem((home, ff), BF), sems((3,))],
    )(meta, cotangent, layer_scale, hidden_pre)
    arrived_early = swapped(early, "dp", n // 2)

    late_c, late_y = swapped(late, "tensor", 1), swapped(late, "tensor", 2)
    rest_c, rest_y = swapped(rest, "tensor", 1), swapped(rest, "tensor", 2)
    act_late, der_late = gelu(after(meta, late), True, 0, ff)
    late_y = after(late_y, act_late, late_c, rest_c, arrived_early)
    late_yc = swapped(late_y, "tensor", 1)
    lates = (late, late_c, late_y, late_yc)

    moves = (1024, ff - 1024)
    moving = grads(after(meta, late_y), lates, 0, 0, LATE, (der_late,), moves)
    arrived_a = swapped(moving[0], "dp", n // 2)
    rest_y = after(rest_y, *moving)
    rest_yc = swapped(rest_y, "tensor", 1)
    rests = (rest, rest_c, rest_y, rest_yc)

    act_a, der_a = gelu(after(meta, *moving), False, 0, part)
    send_a, keep_a, *lhs = weight_first(after(meta, act_a), act_a)
    got_a = swapped(send_a, "dp", 1)
    early_sent = after(arrived_early[:, :width], send_a)
    early_c, early_y = swapped(early_sent, "tensor", 1), swapped(early_sent, "tensor", 2)
    act_b, der_b = gelu(after(meta, send_a), False, part, part)
    send_b, keep_b = weight_again(after(meta, act_b, early_c, early_y), part, act_b)
    got_b = swapped(send_b, "dp", 1)
    early_y = after(early_y, send_b)
    early_yc = swapped(early_y, "tensor", 1)
    act_c, der_c = gelu(after(meta, send_b), False, 2 * part, part)
    send_c, keep_c = weight_again(after(meta, act_c, early_yc), 2 * part, act_c)
    got_c = swapped(send_c, "dp", 1)

    (kept_grad,) = grads(after(meta, send_c), rests, EARLY, EARLY, KEEP, (der_a, der_b, der_c), (ff,))
    early_grad = kernel_call(
        functools.partial(early_kernel, 256), shape(EARLY, ff), [IN_VMEM] * 5, IN_VMEM,
        [vmem((EARLY, features), BF), vmem((EARLY, 256), F32)],
    )(after(meta, kept_grad), arrived_early, early_c, early_y, early_yc, down_weight)

    out_na, mine_a = near_step(after(meta, early_grad, arrived_a), (keep_a,), (got_a,))
    got_na = swapped(out_na, "dp", 2)
    out_nb, mine_b = near_step(after(meta, out_na), (keep_b,), (got_b,))
    got_nb = swapped(out_nb, "dp", 2)
    arrived_b = swapped(after(moving[1], out_nb), "dp", n // 2)
    out_fa, own_a = far_step(after(meta, out_nb), mine_a, got_na)
    got_fa = swapped(out_fa, "dp", 4)
    out_nc, mine_c = near_step(after(meta, out_fa), (keep_c,), (got_c,))
    got_nc = swapped(out_nc, "dp", 2)
    out_fb, own_b = far_step(after(meta, out_nc), mine_b, got_nb)
    got_fb = swapped(out_fb, "dp", 4)
    out_fc, own_c = far_step(after(meta, out_fb, arrived_b, got_fa), mine_c, got_nc)
    got_fc = swapped(out_fc, "dp", 4)
    total = [a + b.astype(F32) for a, b in ((own_a, got_fa), (own_b, got_fb), (own_c, got_fc))]
    down_grad = jnp.concatenate(total, axis=1) / math.sqrt(n * home)

    hidden_grad = kernel_call(
        functools.partial(place_kernel, moves), shape(BAL, ff), [IN_VMEM] * (2 + len(moves)),
        pl.BlockSpec((BAL, 256), lambda i, *_: (0, i)), grid=(ff // 256,),
    )(after(meta, out_fc), kept_grad, early_grad, arrived_a, arrived_b)
    return (hidden_grad, down_grad)


def solution(mesh):
    pairs_and_fours = (mesh.shape["dp"], mesh.shape["tensor"]) == (8, 4)
    return jax.shard_map(
        shards if pairs_and_fours else general_shards,
        mesh=mesh,
        in_specs=(P("dp", "tensor"), P("dp", "tensor"), P(None, "tensor"), P(), P(), P()),
        out_specs=(P("dp", "tensor"), P("dp", "tensor")),
        check_vma=False,
    )


def shifted(block, axis, distance):
    devices = range(lax.axis_size(axis))
    route = [((i - distance) % len(devices), i) for i in devices]
    return lax.ppermute(block, axis, route)


def crop_rows(row_total, crop_sizes, crop_starts):
    crop_ends = jnp.cumsum(crop_sizes)
    crop_begins = crop_ends - crop_sizes
    target_rows = jnp.arange(row_total, dtype=jnp.int32)[:, None]
    inside_crop = (target_rows >= crop_begins[None, :]) & (target_rows < crop_ends[None, :])
    source_rows = jnp.sum(
        jnp.where(inside_crop, crop_starts[None, :] + target_rows - crop_begins[None, :], 0), axis=1
    )
    return (source_rows, jnp.any(inside_crop, axis=1))


def select_rows(row_block, source_rows, valid_rows):
    taken = jnp.take(row_block, source_rows, axis=0)
    return jnp.where(valid_rows[:, None], taken, jnp.zeros((), row_block.dtype))


def gelu_parts(pre_act):
    cumulative = 0.5 * (1.0 + jax.scipy.special.erf(pre_act * inv_root_two))
    activated = pre_act * cumulative
    derivative = cumulative + pre_act * jnp.exp(-0.5 * pre_act * pre_act) * inv_root_tau
    return (activated, derivative)


def local_grads(pre_rows, cot_part, live_rows, layer_scale, down_weight, home_rows):
    cot_full = lax.all_gather(cot_part, "tensor", axis=1, tiled=True)
    scaled = (cot_full.astype(F32) * layer_scale[None, :]).astype(BF)
    activated, derivative = gelu_parts(pre_rows.astype(F32))
    activation = jnp.where(live_rows[:, None], activated, 0.0).astype(BF)
    backward = jnp.dot(scaled, down_weight, preferred_element_type=F32) * derivative
    gradient_rows = jnp.where(live_rows[:, None], backward, 0.0).astype(BF)
    weight_grad = lax.psum_scatter(
        lax.dot_general(scaled, activation, (((0,), (0,)), ((), ())), preferred_element_type=F32),
        "dp",
        scatter_dimension=0,
        tiled=True,
    )
    return (gradient_rows, weight_grad / math.sqrt(lax.axis_size("dp") * home_rows))


def general_shards(hidden_pre, cotangent, down_weight, layer_scale, crop_lengths, crop_moves):
    devices = lax.axis_size("dp")
    half_axis = devices // 2
    device_index = lax.axis_index("dp")
    partner_index = (device_index + half_axis) % devices
    own_lengths = lax.dynamic_index_in_dim(crop_lengths, device_index, 0, keepdims=False)
    own_moves = lax.dynamic_index_in_dim(crop_moves, device_index, 0, keepdims=False)
    partner_lengths = lax.dynamic_index_in_dim(crop_lengths, partner_index, 0, keepdims=False)
    partner_moves = lax.dynamic_index_in_dim(crop_moves, partner_index, 0, keepdims=False)
    home_rows = hidden_pre.shape[0]
    own_starts = jnp.cumsum(own_lengths) - own_lengths
    sent_sizes = own_lengths * own_moves
    kept_sizes = own_lengths * (1 - own_moves)
    arrived = jnp.sum(partner_lengths * partner_moves)
    send_source, send_valid = crop_rows(SEND, sent_sizes, own_starts)
    keep_sizes = jnp.concatenate([kept_sizes, arrived[None]])
    keep_starts = jnp.concatenate([own_starts, jnp.full((1,), home_rows, jnp.int32)])
    keep_source, keep_valid = crop_rows(BAL, keep_sizes, keep_starts)
    live_home = jnp.arange(home_rows, dtype=jnp.int32) < jnp.sum(own_lengths)
    gradient_rows, weight_grad = local_grads(
        hidden_pre, cotangent, live_home, layer_scale, down_weight, home_rows
    )
    outgoing = select_rows(gradient_rows, send_source, send_valid)
    incoming = shifted(outgoing, "dp", half_axis)
    balanced = select_rows(jnp.concatenate([gradient_rows, incoming], 0), keep_source, keep_valid)
    return (balanced, weight_grad)
```

```python
import functools
import math

import jax
import jax.numpy as jnp
from jax import lax
from jax.experimental import pallas as pl
from jax.experimental.pallas import tpu as pltpu
from jax.sharding import PartitionSpec as P

SEND = 528
KEEP = 528
TILE = 16
EARLY = 48
LATE = SEND - EARLY
SLOTS = 4
BAL = 720
BF = jnp.bfloat16
F32 = jnp.float32

inv_root_two = 0.7071067811865476
inv_root_tau = 0.3989422804014327


def kernel_call(kernel, out_shape, in_specs, out_specs, scratch=(), grid=(1,)):
    return pl.pallas_call(
        kernel,
        grid_spec=pltpu.PrefetchScalarGridSpec(
            num_scalar_prefetch=1,
            grid=grid,
            in_specs=in_specs,
            out_specs=out_specs,
            scratch_shapes=list(scratch),
        ),
        out_shape=out_shape,
        cost_estimate=pl.CostEstimate(flops=1, bytes_accessed=1, transcendentals=0),
        compiler_params=pltpu.CompilerParams(vmem_limit_bytes=16 * 1024 * 1024),
    )


IN_VMEM = pl.BlockSpec(memory_space=pltpu.VMEM)
IN_HBM = pl.BlockSpec(memory_space=pltpu.HBM)


def shape(a, b, dtype=BF):
    return jax.ShapeDtypeStruct((a, b), dtype)


def lengths_of(meta, d):
    return [meta[j, d] for j in range(SLOTS)]


def moves_of(meta, d):
    return [meta[SLOTS + j, d] for j in range(SLOTS)]


def dp_at(meta):
    return meta[2 * SLOTS, 0]


def tensor_at(meta):
    return meta[2 * SLOTS, 1]


def kept_total(meta, d):
    return sum(a * (1 - b) for a, b in zip(lengths_of(meta, d), moves_of(meta, d)))


def picks(meta, moved, first, rows, home):
    d = dp_at(meta)
    at = lax.broadcasted_iota(jnp.int32, (rows, 1), 0) - first
    source = jnp.full((rows, 1), -1, jnp.int32)
    begin = jnp.int32(0)
    start = jnp.int32(0)
    for length, move in zip(lengths_of(meta, d), moves_of(meta, d)):
        size = length * (move if moved else 1 - move)
        inside = (at >= begin) & (at < begin + size)
        source = jnp.where(inside, at + (start - begin), source)
        begin = begin + size
        start = start + length
    columns = lax.broadcasted_iota(jnp.int32, (rows, home), 1)
    return jnp.where(columns == source, 1.0, 0.0).astype(BF)


def sent_first(meta):
    n = meta.shape[1]
    partner = lax.rem(dp_at(meta) + n // 2, n)
    return lax.rem(kept_total(meta, partner), TILE)


def early_picks(meta, home):
    return picks(meta, True, sent_first(meta), EARLY, home)


def late_picks(meta, home):
    return picks(meta, True, sent_first(meta) - EARLY, LATE, home)


def kept_picks(meta, home):
    return picks(meta, False, 0, KEEP, home)


def scaled_rows(meta, pick, cot, scale):
    width = cot.shape[1]
    rows = jnp.dot(pick, cot[...], preferred_element_type=F32)
    own = scale[pl.ds(pl.multiple_of(tensor_at(meta) * width, 128), width)]
    return (rows * own[None, :]).astype(BF)


def first_kernel(meta, cot_hbm, scale_hbm, pre_hbm, late_out, rest_out, early_out, cot, scale, pre, sems):
    home, width = cot.shape
    pairs = ((cot_hbm, cot), (scale_hbm, scale), (pre_hbm, pre))
    copies = [pltpu.make_async_copy(a, b, sems.at[i]) for i, (a, b) in enumerate(pairs)]
    for copy in copies:
        copy.start()
    early = early_picks(meta, home)
    copies[0].wait()
    copies[1].wait()
    early_rows = scaled_rows(meta, early, cot, scale)
    early_out[:, :width] = early_rows
    late_out[...] = scaled_rows(meta, late_picks(meta, home), cot, scale)
    rest_out[0:EARLY, :] = early_rows
    rest_out[EARLY:, :] = scaled_rows(meta, kept_picks(meta, home), cot, scale)
    copies[2].wait()
    early_out[:, width:] = jnp.dot(early, pre[...], preferred_element_type=F32).astype(BF)


def gelu_and_slope(x):
    cumulative = 0.5 * (1.0 + lax.erf(x * inv_root_two))
    return x * cumulative, cumulative + x * jnp.exp(-0.5 * x * x) * inv_root_tau


def gelu_kernel(late, base, block, meta, pre_hbm, act_out, der_out, pick, rows_f32, pre, sems):
    home = pre.shape[1]
    rows = pick.shape[0]
    blocks = act_out.shape[1] // block

    def fetch(i):
        columns = pl.ds(base + i * block, block)
        return pltpu.make_async_copy(pre_hbm.at[:, columns], pre.at[i], sems.at[i])

    for i in range(blocks):
        fetch(i).start()
    if late:
        pick[...] = late_picks(meta, home)
    else:
        pick[0:EARLY, :] = early_picks(meta, home)
        pick[EARLY:, :] = kept_picks(meta, home)
    step = next(TILE * k for k in (3, 4, 2, 1) if rows % (TILE * k) == 0)
    for i in range(blocks):
        fetch(i).wait()
        rows_f32[...] = jnp.dot(pick[...], pre[i], preferred_element_type=F32)
        columns = slice(i * block, (i + 1) * block)

        def body(k, _):
            at = pl.ds(pl.multiple_of(k * step, step), step)
            value, slope = gelu_and_slope(rows_f32[at, :])
            act_out[at, columns] = value.astype(BF)
            der_out[at, columns] = slope
            return 0

        lax.fori_loop(0, rows // step, body, 0)


def assemble(meta, pieces, first_row, lhs):
    rows = lhs.shape[0]
    width = pieces[1].shape[1]
    for j, piece in enumerate(pieces):
        columns = pl.ds(pl.multiple_of((tensor_at(meta) ^ j) * width, 128), width)
        lhs[:, columns] = piece[first_row : first_row + rows, 0:width]


def grad_kernel(first_row, first_slope, slope_count, block, meta, p0, p1, p2, p3, weight, *rest):
    slopes, outs, lhs = rest[:slope_count], rest[slope_count:-1], rest[-1]
    rows = lhs.shape[0]
    assemble(meta, (p0, p1, p2, p3), first_row, lhs)
    part = slopes[0].shape[1]
    at = 0
    for out in outs:
        for c in range(0, out.shape[1], block):
            wide = min(block, out.shape[1] - c)
            slope = slopes[at // part][first_slope : first_slope + rows, at % part : at % part + wide]
            value = jnp.dot(lhs[...], weight[:, at : at + wide], preferred_element_type=F32)
            out[:, c : c + wide] = (value * slope).astype(BF)
            at += wide


def early_kernel(block, meta, own, p1, p2, p3, weight, out, lhs, acc):
    width = p1.shape[1]
    assemble(meta, (own, p1, p2, p3), 0, lhs)
    for at in range(0, out.shape[1], block):
        columns = slice(at, at + block)
        acc[...] = jnp.dot(lhs[...], weight[:, columns], preferred_element_type=F32)

        def body(k, _):
            rows = pl.ds(pl.multiple_of(k * TILE, TILE), TILE)
            _, slope = gelu_and_slope(own[rows, width + at : width + at + block].astype(F32))
            out[rows, columns] = (acc[rows, :] * slope).astype(BF)
            return 0

        lax.fori_loop(0, EARLY // TILE, body, 0)


def weight_kernel(count, base, meta, *refs):
    lates, rests = refs[:count], refs[count : 2 * count]
    act_late, act_rest, *outs, lhs_late, lhs_rest = refs[2 * count :]
    half = lates[0].shape[1] // 2
    mine = dp_at(meta) % 2 == 0
    for i in range(count):
        for piece, lhs in ((lates[i], lhs_late), (rests[i], lhs_rest)):
            both = piece[...].T
            lo, hi = both[:half], both[half:]
            lhs[i * half : (i + 1) * half, :] = jnp.where(mine, hi, lo)
            lhs[(count + i) * half : (count + i + 1) * half, :] = jnp.where(mine, lo, hi)
    again_kernel(base, meta, lhs_late, lhs_rest, act_late, act_rest, *outs)


def again_kernel(base, meta, lhs_late, lhs_rest, act_late, act_rest, *outs):
    columns = slice(base, base + act_rest.shape[1])
    step = lhs_late.shape[0] // 4
    at = 0
    for out in outs:
        for i in range(0, out.shape[0], step):
            part = slice(at, at + step)
            value = jnp.dot(lhs_late[part, :], act_late[:, columns], preferred_element_type=F32)
            value += jnp.dot(lhs_rest[part, :], act_rest[...], preferred_element_type=F32)
            out[i : i + step, :] = value.astype(out.dtype)
            at += step


def tick_kernel(meta, out):
    out[...] = jnp.zeros(out.shape, out.dtype)


def near_kernel(count, meta, *refs):
    keeps, gots, (out, mine) = refs[:count], refs[count : 2 * count], refs[2 * count :]
    half = out.shape[0] // 2
    parts = [(k, g, at) for k, g in zip(keeps, gots) for at in range(0, k.shape[0], half)]
    keeps_even = (dp_at(meta) // 2 + tensor_at(meta)) % 2 == 0
    step = 2 * TILE

    for pair in range(2):
        (k0, g0, a0), (k1, g1, a1) = parts[2 * pair], parts[2 * pair + 1]

        def body(i, _):
            def rows(at):
                return pl.ds(pl.multiple_of(at + i * step, TILE), step)

            even = k0[rows(a0), :] + g0[rows(a0), :].astype(F32)
            odd = k1[rows(a1), :] + g1[rows(a1), :].astype(F32)
            out[rows(pair * half), :] = jnp.where(keeps_even, odd, even).astype(BF)
            mine[rows(pair * half), :] = jnp.where(keeps_even, even, odd)
            return 0

        lax.fori_loop(0, half // step, body, 0)


def far_kernel(meta, held, got, out, mine):
    half = out.shape[0]
    keeps_first = (dp_at(meta) // 4 + tensor_at(meta) // 2) % 2 == 0
    step = 2 * TILE

    def body(i, _):
        first = pl.ds(pl.multiple_of(i * step, TILE), step)
        second = pl.ds(pl.multiple_of(half + i * step, TILE), step)
        a = held[first, :] + got[first, :].astype(F32)
        b = held[second, :] + got[second, :].astype(F32)
        out[first, :] = jnp.where(keeps_first, b, a).astype(BF)
        mine[first, :] = jnp.where(keeps_first, a, b)
        return 0

    lax.fori_loop(0, half // step, body, 0)


def place_kernel(cuts, meta, kept, early, *rest):
    lates, out = rest[:-1], rest[-1]
    count = kept_total(meta, dp_at(meta))
    first = jnp.minimum(count - lax.rem(count, TILE), BAL - SEND)
    first = pl.multiple_of(first, TILE)
    wide = out.shape[1]
    step = pl.program_id(0)
    columns = pl.ds(pl.multiple_of(step * wide, wide), wide)
    out[0:KEEP, :] = kept[:, columns]
    out[KEEP:, :] = jnp.zeros((out.shape[0] - KEEP, wide), BF)

    def put(block, at):
        rows = lax.broadcasted_iota(jnp.int32, (block.shape[0], 1), 0) + at
        window = pl.ds(at, block.shape[0])
        out[window, :] = jnp.where(rows < count, out[window, :], block)

    put(early[:, columns], first)
    sources = [(late, c) for late, cut in zip(lates, cuts) for c in range(0, cut, wide)]
    for i, (late, c) in enumerate(sources):

        @pl.when(step == i)
        def _():
            put(late[:, c : c + wide], pl.multiple_of(first + EARLY, TILE))


def swapped(block, axis, distance):
    n = lax.axis_size(axis)
    return lax.ppermute(block, axis, [(i, i ^ distance) for i in range(n)])


def after(value, *others):
    return lax.optimization_barrier((value, *others))[0]


def shards(hidden_pre, cotangent, down_weight, layer_scale, crop_lengths, crop_moves):
    hidden_pre, cotangent, layer_scale = (
        pltpu.with_memory_space_constraint(x, pltpu.HBM) for x in (hidden_pre, cotangent, layer_scale)
    )
    home, ff = hidden_pre.shape
    width = cotangent.shape[1]
    features = down_weight.shape[0]
    half, part = width // 2, ff // 3
    others = EARLY + KEEP
    n = lax.axis_size("dp")
    d = lax.axis_index("dp").astype(jnp.int32)
    t = lax.axis_index("tensor").astype(jnp.int32)
    column = lax.broadcasted_iota(jnp.int32, (1, n), 1)
    own = jnp.where(column == 0, d, jnp.where(column == 1, t, 0))
    meta = jnp.concatenate([crop_lengths.T, crop_moves.T, own])
    vmem = pltpu.VMEM
    sems = pltpu.SemaphoreType.DMA

    def gelu(meta, late, base, columns):
        block = 256
        rows = LATE if late else others
        return kernel_call(
            functools.partial(gelu_kernel, late, base, block),
            [shape(rows, columns), shape(rows, columns, F32)],
            [IN_HBM], [IN_VMEM] * 2,
            [vmem((rows, home), BF), vmem((rows, block), F32), vmem((columns // block, home, block), BF),
             sems((columns // block,))],
        )(meta, hidden_pre)

    def weight_first(meta, act):
        count = len(lates)
        return kernel_call(
            functools.partial(weight_kernel, count, 0),
            [shape(width, part)] * 2 + [shape(width, part, F32)] * 2
            + [shape(count * width, LATE), shape(count * width, others)],
            [IN_VMEM] * (2 * count + 2), [IN_VMEM] * 6,
        )(meta, *lates, *rests, act_late, act)

    def weight_again(meta, base, act):
        return kernel_call(
            functools.partial(again_kernel, base),
            [shape(4 * half, part), shape(4 * half, part, F32)], [IN_VMEM] * 4, [IN_VMEM] * 2,
        )(meta, *lhs, act_late, act)

    def grads(meta, pieces, first_row, first_slope, rows, slopes, cuts):
        return kernel_call(
            functools.partial(grad_kernel, first_row, first_slope, len(slopes), 256),
            [shape(rows, c) for c in cuts], [IN_VMEM] * (5 + len(slopes)), [IN_VMEM] * len(cuts),
            [vmem((rows, features), BF)],
        )(meta, *pieces, down_weight, *slopes)

    def tick(meta):
        return kernel_call(tick_kernel, shape(8, 128, F32), [], IN_VMEM)(meta)

    def near_step(meta, keeps, gots):
        count = len(keeps)
        return kernel_call(
            functools.partial(near_kernel, count),
            [shape(width, part), shape(width, part, F32)], [IN_VMEM] * (2 * count), [IN_VMEM] * 2,
        )(meta, *keeps, *gots)

    def far_step(meta, mine, got):
        return kernel_call(
            far_kernel, [shape(half, part), shape(half, part, F32)], [IN_VMEM] * 2, [IN_VMEM] * 2
        )(meta, mine, got)

    late, rest, early = kernel_call(
        first_kernel, [shape(LATE, width), shape(others, width), shape(EARLY, width + ff)],
        [IN_HBM] * 3, [IN_VMEM] * 3,
        [vmem((home, width), BF), vmem((features,), F32), vmem((home, ff), BF), sems((3,))],
    )(meta, cotangent, layer_scale, hidden_pre)
    arrived_early = swapped(early, "dp", n // 2)

    late_c, late_y = swapped(late, "tensor", 1), swapped(late, "tensor", 2)
    rest_c, rest_y = swapped(rest, "tensor", 1), swapped(rest, "tensor", 2)
    act_late, der_late = gelu(after(meta, late), True, 0, ff)
    late_y = after(late_y, act_late, late_c, rest_c, arrived_early)
    late_yc = swapped(late_y, "tensor", 1)
    lates = (late, late_c, late_y, late_yc)

    moves = (640, 512, ff - 1152)
    moving = grads(after(meta, late_y), lates, 0, 0, LATE, (der_late,), moves)
    arrived_a = swapped(moving[0], "dp", n // 2)
    rest_y = after(rest_y, *moving)
    rest_yc = swapped(rest_y, "tensor", 1)
    rests = (rest, rest_c, rest_y, rest_yc)

    act_a, der_a = gelu(after(meta, *moving), False, 0, part)
    *sends_a, keep_01, keep_23, lhs_late, lhs_rest = weight_first(after(meta, act_a), act_a)
    lhs = (lhs_late, lhs_rest)
    gots_a = [swapped(send, "dp", 1) for send in sends_a]
    early_sent = after(arrived_early[:, :width], keep_01)
    early_c, early_y = swapped(early_sent, "tensor", 1), swapped(early_sent, "tensor", 2)
    act_b, der_b = gelu(after(meta, keep_01), False, part, part)
    send_b, keep_b = weight_again(after(meta, act_b, early_c, early_y), part, act_b)
    got_b = swapped(send_b, "dp", 1)
    early_y = after(early_y, send_b)
    early_yc = swapped(early_y, "tensor", 1)
    act_c, der_c = gelu(after(meta, send_b), False, 2 * part, part)
    send_c, keep_c = weight_again(after(meta, act_c, early_yc), 2 * part, act_c)
    got_c = swapped(send_c, "dp", 1)

    out_na, mine_a = near_step(after(meta, send_c, arrived_a), (keep_01, keep_23), gots_a)
    got_na = swapped(out_na, "dp", 2)
    tick_a = tick(after(meta, out_na))
    arrived_b = swapped(after(moving[1], tick_a), "dp", n // 2)

    (kept_grad,) = grads(after(meta, tick_a), rests, EARLY, EARLY, KEEP, (der_a, der_b, der_c), (ff,))
    early_grad = kernel_call(
        functools.partial(early_kernel, 256), shape(EARLY, ff), [IN_VMEM] * 5, IN_VMEM,
        [vmem((EARLY, features), BF), vmem((EARLY, 256), F32)],
    )(after(meta, kept_grad), arrived_early, early_c, early_y, early_yc, down_weight)

    out_nb, mine_b = near_step(after(meta, early_grad, got_na), (keep_b,), (got_b,))
    got_nb = swapped(out_nb, "dp", 2)
    tick_b = tick(after(meta, out_nb))
    arrived_c = swapped(after(moving[2], tick_b), "dp", n // 2)
    out_fa, own_a = far_step(after(meta, tick_b), mine_a, got_na)
    got_fa = swapped(out_fa, "dp", 4)
    out_nc, mine_c = near_step(after(meta, out_fa, arrived_b), (keep_c,), (got_c,))
    got_nc = swapped(out_nc, "dp", 2)
    out_fb, own_b = far_step(after(meta, out_nc), mine_b, got_nb)
    got_fb = swapped(out_fb, "dp", 4)
    out_fc, own_c = far_step(after(meta, out_fb, arrived_c, got_fa), mine_c, got_nc)
    got_fc = swapped(out_fc, "dp", 4)
    total = [a + b.astype(F32) for a, b in ((own_a, got_fa), (own_b, got_fb), (own_c, got_fc))]
    down_grad = jnp.concatenate(total, axis=1) / math.sqrt(n * home)

    hidden_grad = kernel_call(
        functools.partial(place_kernel, moves), shape(BAL, ff), [IN_VMEM] * (2 + len(moves)),
        pl.BlockSpec((BAL, 128), lambda i, *_: (0, i)), grid=(ff // 128,),
    )(after(meta, out_fc), kept_grad, early_grad, arrived_a, arrived_b, arrived_c)
    return (hidden_grad, down_grad)


def solution(mesh):
    pairs_and_fours = (mesh.shape["dp"], mesh.shape["tensor"]) == (8, 4)
    return jax.shard_map(
        shards if pairs_and_fours else general_shards,
        mesh=mesh,
        in_specs=(P("dp", "tensor"), P("dp", "tensor"), P(None, "tensor"), P(), P(), P()),
        out_specs=(P("dp", "tensor"), P("dp", "tensor")),
        check_vma=False,
    )


def shifted(block, axis, distance):
    devices = range(lax.axis_size(axis))
    route = [((i - distance) % len(devices), i) for i in devices]
    return lax.ppermute(block, axis, route)


def crop_rows(row_total, crop_sizes, crop_starts):
    crop_ends = jnp.cumsum(crop_sizes)
    crop_begins = crop_ends - crop_sizes
    target_rows = jnp.arange(row_total, dtype=jnp.int32)[:, None]
    inside_crop = (target_rows >= crop_begins[None, :]) & (target_rows < crop_ends[None, :])
    source_rows = jnp.sum(
        jnp.where(inside_crop, crop_starts[None, :] + target_rows - crop_begins[None, :], 0), axis=1
    )
    return (source_rows, jnp.any(inside_crop, axis=1))


def select_rows(row_block, source_rows, valid_rows):
    taken = jnp.take(row_block, source_rows, axis=0)
    return jnp.where(valid_rows[:, None], taken, jnp.zeros((), row_block.dtype))


def gelu_parts(pre_act):
    cumulative = 0.5 * (1.0 + jax.scipy.special.erf(pre_act * inv_root_two))
    activated = pre_act * cumulative
    derivative = cumulative + pre_act * jnp.exp(-0.5 * pre_act * pre_act) * inv_root_tau
    return (activated, derivative)


def local_grads(pre_rows, cot_part, live_rows, layer_scale, down_weight, home_rows):
    cot_full = lax.all_gather(cot_part, "tensor", axis=1, tiled=True)
    scaled = (cot_full.astype(F32) * layer_scale[None, :]).astype(BF)
    activated, derivative = gelu_parts(pre_rows.astype(F32))
    activation = jnp.where(live_rows[:, None], activated, 0.0).astype(BF)
    backward = jnp.dot(scaled, down_weight, preferred_element_type=F32) * derivative
    gradient_rows = jnp.where(live_rows[:, None], backward, 0.0).astype(BF)
    weight_grad = lax.psum_scatter(
        lax.dot_general(scaled, activation, (((0,), (0,)), ((), ())), preferred_element_type=F32),
        "dp",
        scatter_dimension=0,
        tiled=True,
    )
    return (gradient_rows, weight_grad / math.sqrt(lax.axis_size("dp") * home_rows))


def general_shards(hidden_pre, cotangent, down_weight, layer_scale, crop_lengths, crop_moves):
    devices = lax.axis_size("dp")
    half_axis = devices // 2
    device_index = lax.axis_index("dp")
    partner_index = (device_index + half_axis) % devices
    own_lengths = lax.dynamic_index_in_dim(crop_lengths, device_index, 0, keepdims=False)
    own_moves = lax.dynamic_index_in_dim(crop_moves, device_index, 0, keepdims=False)
    partner_lengths = lax.dynamic_index_in_dim(crop_lengths, partner_index, 0, keepdims=False)
    partner_moves = lax.dynamic_index_in_dim(crop_moves, partner_index, 0, keepdims=False)
    home_rows = hidden_pre.shape[0]
    own_starts = jnp.cumsum(own_lengths) - own_lengths
    sent_sizes = own_lengths * own_moves
    kept_sizes = own_lengths * (1 - own_moves)
    arrived = jnp.sum(partner_lengths * partner_moves)
    send_source, send_valid = crop_rows(SEND, sent_sizes, own_starts)
    keep_sizes = jnp.concatenate([kept_sizes, arrived[None]])
    keep_starts = jnp.concatenate([own_starts, jnp.full((1,), home_rows, jnp.int32)])
    keep_source, keep_valid = crop_rows(BAL, keep_sizes, keep_starts)
    live_home = jnp.arange(home_rows, dtype=jnp.int32) < jnp.sum(own_lengths)
    gradient_rows, weight_grad = local_grads(
        hidden_pre, cotangent, live_home, layer_scale, down_weight, home_rows
    )
    outgoing = select_rows(gradient_rows, send_source, send_valid)
    incoming = shifted(outgoing, "dp", half_axis)
    balanced = select_rows(jnp.concatenate([gradient_rows, incoming], 0), keep_source, keep_valid)
    return (balanced, weight_grad)
```

```python
import functools
import math

import jax
import jax.numpy as jnp
from jax import lax
from jax.experimental import pallas as pl
from jax.experimental.pallas import tpu as pltpu
from jax.sharding import PartitionSpec as P

SEND = 528
KEEP = 528
TILE = 16
EARLY = 48
LATE = SEND - EARLY
SLOTS = 4
BAL = 720
BF = jnp.bfloat16
F32 = jnp.float32

inv_root_two = 0.7071067811865476
inv_root_tau = 0.3989422804014327


def kernel_call(kernel, out_shape, in_specs, out_specs, scratch=(), grid=(1,)):
    return pl.pallas_call(
        kernel,
        grid_spec=pltpu.PrefetchScalarGridSpec(
            num_scalar_prefetch=1,
            grid=grid,
            in_specs=in_specs,
            out_specs=out_specs,
            scratch_shapes=list(scratch),
        ),
        out_shape=out_shape,
        cost_estimate=pl.CostEstimate(flops=1, bytes_accessed=1, transcendentals=0),
        compiler_params=pltpu.CompilerParams(vmem_limit_bytes=16 * 1024 * 1024),
    )


IN_VMEM = pl.BlockSpec(memory_space=pltpu.VMEM)
IN_HBM = pl.BlockSpec(memory_space=pltpu.HBM)


def shape(a, b, dtype=BF):
    return jax.ShapeDtypeStruct((a, b), dtype)


def lengths_of(meta, d):
    return [meta[j, d] for j in range(SLOTS)]


def moves_of(meta, d):
    return [meta[SLOTS + j, d] for j in range(SLOTS)]


def dp_at(meta):
    return meta[2 * SLOTS, 0]


def tensor_at(meta):
    return meta[2 * SLOTS, 1]


def kept_total(meta, d):
    return sum(a * (1 - b) for a, b in zip(lengths_of(meta, d), moves_of(meta, d)))


def picks(meta, moved, first, rows, home):
    d = dp_at(meta)
    at = lax.broadcasted_iota(jnp.int32, (rows, 1), 0) - first
    source = jnp.full((rows, 1), -1, jnp.int32)
    begin = jnp.int32(0)
    start = jnp.int32(0)
    for length, move in zip(lengths_of(meta, d), moves_of(meta, d)):
        size = length * (move if moved else 1 - move)
        inside = (at >= begin) & (at < begin + size)
        source = jnp.where(inside, at + (start - begin), source)
        begin = begin + size
        start = start + length
    columns = lax.broadcasted_iota(jnp.int32, (rows, home), 1)
    return jnp.where(columns == source, 1.0, 0.0).astype(BF)


def sent_first(meta):
    n = meta.shape[1]
    partner = lax.rem(dp_at(meta) + n // 2, n)
    return lax.rem(kept_total(meta, partner), TILE)


def early_picks(meta, home):
    return picks(meta, True, sent_first(meta), EARLY, home)


def late_picks(meta, home):
    return picks(meta, True, sent_first(meta) - EARLY, LATE, home)


def kept_picks(meta, home):
    return picks(meta, False, 0, KEEP, home)


def scaled_rows(meta, pick, cot, scale):
    width = cot.shape[1]
    rows = jnp.dot(pick, cot[...], preferred_element_type=F32)
    own = scale[pl.ds(pl.multiple_of(tensor_at(meta) * width, 128), width)]
    return (rows * own[None, :]).astype(BF)


def first_kernel(meta, cot_hbm, scale_hbm, pre_hbm, late_out, rest_out, early_out, cot, scale, pre, sems):
    home, width = cot.shape
    pairs = ((cot_hbm, cot), (scale_hbm, scale), (pre_hbm, pre))
    copies = [pltpu.make_async_copy(a, b, sems.at[i]) for i, (a, b) in enumerate(pairs)]
    for copy in copies:
        copy.start()
    early = early_picks(meta, home)
    copies[0].wait()
    copies[1].wait()
    early_rows = scaled_rows(meta, early, cot, scale)
    early_out[:, :width] = early_rows
    late_out[...] = scaled_rows(meta, late_picks(meta, home), cot, scale)
    rest_out[0:EARLY, :] = early_rows
    rest_out[EARLY:, :] = scaled_rows(meta, kept_picks(meta, home), cot, scale)
    copies[2].wait()
    early_out[:, width:] = jnp.dot(early, pre[...], preferred_element_type=F32).astype(BF)


def gelu_and_slope(x):
    cumulative = 0.5 * (1.0 + lax.erf(x * inv_root_two))
    return x * cumulative, cumulative + x * jnp.exp(-0.5 * x * x) * inv_root_tau


def cut_at(widths, block):
    return [
        (i, c, min(block, width - c)) for i, width in enumerate(widths) for c in range(0, width, block)
    ]


def gelu_kernel(late, base, block, meta, pre_hbm, act_out, der_out, pick, rows_f32, pre, sems):
    home = pre.shape[1]
    rows = pick.shape[0]
    blocks = cut_at((act_out.shape[1],), block)
    copies = [
        pltpu.make_async_copy(
            pre_hbm.at[:, pl.ds(base + at, wide)], pre.at[i, :, pl.ds(0, wide)], sems.at[i]
        )
        for i, (_, at, wide) in enumerate(blocks)
    ]
    for copy in copies:
        copy.start()
    if late:
        pick[...] = late_picks(meta, home)
    else:
        pick[0:EARLY, :] = early_picks(meta, home)
        pick[EARLY:, :] = kept_picks(meta, home)
    step = next(TILE * k for k in (3, 4, 2, 1) if rows % (TILE * k) == 0)
    for i, (_, at, wide) in enumerate(blocks):
        copies[i].wait()
        rows_f32[:, 0:wide] = jnp.dot(pick[...], pre[i, :, 0:wide], preferred_element_type=F32)
        columns = slice(at, at + wide)

        def body(k, _):
            rows = pl.ds(pl.multiple_of(k * step, step), step)
            value, slope = gelu_and_slope(rows_f32[rows, 0:wide])
            act_out[rows, columns] = value.astype(BF)
            der_out[rows, columns] = slope
            return 0

        lax.fori_loop(0, rows // step, body, 0)


def assemble(meta, pieces, first_row, lhs):
    rows = lhs.shape[0]
    width = pieces[1].shape[1]
    for j, piece in enumerate(pieces):
        columns = pl.ds(pl.multiple_of((tensor_at(meta) ^ j) * width, 128), width)
        lhs[:, columns] = piece[first_row : first_row + rows, 0:width]


def grad_kernel(first_row, first_slope, base, slope_count, block, meta, p0, p1, p2, p3, weight, *rest):
    slopes, outs, lhs = rest[:slope_count], rest[slope_count:-1], rest[-1]
    rows = lhs.shape[0]
    assemble(meta, (p0, p1, p2, p3), first_row, lhs)
    parts = slopes if slope_count > len(outs) else outs
    starts = [sum(part.shape[1] for part in parts[:i]) for i in range(len(parts))]
    slope_rows = slice(first_slope, first_slope + rows)
    for i, c, wide in cut_at([part.shape[1] for part in parts], block):
        at = starts[i] + c
        inside, whole_at = slice(c, c + wide), slice(at, at + wide)
        slope = slopes[i][slope_rows, inside] if slope_count == len(parts) else slopes[0][slope_rows, whole_at]
        columns = slice(base + at, base + at + wide)
        value = (jnp.dot(lhs[...], weight[:, columns], preferred_element_type=F32) * slope).astype(BF)
        if len(outs) == len(parts):
            outs[i][:, inside] = value
        else:
            outs[0][:, whole_at] = value


def early_kernel(block, meta, own, p1, p2, p3, weight, out, lhs, acc):
    width = p1.shape[1]
    assemble(meta, (own, p1, p2, p3), 0, lhs)
    for at in range(0, out.shape[1], block):
        columns = slice(at, at + block)
        acc[...] = jnp.dot(lhs[...], weight[:, columns], preferred_element_type=F32)

        def body(k, _):
            rows = pl.ds(pl.multiple_of(k * TILE, TILE), TILE)
            _, slope = gelu_and_slope(own[rows, width + at : width + at + block].astype(F32))
            out[rows, columns] = (acc[rows, :] * slope).astype(BF)
            return 0

        lax.fori_loop(0, EARLY // TILE, body, 0)


def weight_kernel(count, meta, *refs):
    lates, rests = refs[:count], refs[count : 2 * count]
    act_late, act_rest, *outs, lhs_late, lhs_rest = refs[2 * count :]
    half = lates[0].shape[1] // 2
    mine = dp_at(meta) % 2 == 0
    for i in range(count):
        for piece, lhs in ((lates[i], lhs_late), (rests[i], lhs_rest)):
            both = piece[...].T
            lo, hi = both[:half], both[half:]
            lhs[i * half : (i + 1) * half, :] = jnp.where(mine, hi, lo)
            lhs[(count + i) * half : (count + i + 1) * half, :] = jnp.where(mine, lo, hi)
    again_kernel(meta, lhs_late, lhs_rest, act_late, act_rest, *outs)


def again_kernel(meta, lhs_late, lhs_rest, act_late, act_rest, *outs):
    step = lhs_late.shape[0] // 4
    at = 0
    for out in outs:
        for i in range(0, out.shape[0], step):
            part = slice(at, at + step)
            value = jnp.dot(lhs_late[part, :], act_late[...], preferred_element_type=F32)
            value += jnp.dot(lhs_rest[part, :], act_rest[...], preferred_element_type=F32)
            out[i : i + step, :] = value.astype(out.dtype)
            at += step


def tick_kernel(meta, out):
    out[...] = jnp.zeros(out.shape, out.dtype)


def near_kernel(count, meta, *refs):
    keeps, gots, (out, mine) = refs[:count], refs[count : 2 * count], refs[2 * count :]
    half = out.shape[0] // 2
    parts = [(k, g, at) for k, g in zip(keeps, gots) for at in range(0, k.shape[0], half)]
    keeps_even = (dp_at(meta) // 2 + tensor_at(meta)) % 2 == 0
    step = 2 * TILE

    for pair in range(2):
        (k0, g0, a0), (k1, g1, a1) = parts[2 * pair], parts[2 * pair + 1]

        def body(i, _):
            def rows(at):
                return pl.ds(pl.multiple_of(at + i * step, TILE), step)

            even = k0[rows(a0), :] + g0[rows(a0), :].astype(F32)
            odd = k1[rows(a1), :] + g1[rows(a1), :].astype(F32)
            out[rows(pair * half), :] = jnp.where(keeps_even, odd, even).astype(BF)
            mine[rows(pair * half), :] = jnp.where(keeps_even, even, odd)
            return 0

        lax.fori_loop(0, half // step, body, 0)


def far_kernel(meta, held, got, out, mine):
    half = out.shape[0]
    keeps_first = (dp_at(meta) // 4 + tensor_at(meta) // 2) % 2 == 0
    step = 2 * TILE

    def body(i, _):
        first = pl.ds(pl.multiple_of(i * step, TILE), step)
        second = pl.ds(pl.multiple_of(half + i * step, TILE), step)
        a = held[first, :] + got[first, :].astype(F32)
        b = held[second, :] + got[second, :].astype(F32)
        out[first, :] = jnp.where(keeps_first, b, a).astype(BF)
        mine[first, :] = jnp.where(keeps_first, a, b)
        return 0

    lax.fori_loop(0, half // step, body, 0)


def place_kernel(cuts, meta, kept, early, *rest):
    lates, out = rest[:-1], rest[-1]
    count = kept_total(meta, dp_at(meta))
    first = jnp.minimum(count - lax.rem(count, TILE), BAL - SEND)
    first = pl.multiple_of(first, TILE)
    wide = out.shape[1]
    step = pl.program_id(0)
    columns = pl.ds(pl.multiple_of(step * wide, wide), wide)
    out[0:KEEP, :] = kept[:, columns]
    out[KEEP:, :] = jnp.zeros((out.shape[0] - KEEP, wide), BF)

    def put(block, at):
        rows = lax.broadcasted_iota(jnp.int32, (block.shape[0], 1), 0) + at
        window = pl.ds(at, block.shape[0])
        out[window, :] = jnp.where(rows < count, out[window, :], block)

    put(early[:, columns], first)
    sources = [(late, c) for late, cut in zip(lates, cuts) for c in range(0, cut, wide)]
    for i, (late, c) in enumerate(sources):

        @pl.when(step == i)
        def _():
            put(late[:, c : c + wide], pl.multiple_of(first + EARLY, TILE))


def swapped(block, axis, distance):
    n = lax.axis_size(axis)
    return lax.ppermute(block, axis, [(i, i ^ distance) for i in range(n)])


def after(value, *others):
    return lax.optimization_barrier((value, *others))[0]


def shards(hidden_pre, cotangent, down_weight, layer_scale, crop_lengths, crop_moves):
    hidden_pre, cotangent, layer_scale = (
        pltpu.with_memory_space_constraint(x, pltpu.HBM) for x in (hidden_pre, cotangent, layer_scale)
    )
    home, ff = hidden_pre.shape
    width = cotangent.shape[1]
    features = down_weight.shape[0]
    half = width // 2
    parts = (640, 512, ff - 1152)
    begins = (0, 640, 1152)
    others = EARLY + KEEP
    n = lax.axis_size("dp")
    d = lax.axis_index("dp").astype(jnp.int32)
    t = lax.axis_index("tensor").astype(jnp.int32)
    column = lax.broadcasted_iota(jnp.int32, (1, n), 1)
    own = jnp.where(column == 0, d, jnp.where(column == 1, t, 0))
    meta = jnp.concatenate([crop_lengths.T, crop_moves.T, own])
    vmem = pltpu.VMEM
    sems = pltpu.SemaphoreType.DMA

    def gelu(meta, late, base, columns):
        block = 256
        rows = LATE if late else others
        count = pl.cdiv(columns, block)
        return kernel_call(
            functools.partial(gelu_kernel, late, base, block),
            [shape(rows, columns), shape(rows, columns, F32)],
            [IN_HBM], [IN_VMEM] * 2,
            [vmem((rows, home), BF), vmem((rows, block), F32), vmem((count, home, block), BF), sems((count,))],
        )(meta, hidden_pre)

    def weight_first(meta, act_late, act):
        count = len(lates)
        return kernel_call(
            functools.partial(weight_kernel, count),
            [shape(width, parts[0])] * 2 + [shape(width, parts[0], F32)] * 2
            + [shape(count * width, LATE), shape(count * width, others)],
            [IN_VMEM] * (2 * count + 2), [IN_VMEM] * 6,
        )(meta, *lates, *rests, act_late, act)

    def weight_again(meta, act_late, act):
        columns = act.shape[1]
        return kernel_call(
            again_kernel,
            [shape(4 * half, columns), shape(4 * half, columns, F32)], [IN_VMEM] * 4, [IN_VMEM] * 2,
        )(meta, *lhs, act_late, act)

    def grads(meta, pieces, first_row, first_slope, rows, base, slopes, cuts):
        return kernel_call(
            functools.partial(grad_kernel, first_row, first_slope, base, len(slopes), 256),
            [shape(rows, c) for c in cuts], [IN_VMEM] * (5 + len(slopes)), [IN_VMEM] * len(cuts),
            [vmem((rows, features), BF)],
        )(meta, *pieces, down_weight, *slopes)

    def tick(meta):
        return kernel_call(tick_kernel, shape(8, 128, F32), [], IN_VMEM)(meta)

    def near_step(meta, keeps, gots):
        count, columns = len(keeps), keeps[0].shape[1]
        return kernel_call(
            functools.partial(near_kernel, count),
            [shape(width, columns), shape(width, columns, F32)], [IN_VMEM] * (2 * count), [IN_VMEM] * 2,
        )(meta, *keeps, *gots)

    def far_step(meta, mine, got):
        columns = got.shape[1]
        return kernel_call(
            far_kernel, [shape(half, columns), shape(half, columns, F32)], [IN_VMEM] * 2, [IN_VMEM] * 2
        )(meta, mine, got)

    late, rest, early = kernel_call(
        first_kernel, [shape(LATE, width), shape(others, width), shape(EARLY, width + ff)],
        [IN_HBM] * 3, [IN_VMEM] * 3,
        [vmem((home, width), BF), vmem((features,), F32), vmem((home, ff), BF), sems((3,))],
    )(meta, cotangent, layer_scale, hidden_pre)
    arrived_early = swapped(early, "dp", n // 2)

    late_c, late_y = swapped(late, "tensor", 1), swapped(late, "tensor", 2)
    rest_c, rest_y = swapped(rest, "tensor", 1), swapped(rest, "tensor", 2)
    act_l1, der_l1 = gelu(after(meta, late), True, 0, parts[0])
    late_y = after(late_y, act_l1, late_c, rest_c, arrived_early)
    late_yc = swapped(late_y, "tensor", 1)
    lates = (late, late_c, late_y, late_yc)

    (moving_a,) = grads(after(meta, late_y), lates, 0, 0, LATE, 0, (der_l1,), parts[:1])
    arrived_a = swapped(moving_a, "dp", n // 2)

    act_a, der_a = gelu(after(meta, moving_a), False, 0, parts[0])
    rest_y = after(rest_y, act_a)
    rest_yc = swapped(rest_y, "tensor", 1)
    rests = (rest, rest_c, rest_y, rest_yc)
    *sends_a, keep_01, keep_23, lhs_late, lhs_rest = weight_first(after(meta, act_a), act_l1, act_a)
    lhs = (lhs_late, lhs_rest)
    gots_a = [swapped(send, "dp", 1) for send in sends_a]

    act_l2, der_l2 = gelu(after(meta, keep_01), True, begins[1], parts[1])
    (moving_b,) = grads(after(meta, act_l2), lates, 0, 0, LATE, begins[1], (der_l2,), parts[1:2])
    act_b, der_b = gelu(after(meta, moving_b), False, begins[1], parts[1])
    send_b, keep_b = weight_again(after(meta, act_b, arrived_a), act_l2, act_b)
    got_b = swapped(send_b, "dp", 1)
    arrived_b = swapped(after(moving_b, send_b), "dp", n // 2)

    act_l3, der_l3 = gelu(after(meta, send_b), True, begins[2], parts[2])
    early_sent = after(arrived_early[:, :width], act_l3)
    early_c, early_y = swapped(early_sent, "tensor", 1), swapped(early_sent, "tensor", 2)
    act_c, der_c = gelu(after(meta, act_l3), False, begins[2], parts[2])
    send_c, keep_c = weight_again(after(meta, act_c, early_c, early_y), act_l3, act_c)
    got_c = swapped(send_c, "dp", 1)
    early_y = after(early_y, send_c)
    early_yc = swapped(early_y, "tensor", 1)

    out_na, mine_a = near_step(after(meta, send_c), (keep_01, keep_23), gots_a)
    got_na = swapped(out_na, "dp", 2)

    (moving_c,) = grads(after(meta, out_na), lates, 0, 0, LATE, begins[2], (der_l3,), parts[2:])
    (kept_grad,) = grads(after(meta, moving_c), rests, EARLY, EARLY, KEEP, 0, (der_a, der_b, der_c), (ff,))
    early_grad = kernel_call(
        functools.partial(early_kernel, 256), shape(EARLY, ff), [IN_VMEM] * 5, IN_VMEM,
        [vmem((EARLY, features), BF), vmem((EARLY, 256), F32)],
    )(after(meta, kept_grad), arrived_early, early_c, early_y, early_yc, down_weight)

    out_nb, mine_b = near_step(after(meta, early_grad, arrived_b), (keep_b,), (got_b,))
    got_nb = swapped(out_nb, "dp", 2)
    tick_b = tick(after(meta, out_nb))
    arrived_c = swapped(after(moving_c, tick_b), "dp", n // 2)
    out_fa, own_a = far_step(after(meta, tick_b), mine_a, got_na)
    got_fa = swapped(out_fa, "dp", 4)
    out_nc, mine_c = near_step(after(meta, out_fa, arrived_c), (keep_c,), (got_c,))
    got_nc = swapped(out_nc, "dp", 2)
    out_fb, own_b = far_step(after(meta, out_nc), mine_b, got_nb)
    got_fb = swapped(out_fb, "dp", 4)
    out_fc, own_c = far_step(after(meta, out_fb, got_fa), mine_c, got_nc)
    got_fc = swapped(out_fc, "dp", 4)
    total = [a + b.astype(F32) for a, b in ((own_a, got_fa), (own_b, got_fb), (own_c, got_fc))]
    down_grad = jnp.concatenate(total, axis=1) / math.sqrt(n * home)

    hidden_grad = kernel_call(
        functools.partial(place_kernel, parts), shape(BAL, ff), [IN_VMEM] * (2 + len(parts)),
        pl.BlockSpec((BAL, 128), lambda i, *_: (0, i)), grid=(ff // 128,),
    )(after(meta, out_fc), kept_grad, early_grad, arrived_a, arrived_b, arrived_c)
    return (hidden_grad, down_grad)


def solution(mesh):
    pairs_and_fours = (mesh.shape["dp"], mesh.shape["tensor"]) == (8, 4)
    return jax.shard_map(
        shards if pairs_and_fours else general_shards,
        mesh=mesh,
        in_specs=(P("dp", "tensor"), P("dp", "tensor"), P(None, "tensor"), P(), P(), P()),
        out_specs=(P("dp", "tensor"), P("dp", "tensor")),
        check_vma=False,
    )


def shifted(block, axis, distance):
    devices = range(lax.axis_size(axis))
    route = [((i - distance) % len(devices), i) for i in devices]
    return lax.ppermute(block, axis, route)


def crop_rows(row_total, crop_sizes, crop_starts):
    crop_ends = jnp.cumsum(crop_sizes)
    crop_begins = crop_ends - crop_sizes
    target_rows = jnp.arange(row_total, dtype=jnp.int32)[:, None]
    inside_crop = (target_rows >= crop_begins[None, :]) & (target_rows < crop_ends[None, :])
    source_rows = jnp.sum(
        jnp.where(inside_crop, crop_starts[None, :] + target_rows - crop_begins[None, :], 0), axis=1
    )
    return (source_rows, jnp.any(inside_crop, axis=1))


def select_rows(row_block, source_rows, valid_rows):
    taken = jnp.take(row_block, source_rows, axis=0)
    return jnp.where(valid_rows[:, None], taken, jnp.zeros((), row_block.dtype))


def gelu_parts(pre_act):
    cumulative = 0.5 * (1.0 + jax.scipy.special.erf(pre_act * inv_root_two))
    activated = pre_act * cumulative
    derivative = cumulative + pre_act * jnp.exp(-0.5 * pre_act * pre_act) * inv_root_tau
    return (activated, derivative)


def local_grads(pre_rows, cot_part, live_rows, layer_scale, down_weight, home_rows):
    cot_full = lax.all_gather(cot_part, "tensor", axis=1, tiled=True)
    scaled = (cot_full.astype(F32) * layer_scale[None, :]).astype(BF)
    activated, derivative = gelu_parts(pre_rows.astype(F32))
    activation = jnp.where(live_rows[:, None], activated, 0.0).astype(BF)
    backward = jnp.dot(scaled, down_weight, preferred_element_type=F32) * derivative
    gradient_rows = jnp.where(live_rows[:, None], backward, 0.0).astype(BF)
    weight_grad = lax.psum_scatter(
        lax.dot_general(scaled, activation, (((0,), (0,)), ((), ())), preferred_element_type=F32),
        "dp",
        scatter_dimension=0,
        tiled=True,
    )
    return (gradient_rows, weight_grad / math.sqrt(lax.axis_size("dp") * home_rows))


def general_shards(hidden_pre, cotangent, down_weight, layer_scale, crop_lengths, crop_moves):
    devices = lax.axis_size("dp")
    half_axis = devices // 2
    device_index = lax.axis_index("dp")
    partner_index = (device_index + half_axis) % devices
    own_lengths = lax.dynamic_index_in_dim(crop_lengths, device_index, 0, keepdims=False)
    own_moves = lax.dynamic_index_in_dim(crop_moves, device_index, 0, keepdims=False)
    partner_lengths = lax.dynamic_index_in_dim(crop_lengths, partner_index, 0, keepdims=False)
    partner_moves = lax.dynamic_index_in_dim(crop_moves, partner_index, 0, keepdims=False)
    home_rows = hidden_pre.shape[0]
    own_starts = jnp.cumsum(own_lengths) - own_lengths
    sent_sizes = own_lengths * own_moves
    kept_sizes = own_lengths * (1 - own_moves)
    arrived = jnp.sum(partner_lengths * partner_moves)
    send_source, send_valid = crop_rows(SEND, sent_sizes, own_starts)
    keep_sizes = jnp.concatenate([kept_sizes, arrived[None]])
    keep_starts = jnp.concatenate([own_starts, jnp.full((1,), home_rows, jnp.int32)])
    keep_source, keep_valid = crop_rows(BAL, keep_sizes, keep_starts)
    live_home = jnp.arange(home_rows, dtype=jnp.int32) < jnp.sum(own_lengths)
    gradient_rows, weight_grad = local_grads(
        hidden_pre, cotangent, live_home, layer_scale, down_weight, home_rows
    )
    outgoing = select_rows(gradient_rows, send_source, send_valid)
    incoming = shifted(outgoing, "dp", half_axis)
    balanced = select_rows(jnp.concatenate([gradient_rows, incoming], 0), keep_source, keep_valid)
    return (balanced, weight_grad)
```

```python
import functools
import math

import jax
import jax.numpy as jnp
from jax import lax
from jax.experimental import pallas as pl
from jax.experimental.pallas import tpu as pltpu
from jax.sharding import PartitionSpec as P

SEND = 528
KEEP = 528
TILE = 16
SLOTS = 4
BAL = 720
BF = jnp.bfloat16
F32 = jnp.float32

inv_root_two = 0.7071067811865476
inv_root_tau = 0.3989422804014327


def kernel_call(kernel, out_shape, in_specs, out_specs, scratch=(), grid=(1,)):
    return pl.pallas_call(
        kernel,
        grid_spec=pltpu.PrefetchScalarGridSpec(
            num_scalar_prefetch=1,
            grid=grid,
            in_specs=in_specs,
            out_specs=out_specs,
            scratch_shapes=list(scratch),
        ),
        out_shape=out_shape,
        cost_estimate=pl.CostEstimate(flops=1, bytes_accessed=1, transcendentals=0),
        compiler_params=pltpu.CompilerParams(vmem_limit_bytes=16 * 1024 * 1024),
    )


IN_VMEM = pl.BlockSpec(memory_space=pltpu.VMEM)
IN_HBM = pl.BlockSpec(memory_space=pltpu.HBM)


def shape(a, b, dtype=BF):
    return jax.ShapeDtypeStruct((a, b), dtype)


def lengths_of(meta, d):
    return [meta[j, d] for j in range(SLOTS)]


def moves_of(meta, d):
    return [meta[SLOTS + j, d] for j in range(SLOTS)]


def dp_at(meta):
    return meta[2 * SLOTS, 0]


def tensor_at(meta):
    return meta[2 * SLOTS, 1]


def kept_total(meta, d):
    return sum(a * (1 - b) for a, b in zip(lengths_of(meta, d), moves_of(meta, d)))


def picks(meta, moved, first, rows, home):
    d = dp_at(meta)
    at = lax.broadcasted_iota(jnp.int32, (rows, 1), 0) - first
    source = jnp.full((rows, 1), -1, jnp.int32)
    begin = jnp.int32(0)
    start = jnp.int32(0)
    for length, move in zip(lengths_of(meta, d), moves_of(meta, d)):
        size = length * (move if moved else 1 - move)
        inside = (at >= begin) & (at < begin + size)
        source = jnp.where(inside, at + (start - begin), source)
        begin = begin + size
        start = start + length
    columns = lax.broadcasted_iota(jnp.int32, (rows, home), 1)
    return jnp.where(columns == source, 1.0, 0.0).astype(BF)


def moved_picks(meta, home):
    n = meta.shape[1]
    partner = lax.rem(dp_at(meta) + n // 2, n)
    return picks(meta, True, lax.rem(kept_total(meta, partner), TILE), SEND, home)


def kept_picks(meta, home):
    return picks(meta, False, 0, KEEP, home)


def scaled_rows(meta, pick, cot, scale):
    width = cot.shape[1]
    rows = jnp.dot(pick, cot[...], preferred_element_type=F32)
    own = scale[pl.ds(pl.multiple_of(tensor_at(meta) * width, 128), width)]
    return (rows * own[None, :]).astype(BF)


def first_kernel(meta, cot_hbm, scale_hbm, moved_out, kept_out, cot, scale, sems):
    home = cot.shape[0]
    pairs = ((cot_hbm, cot), (scale_hbm, scale))
    copies = [pltpu.make_async_copy(a, b, sems.at[i]) for i, (a, b) in enumerate(pairs)]
    for copy in copies:
        copy.start()
    moved = moved_picks(meta, home)
    kept = kept_picks(meta, home)
    for copy in copies:
        copy.wait()
    moved_out[...] = scaled_rows(meta, moved, cot, scale)
    kept_out[...] = scaled_rows(meta, kept, cot, scale)


def gelu_and_slope(x):
    cumulative = 0.5 * (1.0 + lax.erf(x * inv_root_two))
    return x * cumulative, cumulative + x * jnp.exp(-0.5 * x * x) * inv_root_tau


def cut_at(widths, block):
    return [
        (i, c, min(block, width - c)) for i, width in enumerate(widths) for c in range(0, width, block)
    ]


def gelu_kernel(moved, base, block, meta, pre_hbm, act_out, der_out, pick, rows_f32, pre, sems):
    home = pre.shape[1]
    rows = pick.shape[0]
    blocks = cut_at((act_out.shape[1],), block)
    copies = [
        pltpu.make_async_copy(
            pre_hbm.at[:, pl.ds(base + at, wide)], pre.at[i, :, pl.ds(0, wide)], sems.at[i]
        )
        for i, (_, at, wide) in enumerate(blocks)
    ]
    for copy in copies:
        copy.start()
    pick[...] = moved_picks(meta, home) if moved else kept_picks(meta, home)
    step = next(TILE * k for k in (3, 4, 2, 1) if rows % (TILE * k) == 0)
    for i, (_, at, wide) in enumerate(blocks):
        copies[i].wait()
        rows_f32[:, 0:wide] = jnp.dot(pick[...], pre[i, :, 0:wide], preferred_element_type=F32)
        columns = slice(at, at + wide)

        def body(k, _):
            rows = pl.ds(pl.multiple_of(k * step, step), step)
            value, slope = gelu_and_slope(rows_f32[rows, 0:wide])
            act_out[rows, columns] = value.astype(BF)
            der_out[rows, columns] = slope
            return 0

        lax.fori_loop(0, rows // step, body, 0)


def grad_kernel(base, slope_count, block, meta, p0, p1, p2, p3, weight_hbm, *rest):
    slopes, outs, (lhs, weight, sems) = rest[:slope_count], rest[slope_count:-3], rest[-3:]
    parts = slopes if slope_count > len(outs) else outs
    starts = [sum(part.shape[1] for part in parts[:i]) for i in range(len(parts))]
    blocks = cut_at([part.shape[1] for part in parts], block)
    copies = [
        pltpu.make_async_copy(
            weight_hbm.at[:, pl.ds(base + starts[i] + c, wide)], weight.at[k, :, pl.ds(0, wide)], sems.at[k]
        )
        for k, (i, c, wide) in enumerate(blocks)
    ]
    for copy in copies:
        copy.start()
    width = p0.shape[1]
    for j, piece in enumerate((p0, p1, p2, p3)):
        lhs[:, pl.ds(pl.multiple_of((tensor_at(meta) ^ j) * width, 128), width)] = piece[...]
    for k, (i, c, wide) in enumerate(blocks):
        at = starts[i] + c
        inside, whole_at = slice(c, c + wide), slice(at, at + wide)
        slope = slopes[i][:, inside] if slope_count == len(parts) else slopes[0][:, whole_at]
        copies[k].wait()
        value = jnp.dot(lhs[...], weight[k, :, 0:wide], preferred_element_type=F32)
        value = (value * slope).astype(BF)
        if len(outs) == len(parts):
            outs[i][:, inside] = value
        else:
            outs[0][:, whole_at] = value


def weight_kernel(count, meta, *refs):
    moved, kept = refs[:count], refs[count : 2 * count]
    act_moved, act_kept, *outs, lhs_moved, lhs_kept = refs[2 * count :]
    half = moved[0].shape[1] // 2
    mine = dp_at(meta) % 2 == 0
    for i in range(count):
        for piece, lhs in ((moved[i], lhs_moved), (kept[i], lhs_kept)):
            both = piece[...].T
            lo, hi = both[:half], both[half:]
            lhs[i * half : (i + 1) * half, :] = jnp.where(mine, hi, lo)
            lhs[(count + i) * half : (count + i + 1) * half, :] = jnp.where(mine, lo, hi)
    again_kernel(0, meta, lhs_moved, lhs_kept, act_moved, act_kept, *outs)


def again_kernel(base, meta, lhs_moved, lhs_kept, act_moved, act_kept, *outs):
    columns = slice(base, base + act_kept.shape[1])
    step = lhs_moved.shape[0] // 4
    at = 0
    for out in outs:
        for i in range(0, out.shape[0], step):
            part = slice(at, at + step)
            value = jnp.dot(lhs_moved[part, :], act_moved[:, columns], preferred_element_type=F32)
            value += jnp.dot(lhs_kept[part, :], act_kept[...], preferred_element_type=F32)
            out[i : i + step, :] = value.astype(out.dtype)
            at += step


def near_kernel(count, meta, *refs):
    keeps, gots, (out, mine) = refs[:count], refs[count : 2 * count], refs[2 * count :]
    half = out.shape[0] // 2
    parts = [(k, g, at) for k, g in zip(keeps, gots) for at in range(0, k.shape[0], half)]
    keeps_even = (dp_at(meta) // 2 + tensor_at(meta)) % 2 == 0
    step = 2 * TILE

    for pair in range(2):
        (k0, g0, a0), (k1, g1, a1) = parts[2 * pair], parts[2 * pair + 1]

        def body(i, _):
            def rows(at):
                return pl.ds(pl.multiple_of(at + i * step, TILE), step)

            even = k0[rows(a0), :] + g0[rows(a0), :].astype(F32)
            odd = k1[rows(a1), :] + g1[rows(a1), :].astype(F32)
            out[rows(pair * half), :] = jnp.where(keeps_even, odd, even).astype(BF)
            mine[rows(pair * half), :] = jnp.where(keeps_even, even, odd)
            return 0

        lax.fori_loop(0, half // step, body, 0)


def far_kernel(meta, held, got, out, mine):
    half = out.shape[0]
    keeps_first = (dp_at(meta) // 4 + tensor_at(meta) // 2) % 2 == 0
    step = 2 * TILE

    def body(i, _):
        first = pl.ds(pl.multiple_of(i * step, TILE), step)
        second = pl.ds(pl.multiple_of(half + i * step, TILE), step)
        a = held[first, :] + got[first, :].astype(F32)
        b = held[second, :] + got[second, :].astype(F32)
        out[first, :] = jnp.where(keeps_first, b, a).astype(BF)
        mine[first, :] = jnp.where(keeps_first, a, b)
        return 0

    lax.fori_loop(0, half // step, body, 0)


def place_kernel(cuts, meta, kept, *rest):
    moved, out = rest[:-1], rest[-1]
    count = kept_total(meta, dp_at(meta))
    first = jnp.minimum(count - lax.rem(count, TILE), BAL - SEND)
    first = pl.multiple_of(first, TILE)
    wide = out.shape[1]
    step = pl.program_id(0)
    out[0:KEEP, :] = kept[:, pl.ds(pl.multiple_of(step * wide, wide), wide)]
    out[KEEP:, :] = jnp.zeros((out.shape[0] - KEEP, wide), BF)
    rows = lax.broadcasted_iota(jnp.int32, (SEND, 1), 0) + first
    window = pl.ds(first, SEND)
    for i, (part, c, _) in enumerate(cut_at(cuts, wide)):

        @pl.when(step == i)
        def _():
            out[window, :] = jnp.where(rows < count, out[window, :], moved[part][:, c : c + wide])


def swapped(block, axis, distance):
    n = lax.axis_size(axis)
    return lax.ppermute(block, axis, [(i, i ^ distance) for i in range(n)])


def after(value, *others):
    return lax.optimization_barrier((value, *others))[0]


def shards(hidden_pre, cotangent, down_weight, layer_scale, crop_lengths, crop_moves):
    hidden_pre, cotangent, down_weight, layer_scale = (
        pltpu.with_memory_space_constraint(x, pltpu.HBM)
        for x in (hidden_pre, cotangent, down_weight, layer_scale)
    )
    home, ff = hidden_pre.shape
    width = cotangent.shape[1]
    features = down_weight.shape[0]
    half = width // 2
    part = ff // 3
    n = lax.axis_size("dp")
    d = lax.axis_index("dp").astype(jnp.int32)
    t = lax.axis_index("tensor").astype(jnp.int32)
    column = lax.broadcasted_iota(jnp.int32, (1, n), 1)
    own = jnp.where(column == 0, d, jnp.where(column == 1, t, 0))
    meta = jnp.concatenate([crop_lengths.T, crop_moves.T, own])
    vmem = pltpu.VMEM
    sems = pltpu.SemaphoreType.DMA

    def gelu(meta, moved, base, columns):
        block = 256
        rows = SEND if moved else KEEP
        count = pl.cdiv(columns, block)
        return kernel_call(
            functools.partial(gelu_kernel, moved, base, block),
            [shape(rows, columns), shape(rows, columns, F32)],
            [IN_HBM], [IN_VMEM] * 2,
            [vmem((rows, home), BF), vmem((rows, block), F32), vmem((count, home, block), BF), sems((count,))],
        )(meta, hidden_pre)

    def weight_first(meta, act_moved, act_kept):
        return kernel_call(
            functools.partial(weight_kernel, 4),
            [shape(width, part)] * 2 + [shape(width, part, F32)] * 2
            + [shape(features, SEND), shape(features, KEEP)],
            [IN_VMEM] * 10, [IN_VMEM] * 6,
        )(meta, *moved, *kept, act_moved, act_kept)

    def weight_again(meta, base, act_moved, act_kept, count):
        rows = features // 2 // count
        return kernel_call(
            functools.partial(again_kernel, base),
            [shape(rows, part)] * count + [shape(rows, part, F32)] * count,
            [IN_VMEM] * 4, [IN_VMEM] * (2 * count),
        )(meta, *lhs, act_moved, act_kept)

    def grads(meta, pieces, base, slopes, cuts):
        rows, block = pieces[0].shape[0], 256
        count = sum(cuts) // block
        return kernel_call(
            functools.partial(grad_kernel, base, len(slopes), block),
            [shape(rows, c) for c in cuts],
            [IN_VMEM] * 4 + [IN_HBM] + [IN_VMEM] * len(slopes), [IN_VMEM] * len(cuts),
            [vmem((rows, features), BF), vmem((count, features, block), BF), sems((count,))],
        )(meta, *pieces, down_weight, *slopes)

    def near_step(meta, keeps, gots):
        count = len(keeps)
        return kernel_call(
            functools.partial(near_kernel, count),
            [shape(width, part), shape(width, part, F32)], [IN_VMEM] * (2 * count), [IN_VMEM] * 2,
        )(meta, *keeps, *gots)

    def far_step(meta, mine, got):
        return kernel_call(
            far_kernel, [shape(half, part), shape(half, part, F32)], [IN_VMEM] * 2, [IN_VMEM] * 2
        )(meta, mine, got)

    moved_0, kept_0 = kernel_call(
        first_kernel, [shape(SEND, width), shape(KEEP, width)], [IN_HBM] * 2, [IN_VMEM] * 2,
        [vmem((home, width), BF), vmem((features,), F32), sems((2,))],
    )(meta, cotangent, layer_scale)

    moved_1, moved_2 = swapped(moved_0, "tensor", 1), swapped(moved_0, "tensor", 2)
    kept_1, kept_2 = swapped(kept_0, "tensor", 1), swapped(kept_0, "tensor", 2)
    act_ma, der_ma = gelu(after(meta, moved_0), True, 0, part)
    moved_2 = after(moved_2, act_ma, moved_1, kept_1)
    moved_3 = swapped(moved_2, "tensor", 1)
    moved = (moved_0, moved_1, moved_2, moved_3)

    (moving_a,) = grads(after(meta, moved_2), moved, 0, (der_ma,), (part,))
    arrived_a = swapped(moving_a, "dp", n // 2)

    act_ka, der_ka = gelu(after(meta, moving_a), False, 0, part)
    kept_2 = after(kept_2, act_ka)
    kept_3 = swapped(kept_2, "tensor", 1)
    kept = (kept_0, kept_1, kept_2, kept_3)
    *sends_a, keep_01, keep_23, lhs_moved, lhs_kept = weight_first(after(meta, act_ka), act_ma, act_ka)
    lhs = (lhs_moved, lhs_kept)
    gots_a = [swapped(send, "dp", 1) for send in sends_a]

    act_m, der_m = gelu(after(meta, keep_01), True, part, 2 * part)
    moving_b, moving_c = grads(after(meta, act_m), moved, part, (der_m,), (part, part))
    act_kb, der_kb = gelu(after(meta, moving_b), False, part, part)
    send_b, keep_b = weight_again(after(meta, act_kb, arrived_a), 0, act_m, act_kb, 1)
    got_b = swapped(send_b, "dp", 1)
    arrived_b = swapped(after(moving_b, send_b), "dp", n // 2)

    out_na, mine_a = near_step(after(meta, send_b), (keep_01, keep_23), gots_a)
    got_na = swapped(out_na, "dp", 2)
    act_kc, der_kc = gelu(after(meta, out_na), False, 2 * part, part)
    *sends_c, keep_c01, keep_c23 = weight_again(after(meta, act_kc), part, act_m, act_kc, 2)
    gots_c = [swapped(send, "dp", 1) for send in sends_c]
    (kept_grad,) = grads(after(meta, keep_c01), kept, 0, (der_ka, der_kb, der_kc), (ff,))

    out_nb, mine_b = near_step(after(meta, kept_grad, arrived_b, got_na), (keep_b,), (got_b,))
    got_nb = swapped(out_nb, "dp", 2)
    arrived_c = swapped(after(moving_c, out_nb), "dp", n // 2)
    out_fa, own_a = far_step(after(meta, out_nb), mine_a, got_na)
    got_fa = swapped(out_fa, "dp", 4)
    out_nc, mine_c = near_step(after(meta, out_fa), (keep_c01, keep_c23), gots_c)
    got_nc = swapped(out_nc, "dp", 2)
    out_fb, own_b = far_step(after(meta, out_nc), mine_b, got_nb)
    got_fb = swapped(out_fb, "dp", 4)
    out_fc, own_c = far_step(after(meta, out_fb, got_fa, arrived_c), mine_c, got_nc)
    got_fc = swapped(out_fc, "dp", 4)
    total = [a + b.astype(F32) for a, b in ((own_a, got_fa), (own_b, got_fb), (own_c, got_fc))]
    down_grad = jnp.concatenate(total, axis=1) / math.sqrt(n * home)

    hidden_grad = kernel_call(
        functools.partial(place_kernel, (part,) * 3), shape(BAL, ff), [IN_VMEM] * 4,
        pl.BlockSpec((BAL, 256), lambda i, *_: (0, i)), grid=(ff // 256,),
    )(after(meta, out_fc), kept_grad, arrived_a, arrived_b, arrived_c)
    return (hidden_grad, down_grad)


def solution(mesh):
    pairs_and_fours = (mesh.shape["dp"], mesh.shape["tensor"]) == (8, 4)
    return jax.shard_map(
        shards if pairs_and_fours else general_shards,
        mesh=mesh,
        in_specs=(P("dp", "tensor"), P("dp", "tensor"), P(None, "tensor"), P(), P(), P()),
        out_specs=(P("dp", "tensor"), P("dp", "tensor")),
        check_vma=False,
    )


def shifted(block, axis, distance):
    devices = range(lax.axis_size(axis))
    route = [((i - distance) % len(devices), i) for i in devices]
    return lax.ppermute(block, axis, route)


def crop_rows(row_total, crop_sizes, crop_starts):
    crop_ends = jnp.cumsum(crop_sizes)
    crop_begins = crop_ends - crop_sizes
    target_rows = jnp.arange(row_total, dtype=jnp.int32)[:, None]
    inside_crop = (target_rows >= crop_begins[None, :]) & (target_rows < crop_ends[None, :])
    source_rows = jnp.sum(
        jnp.where(inside_crop, crop_starts[None, :] + target_rows - crop_begins[None, :], 0), axis=1
    )
    return (source_rows, jnp.any(inside_crop, axis=1))


def select_rows(row_block, source_rows, valid_rows):
    taken = jnp.take(row_block, source_rows, axis=0)
    return jnp.where(valid_rows[:, None], taken, jnp.zeros((), row_block.dtype))


def gelu_parts(pre_act):
    cumulative = 0.5 * (1.0 + jax.scipy.special.erf(pre_act * inv_root_two))
    activated = pre_act * cumulative
    derivative = cumulative + pre_act * jnp.exp(-0.5 * pre_act * pre_act) * inv_root_tau
    return (activated, derivative)


def local_grads(pre_rows, cot_part, live_rows, layer_scale, down_weight, home_rows):
    cot_full = lax.all_gather(cot_part, "tensor", axis=1, tiled=True)
    scaled = (cot_full.astype(F32) * layer_scale[None, :]).astype(BF)
    activated, derivative = gelu_parts(pre_rows.astype(F32))
    activation = jnp.where(live_rows[:, None], activated, 0.0).astype(BF)
    backward = jnp.dot(scaled, down_weight, preferred_element_type=F32) * derivative
    gradient_rows = jnp.where(live_rows[:, None], backward, 0.0).astype(BF)
    weight_grad = lax.psum_scatter(
        lax.dot_general(scaled, activation, (((0,), (0,)), ((), ())), preferred_element_type=F32),
        "dp",
        scatter_dimension=0,
        tiled=True,
    )
    return (gradient_rows, weight_grad / math.sqrt(lax.axis_size("dp") * home_rows))


def general_shards(hidden_pre, cotangent, down_weight, layer_scale, crop_lengths, crop_moves):
    devices = lax.axis_size("dp")
    half_axis = devices // 2
    device_index = lax.axis_index("dp")
    partner_index = (device_index + half_axis) % devices
    own_lengths = lax.dynamic_index_in_dim(crop_lengths, device_index, 0, keepdims=False)
    own_moves = lax.dynamic_index_in_dim(crop_moves, device_index, 0, keepdims=False)
    partner_lengths = lax.dynamic_index_in_dim(crop_lengths, partner_index, 0, keepdims=False)
    partner_moves = lax.dynamic_index_in_dim(crop_moves, partner_index, 0, keepdims=False)
    home_rows = hidden_pre.shape[0]
    own_starts = jnp.cumsum(own_lengths) - own_lengths
    sent_sizes = own_lengths * own_moves
    kept_sizes = own_lengths * (1 - own_moves)
    arrived = jnp.sum(partner_lengths * partner_moves)
    send_source, send_valid = crop_rows(SEND, sent_sizes, own_starts)
    keep_sizes = jnp.concatenate([kept_sizes, arrived[None]])
    keep_starts = jnp.concatenate([own_starts, jnp.full((1,), home_rows, jnp.int32)])
    keep_source, keep_valid = crop_rows(BAL, keep_sizes, keep_starts)
    live_home = jnp.arange(home_rows, dtype=jnp.int32) < jnp.sum(own_lengths)
    gradient_rows, weight_grad = local_grads(
        hidden_pre, cotangent, live_home, layer_scale, down_weight, home_rows
    )
    outgoing = select_rows(gradient_rows, send_source, send_valid)
    incoming = shifted(outgoing, "dp", half_axis)
    balanced = select_rows(jnp.concatenate([gradient_rows, incoming], 0), keep_source, keep_valid)
    return (balanced, weight_grad)
```

```python
import functools
import math

import jax
import jax.numpy as jnp
from jax import lax
from jax.experimental import pallas as pl
from jax.experimental.pallas import tpu as pltpu
from jax.sharding import PartitionSpec as P

SEND = 528
KEEP = 528
TILE = 16
EARLY = 48
LATE = SEND - EARLY
SLOTS = 4
BAL = 720
BF = jnp.bfloat16
F32 = jnp.float32

inv_root_two = 0.7071067811865476
inv_root_tau = 0.3989422804014327


def kernel_call(kernel, out_shape, in_specs, out_specs, scratch=(), grid=(1,)):
    return pl.pallas_call(
        kernel,
        grid_spec=pltpu.PrefetchScalarGridSpec(
            num_scalar_prefetch=1,
            grid=grid,
            in_specs=in_specs,
            out_specs=out_specs,
            scratch_shapes=list(scratch),
        ),
        out_shape=out_shape,
        cost_estimate=pl.CostEstimate(flops=1, bytes_accessed=1, transcendentals=0),
        compiler_params=pltpu.CompilerParams(vmem_limit_bytes=16 * 1024 * 1024),
    )


IN_VMEM = pl.BlockSpec(memory_space=pltpu.VMEM)
IN_HBM = pl.BlockSpec(memory_space=pltpu.HBM)


def shape(a, b, dtype=BF):
    return jax.ShapeDtypeStruct((a, b), dtype)


def lengths_of(meta, d):
    return [meta[j, d] for j in range(SLOTS)]


def moves_of(meta, d):
    return [meta[SLOTS + j, d] for j in range(SLOTS)]


def dp_at(meta):
    return meta[2 * SLOTS, 0]


def tensor_at(meta):
    return meta[2 * SLOTS, 1]


def kept_total(meta, d):
    return sum(a * (1 - b) for a, b in zip(lengths_of(meta, d), moves_of(meta, d)))


def picks(meta, moved, first, rows, home):
    d = dp_at(meta)
    at = lax.broadcasted_iota(jnp.int32, (rows, 1), 0) - first
    source = jnp.full((rows, 1), -1, jnp.int32)
    begin = jnp.int32(0)
    start = jnp.int32(0)
    for length, move in zip(lengths_of(meta, d), moves_of(meta, d)):
        size = length * (move if moved else 1 - move)
        inside = (at >= begin) & (at < begin + size)
        source = jnp.where(inside, at + (start - begin), source)
        begin = begin + size
        start = start + length
    columns = lax.broadcasted_iota(jnp.int32, (rows, home), 1)
    return jnp.where(columns == source, 1.0, 0.0).astype(BF)


def sent_first(meta):
    n = meta.shape[1]
    partner = lax.rem(dp_at(meta) + n // 2, n)
    return lax.rem(kept_total(meta, partner), TILE)


def early_picks(meta, home):
    return picks(meta, True, sent_first(meta), EARLY, home)


def late_picks(meta, home):
    return picks(meta, True, sent_first(meta) - EARLY, LATE, home)


def kept_picks(meta, home):
    return picks(meta, False, 0, KEEP, home)


def scaled_rows(meta, pick, cot, scale):
    width = cot.shape[1]
    rows = jnp.dot(pick, cot[...], preferred_element_type=F32)
    own = scale[pl.ds(pl.multiple_of(tensor_at(meta) * width, 128), width)]
    return (rows * own[None, :]).astype(BF)


def first_kernel(
    meta, cot_hbm, scale_hbm, pre_hbm, late_out, rest_out, early_out, late_pick, rest_pick, pre, cot, scale, sems
):
    home, width = cot.shape
    pairs = ((cot_hbm, cot), (scale_hbm, scale), (pre_hbm, pre))
    copies = [pltpu.make_async_copy(a, b, sems.at[i]) for i, (a, b) in enumerate(pairs)]
    for copy in copies:
        copy.start()
    early = early_picks(meta, home)
    late = late_picks(meta, home)
    kept = kept_picks(meta, home)
    late_pick[...] = late
    rest_pick[0:EARLY, :] = early
    rest_pick[EARLY:, :] = kept
    copies[0].wait()
    copies[1].wait()
    early_rows = scaled_rows(meta, early, cot, scale)
    early_out[:, :width] = early_rows
    late_out[...] = scaled_rows(meta, late, cot, scale)
    rest_out[0:EARLY, :] = early_rows
    rest_out[EARLY:, :] = scaled_rows(meta, kept, cot, scale)
    copies[2].wait()
    early_out[:, width:] = jnp.dot(early, pre[...], preferred_element_type=F32).astype(BF)


def gelu_and_slope(x):
    cumulative = 0.5 * (1.0 + lax.erf(x * inv_root_two))
    return x * cumulative, cumulative + x * jnp.exp(-0.5 * x * x) * inv_root_tau


def cut_at(widths, block):
    return [
        (i, c, min(block, width - c)) for i, width in enumerate(widths) for c in range(0, width, block)
    ]


def gelu_kernel(base, block, meta, pick, pre, act_out, der_out, rows_f32):
    rows = pick.shape[0]
    step = next(TILE * k for k in (3, 4, 2, 1) if rows % (TILE * k) == 0)
    for at in range(0, act_out.shape[1], block):
        source = slice(base + at, base + at + block)
        rows_f32[...] = jnp.dot(pick[...], pre[:, source], preferred_element_type=F32)
        columns = slice(at, at + block)

        def body(k, _):
            part = pl.ds(pl.multiple_of(k * step, step), step)
            value, slope = gelu_and_slope(rows_f32[part, :])
            act_out[part, columns] = value.astype(BF)
            der_out[part, columns] = slope
            return 0

        lax.fori_loop(0, rows // step, body, 0)


def assemble(meta, pieces, first_row, lhs):
    rows = lhs.shape[0]
    width = pieces[1].shape[1]
    for j, piece in enumerate(pieces):
        columns = pl.ds(pl.multiple_of((tensor_at(meta) ^ j) * width, 128), width)
        lhs[:, columns] = piece[first_row : first_row + rows, 0:width]


def grad_kernel(first_row, first_slope, base, slope_count, block, meta, p0, p1, p2, p3, weight, *rest):
    slopes, outs, lhs = rest[:slope_count], rest[slope_count:-1], rest[-1]
    rows = lhs.shape[0]
    assemble(meta, (p0, p1, p2, p3), first_row, lhs)
    parts = slopes if slope_count > len(outs) else outs
    starts = [sum(part.shape[1] for part in parts[:i]) for i in range(len(parts))]
    slope_rows = slice(first_slope, first_slope + rows)
    for i, c, wide in cut_at([part.shape[1] for part in parts], block):
        at = starts[i] + c
        inside, whole_at = slice(c, c + wide), slice(at, at + wide)
        slope = slopes[i][slope_rows, inside] if slope_count == len(parts) else slopes[0][slope_rows, whole_at]
        columns = slice(base + at, base + at + wide)
        value = (jnp.dot(lhs[...], weight[:, columns], preferred_element_type=F32) * slope).astype(BF)
        if len(outs) == len(parts):
            outs[i][:, inside] = value
        else:
            outs[0][:, whole_at] = value


def early_kernel(block, meta, own, p1, p2, p3, weight, out, lhs, acc):
    width = p1.shape[1]
    assemble(meta, (own, p1, p2, p3), 0, lhs)
    for at in range(0, out.shape[1], block):
        columns = slice(at, at + block)
        acc[...] = jnp.dot(lhs[...], weight[:, columns], preferred_element_type=F32)

        def body(k, _):
            rows = pl.ds(pl.multiple_of(k * TILE, TILE), TILE)
            _, slope = gelu_and_slope(own[rows, width + at : width + at + block].astype(F32))
            out[rows, columns] = (acc[rows, :] * slope).astype(BF)
            return 0

        lax.fori_loop(0, EARLY // TILE, body, 0)


def weight_kernel(count, meta, *refs):
    moved, kept = refs[:count], refs[count : 2 * count]
    act_moved, act_kept, *outs, lhs_moved, lhs_kept = refs[2 * count :]
    half = moved[0].shape[1] // 2
    mine = dp_at(meta) % 2 == 0
    for i in range(count):
        for piece, lhs in ((moved[i], lhs_moved), (kept[i], lhs_kept)):
            both = piece[...].T
            lo, hi = both[:half], both[half:]
            lhs[i * half : (i + 1) * half, :] = jnp.where(mine, hi, lo)
            lhs[(count + i) * half : (count + i + 1) * half, :] = jnp.where(mine, lo, hi)
    again_kernel(0, meta, lhs_moved, lhs_kept, act_moved, act_kept, *outs)


def again_kernel(base, meta, lhs_moved, lhs_kept, act_moved, act_kept, *outs):
    columns = slice(base, base + act_kept.shape[1])
    step = lhs_moved.shape[0] // 4
    at = 0
    for out in outs:
        for i in range(0, out.shape[0], step):
            part = slice(at, at + step)
            value = jnp.dot(lhs_moved[part, :], act_moved[:, columns], preferred_element_type=F32)
            value += jnp.dot(lhs_kept[part, :], act_kept[...], preferred_element_type=F32)
            out[i : i + step, :] = value.astype(out.dtype)
            at += step


def near_kernel(count, meta, *refs):
    keeps, gots, (out, mine) = refs[:count], refs[count : 2 * count], refs[2 * count :]
    half = out.shape[0] // 2
    parts = [(k, g, at) for k, g in zip(keeps, gots) for at in range(0, k.shape[0], half)]
    keeps_even = (dp_at(meta) // 2 + tensor_at(meta)) % 2 == 0
    step = 2 * TILE

    for pair in range(2):
        (k0, g0, a0), (k1, g1, a1) = parts[2 * pair], parts[2 * pair + 1]

        def body(i, _):
            def rows(at):
                return pl.ds(pl.multiple_of(at + i * step, TILE), step)

            even = k0[rows(a0), :] + g0[rows(a0), :].astype(F32)
            odd = k1[rows(a1), :] + g1[rows(a1), :].astype(F32)
            out[rows(pair * half), :] = jnp.where(keeps_even, odd, even).astype(BF)
            mine[rows(pair * half), :] = jnp.where(keeps_even, even, odd)
            return 0

        lax.fori_loop(0, half // step, body, 0)


def far_kernel(meta, held, got, out, mine):
    half = out.shape[0]
    keeps_first = (dp_at(meta) // 4 + tensor_at(meta) // 2) % 2 == 0
    step = 2 * TILE

    def body(i, _):
        first = pl.ds(pl.multiple_of(i * step, TILE), step)
        second = pl.ds(pl.multiple_of(half + i * step, TILE), step)
        a = held[first, :] + got[first, :].astype(F32)
        b = held[second, :] + got[second, :].astype(F32)
        out[first, :] = jnp.where(keeps_first, b, a).astype(BF)
        mine[first, :] = jnp.where(keeps_first, a, b)
        return 0

    lax.fori_loop(0, half // step, body, 0)


def place_kernel(cuts, meta, kept, early, *rest):
    lates, out = rest[:-1], rest[-1]
    count = kept_total(meta, dp_at(meta))
    first = jnp.minimum(count - lax.rem(count, TILE), BAL - SEND)
    first = pl.multiple_of(first, TILE)
    wide = out.shape[1]
    step = pl.program_id(0)
    columns = pl.ds(pl.multiple_of(step * wide, wide), wide)
    out[0:KEEP, :] = kept[:, columns]
    out[KEEP:, :] = jnp.zeros((out.shape[0] - KEEP, wide), BF)

    def put(block, at):
        rows = lax.broadcasted_iota(jnp.int32, (block.shape[0], 1), 0) + at
        window = pl.ds(at, block.shape[0])
        out[window, :] = jnp.where(rows < count, out[window, :], block)

    put(early[:, columns], first)
    sources = [(late, c) for late, cut in zip(lates, cuts) for c in range(0, cut, wide)]
    for i, (late, c) in enumerate(sources):

        @pl.when(step == i)
        def _():
            put(late[:, c : c + wide], pl.multiple_of(first + EARLY, TILE))


def swapped(block, axis, distance):
    n = lax.axis_size(axis)
    return lax.ppermute(block, axis, [(i, i ^ distance) for i in range(n)])


def after(value, *others):
    return lax.optimization_barrier((value, *others))[0]


def shards(hidden_pre, cotangent, down_weight, layer_scale, crop_lengths, crop_moves):
    hidden_pre, cotangent, layer_scale = (
        pltpu.with_memory_space_constraint(x, pltpu.HBM) for x in (hidden_pre, cotangent, layer_scale)
    )
    home, ff = hidden_pre.shape
    width = cotangent.shape[1]
    features = down_weight.shape[0]
    half = width // 2
    part = ff // 3
    others = EARLY + KEEP
    n = lax.axis_size("dp")
    d = lax.axis_index("dp").astype(jnp.int32)
    t = lax.axis_index("tensor").astype(jnp.int32)
    column = lax.broadcasted_iota(jnp.int32, (1, n), 1)
    own = jnp.where(column == 0, d, jnp.where(column == 1, t, 0))
    meta = jnp.concatenate([crop_lengths.T, crop_moves.T, own])
    vmem = pltpu.VMEM
    sems = pltpu.SemaphoreType.DMA

    def gelu(meta, pick, base, columns):
        rows, block = pick.shape[0], 256
        return kernel_call(
            functools.partial(gelu_kernel, base, block),
            [shape(rows, columns), shape(rows, columns, F32)],
            [IN_VMEM] * 2, [IN_VMEM] * 2, [vmem((rows, block), F32)],
        )(meta, pick, pre)

    def weight_first(meta, act_moved, act_kept):
        return kernel_call(
            functools.partial(weight_kernel, 4),
            [shape(width, part)] * 2 + [shape(width, part, F32)] * 2
            + [shape(features, LATE), shape(features, others)],
            [IN_VMEM] * 10, [IN_VMEM] * 6,
        )(meta, *lates, *rests, act_moved, act_kept)

    def weight_again(meta, base, act_moved, act_kept, count):
        rows = features // 2 // count
        return kernel_call(
            functools.partial(again_kernel, base),
            [shape(rows, part)] * count + [shape(rows, part, F32)] * count,
            [IN_VMEM] * 4, [IN_VMEM] * (2 * count),
        )(meta, *lhs, act_moved, act_kept)

    def grads(meta, pieces, first_row, first_slope, rows, base, slopes, cuts):
        return kernel_call(
            functools.partial(grad_kernel, first_row, first_slope, base, len(slopes), 256),
            [shape(rows, c) for c in cuts], [IN_VMEM] * (5 + len(slopes)), [IN_VMEM] * len(cuts),
            [vmem((rows, features), BF)],
        )(meta, *pieces, down_weight, *slopes)

    def near_step(meta, keeps, gots):
        count = len(keeps)
        return kernel_call(
            functools.partial(near_kernel, count),
            [shape(width, part), shape(width, part, F32)], [IN_VMEM] * (2 * count), [IN_VMEM] * 2,
        )(meta, *keeps, *gots)

    def far_step(meta, mine, got):
        return kernel_call(
            far_kernel, [shape(half, part), shape(half, part, F32)], [IN_VMEM] * 2, [IN_VMEM] * 2
        )(meta, mine, got)

    late, rest, early, late_pick, rest_pick, pre = kernel_call(
        first_kernel,
        [shape(LATE, width), shape(others, width), shape(EARLY, width + ff),
         shape(LATE, home), shape(others, home), shape(home, ff)],
        [IN_HBM] * 3, [IN_VMEM] * 6,
        [vmem((home, width), BF), vmem((features,), F32), sems((3,))],
    )(meta, cotangent, layer_scale, hidden_pre)
    arrived_early = swapped(early, "dp", n // 2)

    late_c, late_y = swapped(late, "tensor", 1), swapped(late, "tensor", 2)
    rest_c, rest_y = swapped(rest, "tensor", 1), swapped(rest, "tensor", 2)
    act_la, der_la = gelu(after(meta, late), late_pick, 0, part)
    act_ra, der_ra = gelu(after(meta, act_la), rest_pick, 0, part)
    late_y = after(late_y, act_ra, late_c, rest_c, arrived_early)
    late_yc = swapped(late_y, "tensor", 1)
    lates = (late, late_c, late_y, late_yc)

    (moving_a,) = grads(after(meta, late_y), lates, 0, 0, LATE, 0, (der_la,), (part,))
    arrived_a = swapped(moving_a, "dp", n // 2)

    rest_y = after(rest_y, moving_a)
    rest_yc = swapped(rest_y, "tensor", 1)
    rests = (rest, rest_c, rest_y, rest_yc)
    *sends_a, keep_01, keep_23, lhs_moved, lhs_kept = weight_first(after(meta, moving_a), act_la, act_ra)
    lhs = (lhs_moved, lhs_kept)
    gots_a = [swapped(send, "dp", 1) for send in sends_a]

    act_l, der_l = gelu(after(meta, keep_01), late_pick, part, 2 * part)
    moving_b, moving_c = grads(after(meta, act_l), lates, 0, 0, LATE, part, (der_l,), (part, part))
    act_rb, der_rb = gelu(after(meta, moving_b), rest_pick, part, part)
    send_b, keep_b = weight_again(after(meta, act_rb, arrived_a), 0, act_l, act_rb, 1)
    got_b = swapped(send_b, "dp", 1)
    arrived_b = swapped(after(moving_b, send_b), "dp", n // 2)

    out_na, mine_a = near_step(after(meta, send_b), (keep_01, keep_23), gots_a)
    got_na = swapped(out_na, "dp", 2)
    early_sent = after(arrived_early[:, :width], out_na)
    early_c, early_y = swapped(early_sent, "tensor", 1), swapped(early_sent, "tensor", 2)
    act_rc, der_rc = gelu(after(meta, out_na), rest_pick, 2 * part, part)
    early_y = after(early_y, early_c, act_rc)
    early_yc = swapped(early_y, "tensor", 1)
    *sends_c, keep_c01, keep_c23 = weight_again(after(meta, early_yc), part, act_l, act_rc, 2)
    gots_c = [swapped(send, "dp", 1) for send in sends_c]

    (kept_grad,) = grads(after(meta, keep_c01), rests, EARLY, EARLY, KEEP, 0, (der_ra, der_rb, der_rc), (ff,))
    early_grad = kernel_call(
        functools.partial(early_kernel, 256), shape(EARLY, ff), [IN_VMEM] * 5, IN_VMEM,
        [vmem((EARLY, features), BF), vmem((EARLY, 256), F32)],
    )(after(meta, kept_grad), arrived_early, early_c, early_y, early_yc, down_weight)

    out_nb, mine_b = near_step(after(meta, early_grad, arrived_b, got_na), (keep_b,), (got_b,))
    got_nb = swapped(out_nb, "dp", 2)
    arrived_c = swapped(after(moving_c, out_nb), "dp", n // 2)
    out_fa, own_a = far_step(after(meta, out_nb), mine_a, got_na)
    got_fa = swapped(out_fa, "dp", 4)
    out_nc, mine_c = near_step(after(meta, out_fa), (keep_c01, keep_c23), gots_c)
    got_nc = swapped(out_nc, "dp", 2)
    out_fb, own_b = far_step(after(meta, out_nc), mine_b, got_nb)
    got_fb = swapped(out_fb, "dp", 4)
    out_fc, own_c = far_step(after(meta, out_fb, got_fa, arrived_c), mine_c, got_nc)
    got_fc = swapped(out_fc, "dp", 4)
    total = [a + b.astype(F32) for a, b in ((own_a, got_fa), (own_b, got_fb), (own_c, got_fc))]
    down_grad = jnp.concatenate(total, axis=1) / math.sqrt(n * home)

    hidden_grad = kernel_call(
        functools.partial(place_kernel, (part,) * 3), shape(BAL, ff), [IN_VMEM] * 5,
        pl.BlockSpec((BAL, 256), lambda i, *_: (0, i)), grid=(ff // 256,),
    )(after(meta, out_fc), kept_grad, early_grad, arrived_a, arrived_b, arrived_c)
    return (hidden_grad, down_grad)


def solution(mesh):
    pairs_and_fours = (mesh.shape["dp"], mesh.shape["tensor"]) == (8, 4)
    return jax.shard_map(
        shards if pairs_and_fours else general_shards,
        mesh=mesh,
        in_specs=(P("dp", "tensor"), P("dp", "tensor"), P(None, "tensor"), P(), P(), P()),
        out_specs=(P("dp", "tensor"), P("dp", "tensor")),
        check_vma=False,
    )


def shifted(block, axis, distance):
    devices = range(lax.axis_size(axis))
    route = [((i - distance) % len(devices), i) for i in devices]
    return lax.ppermute(block, axis, route)


def crop_rows(row_total, crop_sizes, crop_starts):
    crop_ends = jnp.cumsum(crop_sizes)
    crop_begins = crop_ends - crop_sizes
    target_rows = jnp.arange(row_total, dtype=jnp.int32)[:, None]
    inside_crop = (target_rows >= crop_begins[None, :]) & (target_rows < crop_ends[None, :])
    source_rows = jnp.sum(
        jnp.where(inside_crop, crop_starts[None, :] + target_rows - crop_begins[None, :], 0), axis=1
    )
    return (source_rows, jnp.any(inside_crop, axis=1))


def select_rows(row_block, source_rows, valid_rows):
    taken = jnp.take(row_block, source_rows, axis=0)
    return jnp.where(valid_rows[:, None], taken, jnp.zeros((), row_block.dtype))


def gelu_parts(pre_act):
    cumulative = 0.5 * (1.0 + jax.scipy.special.erf(pre_act * inv_root_two))
    activated = pre_act * cumulative
    derivative = cumulative + pre_act * jnp.exp(-0.5 * pre_act * pre_act) * inv_root_tau
    return (activated, derivative)


def local_grads(pre_rows, cot_part, live_rows, layer_scale, down_weight, home_rows):
    cot_full = lax.all_gather(cot_part, "tensor", axis=1, tiled=True)
    scaled = (cot_full.astype(F32) * layer_scale[None, :]).astype(BF)
    activated, derivative = gelu_parts(pre_rows.astype(F32))
    activation = jnp.where(live_rows[:, None], activated, 0.0).astype(BF)
    backward = jnp.dot(scaled, down_weight, preferred_element_type=F32) * derivative
    gradient_rows = jnp.where(live_rows[:, None], backward, 0.0).astype(BF)
    weight_grad = lax.psum_scatter(
        lax.dot_general(scaled, activation, (((0,), (0,)), ((), ())), preferred_element_type=F32),
        "dp",
        scatter_dimension=0,
        tiled=True,
    )
    return (gradient_rows, weight_grad / math.sqrt(lax.axis_size("dp") * home_rows))


def general_shards(hidden_pre, cotangent, down_weight, layer_scale, crop_lengths, crop_moves):
    devices = lax.axis_size("dp")
    half_axis = devices // 2
    device_index = lax.axis_index("dp")
    partner_index = (device_index + half_axis) % devices
    own_lengths = lax.dynamic_index_in_dim(crop_lengths, device_index, 0, keepdims=False)
    own_moves = lax.dynamic_index_in_dim(crop_moves, device_index, 0, keepdims=False)
    partner_lengths = lax.dynamic_index_in_dim(crop_lengths, partner_index, 0, keepdims=False)
    partner_moves = lax.dynamic_index_in_dim(crop_moves, partner_index, 0, keepdims=False)
    home_rows = hidden_pre.shape[0]
    own_starts = jnp.cumsum(own_lengths) - own_lengths
    sent_sizes = own_lengths * own_moves
    kept_sizes = own_lengths * (1 - own_moves)
    arrived = jnp.sum(partner_lengths * partner_moves)
    send_source, send_valid = crop_rows(SEND, sent_sizes, own_starts)
    keep_sizes = jnp.concatenate([kept_sizes, arrived[None]])
    keep_starts = jnp.concatenate([own_starts, jnp.full((1,), home_rows, jnp.int32)])
    keep_source, keep_valid = crop_rows(BAL, keep_sizes, keep_starts)
    live_home = jnp.arange(home_rows, dtype=jnp.int32) < jnp.sum(own_lengths)
    gradient_rows, weight_grad = local_grads(
        hidden_pre, cotangent, live_home, layer_scale, down_weight, home_rows
    )
    outgoing = select_rows(gradient_rows, send_source, send_valid)
    incoming = shifted(outgoing, "dp", half_axis)
    balanced = select_rows(jnp.concatenate([gradient_rows, incoming], 0), keep_source, keep_valid)
    return (balanced, weight_grad)
```

```python
import functools
import math

import jax
import jax.numpy as jnp
from jax import lax
from jax.experimental import pallas as pl
from jax.experimental.pallas import tpu as pltpu
from jax.sharding import PartitionSpec as P

SEND = 528
KEEP = 528
TILE = 16
EARLY = 48
LATE = SEND - EARLY
SLOTS = 4
BAL = 720
BF = jnp.bfloat16
F32 = jnp.float32

inv_root_two = 0.7071067811865476
inv_root_tau = 0.3989422804014327


def kernel_call(kernel, out_shape, in_specs, out_specs, scratch=(), grid=(1,)):
    return pl.pallas_call(
        kernel,
        grid_spec=pltpu.PrefetchScalarGridSpec(
            num_scalar_prefetch=1,
            grid=grid,
            in_specs=in_specs,
            out_specs=out_specs,
            scratch_shapes=list(scratch),
        ),
        out_shape=out_shape,
        cost_estimate=pl.CostEstimate(flops=1, bytes_accessed=1, transcendentals=0),
        compiler_params=pltpu.CompilerParams(vmem_limit_bytes=16 * 1024 * 1024),
    )


IN_VMEM = pl.BlockSpec(memory_space=pltpu.VMEM)
IN_HBM = pl.BlockSpec(memory_space=pltpu.HBM)


def shape(a, b, dtype=BF):
    return jax.ShapeDtypeStruct((a, b), dtype)


def lengths_of(meta, d):
    return [meta[j, d] for j in range(SLOTS)]


def moves_of(meta, d):
    return [meta[SLOTS + j, d] for j in range(SLOTS)]


def dp_at(meta):
    return meta[2 * SLOTS, 0]


def tensor_at(meta):
    return meta[2 * SLOTS, 1]


def kept_total(meta, d):
    return sum(a * (1 - b) for a, b in zip(lengths_of(meta, d), moves_of(meta, d)))


def picks(meta, moved, first, rows, home):
    d = dp_at(meta)
    at = lax.broadcasted_iota(jnp.int32, (rows, 1), 0) - first
    source = jnp.full((rows, 1), -1, jnp.int32)
    begin = jnp.int32(0)
    start = jnp.int32(0)
    for length, move in zip(lengths_of(meta, d), moves_of(meta, d)):
        size = length * (move if moved else 1 - move)
        inside = (at >= begin) & (at < begin + size)
        source = jnp.where(inside, at + (start - begin), source)
        begin = begin + size
        start = start + length
    columns = lax.broadcasted_iota(jnp.int32, (rows, home), 1)
    return jnp.where(columns == source, 1.0, 0.0).astype(BF)


def sent_first(meta):
    n = meta.shape[1]
    partner = lax.rem(dp_at(meta) + n // 2, n)
    return lax.rem(kept_total(meta, partner), TILE)


def early_picks(meta, home):
    return picks(meta, True, sent_first(meta), EARLY, home)


def late_picks(meta, home):
    return picks(meta, True, sent_first(meta) - EARLY, LATE, home)


def kept_picks(meta, home):
    return picks(meta, False, 0, KEEP, home)


def scaled_rows(meta, pick, cot, scale):
    width = cot.shape[1]
    rows = jnp.dot(pick, cot[...], preferred_element_type=F32)
    own = scale[pl.ds(pl.multiple_of(tensor_at(meta) * width, 128), width)]
    return (rows * own[None, :]).astype(BF)


def first_kernel(
    meta, cot_hbm, scale_hbm, pre_hbm, late_out, rest_out, early_out, late_pick, rest_pick, pre, cot, scale, sems
):
    home, width = cot.shape
    pairs = ((cot_hbm, cot), (scale_hbm, scale), (pre_hbm, pre))
    copies = [pltpu.make_async_copy(a, b, sems.at[i]) for i, (a, b) in enumerate(pairs)]
    for copy in copies:
        copy.start()
    early = early_picks(meta, home)
    late = late_picks(meta, home)
    kept = kept_picks(meta, home)
    late_pick[...] = late
    rest_pick[0:EARLY, :] = early
    rest_pick[EARLY:, :] = kept
    copies[0].wait()
    copies[1].wait()
    early_rows = scaled_rows(meta, early, cot, scale)
    early_out[:, :width] = early_rows
    late_out[...] = scaled_rows(meta, late, cot, scale)
    rest_out[0:EARLY, :] = early_rows
    rest_out[EARLY:, :] = scaled_rows(meta, kept, cot, scale)
    copies[2].wait()
    early_out[:, width:] = jnp.dot(early, pre[...], preferred_element_type=F32).astype(BF)


def gelu_and_slope(x):
    cumulative = 0.5 * (1.0 + lax.erf(x * inv_root_two))
    return x * cumulative, cumulative + x * jnp.exp(-0.5 * x * x) * inv_root_tau


def cut_at(widths, block):
    return [
        (i, c, min(block, width - c)) for i, width in enumerate(widths) for c in range(0, width, block)
    ]


def gelu_kernel(base, block, meta, pick, pre, act_out, der_out, rows_f32):
    rows = pick.shape[0]
    step = next(TILE * k for k in (3, 4, 2, 1) if rows % (TILE * k) == 0)
    for at in range(0, act_out.shape[1], block):
        source = slice(base + at, base + at + block)
        rows_f32[...] = jnp.dot(pick[...], pre[:, source], preferred_element_type=F32)
        columns = slice(at, at + block)

        def body(k, _):
            part = pl.ds(pl.multiple_of(k * step, step), step)
            value, slope = gelu_and_slope(rows_f32[part, :])
            act_out[part, columns] = value.astype(BF)
            der_out[part, columns] = slope
            return 0

        lax.fori_loop(0, rows // step, body, 0)


def assemble(meta, pieces, first_row, lhs):
    rows = lhs.shape[0]
    width = pieces[1].shape[1]
    for j, piece in enumerate(pieces):
        columns = pl.ds(pl.multiple_of((tensor_at(meta) ^ j) * width, 128), width)
        lhs[:, columns] = piece[first_row : first_row + rows, 0:width]


def grad_kernel(first_row, first_slope, base, slope_count, block, meta, p0, p1, p2, p3, weight, *rest):
    slopes, outs, lhs = rest[:slope_count], rest[slope_count:-1], rest[-1]
    rows = lhs.shape[0]
    assemble(meta, (p0, p1, p2, p3), first_row, lhs)
    parts = slopes if slope_count > len(outs) else outs
    starts = [sum(part.shape[1] for part in parts[:i]) for i in range(len(parts))]
    slope_rows = slice(first_slope, first_slope + rows)
    for i, c, wide in cut_at([part.shape[1] for part in parts], block):
        at = starts[i] + c
        inside, whole_at = slice(c, c + wide), slice(at, at + wide)
        slope = slopes[i][slope_rows, inside] if slope_count == len(parts) else slopes[0][slope_rows, whole_at]
        columns = slice(base + at, base + at + wide)
        value = (jnp.dot(lhs[...], weight[:, columns], preferred_element_type=F32) * slope).astype(BF)
        if len(outs) == len(parts):
            outs[i][:, inside] = value
        else:
            outs[0][:, whole_at] = value


def early_kernel(block, meta, own, p1, p2, p3, weight, out, lhs, acc):
    width = p1.shape[1]
    assemble(meta, (own, p1, p2, p3), 0, lhs)
    for at in range(0, out.shape[1], block):
        columns = slice(at, at + block)
        acc[...] = jnp.dot(lhs[...], weight[:, columns], preferred_element_type=F32)

        def body(k, _):
            rows = pl.ds(pl.multiple_of(k * TILE, TILE), TILE)
            _, slope = gelu_and_slope(own[rows, width + at : width + at + block].astype(F32))
            out[rows, columns] = (acc[rows, :] * slope).astype(BF)
            return 0

        lax.fori_loop(0, EARLY // TILE, body, 0)


def weight_kernel(count, meta, *refs):
    moved, kept = refs[:count], refs[count : 2 * count]
    act_moved, act_kept, *outs, lhs_moved, lhs_kept = refs[2 * count :]
    half = moved[0].shape[1] // 2
    mine = dp_at(meta) % 2 == 0
    for i in range(count):
        for piece, lhs in ((moved[i], lhs_moved), (kept[i], lhs_kept)):
            both = piece[...].T
            lo, hi = both[:half], both[half:]
            lhs[i * half : (i + 1) * half, :] = jnp.where(mine, hi, lo)
            lhs[(count + i) * half : (count + i + 1) * half, :] = jnp.where(mine, lo, hi)
    again_kernel(0, meta, lhs_moved, lhs_kept, act_moved, act_kept, *outs)


def again_kernel(base, meta, lhs_moved, lhs_kept, act_moved, act_kept, *outs):
    columns = slice(base, base + act_kept.shape[1])
    step = lhs_moved.shape[0] // 4
    at = 0
    for out in outs:
        for i in range(0, out.shape[0], step):
            part = slice(at, at + step)
            value = jnp.dot(lhs_moved[part, :], act_moved[:, columns], preferred_element_type=F32)
            value += jnp.dot(lhs_kept[part, :], act_kept[...], preferred_element_type=F32)
            out[i : i + step, :] = value.astype(out.dtype)
            at += step


def near_kernel(count, meta, *refs):
    keeps, gots, (out, mine) = refs[:count], refs[count : 2 * count], refs[2 * count :]
    half = out.shape[0] // 2
    parts = [(k, g, at) for k, g in zip(keeps, gots) for at in range(0, k.shape[0], half)]
    keeps_even = (dp_at(meta) // 2 + tensor_at(meta)) % 2 == 0
    step = 2 * TILE

    for pair in range(2):
        (k0, g0, a0), (k1, g1, a1) = parts[2 * pair], parts[2 * pair + 1]

        def body(i, _):
            def rows(at):
                return pl.ds(pl.multiple_of(at + i * step, TILE), step)

            even = k0[rows(a0), :] + g0[rows(a0), :].astype(F32)
            odd = k1[rows(a1), :] + g1[rows(a1), :].astype(F32)
            out[rows(pair * half), :] = jnp.where(keeps_even, odd, even).astype(BF)
            mine[rows(pair * half), :] = jnp.where(keeps_even, even, odd)
            return 0

        lax.fori_loop(0, half // step, body, 0)


def far_kernel(meta, held, got, out, mine):
    half = out.shape[0]
    keeps_first = (dp_at(meta) // 4 + tensor_at(meta) // 2) % 2 == 0
    step = 2 * TILE

    def body(i, _):
        first = pl.ds(pl.multiple_of(i * step, TILE), step)
        second = pl.ds(pl.multiple_of(half + i * step, TILE), step)
        a = held[first, :] + got[first, :].astype(F32)
        b = held[second, :] + got[second, :].astype(F32)
        out[first, :] = jnp.where(keeps_first, b, a).astype(BF)
        mine[first, :] = jnp.where(keeps_first, a, b)
        return 0

    lax.fori_loop(0, half // step, body, 0)


def place_kernel(cuts, meta, kept, early, *rest):
    lates, out = rest[:-1], rest[-1]
    count = kept_total(meta, dp_at(meta))
    first = jnp.minimum(count - lax.rem(count, TILE), BAL - SEND)
    first = pl.multiple_of(first, TILE)
    wide = out.shape[1]
    step = pl.program_id(0)
    columns = pl.ds(pl.multiple_of(step * wide, wide), wide)
    out[0:KEEP, :] = kept[:, columns]
    out[KEEP:, :] = jnp.zeros((out.shape[0] - KEEP, wide), BF)

    def put(block, at):
        rows = lax.broadcasted_iota(jnp.int32, (block.shape[0], 1), 0) + at
        window = pl.ds(at, block.shape[0])
        out[window, :] = jnp.where(rows < count, out[window, :], block)

    put(early[:, columns], first)
    sources = [(late, c) for late, cut in zip(lates, cuts) for c in range(0, cut, wide)]
    for i, (late, c) in enumerate(sources):

        @pl.when(step == i)
        def _():
            put(late[:, c : c + wide], pl.multiple_of(first + EARLY, TILE))


def swapped(block, axis, distance):
    n = lax.axis_size(axis)
    return lax.ppermute(block, axis, [(i, i ^ distance) for i in range(n)])


def after(value, *others):
    return lax.optimization_barrier((value, *others))[0]


def shards(hidden_pre, cotangent, down_weight, layer_scale, crop_lengths, crop_moves):
    hidden_pre, cotangent, layer_scale = (
        pltpu.with_memory_space_constraint(x, pltpu.HBM) for x in (hidden_pre, cotangent, layer_scale)
    )
    home, ff = hidden_pre.shape
    width = cotangent.shape[1]
    features = down_weight.shape[0]
    half = width // 2
    part = ff // 3
    others = EARLY + KEEP
    n = lax.axis_size("dp")
    d = lax.axis_index("dp").astype(jnp.int32)
    t = lax.axis_index("tensor").astype(jnp.int32)
    column = lax.broadcasted_iota(jnp.int32, (1, n), 1)
    own = jnp.where(column == 0, d, jnp.where(column == 1, t, 0))
    meta = jnp.concatenate([crop_lengths.T, crop_moves.T, own])
    vmem = pltpu.VMEM
    sems = pltpu.SemaphoreType.DMA

    def gelu(meta, pick, base, columns):
        rows, block = pick.shape[0], 256
        return kernel_call(
            functools.partial(gelu_kernel, base, block),
            [shape(rows, columns), shape(rows, columns, F32)],
            [IN_VMEM] * 2, [IN_VMEM] * 2, [vmem((rows, block), F32)],
        )(meta, pick, pre)

    def weight_first(meta, act_moved, act_kept):
        return kernel_call(
            functools.partial(weight_kernel, 4),
            [shape(width, part)] * 2 + [shape(width, part, F32)] * 2
            + [shape(features, LATE), shape(features, others)],
            [IN_VMEM] * 10, [IN_VMEM] * 6,
        )(meta, *lates, *rests, act_moved, act_kept)

    def weight_again(meta, base, act_moved, act_kept, count):
        rows = features // 2 // count
        return kernel_call(
            functools.partial(again_kernel, base),
            [shape(rows, part)] * count + [shape(rows, part, F32)] * count,
            [IN_VMEM] * 4, [IN_VMEM] * (2 * count),
        )(meta, *lhs, act_moved, act_kept)

    def grads(meta, pieces, first_row, first_slope, rows, base, slopes, cuts):
        return kernel_call(
            functools.partial(grad_kernel, first_row, first_slope, base, len(slopes), 256),
            [shape(rows, c) for c in cuts], [IN_VMEM] * (5 + len(slopes)), [IN_VMEM] * len(cuts),
            [vmem((rows, features), BF)],
        )(meta, *pieces, down_weight, *slopes)

    def near_step(meta, keeps, gots):
        count = len(keeps)
        return kernel_call(
            functools.partial(near_kernel, count),
            [shape(width, part), shape(width, part, F32)], [IN_VMEM] * (2 * count), [IN_VMEM] * 2,
        )(meta, *keeps, *gots)

    def far_step(meta, mine, got):
        return kernel_call(
            far_kernel, [shape(half, part), shape(half, part, F32)], [IN_VMEM] * 2, [IN_VMEM] * 2
        )(meta, mine, got)

    late, rest, early, late_pick, rest_pick, pre = kernel_call(
        first_kernel,
        [shape(LATE, width), shape(others, width), shape(EARLY, width + ff),
         shape(LATE, home), shape(others, home), shape(home, ff)],
        [IN_HBM] * 3, [IN_VMEM] * 6,
        [vmem((home, width), BF), vmem((features,), F32), sems((3,))],
    )(meta, cotangent, layer_scale, hidden_pre)
    arrived_early = swapped(early, "dp", n // 2)

    late_c, late_y = swapped(late, "tensor", 1), swapped(late, "tensor", 2)
    rest_c, rest_y = swapped(rest, "tensor", 1), swapped(rest, "tensor", 2)
    act_la, der_la = gelu(after(meta, late), late_pick, 0, part)
    act_ra, der_ra = gelu(after(meta, act_la), rest_pick, 0, part)
    late_y = after(late_y, act_ra, late_c, rest_c, arrived_early)
    late_yc = swapped(late_y, "tensor", 1)
    lates = (late, late_c, late_y, late_yc)

    (moving_a,) = grads(after(meta, late_y), lates, 0, 0, LATE, 0, (der_la,), (part,))
    arrived_a = swapped(moving_a, "dp", n // 2)

    rest_y = after(rest_y, moving_a)
    rest_yc = swapped(rest_y, "tensor", 1)
    rests = (rest, rest_c, rest_y, rest_yc)
    *sends_a, keep_01, keep_23, lhs_moved, lhs_kept = weight_first(after(meta, moving_a), act_la, act_ra)
    lhs = (lhs_moved, lhs_kept)
    gots_a = [swapped(send, "dp", 1) for send in sends_a]

    act_l, der_l = gelu(after(meta, keep_01), late_pick, part, 2 * part)
    moving_b, moving_c = grads(after(meta, act_l), lates, 0, 0, LATE, part, (der_l,), (part, part))
    act_rb, der_rb = gelu(after(meta, moving_b, gots_a[0]), rest_pick, part, part)
    send_b, keep_b = weight_again(after(meta, act_rb, arrived_a), 0, act_l, act_rb, 1)
    got_b = swapped(send_b, "dp", 1)
    arrived_b = swapped(after(moving_b, send_b), "dp", n // 2)

    out_na, mine_a = near_step(after(meta, send_b), (keep_01, keep_23), gots_a)
    got_na = swapped(out_na, "dp", 2)
    early_sent = after(arrived_early[:, :width], out_na)
    early_c, early_y = swapped(early_sent, "tensor", 1), swapped(early_sent, "tensor", 2)
    act_rc, der_rc = gelu(after(meta, out_na), rest_pick, 2 * part, part)
    early_y = after(early_y, early_c, act_rc)
    early_yc = swapped(early_y, "tensor", 1)
    *sends_c, keep_c01, keep_c23 = weight_again(after(meta, early_yc), part, act_l, act_rc, 2)
    gots_c = [swapped(send, "dp", 1) for send in sends_c]

    (kept_grad,) = grads(after(meta, keep_c01), rests, EARLY, EARLY, KEEP, 0, (der_ra, der_rb, der_rc), (ff,))
    early_grad = kernel_call(
        functools.partial(early_kernel, 256), shape(EARLY, ff), [IN_VMEM] * 5, IN_VMEM,
        [vmem((EARLY, features), BF), vmem((EARLY, 256), F32)],
    )(after(meta, kept_grad), arrived_early, early_c, early_y, early_yc, down_weight)

    out_nb, mine_b = near_step(after(meta, early_grad, arrived_b, got_na), (keep_b,), (got_b,))
    got_nb = swapped(out_nb, "dp", 2)
    arrived_c = swapped(after(moving_c, keep_c01), "dp", n // 2)
    out_fa, own_a = far_step(after(meta, out_nb), mine_a, got_na)
    got_fa = swapped(out_fa, "dp", 4)
    out_nc, mine_c = near_step(after(meta, out_fa), (keep_c01, keep_c23), gots_c)
    got_nc = swapped(out_nc, "dp", 2)
    out_fb, own_b = far_step(after(meta, out_nc, arrived_c), mine_b, got_nb)
    got_fb = swapped(out_fb, "dp", 4)
    out_fc, own_c = far_step(after(meta, out_fb, got_fa), mine_c, got_nc)
    got_fc = swapped(out_fc, "dp", 4)
    total = [a + b.astype(F32) for a, b in ((own_a, got_fa), (own_b, got_fb), (own_c, got_fc))]
    down_grad = jnp.concatenate(total, axis=1) / math.sqrt(n * home)

    hidden_grad = kernel_call(
        functools.partial(place_kernel, (part,) * 3), shape(BAL, ff), [IN_VMEM] * 5,
        pl.BlockSpec((BAL, 256), lambda i, *_: (0, i)), grid=(ff // 256,),
    )(after(meta, out_fc), kept_grad, early_grad, arrived_a, arrived_b, arrived_c)
    return (hidden_grad, down_grad)


def solution(mesh):
    pairs_and_fours = (mesh.shape["dp"], mesh.shape["tensor"]) == (8, 4)
    return jax.shard_map(
        shards if pairs_and_fours else general_shards,
        mesh=mesh,
        in_specs=(P("dp", "tensor"), P("dp", "tensor"), P(None, "tensor"), P(), P(), P()),
        out_specs=(P("dp", "tensor"), P("dp", "tensor")),
        check_vma=False,
    )


def shifted(block, axis, distance):
    devices = range(lax.axis_size(axis))
    route = [((i - distance) % len(devices), i) for i in devices]
    return lax.ppermute(block, axis, route)


def crop_rows(row_total, crop_sizes, crop_starts):
    crop_ends = jnp.cumsum(crop_sizes)
    crop_begins = crop_ends - crop_sizes
    target_rows = jnp.arange(row_total, dtype=jnp.int32)[:, None]
    inside_crop = (target_rows >= crop_begins[None, :]) & (target_rows < crop_ends[None, :])
    source_rows = jnp.sum(
        jnp.where(inside_crop, crop_starts[None, :] + target_rows - crop_begins[None, :], 0), axis=1
    )
    return (source_rows, jnp.any(inside_crop, axis=1))


def select_rows(row_block, source_rows, valid_rows):
    taken = jnp.take(row_block, source_rows, axis=0)
    return jnp.where(valid_rows[:, None], taken, jnp.zeros((), row_block.dtype))


def gelu_parts(pre_act):
    cumulative = 0.5 * (1.0 + jax.scipy.special.erf(pre_act * inv_root_two))
    activated = pre_act * cumulative
    derivative = cumulative + pre_act * jnp.exp(-0.5 * pre_act * pre_act) * inv_root_tau
    return (activated, derivative)


def local_grads(pre_rows, cot_part, live_rows, layer_scale, down_weight, home_rows):
    cot_full = lax.all_gather(cot_part, "tensor", axis=1, tiled=True)
    scaled = (cot_full.astype(F32) * layer_scale[None, :]).astype(BF)
    activated, derivative = gelu_parts(pre_rows.astype(F32))
    activation = jnp.where(live_rows[:, None], activated, 0.0).astype(BF)
    backward = jnp.dot(scaled, down_weight, preferred_element_type=F32) * derivative
    gradient_rows = jnp.where(live_rows[:, None], backward, 0.0).astype(BF)
    weight_grad = lax.psum_scatter(
        lax.dot_general(scaled, activation, (((0,), (0,)), ((), ())), preferred_element_type=F32),
        "dp",
        scatter_dimension=0,
        tiled=True,
    )
    return (gradient_rows, weight_grad / math.sqrt(lax.axis_size("dp") * home_rows))


def general_shards(hidden_pre, cotangent, down_weight, layer_scale, crop_lengths, crop_moves):
    devices = lax.axis_size("dp")
    half_axis = devices // 2
    device_index = lax.axis_index("dp")
    partner_index = (device_index + half_axis) % devices
    own_lengths = lax.dynamic_index_in_dim(crop_lengths, device_index, 0, keepdims=False)
    own_moves = lax.dynamic_index_in_dim(crop_moves, device_index, 0, keepdims=False)
    partner_lengths = lax.dynamic_index_in_dim(crop_lengths, partner_index, 0, keepdims=False)
    partner_moves = lax.dynamic_index_in_dim(crop_moves, partner_index, 0, keepdims=False)
    home_rows = hidden_pre.shape[0]
    own_starts = jnp.cumsum(own_lengths) - own_lengths
    sent_sizes = own_lengths * own_moves
    kept_sizes = own_lengths * (1 - own_moves)
    arrived = jnp.sum(partner_lengths * partner_moves)
    send_source, send_valid = crop_rows(SEND, sent_sizes, own_starts)
    keep_sizes = jnp.concatenate([kept_sizes, arrived[None]])
    keep_starts = jnp.concatenate([own_starts, jnp.full((1,), home_rows, jnp.int32)])
    keep_source, keep_valid = crop_rows(BAL, keep_sizes, keep_starts)
    live_home = jnp.arange(home_rows, dtype=jnp.int32) < jnp.sum(own_lengths)
    gradient_rows, weight_grad = local_grads(
        hidden_pre, cotangent, live_home, layer_scale, down_weight, home_rows
    )
    outgoing = select_rows(gradient_rows, send_source, send_valid)
    incoming = shifted(outgoing, "dp", half_axis)
    balanced = select_rows(jnp.concatenate([gradient_rows, incoming], 0), keep_source, keep_valid)
    return (balanced, weight_grad)
```

```python
import functools
import math

import jax
import jax.numpy as jnp
from jax import lax
from jax.experimental import pallas as pl
from jax.experimental.pallas import tpu as pltpu
from jax.sharding import PartitionSpec as P

SEND = 528
KEEP = 528
TILE = 16
SLOTS = 4
BAL = 720
BF = jnp.bfloat16
F32 = jnp.float32

inv_root_two = 0.7071067811865476
inv_root_tau = 0.3989422804014327


def kernel_call(kernel, out_shape, in_specs, out_specs, scratch=(), grid=(1,)):
    return pl.pallas_call(
        kernel,
        grid_spec=pltpu.PrefetchScalarGridSpec(
            num_scalar_prefetch=1,
            grid=grid,
            in_specs=in_specs,
            out_specs=out_specs,
            scratch_shapes=list(scratch),
        ),
        out_shape=out_shape,
        cost_estimate=pl.CostEstimate(flops=1, bytes_accessed=1, transcendentals=0),
        compiler_params=pltpu.CompilerParams(vmem_limit_bytes=16 * 1024 * 1024),
    )


IN_VMEM = pl.BlockSpec(memory_space=pltpu.VMEM)
IN_HBM = pl.BlockSpec(memory_space=pltpu.HBM)


def shape(a, b, dtype=BF):
    return jax.ShapeDtypeStruct((a, b), dtype)


def lengths_of(meta, d):
    return [meta[j, d] for j in range(SLOTS)]


def moves_of(meta, d):
    return [meta[SLOTS + j, d] for j in range(SLOTS)]


def dp_at(meta):
    return meta[2 * SLOTS, 0]


def tensor_at(meta):
    return meta[2 * SLOTS, 1]


def kept_total(meta, d):
    return sum(a * (1 - b) for a, b in zip(lengths_of(meta, d), moves_of(meta, d)))


def picks(meta, moved, first, rows, home):
    d = dp_at(meta)
    at = lax.broadcasted_iota(jnp.int32, (rows, 1), 0) - first
    source = jnp.full((rows, 1), -1, jnp.int32)
    begin = jnp.int32(0)
    start = jnp.int32(0)
    for length, move in zip(lengths_of(meta, d), moves_of(meta, d)):
        size = length * (move if moved else 1 - move)
        inside = (at >= begin) & (at < begin + size)
        source = jnp.where(inside, at + (start - begin), source)
        begin = begin + size
        start = start + length
    columns = lax.broadcasted_iota(jnp.int32, (rows, home), 1)
    return jnp.where(columns == source, 1.0, 0.0).astype(BF)


def moved_picks(meta, home):
    n = meta.shape[1]
    partner = lax.rem(dp_at(meta) + n // 2, n)
    return picks(meta, True, lax.rem(kept_total(meta, partner), TILE), SEND, home)


def kept_picks(meta, home):
    return picks(meta, False, 0, KEEP, home)


def scaled_rows(meta, pick, cot, scale):
    width = cot.shape[1]
    rows = jnp.dot(pick, cot[...], preferred_element_type=F32)
    own = scale[pl.ds(pl.multiple_of(tensor_at(meta) * width, 128), width)]
    return (rows * own[None, :]).astype(BF)


def first_kernel(
    meta, cot_hbm, scale_hbm, pre_hbm, moved_out, kept_out, moved_pick, kept_pick, pre, cot, scale, sems
):
    home = cot.shape[0]
    pairs = ((cot_hbm, cot), (scale_hbm, scale), (pre_hbm, pre))
    copies = [pltpu.make_async_copy(a, b, sems.at[i]) for i, (a, b) in enumerate(pairs)]
    for copy in copies:
        copy.start()
    moved = moved_picks(meta, home)
    kept = kept_picks(meta, home)
    moved_pick[...] = moved
    kept_pick[...] = kept
    copies[0].wait()
    copies[1].wait()
    moved_out[...] = scaled_rows(meta, moved, cot, scale)
    kept_out[...] = scaled_rows(meta, kept, cot, scale)
    copies[2].wait()


def gelu_and_slope(x):
    cumulative = 0.5 * (1.0 + lax.erf(x * inv_root_two))
    return x * cumulative, cumulative + x * jnp.exp(-0.5 * x * x) * inv_root_tau


def cut_at(widths, block):
    return [
        (i, c, min(block, width - c)) for i, width in enumerate(widths) for c in range(0, width, block)
    ]


def gelu_kernel(base, block, meta, pick, pre, act_out, der_out, rows_f32):
    rows = pick.shape[0]
    step = next(TILE * k for k in (3, 4, 2, 1) if rows % (TILE * k) == 0)
    for at in range(0, act_out.shape[1], block):
        source = slice(base + at, base + at + block)
        rows_f32[...] = jnp.dot(pick[...], pre[:, source], preferred_element_type=F32)
        columns = slice(at, at + block)

        def body(k, _):
            part = pl.ds(pl.multiple_of(k * step, step), step)
            value, slope = gelu_and_slope(rows_f32[part, :])
            act_out[part, columns] = value.astype(BF)
            der_out[part, columns] = slope
            return 0

        lax.fori_loop(0, rows // step, body, 0)


def grad_kernel(slope_count, block, meta, p0, p1, p2, p3, weight, *rest):
    slopes, (out, lhs) = rest[:slope_count], rest[slope_count:]
    width = p0.shape[1]
    for j, piece in enumerate((p0, p1, p2, p3)):
        lhs[:, pl.ds(pl.multiple_of((tensor_at(meta) ^ j) * width, 128), width)] = piece[...]
    at = 0
    for i, c, wide in cut_at([slope.shape[1] for slope in slopes], block):
        columns = slice(at, at + wide)
        value = jnp.dot(lhs[...], weight[:, columns], preferred_element_type=F32)
        out[:, columns] = (value * slopes[i][:, c : c + wide]).astype(BF)
        at += wide


def weight_kernel(count, meta, *refs):
    moved, kept = refs[:count], refs[count : 2 * count]
    act_moved, act_kept, *outs, lhs_moved, lhs_kept = refs[2 * count :]
    half = moved[0].shape[1] // 2
    mine = dp_at(meta) % 2 == 0
    for i in range(count):
        for piece, lhs in ((moved[i], lhs_moved), (kept[i], lhs_kept)):
            both = piece[...].T
            lo, hi = both[:half], both[half:]
            lhs[i * half : (i + 1) * half, :] = jnp.where(mine, hi, lo)
            lhs[(count + i) * half : (count + i + 1) * half, :] = jnp.where(mine, lo, hi)
    again_kernel(0, meta, lhs_moved, lhs_kept, act_moved, act_kept, *outs)


def again_kernel(base, meta, lhs_moved, lhs_kept, act_moved, act_kept, *outs):
    columns = slice(base, base + act_kept.shape[1])
    step = lhs_moved.shape[0] // 4
    at = 0
    for out in outs:
        for i in range(0, out.shape[0], step):
            part = slice(at, at + step)
            value = jnp.dot(lhs_moved[part, :], act_moved[:, columns], preferred_element_type=F32)
            value += jnp.dot(lhs_kept[part, :], act_kept[...], preferred_element_type=F32)
            out[i : i + step, :] = value.astype(out.dtype)
            at += step


def near_kernel(count, meta, *refs):
    keeps, gots, (out, mine) = refs[:count], refs[count : 2 * count], refs[2 * count :]
    half = out.shape[0] // 2
    parts = [(k, g, at) for k, g in zip(keeps, gots) for at in range(0, k.shape[0], half)]
    keeps_even = (dp_at(meta) // 2 + tensor_at(meta)) % 2 == 0
    step = 2 * TILE

    for pair in range(2):
        (k0, g0, a0), (k1, g1, a1) = parts[2 * pair], parts[2 * pair + 1]

        def body(i, _):
            def rows(at):
                return pl.ds(pl.multiple_of(at + i * step, TILE), step)

            even = k0[rows(a0), :] + g0[rows(a0), :].astype(F32)
            odd = k1[rows(a1), :] + g1[rows(a1), :].astype(F32)
            out[rows(pair * half), :] = jnp.where(keeps_even, odd, even).astype(BF)
            mine[rows(pair * half), :] = jnp.where(keeps_even, even, odd)
            return 0

        lax.fori_loop(0, half // step, body, 0)


def far_kernel(meta, held, got, out, mine):
    half = out.shape[0]
    keeps_first = (dp_at(meta) // 4 + tensor_at(meta) // 2) % 2 == 0
    step = 2 * TILE

    def body(i, _):
        first = pl.ds(pl.multiple_of(i * step, TILE), step)
        second = pl.ds(pl.multiple_of(half + i * step, TILE), step)
        a = held[first, :] + got[first, :].astype(F32)
        b = held[second, :] + got[second, :].astype(F32)
        out[first, :] = jnp.where(keeps_first, b, a).astype(BF)
        mine[first, :] = jnp.where(keeps_first, a, b)
        return 0

    lax.fori_loop(0, half // step, body, 0)


def place_kernel(meta, kept, inner, *rest):
    outer, out = rest[:-1], rest[-1]
    d = dp_at(meta)
    count = kept_total(meta, d)
    first = jnp.minimum(count - lax.rem(count, TILE), BAL - SEND)
    first = pl.multiple_of(first, TILE)
    wide = out.shape[1]
    step = pl.program_id(0)
    columns = pl.ds(pl.multiple_of(step * wide, wide), wide)
    out[0:KEEP, :] = kept[:, columns]
    out[KEEP:, :] = jnp.zeros((out.shape[0] - KEEP, wide), BF)
    rows = lax.broadcasted_iota(jnp.int32, (SEND, 1), 0) + first
    window = pl.ds(first, SEND)
    is_inner = (d // 2 == 1) | (d // 2 == 2)
    for i, (part, c, _) in enumerate(cut_at([x.shape[1] for x in outer], wide)):

        @pl.when(step == i)
        def _():
            block = jnp.where(is_inner, inner[:, columns], outer[part][:, c : c + wide])
            out[window, :] = jnp.where(rows < count, out[window, :], block)


def swapped(block, axis, distance):
    n = lax.axis_size(axis)
    return lax.ppermute(block, axis, [(i, i ^ distance) for i in range(n)])


def routed(block, pairs):
    return lax.ppermute(block, "dp", [(2 * a + x, 2 * b + x) for a, b in pairs for x in range(2)])


def after(value, *others):
    return lax.optimization_barrier((value, *others))[0]


def shards(hidden_pre, cotangent, down_weight, layer_scale, crop_lengths, crop_moves):
    hidden_pre, cotangent, layer_scale = (
        pltpu.with_memory_space_constraint(x, pltpu.HBM) for x in (hidden_pre, cotangent, layer_scale)
    )
    home, ff = hidden_pre.shape
    width = cotangent.shape[1]
    features = down_weight.shape[0]
    half = width // 2
    part = ff // 3
    n = lax.axis_size("dp")
    d = lax.axis_index("dp").astype(jnp.int32)
    t = lax.axis_index("tensor").astype(jnp.int32)
    column = lax.broadcasted_iota(jnp.int32, (1, n), 1)
    own = jnp.where(column == 0, d, jnp.where(column == 1, t, 0))
    meta = jnp.concatenate([crop_lengths.T, crop_moves.T, own])
    vmem = pltpu.VMEM
    sems = pltpu.SemaphoreType.DMA

    def gelu(meta, pick, base, columns):
        rows, block = pick.shape[0], 256
        return kernel_call(
            functools.partial(gelu_kernel, base, block),
            [shape(rows, columns), shape(rows, columns, F32)],
            [IN_VMEM] * 2, [IN_VMEM] * 2, [vmem((rows, block), F32)],
        )(meta, pick, pre)

    def weight_first(meta, act_moved, act_kept):
        return kernel_call(
            functools.partial(weight_kernel, 4),
            [shape(features // 2, part), shape(features // 2, part, F32)]
            + [shape(features, SEND), shape(features, KEEP)],
            [IN_VMEM] * 10, [IN_VMEM] * 4,
        )(meta, *moved, *kept, act_moved, act_kept)

    def weight_again(meta, base, act_moved, act_kept):
        return kernel_call(
            functools.partial(again_kernel, base),
            [shape(features // 2, part), shape(features // 2, part, F32)], [IN_VMEM] * 4, [IN_VMEM] * 2,
        )(meta, *lhs, act_moved, act_kept)

    def grads(meta, pieces, slopes):
        rows = pieces[0].shape[0]
        return kernel_call(
            functools.partial(grad_kernel, len(slopes), 256), shape(rows, ff),
            [IN_VMEM] * (5 + len(slopes)), IN_VMEM, [vmem((rows, features), BF)],
        )(meta, *pieces, down_weight, *slopes)

    def near_step(meta, keeps, gots):
        count = len(keeps)
        return kernel_call(
            functools.partial(near_kernel, count),
            [shape(width, part), shape(width, part, F32)], [IN_VMEM] * (2 * count), [IN_VMEM] * 2,
        )(meta, *keeps, *gots)

    def far_step(meta, mine, got):
        return kernel_call(
            far_kernel, [shape(half, part), shape(half, part, F32)], [IN_VMEM] * 2, [IN_VMEM] * 2
        )(meta, mine, got)

    moved_0, kept_0, moved_pick, kept_pick, pre = kernel_call(
        first_kernel,
        [shape(SEND, width), shape(KEEP, width), shape(SEND, home), shape(KEEP, home), shape(home, ff)],
        [IN_HBM] * 3, [IN_VMEM] * 5,
        [vmem((home, width), BF), vmem((features,), F32), sems((3,))],
    )(meta, cotangent, layer_scale, hidden_pre)

    moved_1, moved_2 = swapped(moved_0, "tensor", 1), swapped(moved_0, "tensor", 2)
    kept_1, kept_2 = swapped(kept_0, "tensor", 1), swapped(kept_0, "tensor", 2)
    act_m, der_m = gelu(after(meta, moved_0), moved_pick, 0, ff)
    moved_2 = after(moved_2, act_m, moved_1, kept_1)
    moved_3 = swapped(moved_2, "tensor", 1)
    moved = (moved_0, moved_1, moved_2, moved_3)

    moving = grads(after(meta, moved_2), moved, (der_m,))
    to_inner, across, to_outer = ((0, 1), (3, 2)), ((1, 2), (2, 1)), ((1, 0), (2, 3))
    relayed = routed(moving, to_inner)
    crossed = routed(moving, across)

    act_ka, der_ka = gelu(after(meta, moving), kept_pick, 0, part)
    kept_2 = after(kept_2, act_ka)
    kept_3 = swapped(kept_2, "tensor", 1)
    kept = (kept_0, kept_1, kept_2, kept_3)
    send_a, keep_a, *lhs = weight_first(after(meta, act_ka), act_m, act_ka)
    got_a = swapped(send_a, "dp", 1)
    act_kb, der_kb = gelu(after(meta, send_a), kept_pick, part, part)
    send_b, keep_b = weight_again(after(meta, act_kb), part, act_m, act_kb)
    got_b = swapped(send_b, "dp", 1)
    act_kc, der_kc = gelu(after(meta, send_b), kept_pick, 2 * part, part)
    send_c, keep_c = weight_again(after(meta, act_kc), 2 * part, act_m, act_kc)
    kept_grad = grads(after(meta, send_c), kept, (der_ka, der_kb, der_kc))

    out_na, mine_a = near_step(after(meta, kept_grad, relayed, crossed), (keep_a,), (got_a,))
    got_na = swapped(out_na, "dp", 2)
    inner = routed(after(relayed, out_na), across)
    outer_a = routed(after(crossed[:, :part], got_na), to_outer)
    out_fa, own_a = far_step(after(meta, out_na), mine_a, got_na)
    got_fa = swapped(out_fa, "dp", 4)
    out_nb, mine_b = near_step(after(meta, out_fa, outer_a), (keep_b,), (got_b,))
    got_nb = swapped(out_nb, "dp", 2)
    got_c = swapped(after(send_c, out_nb), "dp", 1)
    outer_b = routed(after(crossed[:, part : 2 * part], out_nb), to_outer)
    out_nc, mine_c = near_step(after(meta, out_nb), (keep_c,), (got_c,))
    got_nc = swapped(out_nc, "dp", 2)
    outer_c = routed(after(crossed[:, 2 * part :], out_nc), to_outer)
    out_fb, own_b = far_step(after(meta, out_nc, got_fa), mine_b, got_nb)
    got_fb = swapped(out_fb, "dp", 4)
    out_fc, own_c = far_step(after(meta, out_fb, inner, outer_b), mine_c, got_nc)
    got_fc = swapped(out_fc, "dp", 4)
    total = [a + b.astype(F32) for a, b in ((own_a, got_fa), (own_b, got_fb), (own_c, got_fc))]
    down_grad = jnp.concatenate(total, axis=1) / math.sqrt(n * home)

    hidden_grad = kernel_call(
        place_kernel, shape(BAL, ff), [IN_VMEM] * 5,
        pl.BlockSpec((BAL, 256), lambda i, *_: (0, i)), grid=(ff // 256,),
    )(after(meta, out_fc), kept_grad, inner, outer_a, outer_b, outer_c)
    return (hidden_grad, down_grad)


def solution(mesh):
    pairs_and_fours = (mesh.shape["dp"], mesh.shape["tensor"]) == (8, 4)
    return jax.shard_map(
        shards if pairs_and_fours else general_shards,
        mesh=mesh,
        in_specs=(P("dp", "tensor"), P("dp", "tensor"), P(None, "tensor"), P(), P(), P()),
        out_specs=(P("dp", "tensor"), P("dp", "tensor")),
        check_vma=False,
    )


def shifted(block, axis, distance):
    devices = range(lax.axis_size(axis))
    route = [((i - distance) % len(devices), i) for i in devices]
    return lax.ppermute(block, axis, route)


def crop_rows(row_total, crop_sizes, crop_starts):
    crop_ends = jnp.cumsum(crop_sizes)
    crop_begins = crop_ends - crop_sizes
    target_rows = jnp.arange(row_total, dtype=jnp.int32)[:, None]
    inside_crop = (target_rows >= crop_begins[None, :]) & (target_rows < crop_ends[None, :])
    source_rows = jnp.sum(
        jnp.where(inside_crop, crop_starts[None, :] + target_rows - crop_begins[None, :], 0), axis=1
    )
    return (source_rows, jnp.any(inside_crop, axis=1))


def select_rows(row_block, source_rows, valid_rows):
    taken = jnp.take(row_block, source_rows, axis=0)
    return jnp.where(valid_rows[:, None], taken, jnp.zeros((), row_block.dtype))


def gelu_parts(pre_act):
    cumulative = 0.5 * (1.0 + jax.scipy.special.erf(pre_act * inv_root_two))
    activated = pre_act * cumulative
    derivative = cumulative + pre_act * jnp.exp(-0.5 * pre_act * pre_act) * inv_root_tau
    return (activated, derivative)


def local_grads(pre_rows, cot_part, live_rows, layer_scale, down_weight, home_rows):
    cot_full = lax.all_gather(cot_part, "tensor", axis=1, tiled=True)
    scaled = (cot_full.astype(F32) * layer_scale[None, :]).astype(BF)
    activated, derivative = gelu_parts(pre_rows.astype(F32))
    activation = jnp.where(live_rows[:, None], activated, 0.0).astype(BF)
    backward = jnp.dot(scaled, down_weight, preferred_element_type=F32) * derivative
    gradient_rows = jnp.where(live_rows[:, None], backward, 0.0).astype(BF)
    weight_grad = lax.psum_scatter(
        lax.dot_general(scaled, activation, (((0,), (0,)), ((), ())), preferred_element_type=F32),
        "dp",
        scatter_dimension=0,
        tiled=True,
    )
    return (gradient_rows, weight_grad / math.sqrt(lax.axis_size("dp") * home_rows))


def general_shards(hidden_pre, cotangent, down_weight, layer_scale, crop_lengths, crop_moves):
    devices = lax.axis_size("dp")
    half_axis = devices // 2
    device_index = lax.axis_index("dp")
    partner_index = (device_index + half_axis) % devices
    own_lengths = lax.dynamic_index_in_dim(crop_lengths, device_index, 0, keepdims=False)
    own_moves = lax.dynamic_index_in_dim(crop_moves, device_index, 0, keepdims=False)
    partner_lengths = lax.dynamic_index_in_dim(crop_lengths, partner_index, 0, keepdims=False)
    partner_moves = lax.dynamic_index_in_dim(crop_moves, partner_index, 0, keepdims=False)
    home_rows = hidden_pre.shape[0]
    own_starts = jnp.cumsum(own_lengths) - own_lengths
    sent_sizes = own_lengths * own_moves
    kept_sizes = own_lengths * (1 - own_moves)
    arrived = jnp.sum(partner_lengths * partner_moves)
    send_source, send_valid = crop_rows(SEND, sent_sizes, own_starts)
    keep_sizes = jnp.concatenate([kept_sizes, arrived[None]])
    keep_starts = jnp.concatenate([own_starts, jnp.full((1,), home_rows, jnp.int32)])
    keep_source, keep_valid = crop_rows(BAL, keep_sizes, keep_starts)
    live_home = jnp.arange(home_rows, dtype=jnp.int32) < jnp.sum(own_lengths)
    gradient_rows, weight_grad = local_grads(
        hidden_pre, cotangent, live_home, layer_scale, down_weight, home_rows
    )
    outgoing = select_rows(gradient_rows, send_source, send_valid)
    incoming = shifted(outgoing, "dp", half_axis)
    balanced = select_rows(jnp.concatenate([gradient_rows, incoming], 0), keep_source, keep_valid)
    return (balanced, weight_grad)
```

```python
import functools
import math

import jax
import jax.numpy as jnp
from jax import lax
from jax.experimental import pallas as pl
from jax.experimental.pallas import tpu as pltpu
from jax.sharding import PartitionSpec as P

SEND = 528
KEEP = 528
TILE = 16
SLOTS = 4
BAL = 720
BF = jnp.bfloat16
F32 = jnp.float32

inv_root_two = 0.7071067811865476
inv_root_tau = 0.3989422804014327


def kernel_call(kernel, out_shape, in_specs, out_specs, scratch=(), grid=(1,)):
    return pl.pallas_call(
        kernel,
        grid_spec=pltpu.PrefetchScalarGridSpec(
            num_scalar_prefetch=1,
            grid=grid,
            in_specs=in_specs,
            out_specs=out_specs,
            scratch_shapes=list(scratch),
        ),
        out_shape=out_shape,
        cost_estimate=pl.CostEstimate(flops=1, bytes_accessed=1, transcendentals=0),
        compiler_params=pltpu.CompilerParams(vmem_limit_bytes=16 * 1024 * 1024),
    )


IN_VMEM = pl.BlockSpec(memory_space=pltpu.VMEM)
IN_HBM = pl.BlockSpec(memory_space=pltpu.HBM)


def shape(a, b, dtype=BF):
    return jax.ShapeDtypeStruct((a, b), dtype)


def lengths_of(meta, d):
    return [meta[j, d] for j in range(SLOTS)]


def moves_of(meta, d):
    return [meta[SLOTS + j, d] for j in range(SLOTS)]


def dp_at(meta):
    return meta[2 * SLOTS, 0]


def tensor_at(meta):
    return meta[2 * SLOTS, 1]


def kept_total(meta, d):
    return sum(a * (1 - b) for a, b in zip(lengths_of(meta, d), moves_of(meta, d)))


def picks(meta, moved, first, rows, home):
    d = dp_at(meta)
    at = lax.broadcasted_iota(jnp.int32, (rows, 1), 0) - first
    source = jnp.full((rows, 1), -1, jnp.int32)
    begin = jnp.int32(0)
    start = jnp.int32(0)
    for length, move in zip(lengths_of(meta, d), moves_of(meta, d)):
        size = length * (move if moved else 1 - move)
        inside = (at >= begin) & (at < begin + size)
        source = jnp.where(inside, at + (start - begin), source)
        begin = begin + size
        start = start + length
    columns = lax.broadcasted_iota(jnp.int32, (rows, home), 1)
    return jnp.where(columns == source, 1.0, 0.0).astype(BF)


def moved_picks(meta, home):
    n = meta.shape[1]
    partner = lax.rem(dp_at(meta) + n // 2, n)
    return picks(meta, True, lax.rem(kept_total(meta, partner), TILE), SEND, home)


def kept_picks(meta, home):
    return picks(meta, False, 0, KEEP, home)


def scaled_rows(meta, pick, cot, scale):
    width = cot.shape[1]
    rows = jnp.dot(pick, cot[...], preferred_element_type=F32)
    own = scale[pl.ds(pl.multiple_of(tensor_at(meta) * width, 128), width)]
    return (rows * own[None, :]).astype(BF)


def first_kernel(
    meta, cot_hbm, scale_hbm, pre_hbm, moved_out, kept_out, moved_pick, kept_pick, pre, cot, scale, sems
):
    home = cot.shape[0]
    pairs = ((cot_hbm, cot), (scale_hbm, scale), (pre_hbm, pre))
    copies = [pltpu.make_async_copy(a, b, sems.at[i]) for i, (a, b) in enumerate(pairs)]
    for copy in copies:
        copy.start()
    moved = moved_picks(meta, home)
    kept = kept_picks(meta, home)
    moved_pick[...] = moved
    kept_pick[...] = kept
    copies[0].wait()
    copies[1].wait()
    moved_out[...] = scaled_rows(meta, moved, cot, scale)
    kept_out[...] = scaled_rows(meta, kept, cot, scale)
    copies[2].wait()


def gelu_and_slope(x):
    cumulative = 0.5 * (1.0 + lax.erf(x * inv_root_two))
    return x * cumulative, cumulative + x * jnp.exp(-0.5 * x * x) * inv_root_tau


def cut_at(widths, block):
    return [
        (i, c, min(block, width - c)) for i, width in enumerate(widths) for c in range(0, width, block)
    ]


def gelu_kernel(base, block, meta, pick, pre, act_out, der_out, rows_f32):
    rows = pick.shape[0]
    step = next(TILE * k for k in (3, 4, 2, 1) if rows % (TILE * k) == 0)
    for at in range(0, act_out.shape[1], block):
        source = slice(base + at, base + at + block)
        rows_f32[...] = jnp.dot(pick[...], pre[:, source], preferred_element_type=F32)
        columns = slice(at, at + block)

        def body(k, _):
            part = pl.ds(pl.multiple_of(k * step, step), step)
            value, slope = gelu_and_slope(rows_f32[part, :])
            act_out[part, columns] = value.astype(BF)
            der_out[part, columns] = slope
            return 0

        lax.fori_loop(0, rows // step, body, 0)


def grad_kernel(slope_count, block, meta, p0, p1, p2, p3, weight, *rest):
    slopes, outs, lhs = rest[:slope_count], rest[slope_count:-1], rest[-1]
    width = p0.shape[1]
    for j, piece in enumerate((p0, p1, p2, p3)):
        lhs[:, pl.ds(pl.multiple_of((tensor_at(meta) ^ j) * width, 128), width)] = piece[...]
    at = 0
    for i, c, wide in cut_at([slope.shape[1] for slope in slopes], block):
        value = jnp.dot(lhs[...], weight[:, at : at + wide], preferred_element_type=F32)
        part = outs[0].shape[1]
        outs[at // part][:, at % part : at % part + wide] = (value * slopes[i][:, c : c + wide]).astype(BF)
        at += wide


def weight_kernel(count, meta, *refs):
    moved, kept = refs[:count], refs[count : 2 * count]
    act_moved, act_kept, *outs, lhs_moved, lhs_kept = refs[2 * count :]
    half = moved[0].shape[1] // 2
    mine = dp_at(meta) % 2 == 0
    for i in range(count):
        for piece, lhs in ((moved[i], lhs_moved), (kept[i], lhs_kept)):
            both = piece[...].T
            lo, hi = both[:half], both[half:]
            lhs[i * half : (i + 1) * half, :] = jnp.where(mine, hi, lo)
            lhs[(count + i) * half : (count + i + 1) * half, :] = jnp.where(mine, lo, hi)
    again_kernel(0, meta, lhs_moved, lhs_kept, act_moved, act_kept, *outs)


def again_kernel(base, meta, lhs_moved, lhs_kept, act_moved, act_kept, *outs):
    columns = slice(base, base + act_kept.shape[1])
    step = lhs_moved.shape[0] // 4
    at = 0
    for out in outs:
        for i in range(0, out.shape[0], step):
            part = slice(at, at + step)
            value = jnp.dot(lhs_moved[part, :], act_moved[:, columns], preferred_element_type=F32)
            value += jnp.dot(lhs_kept[part, :], act_kept[...], preferred_element_type=F32)
            out[i : i + step, :] = value.astype(out.dtype)
            at += step


def near_kernel(count, meta, *refs):
    keeps, gots, (out, mine) = refs[:count], refs[count : 2 * count], refs[2 * count :]
    half = out.shape[0] // 2
    parts = [(k, g, at) for k, g in zip(keeps, gots) for at in range(0, k.shape[0], half)]
    keeps_even = (dp_at(meta) // 2 + tensor_at(meta)) % 2 == 0
    step = 2 * TILE

    for pair in range(2):
        (k0, g0, a0), (k1, g1, a1) = parts[2 * pair], parts[2 * pair + 1]

        def body(i, _):
            def rows(at):
                return pl.ds(pl.multiple_of(at + i * step, TILE), step)

            even = k0[rows(a0), :] + g0[rows(a0), :].astype(F32)
            odd = k1[rows(a1), :] + g1[rows(a1), :].astype(F32)
            out[rows(pair * half), :] = jnp.where(keeps_even, odd, even).astype(BF)
            mine[rows(pair * half), :] = jnp.where(keeps_even, even, odd)
            return 0

        lax.fori_loop(0, half // step, body, 0)


def far_kernel(meta, held, got, out, mine):
    half = out.shape[0]
    keeps_first = (dp_at(meta) // 4 + tensor_at(meta) // 2) % 2 == 0
    step = 2 * TILE

    def body(i, _):
        first = pl.ds(pl.multiple_of(i * step, TILE), step)
        second = pl.ds(pl.multiple_of(half + i * step, TILE), step)
        a = held[first, :] + got[first, :].astype(F32)
        b = held[second, :] + got[second, :].astype(F32)
        out[first, :] = jnp.where(keeps_first, b, a).astype(BF)
        mine[first, :] = jnp.where(keeps_first, a, b)
        return 0

    lax.fori_loop(0, half // step, body, 0)


def place_kernel(meta, kept, inner_1, inner_2, outer_1, outer_2, out):
    d = dp_at(meta)
    count = kept_total(meta, d)
    first = jnp.minimum(count - lax.rem(count, TILE), BAL - SEND)
    first = pl.multiple_of(first, TILE)
    wide = out.shape[1]
    step = pl.program_id(0)
    out[0:KEEP, :] = kept[:, pl.ds(pl.multiple_of(step * wide, wide), wide)]
    out[KEEP:, :] = jnp.zeros((out.shape[0] - KEEP, wide), BF)
    rows = lax.broadcasted_iota(jnp.int32, (SEND, 1), 0) + first
    window = pl.ds(first, SEND)
    is_inner = (d // 2 == 1) | (d // 2 == 2)
    per = inner_1.shape[1] // wide
    for i, (inner, outer) in enumerate(((inner_1, outer_1), (inner_2, outer_2))):

        @pl.when(step // per == i)
        def _():
            columns = pl.ds(pl.multiple_of((step - i * per) * wide, wide), wide)
            block = jnp.where(is_inner, inner[:, columns], outer[:, columns])
            out[window, :] = jnp.where(rows < count, out[window, :], block)


def swapped(block, axis, distance):
    n = lax.axis_size(axis)
    return lax.ppermute(block, axis, [(i, i ^ distance) for i in range(n)])


def routed(block, pairs):
    return lax.ppermute(block, "dp", [(2 * a + x, 2 * b + x) for a, b in pairs for x in range(2)])


def after(value, *others):
    return lax.optimization_barrier((value, *others))[0]


def shards(hidden_pre, cotangent, down_weight, layer_scale, crop_lengths, crop_moves):
    hidden_pre, cotangent, layer_scale = (
        pltpu.with_memory_space_constraint(x, pltpu.HBM) for x in (hidden_pre, cotangent, layer_scale)
    )
    home, ff = hidden_pre.shape
    width = cotangent.shape[1]
    features = down_weight.shape[0]
    half = width // 2
    part = ff // 3
    n = lax.axis_size("dp")
    d = lax.axis_index("dp").astype(jnp.int32)
    t = lax.axis_index("tensor").astype(jnp.int32)
    column = lax.broadcasted_iota(jnp.int32, (1, n), 1)
    own = jnp.where(column == 0, d, jnp.where(column == 1, t, 0))
    meta = jnp.concatenate([crop_lengths.T, crop_moves.T, own])
    vmem = pltpu.VMEM
    sems = pltpu.SemaphoreType.DMA

    def gelu(meta, pick, base, columns):
        rows, block = pick.shape[0], 256
        return kernel_call(
            functools.partial(gelu_kernel, base, block),
            [shape(rows, columns), shape(rows, columns, F32)],
            [IN_VMEM] * 2, [IN_VMEM] * 2, [vmem((rows, block), F32)],
        )(meta, pick, pre)

    def weight_first(meta, act_moved, act_kept):
        return kernel_call(
            functools.partial(weight_kernel, 4),
            [shape(features // 2, part), shape(features // 2, part, F32)]
            + [shape(features, SEND), shape(features, KEEP)],
            [IN_VMEM] * 10, [IN_VMEM] * 4,
        )(meta, *moved, *kept, act_moved, act_kept)

    def weight_again(meta, base, act_moved, act_kept):
        return kernel_call(
            functools.partial(again_kernel, base),
            [shape(features // 2, part), shape(features // 2, part, F32)], [IN_VMEM] * 4, [IN_VMEM] * 2,
        )(meta, *lhs, act_moved, act_kept)

    def grads(meta, pieces, slopes, cuts):
        rows = pieces[0].shape[0]
        return kernel_call(
            functools.partial(grad_kernel, len(slopes), 256), [shape(rows, c) for c in cuts],
            [IN_VMEM] * (5 + len(slopes)), [IN_VMEM] * len(cuts), [vmem((rows, features), BF)],
        )(meta, *pieces, down_weight, *slopes)

    def near_step(meta, keeps, gots):
        count = len(keeps)
        return kernel_call(
            functools.partial(near_kernel, count),
            [shape(width, part), shape(width, part, F32)], [IN_VMEM] * (2 * count), [IN_VMEM] * 2,
        )(meta, *keeps, *gots)

    def far_step(meta, mine, got):
        return kernel_call(
            far_kernel, [shape(half, part), shape(half, part, F32)], [IN_VMEM] * 2, [IN_VMEM] * 2
        )(meta, mine, got)

    moved_0, kept_0, moved_pick, kept_pick, pre = kernel_call(
        first_kernel,
        [shape(SEND, width), shape(KEEP, width), shape(SEND, home), shape(KEEP, home), shape(home, ff)],
        [IN_HBM] * 3, [IN_VMEM] * 5,
        [vmem((home, width), BF), vmem((features,), F32), sems((3,))],
    )(meta, cotangent, layer_scale, hidden_pre)

    moved_1, moved_2 = swapped(moved_0, "tensor", 1), swapped(moved_0, "tensor", 2)
    kept_1, kept_2 = swapped(kept_0, "tensor", 1), swapped(kept_0, "tensor", 2)
    act_m, der_m = gelu(after(meta, moved_0), moved_pick, 0, ff)
    act_ka, der_ka = gelu(after(meta, act_m), kept_pick, 0, part)
    moved_2 = after(moved_2, act_ka, moved_1, kept_1)
    moved_3 = swapped(moved_2, "tensor", 1)
    moved = (moved_0, moved_1, moved_2, moved_3)
    kept_2 = after(kept_2, moved_2)
    kept_3 = swapped(kept_2, "tensor", 1)
    kept = (kept_0, kept_1, kept_2, kept_3)

    moving = grads(after(meta, moved_2), moved, (der_m,), (ff // 2, ff // 2))
    to_inner, across, to_outer = ((0, 1), (3, 2)), ((1, 2), (2, 1)), ((1, 0), (2, 3))
    relayed_1, relayed_2 = [routed(block, to_inner) for block in moving]
    crossed_1, crossed_2 = [routed(block, across) for block in moving]

    send_a, keep_a, *lhs = weight_first(after(meta, *moving), act_m, act_ka)
    got_a = swapped(send_a, "dp", 1)
    act_kb, der_kb = gelu(after(meta, send_a), kept_pick, part, part)
    send_b, keep_b = weight_again(after(meta, act_kb), part, act_m, act_kb)
    got_b = swapped(send_b, "dp", 1)
    act_kc, der_kc = gelu(after(meta, send_b), kept_pick, 2 * part, part)
    outer_1 = routed(after(crossed_1, act_kc), to_outer)
    send_c, keep_c = weight_again(after(meta, act_kc, relayed_1), 2 * part, act_m, act_kc)
    (kept_grad,) = grads(after(meta, send_c), kept, (der_ka, der_kb, der_kc), (ff,))
    inner_1 = routed(after(relayed_1, send_c), across)

    out_na, mine_a = near_step(after(meta, kept_grad), (keep_a,), (got_a,))
    got_na = swapped(out_na, "dp", 2)
    outer_2 = routed(after(crossed_2, out_na, outer_1), to_outer)
    inner_2 = routed(after(relayed_2, out_na), across)
    out_nb, mine_b = near_step(after(meta, out_na, crossed_2, relayed_2), (keep_b,), (got_b,))
    got_nb = swapped(out_nb, "dp", 2)
    got_c = swapped(after(send_c, out_na), "dp", 1)
    out_fa, own_a = far_step(after(meta, out_nb, inner_1), mine_a, got_na)
    got_fa = swapped(out_fa, "dp", 4)
    out_nc, mine_c = near_step(after(meta, out_fa, outer_2), (keep_c,), (got_c,))
    got_nc = swapped(out_nc, "dp", 2)
    out_fb, own_b = far_step(after(meta, out_nc, inner_2), mine_b, got_nb)
    got_fb = swapped(out_fb, "dp", 4)
    hidden_grad = kernel_call(
        place_kernel, shape(BAL, ff), [IN_VMEM] * 5,
        pl.BlockSpec((BAL, 256), lambda i, *_: (0, i)), grid=(ff // 256,),
    )(after(meta, out_fb), kept_grad, inner_1, inner_2, outer_1, outer_2)
    out_fc, own_c = far_step(after(meta, out_fb), mine_c, got_nc)
    got_fc = swapped(out_fc, "dp", 4)
    total = [a + b.astype(F32) for a, b in ((own_a, got_fa), (own_b, got_fb), (own_c, got_fc))]
    down_grad = jnp.concatenate(total, axis=1) / math.sqrt(n * home)

    return (hidden_grad, down_grad)


def solution(mesh):
    pairs_and_fours = (mesh.shape["dp"], mesh.shape["tensor"]) == (8, 4)
    return jax.shard_map(
        shards if pairs_and_fours else general_shards,
        mesh=mesh,
        in_specs=(P("dp", "tensor"), P("dp", "tensor"), P(None, "tensor"), P(), P(), P()),
        out_specs=(P("dp", "tensor"), P("dp", "tensor")),
        check_vma=False,
    )


def shifted(block, axis, distance):
    devices = range(lax.axis_size(axis))
    route = [((i - distance) % len(devices), i) for i in devices]
    return lax.ppermute(block, axis, route)


def crop_rows(row_total, crop_sizes, crop_starts):
    crop_ends = jnp.cumsum(crop_sizes)
    crop_begins = crop_ends - crop_sizes
    target_rows = jnp.arange(row_total, dtype=jnp.int32)[:, None]
    inside_crop = (target_rows >= crop_begins[None, :]) & (target_rows < crop_ends[None, :])
    source_rows = jnp.sum(
        jnp.where(inside_crop, crop_starts[None, :] + target_rows - crop_begins[None, :], 0), axis=1
    )
    return (source_rows, jnp.any(inside_crop, axis=1))


def select_rows(row_block, source_rows, valid_rows):
    taken = jnp.take(row_block, source_rows, axis=0)
    return jnp.where(valid_rows[:, None], taken, jnp.zeros((), row_block.dtype))


def gelu_parts(pre_act):
    cumulative = 0.5 * (1.0 + jax.scipy.special.erf(pre_act * inv_root_two))
    activated = pre_act * cumulative
    derivative = cumulative + pre_act * jnp.exp(-0.5 * pre_act * pre_act) * inv_root_tau
    return (activated, derivative)


def local_grads(pre_rows, cot_part, live_rows, layer_scale, down_weight, home_rows):
    cot_full = lax.all_gather(cot_part, "tensor", axis=1, tiled=True)
    scaled = (cot_full.astype(F32) * layer_scale[None, :]).astype(BF)
    activated, derivative = gelu_parts(pre_rows.astype(F32))
    activation = jnp.where(live_rows[:, None], activated, 0.0).astype(BF)
    backward = jnp.dot(scaled, down_weight, preferred_element_type=F32) * derivative
    gradient_rows = jnp.where(live_rows[:, None], backward, 0.0).astype(BF)
    weight_grad = lax.psum_scatter(
        lax.dot_general(scaled, activation, (((0,), (0,)), ((), ())), preferred_element_type=F32),
        "dp",
        scatter_dimension=0,
        tiled=True,
    )
    return (gradient_rows, weight_grad / math.sqrt(lax.axis_size("dp") * home_rows))


def general_shards(hidden_pre, cotangent, down_weight, layer_scale, crop_lengths, crop_moves):
    devices = lax.axis_size("dp")
    half_axis = devices // 2
    device_index = lax.axis_index("dp")
    partner_index = (device_index + half_axis) % devices
    own_lengths = lax.dynamic_index_in_dim(crop_lengths, device_index, 0, keepdims=False)
    own_moves = lax.dynamic_index_in_dim(crop_moves, device_index, 0, keepdims=False)
    partner_lengths = lax.dynamic_index_in_dim(crop_lengths, partner_index, 0, keepdims=False)
    partner_moves = lax.dynamic_index_in_dim(crop_moves, partner_index, 0, keepdims=False)
    home_rows = hidden_pre.shape[0]
    own_starts = jnp.cumsum(own_lengths) - own_lengths
    sent_sizes = own_lengths * own_moves
    kept_sizes = own_lengths * (1 - own_moves)
    arrived = jnp.sum(partner_lengths * partner_moves)
    send_source, send_valid = crop_rows(SEND, sent_sizes, own_starts)
    keep_sizes = jnp.concatenate([kept_sizes, arrived[None]])
    keep_starts = jnp.concatenate([own_starts, jnp.full((1,), home_rows, jnp.int32)])
    keep_source, keep_valid = crop_rows(BAL, keep_sizes, keep_starts)
    live_home = jnp.arange(home_rows, dtype=jnp.int32) < jnp.sum(own_lengths)
    gradient_rows, weight_grad = local_grads(
        hidden_pre, cotangent, live_home, layer_scale, down_weight, home_rows
    )
    outgoing = select_rows(gradient_rows, send_source, send_valid)
    incoming = shifted(outgoing, "dp", half_axis)
    balanced = select_rows(jnp.concatenate([gradient_rows, incoming], 0), keep_source, keep_valid)
    return (balanced, weight_grad)
```

```python
import functools
import math

import jax
import jax.numpy as jnp
from jax import lax
from jax.experimental import pallas as pl
from jax.experimental.pallas import tpu as pltpu
from jax.sharding import PartitionSpec as P

SEND = 528
KEEP = 528
TILE = 16
SLOTS = 4
BAL = 720
BF = jnp.bfloat16
F32 = jnp.float32

inv_root_two = 0.7071067811865476
inv_root_tau = 0.3989422804014327


def kernel_call(kernel, out_shape, in_specs, out_specs, scratch=(), grid=(1,)):
    return pl.pallas_call(
        kernel,
        grid_spec=pltpu.PrefetchScalarGridSpec(
            num_scalar_prefetch=1,
            grid=grid,
            in_specs=in_specs,
            out_specs=out_specs,
            scratch_shapes=list(scratch),
        ),
        out_shape=out_shape,
        cost_estimate=pl.CostEstimate(flops=1, bytes_accessed=1, transcendentals=0),
        compiler_params=pltpu.CompilerParams(vmem_limit_bytes=16 * 1024 * 1024),
    )


IN_VMEM = pl.BlockSpec(memory_space=pltpu.VMEM)
IN_HBM = pl.BlockSpec(memory_space=pltpu.HBM)


def shape(a, b, dtype=BF):
    return jax.ShapeDtypeStruct((a, b), dtype)


def lengths_of(meta, d):
    return [meta[j, d] for j in range(SLOTS)]


def moves_of(meta, d):
    return [meta[SLOTS + j, d] for j in range(SLOTS)]


def dp_at(meta):
    return meta[2 * SLOTS, 0]


def tensor_at(meta):
    return meta[2 * SLOTS, 1]


def kept_total(meta, d):
    return sum(a * (1 - b) for a, b in zip(lengths_of(meta, d), moves_of(meta, d)))


def picks(meta, moved, first, rows, home):
    d = dp_at(meta)
    at = lax.broadcasted_iota(jnp.int32, (rows, 1), 0) - first
    source = jnp.full((rows, 1), -1, jnp.int32)
    begin = jnp.int32(0)
    start = jnp.int32(0)
    for length, move in zip(lengths_of(meta, d), moves_of(meta, d)):
        size = length * (move if moved else 1 - move)
        inside = (at >= begin) & (at < begin + size)
        source = jnp.where(inside, at + (start - begin), source)
        begin = begin + size
        start = start + length
    columns = lax.broadcasted_iota(jnp.int32, (rows, home), 1)
    return jnp.where(columns == source, 1.0, 0.0).astype(BF)


def moved_picks(meta, home):
    n = meta.shape[1]
    partner = lax.rem(dp_at(meta) + n // 2, n)
    return picks(meta, True, lax.rem(kept_total(meta, partner), TILE), SEND, home)


def kept_picks(meta, home):
    return picks(meta, False, 0, KEEP, home)


def scaled_rows(meta, pick, cot, scale):
    width = cot.shape[1]
    rows = jnp.dot(pick, cot[...], preferred_element_type=F32)
    own = scale[pl.ds(pl.multiple_of(tensor_at(meta) * width, 128), width)]
    return (rows * own[None, :]).astype(BF)


def first_kernel(
    meta, cot_hbm, scale_hbm, pre_hbm, moved_out, kept_out, moved_pick, kept_pick, pre, cot, scale, sems
):
    home = cot.shape[0]
    pairs = ((cot_hbm, cot), (scale_hbm, scale), (pre_hbm, pre))
    copies = [pltpu.make_async_copy(a, b, sems.at[i]) for i, (a, b) in enumerate(pairs)]
    for copy in copies:
        copy.start()
    moved = moved_picks(meta, home)
    kept = kept_picks(meta, home)
    moved_pick[...] = moved
    kept_pick[...] = kept
    copies[0].wait()
    copies[1].wait()
    moved_out[...] = scaled_rows(meta, moved, cot, scale)
    kept_out[...] = scaled_rows(meta, kept, cot, scale)
    copies[2].wait()


def gelu_and_slope(x):
    cumulative = 0.5 * (1.0 + lax.erf(x * inv_root_two))
    return x * cumulative, cumulative + x * jnp.exp(-0.5 * x * x) * inv_root_tau


def cut_at(widths, block):
    return [
        (i, c, min(block, width - c)) for i, width in enumerate(widths) for c in range(0, width, block)
    ]


def gelu_kernel(base, block, meta, pick, pre, act_out, der_out, rows_f32):
    rows = pick.shape[0]
    step = next(TILE * k for k in (3, 4, 2, 1) if rows % (TILE * k) == 0)
    for at in range(0, act_out.shape[1], block):
        source = slice(base + at, base + at + block)
        rows_f32[...] = jnp.dot(pick[...], pre[:, source], preferred_element_type=F32)
        columns = slice(at, at + block)

        def body(k, _):
            part = pl.ds(pl.multiple_of(k * step, step), step)
            value, slope = gelu_and_slope(rows_f32[part, :])
            act_out[part, columns] = value.astype(BF)
            der_out[part, columns] = slope
            return 0

        lax.fori_loop(0, rows // step, body, 0)


def grad_kernel(slope_count, block, meta, p0, p1, p2, p3, weight, *rest):
    slopes, outs, lhs = rest[:slope_count], rest[slope_count:-1], rest[-1]
    width = p0.shape[1]
    for j, piece in enumerate((p0, p1, p2, p3)):
        lhs[:, pl.ds(pl.multiple_of((tensor_at(meta) ^ j) * width, 128), width)] = piece[...]
    at = 0
    for i, c, wide in cut_at([slope.shape[1] for slope in slopes], block):
        value = jnp.dot(lhs[...], weight[:, at : at + wide], preferred_element_type=F32)
        part = outs[0].shape[1]
        outs[at // part][:, at % part : at % part + wide] = (value * slopes[i][:, c : c + wide]).astype(BF)
        at += wide


def weight_kernel(count, meta, *refs):
    moved, kept = refs[:count], refs[count : 2 * count]
    act_moved, act_kept, *outs, lhs_moved, lhs_kept = refs[2 * count :]
    half = moved[0].shape[1] // 2
    mine = dp_at(meta) % 2 == 0
    for i in range(count):
        for piece, lhs in ((moved[i], lhs_moved), (kept[i], lhs_kept)):
            both = piece[...].T
            lo, hi = both[:half], both[half:]
            lhs[i * half : (i + 1) * half, :] = jnp.where(mine, hi, lo)
            lhs[(count + i) * half : (count + i + 1) * half, :] = jnp.where(mine, lo, hi)
    again_kernel(0, meta, lhs_moved, lhs_kept, act_moved, act_kept, *outs)


def again_kernel(base, meta, lhs_moved, lhs_kept, act_moved, act_kept, *outs):
    columns = slice(base, base + act_kept.shape[1])
    step = lhs_moved.shape[0] // 4
    at = 0
    for out in outs:
        for i in range(0, out.shape[0], step):
            part = slice(at, at + step)
            value = jnp.dot(lhs_moved[part, :], act_moved[:, columns], preferred_element_type=F32)
            value += jnp.dot(lhs_kept[part, :], act_kept[...], preferred_element_type=F32)
            out[i : i + step, :] = value.astype(out.dtype)
            at += step


def near_kernel(count, meta, *refs):
    keeps, gots, (out, mine) = refs[:count], refs[count : 2 * count], refs[2 * count :]
    half = out.shape[0] // 2
    parts = [(k, g, at) for k, g in zip(keeps, gots) for at in range(0, k.shape[0], half)]
    keeps_even = (dp_at(meta) // 2 + tensor_at(meta)) % 2 == 0
    step = 2 * TILE

    for pair in range(2):
        (k0, g0, a0), (k1, g1, a1) = parts[2 * pair], parts[2 * pair + 1]

        def body(i, _):
            def rows(at):
                return pl.ds(pl.multiple_of(at + i * step, TILE), step)

            even = k0[rows(a0), :] + g0[rows(a0), :].astype(F32)
            odd = k1[rows(a1), :] + g1[rows(a1), :].astype(F32)
            out[rows(pair * half), :] = jnp.where(keeps_even, odd, even).astype(BF)
            mine[rows(pair * half), :] = jnp.where(keeps_even, even, odd)
            return 0

        lax.fori_loop(0, half // step, body, 0)


def far_kernel(meta, held, got, out, mine):
    half = out.shape[0]
    keeps_first = (dp_at(meta) // 4 + tensor_at(meta) // 2) % 2 == 0
    step = 2 * TILE

    def body(i, _):
        first = pl.ds(pl.multiple_of(i * step, TILE), step)
        second = pl.ds(pl.multiple_of(half + i * step, TILE), step)
        a = held[first, :] + got[first, :].astype(F32)
        b = held[second, :] + got[second, :].astype(F32)
        out[first, :] = jnp.where(keeps_first, b, a).astype(BF)
        mine[first, :] = jnp.where(keeps_first, a, b)
        return 0

    lax.fori_loop(0, half // step, body, 0)


def place_kernel(meta, kept, inner_1, inner_2, outer_1, outer_2, out):
    d = dp_at(meta)
    count = kept_total(meta, d)
    first = jnp.minimum(count - lax.rem(count, TILE), BAL - SEND)
    first = pl.multiple_of(first, TILE)
    wide = out.shape[1]
    step = pl.program_id(0)
    out[0:KEEP, :] = kept[:, pl.ds(pl.multiple_of(step * wide, wide), wide)]
    out[KEEP:, :] = jnp.zeros((out.shape[0] - KEEP, wide), BF)
    rows = lax.broadcasted_iota(jnp.int32, (SEND, 1), 0) + first
    window = pl.ds(first, SEND)
    is_inner = (d // 2 == 1) | (d // 2 == 2)
    per = inner_1.shape[1] // wide
    for i, (inner, outer) in enumerate(((inner_1, outer_1), (inner_2, outer_2))):

        @pl.when(step // per == i)
        def _():
            columns = pl.ds(pl.multiple_of((step - i * per) * wide, wide), wide)
            block = jnp.where(is_inner, inner[:, columns], outer[:, columns])
            out[window, :] = jnp.where(rows < count, out[window, :], block)


def swapped(block, axis, distance):
    n = lax.axis_size(axis)
    return lax.ppermute(block, axis, [(i, i ^ distance) for i in range(n)])


def routed(block, pairs):
    return lax.ppermute(block, "dp", [(2 * a + x, 2 * b + x) for a, b in pairs for x in range(2)])


def after(value, *others):
    return lax.optimization_barrier((value, *others))[0]


def shards(hidden_pre, cotangent, down_weight, layer_scale, crop_lengths, crop_moves):
    hidden_pre, cotangent, layer_scale = (
        pltpu.with_memory_space_constraint(x, pltpu.HBM) for x in (hidden_pre, cotangent, layer_scale)
    )
    home, ff = hidden_pre.shape
    width = cotangent.shape[1]
    features = down_weight.shape[0]
    half = width // 2
    part = ff // 3
    n = lax.axis_size("dp")
    d = lax.axis_index("dp").astype(jnp.int32)
    t = lax.axis_index("tensor").astype(jnp.int32)
    column = lax.broadcasted_iota(jnp.int32, (1, n), 1)
    own = jnp.where(column == 0, d, jnp.where(column == 1, t, 0))
    meta = jnp.concatenate([crop_lengths.T, crop_moves.T, own])
    vmem = pltpu.VMEM
    sems = pltpu.SemaphoreType.DMA

    def gelu(meta, pick, base, columns):
        rows, block = pick.shape[0], 256
        return kernel_call(
            functools.partial(gelu_kernel, base, block),
            [shape(rows, columns), shape(rows, columns, F32)],
            [IN_VMEM] * 2, [IN_VMEM] * 2, [vmem((rows, block), F32)],
        )(meta, pick, pre)

    def weight_first(meta, act_moved, act_kept):
        return kernel_call(
            functools.partial(weight_kernel, 4),
            [shape(features // 2, part), shape(features // 2, part, F32)]
            + [shape(features, SEND), shape(features, KEEP)],
            [IN_VMEM] * 10, [IN_VMEM] * 4,
        )(meta, *moved, *kept, act_moved, act_kept)

    def weight_again(meta, base, act_moved, act_kept):
        return kernel_call(
            functools.partial(again_kernel, base),
            [shape(features // 2, part), shape(features // 2, part, F32)], [IN_VMEM] * 4, [IN_VMEM] * 2,
        )(meta, *lhs, act_moved, act_kept)

    def grads(meta, pieces, slopes, cuts):
        rows = pieces[0].shape[0]
        return kernel_call(
            functools.partial(grad_kernel, len(slopes), 256), [shape(rows, c) for c in cuts],
            [IN_VMEM] * (5 + len(slopes)), [IN_VMEM] * len(cuts), [vmem((rows, features), BF)],
        )(meta, *pieces, down_weight, *slopes)

    def near_step(meta, keeps, gots):
        count = len(keeps)
        return kernel_call(
            functools.partial(near_kernel, count),
            [shape(width, part), shape(width, part, F32)], [IN_VMEM] * (2 * count), [IN_VMEM] * 2,
        )(meta, *keeps, *gots)

    def far_step(meta, mine, got):
        return kernel_call(
            far_kernel, [shape(half, part), shape(half, part, F32)], [IN_VMEM] * 2, [IN_VMEM] * 2
        )(meta, mine, got)

    moved_0, kept_0, moved_pick, kept_pick, pre = kernel_call(
        first_kernel,
        [shape(SEND, width), shape(KEEP, width), shape(SEND, home), shape(KEEP, home), shape(home, ff)],
        [IN_HBM] * 3, [IN_VMEM] * 5,
        [vmem((home, width), BF), vmem((features,), F32), sems((3,))],
    )(meta, cotangent, layer_scale, hidden_pre)

    moved_1, moved_2 = swapped(moved_0, "tensor", 1), swapped(moved_0, "tensor", 2)
    kept_1, kept_2 = swapped(kept_0, "tensor", 1), swapped(kept_0, "tensor", 2)
    act_m, der_m = gelu(after(meta, moved_0), moved_pick, 0, ff)
    act_ka, der_ka = gelu(after(meta, act_m), kept_pick, 0, part)
    moved_2 = after(moved_2, act_ka, moved_1, kept_1)
    moved_3 = swapped(moved_2, "tensor", 1)
    moved = (moved_0, moved_1, moved_2, moved_3)
    kept_2 = after(kept_2, moved_2)
    kept_3 = swapped(kept_2, "tensor", 1)
    kept = (kept_0, kept_1, kept_2, kept_3)

    moving = grads(after(meta, moved_2), moved, (der_m,), (ff // 2, ff // 2))
    to_inner, across, to_outer = ((0, 1), (3, 2)), ((1, 2), (2, 1)), ((1, 0), (2, 3))
    relayed_1, relayed_2 = [routed(block, to_inner) for block in moving]
    crossed_1, crossed_2 = [routed(block, across) for block in moving]

    send_a, keep_a, *lhs = weight_first(after(meta, *moving), act_m, act_ka)
    got_a = swapped(send_a, "dp", 1)
    act_kb, der_kb = gelu(after(meta, send_a), kept_pick, part, part)
    send_b, keep_b = weight_again(after(meta, act_kb), part, act_m, act_kb)
    got_b = swapped(send_b, "dp", 1)
    act_kc, der_kc = gelu(after(meta, send_b), kept_pick, 2 * part, part)
    outer_1 = routed(after(crossed_1, send_b), to_outer)
    send_c, keep_c = weight_again(after(meta, act_kc, relayed_1, got_a, crossed_2), 2 * part, act_m, act_kc)
    (kept_grad,) = grads(after(meta, send_c), kept, (der_ka, der_kb, der_kc), (ff,))
    inner_1 = routed(after(relayed_1, send_c), across)

    out_na, mine_a = near_step(after(meta, kept_grad, outer_1), (keep_a,), (got_a,))
    got_na = swapped(out_na, "dp", 2)
    inner_2 = routed(after(relayed_2, out_na), across)
    out_nb, mine_b = near_step(after(meta, got_na, relayed_2), (keep_b,), (got_b,))
    got_nb = swapped(out_nb, "dp", 2)
    got_c = swapped(after(send_c, out_na), "dp", 1)
    out_fa, own_a = far_step(after(meta, out_nb, inner_1), mine_a, got_na)
    got_fa = swapped(out_fa, "dp", 4)
    out_nc, mine_c = near_step(after(meta, out_fa), (keep_c,), (got_c,))
    got_nc = swapped(out_nc, "dp", 2)
    out_fb, own_b = far_step(after(meta, out_nc, inner_2), mine_b, got_nb)
    got_fb = swapped(out_fb, "dp", 4)
    outer_2 = routed(after(crossed_2, got_nc), to_outer)
    out_fc, own_c = far_step(after(meta, out_fb), mine_c, got_nc)
    got_fc = swapped(out_fc, "dp", 4)
    hidden_grad = kernel_call(
        place_kernel, shape(BAL, ff), [IN_VMEM] * 5,
        pl.BlockSpec((BAL, 256), lambda i, *_: (0, i)), grid=(ff // 256,),
    )(after(meta, out_fc), kept_grad, inner_1, inner_2, outer_1, outer_2)
    total = [a + b.astype(F32) for a, b in ((own_a, got_fa), (own_b, got_fb), (own_c, got_fc))]
    down_grad = jnp.concatenate(total, axis=1) / math.sqrt(n * home)

    return (hidden_grad, down_grad)


def solution(mesh):
    pairs_and_fours = (mesh.shape["dp"], mesh.shape["tensor"]) == (8, 4)
    return jax.shard_map(
        shards if pairs_and_fours else general_shards,
        mesh=mesh,
        in_specs=(P("dp", "tensor"), P("dp", "tensor"), P(None, "tensor"), P(), P(), P()),
        out_specs=(P("dp", "tensor"), P("dp", "tensor")),
        check_vma=False,
    )


def shifted(block, axis, distance):
    devices = range(lax.axis_size(axis))
    route = [((i - distance) % len(devices), i) for i in devices]
    return lax.ppermute(block, axis, route)


def crop_rows(row_total, crop_sizes, crop_starts):
    crop_ends = jnp.cumsum(crop_sizes)
    crop_begins = crop_ends - crop_sizes
    target_rows = jnp.arange(row_total, dtype=jnp.int32)[:, None]
    inside_crop = (target_rows >= crop_begins[None, :]) & (target_rows < crop_ends[None, :])
    source_rows = jnp.sum(
        jnp.where(inside_crop, crop_starts[None, :] + target_rows - crop_begins[None, :], 0), axis=1
    )
    return (source_rows, jnp.any(inside_crop, axis=1))


def select_rows(row_block, source_rows, valid_rows):
    taken = jnp.take(row_block, source_rows, axis=0)
    return jnp.where(valid_rows[:, None], taken, jnp.zeros((), row_block.dtype))


def gelu_parts(pre_act):
    cumulative = 0.5 * (1.0 + jax.scipy.special.erf(pre_act * inv_root_two))
    activated = pre_act * cumulative
    derivative = cumulative + pre_act * jnp.exp(-0.5 * pre_act * pre_act) * inv_root_tau
    return (activated, derivative)


def local_grads(pre_rows, cot_part, live_rows, layer_scale, down_weight, home_rows):
    cot_full = lax.all_gather(cot_part, "tensor", axis=1, tiled=True)
    scaled = (cot_full.astype(F32) * layer_scale[None, :]).astype(BF)
    activated, derivative = gelu_parts(pre_rows.astype(F32))
    activation = jnp.where(live_rows[:, None], activated, 0.0).astype(BF)
    backward = jnp.dot(scaled, down_weight, preferred_element_type=F32) * derivative
    gradient_rows = jnp.where(live_rows[:, None], backward, 0.0).astype(BF)
    weight_grad = lax.psum_scatter(
        lax.dot_general(scaled, activation, (((0,), (0,)), ((), ())), preferred_element_type=F32),
        "dp",
        scatter_dimension=0,
        tiled=True,
    )
    return (gradient_rows, weight_grad / math.sqrt(lax.axis_size("dp") * home_rows))


def general_shards(hidden_pre, cotangent, down_weight, layer_scale, crop_lengths, crop_moves):
    devices = lax.axis_size("dp")
    half_axis = devices // 2
    device_index = lax.axis_index("dp")
    partner_index = (device_index + half_axis) % devices
    own_lengths = lax.dynamic_index_in_dim(crop_lengths, device_index, 0, keepdims=False)
    own_moves = lax.dynamic_index_in_dim(crop_moves, device_index, 0, keepdims=False)
    partner_lengths = lax.dynamic_index_in_dim(crop_lengths, partner_index, 0, keepdims=False)
    partner_moves = lax.dynamic_index_in_dim(crop_moves, partner_index, 0, keepdims=False)
    home_rows = hidden_pre.shape[0]
    own_starts = jnp.cumsum(own_lengths) - own_lengths
    sent_sizes = own_lengths * own_moves
    kept_sizes = own_lengths * (1 - own_moves)
    arrived = jnp.sum(partner_lengths * partner_moves)
    send_source, send_valid = crop_rows(SEND, sent_sizes, own_starts)
    keep_sizes = jnp.concatenate([kept_sizes, arrived[None]])
    keep_starts = jnp.concatenate([own_starts, jnp.full((1,), home_rows, jnp.int32)])
    keep_source, keep_valid = crop_rows(BAL, keep_sizes, keep_starts)
    live_home = jnp.arange(home_rows, dtype=jnp.int32) < jnp.sum(own_lengths)
    gradient_rows, weight_grad = local_grads(
        hidden_pre, cotangent, live_home, layer_scale, down_weight, home_rows
    )
    outgoing = select_rows(gradient_rows, send_source, send_valid)
    incoming = shifted(outgoing, "dp", half_axis)
    balanced = select_rows(jnp.concatenate([gradient_rows, incoming], 0), keep_source, keep_valid)
    return (balanced, weight_grad)
```

```python
import functools
import math

import jax
import jax.numpy as jnp
from jax import lax
from jax.experimental import pallas as pl
from jax.experimental.pallas import tpu as pltpu
from jax.sharding import PartitionSpec as P

SEND = 528
KEEP = 528
TILE = 16
EARLY = 96
LATE = SEND - EARLY
SLOTS = 4
BAL = 720
BF = jnp.bfloat16
F32 = jnp.float32

inv_root_two = 0.7071067811865476
inv_root_tau = 0.3989422804014327


def kernel_call(kernel, out_shape, in_specs, out_specs, scratch=(), grid=(1,)):
    return pl.pallas_call(
        kernel,
        grid_spec=pltpu.PrefetchScalarGridSpec(
            num_scalar_prefetch=1,
            grid=grid,
            in_specs=in_specs,
            out_specs=out_specs,
            scratch_shapes=list(scratch),
        ),
        out_shape=out_shape,
        cost_estimate=pl.CostEstimate(flops=1, bytes_accessed=1, transcendentals=0),
        compiler_params=pltpu.CompilerParams(vmem_limit_bytes=16 * 1024 * 1024),
    )


IN_VMEM = pl.BlockSpec(memory_space=pltpu.VMEM)
IN_HBM = pl.BlockSpec(memory_space=pltpu.HBM)


def shape(a, b, dtype=BF):
    return jax.ShapeDtypeStruct((a, b), dtype)


def lengths_of(meta, d):
    return [meta[j, d] for j in range(SLOTS)]


def moves_of(meta, d):
    return [meta[SLOTS + j, d] for j in range(SLOTS)]


def dp_at(meta):
    return meta[2 * SLOTS, 0]


def tensor_at(meta):
    return meta[2 * SLOTS, 1]


def kept_total(meta, d):
    return sum(a * (1 - b) for a, b in zip(lengths_of(meta, d), moves_of(meta, d)))


def picks(meta, moved, first, rows, home):
    d = dp_at(meta)
    at = lax.broadcasted_iota(jnp.int32, (rows, 1), 0) - first
    source = jnp.full((rows, 1), -1, jnp.int32)
    begin = jnp.int32(0)
    start = jnp.int32(0)
    for length, move in zip(lengths_of(meta, d), moves_of(meta, d)):
        size = length * (move if moved else 1 - move)
        inside = (at >= begin) & (at < begin + size)
        source = jnp.where(inside, at + (start - begin), source)
        begin = begin + size
        start = start + length
    columns = lax.broadcasted_iota(jnp.int32, (rows, home), 1)
    return jnp.where(columns == source, 1.0, 0.0).astype(BF)


def sent_first(meta):
    n = meta.shape[1]
    partner = lax.rem(dp_at(meta) + n // 2, n)
    return lax.rem(kept_total(meta, partner), TILE)


def early_picks(meta, home):
    return picks(meta, True, sent_first(meta), EARLY, home)


def late_picks(meta, home):
    return picks(meta, True, sent_first(meta) - EARLY, LATE, home)


def kept_picks(meta, home):
    return picks(meta, False, 0, KEEP, home)


def scaled_rows(meta, pick, cot, scale):
    width = cot.shape[1]
    rows = jnp.dot(pick, cot[...], preferred_element_type=F32)
    own = scale[pl.ds(pl.multiple_of(tensor_at(meta) * width, 128), width)]
    return (rows * own[None, :]).astype(BF)


def first_kernel(
    meta, cot_hbm, scale_hbm, pre_hbm, late_out, rest_out, early_out, late_pick, rest_pick, pre, cot, scale, sems
):
    home, width = cot.shape
    pairs = ((cot_hbm, cot), (scale_hbm, scale), (pre_hbm, pre))
    copies = [pltpu.make_async_copy(a, b, sems.at[i]) for i, (a, b) in enumerate(pairs)]
    for copy in copies:
        copy.start()
    early = early_picks(meta, home)
    late = late_picks(meta, home)
    kept = kept_picks(meta, home)
    late_pick[...] = late
    rest_pick[0:EARLY, :] = early
    rest_pick[EARLY:, :] = kept
    copies[0].wait()
    copies[1].wait()
    early_rows = scaled_rows(meta, early, cot, scale)
    early_out[:, :width] = early_rows
    late_out[...] = scaled_rows(meta, late, cot, scale)
    rest_out[0:EARLY, :] = early_rows
    rest_out[EARLY:, :] = scaled_rows(meta, kept, cot, scale)
    copies[2].wait()
    early_out[:, width:] = jnp.dot(early, pre[...], preferred_element_type=F32).astype(BF)


def gelu_and_slope(x):
    cumulative = 0.5 * (1.0 + lax.erf(x * inv_root_two))
    return x * cumulative, cumulative + x * jnp.exp(-0.5 * x * x) * inv_root_tau


def cut_at(widths, block):
    return [
        (i, c, min(block, width - c)) for i, width in enumerate(widths) for c in range(0, width, block)
    ]


def gelu_kernel(base, block, meta, pick, pre, act_out, der_out, rows_f32):
    rows = pick.shape[0]
    step = next(TILE * k for k in (3, 4, 2, 1) if rows % (TILE * k) == 0)
    for at in range(0, act_out.shape[1], block):
        source = slice(base + at, base + at + block)
        rows_f32[...] = jnp.dot(pick[...], pre[:, source], preferred_element_type=F32)
        columns = slice(at, at + block)

        def body(k, _):
            part = pl.ds(pl.multiple_of(k * step, step), step)
            value, slope = gelu_and_slope(rows_f32[part, :])
            act_out[part, columns] = value.astype(BF)
            der_out[part, columns] = slope
            return 0

        lax.fori_loop(0, rows // step, body, 0)


def assemble(meta, pieces, first_row, lhs):
    rows = lhs.shape[0]
    width = pieces[1].shape[1]
    for j, piece in enumerate(pieces):
        columns = pl.ds(pl.multiple_of((tensor_at(meta) ^ j) * width, 128), width)
        lhs[:, columns] = piece[first_row : first_row + rows, 0:width]


def grad_kernel(first_row, first_slope, base, slope_count, block, meta, p0, p1, p2, p3, weight, *rest):
    slopes, outs, lhs = rest[:slope_count], rest[slope_count:-1], rest[-1]
    rows = lhs.shape[0]
    assemble(meta, (p0, p1, p2, p3), first_row, lhs)
    parts = slopes if slope_count > len(outs) else outs
    starts = [sum(part.shape[1] for part in parts[:i]) for i in range(len(parts))]
    slope_rows = slice(first_slope, first_slope + rows)
    for i, c, wide in cut_at([part.shape[1] for part in parts], block):
        at = starts[i] + c
        inside, whole_at = slice(c, c + wide), slice(at, at + wide)
        slope = slopes[i][slope_rows, inside] if slope_count == len(parts) else slopes[0][slope_rows, whole_at]
        columns = slice(base + at, base + at + wide)
        value = (jnp.dot(lhs[...], weight[:, columns], preferred_element_type=F32) * slope).astype(BF)
        if len(outs) == len(parts):
            outs[i][:, inside] = value
        else:
            outs[0][:, whole_at] = value


def early_kernel(block, meta, own, p1, p2, p3, weight, out, lhs, acc):
    width = p1.shape[1]
    assemble(meta, (own, p1, p2, p3), 0, lhs)
    for at in range(0, out.shape[1], block):
        columns = slice(at, at + block)
        acc[...] = jnp.dot(lhs[...], weight[:, columns], preferred_element_type=F32)

        def body(k, _):
            rows = pl.ds(pl.multiple_of(k * TILE, TILE), TILE)
            _, slope = gelu_and_slope(own[rows, width + at : width + at + block].astype(F32))
            out[rows, columns] = (acc[rows, :] * slope).astype(BF)
            return 0

        lax.fori_loop(0, EARLY // TILE, body, 0)


def weight_kernel(count, meta, *refs):
    moved, kept = refs[:count], refs[count : 2 * count]
    act_moved, act_kept, *outs, lhs_moved, lhs_kept = refs[2 * count :]
    half = moved[0].shape[1] // 2
    mine = dp_at(meta) % 2 == 0
    for i in range(count):
        for piece, lhs in ((moved[i], lhs_moved), (kept[i], lhs_kept)):
            both = piece[...].T
            lo, hi = both[:half], both[half:]
            lhs[i * half : (i + 1) * half, :] = jnp.where(mine, hi, lo)
            lhs[(count + i) * half : (count + i + 1) * half, :] = jnp.where(mine, lo, hi)
    again_kernel(0, meta, lhs_moved, lhs_kept, act_moved, act_kept, *outs)


def again_kernel(base, meta, lhs_moved, lhs_kept, act_moved, act_kept, *outs):
    columns = slice(base, base + act_kept.shape[1])
    step = lhs_moved.shape[0] // 4
    at = 0
    for out in outs:
        for i in range(0, out.shape[0], step):
            part = slice(at, at + step)
            value = jnp.dot(lhs_moved[part, :], act_moved[:, columns], preferred_element_type=F32)
            value += jnp.dot(lhs_kept[part, :], act_kept[...], preferred_element_type=F32)
            out[i : i + step, :] = value.astype(out.dtype)
            at += step


def near_kernel(count, meta, *refs):
    keeps, gots, (out, mine) = refs[:count], refs[count : 2 * count], refs[2 * count :]
    half = out.shape[0] // 2
    parts = [(k, g, at) for k, g in zip(keeps, gots) for at in range(0, k.shape[0], half)]
    keeps_even = (dp_at(meta) // 2 + tensor_at(meta)) % 2 == 0
    step = 2 * TILE

    for pair in range(2):
        (k0, g0, a0), (k1, g1, a1) = parts[2 * pair], parts[2 * pair + 1]

        def body(i, _):
            def rows(at):
                return pl.ds(pl.multiple_of(at + i * step, TILE), step)

            even = k0[rows(a0), :] + g0[rows(a0), :].astype(F32)
            odd = k1[rows(a1), :] + g1[rows(a1), :].astype(F32)
            out[rows(pair * half), :] = jnp.where(keeps_even, odd, even).astype(BF)
            mine[rows(pair * half), :] = jnp.where(keeps_even, even, odd)
            return 0

        lax.fori_loop(0, half // step, body, 0)


def far_kernel(meta, held, got, out, mine):
    half = out.shape[0]
    keeps_first = (dp_at(meta) // 4 + tensor_at(meta) // 2) % 2 == 0
    step = 2 * TILE

    def body(i, _):
        first = pl.ds(pl.multiple_of(i * step, TILE), step)
        second = pl.ds(pl.multiple_of(half + i * step, TILE), step)
        a = held[first, :] + got[first, :].astype(F32)
        b = held[second, :] + got[second, :].astype(F32)
        out[first, :] = jnp.where(keeps_first, b, a).astype(BF)
        mine[first, :] = jnp.where(keeps_first, a, b)
        return 0

    lax.fori_loop(0, half // step, body, 0)


def place_kernel(cuts, meta, kept, early, *rest):
    lates, out = rest[:-1], rest[-1]
    count = kept_total(meta, dp_at(meta))
    first = jnp.minimum(count - lax.rem(count, TILE), BAL - SEND)
    first = pl.multiple_of(first, TILE)
    wide = out.shape[1]
    step = pl.program_id(0)
    columns = pl.ds(pl.multiple_of(step * wide, wide), wide)
    out[0:KEEP, :] = kept[:, columns]
    out[KEEP:, :] = jnp.zeros((out.shape[0] - KEEP, wide), BF)

    def put(block, at):
        rows = lax.broadcasted_iota(jnp.int32, (block.shape[0], 1), 0) + at
        window = pl.ds(at, block.shape[0])
        out[window, :] = jnp.where(rows < count, out[window, :], block)

    put(early[:, columns], first)
    sources = [(late, c) for late, cut in zip(lates, cuts) for c in range(0, cut, wide)]
    for i, (late, c) in enumerate(sources):

        @pl.when(step == i)
        def _():
            put(late[:, c : c + wide], pl.multiple_of(first + EARLY, TILE))


def swapped(block, axis, distance):
    n = lax.axis_size(axis)
    return lax.ppermute(block, axis, [(i, i ^ distance) for i in range(n)])


def after(value, *others):
    return lax.optimization_barrier((value, *others))[0]


def shards(hidden_pre, cotangent, down_weight, layer_scale, crop_lengths, crop_moves):
    hidden_pre, cotangent, layer_scale = (
        pltpu.with_memory_space_constraint(x, pltpu.HBM) for x in (hidden_pre, cotangent, layer_scale)
    )
    home, ff = hidden_pre.shape
    width = cotangent.shape[1]
    features = down_weight.shape[0]
    half = width // 2
    part = ff // 3
    others = EARLY + KEEP
    n = lax.axis_size("dp")
    d = lax.axis_index("dp").astype(jnp.int32)
    t = lax.axis_index("tensor").astype(jnp.int32)
    column = lax.broadcasted_iota(jnp.int32, (1, n), 1)
    own = jnp.where(column == 0, d, jnp.where(column == 1, t, 0))
    meta = jnp.concatenate([crop_lengths.T, crop_moves.T, own])
    vmem = pltpu.VMEM
    sems = pltpu.SemaphoreType.DMA

    def gelu(meta, pick, base, columns):
        rows, block = pick.shape[0], 256
        return kernel_call(
            functools.partial(gelu_kernel, base, block),
            [shape(rows, columns), shape(rows, columns, F32)],
            [IN_VMEM] * 2, [IN_VMEM] * 2, [vmem((rows, block), F32)],
        )(meta, pick, pre)

    def weight_first(meta, act_moved, act_kept):
        return kernel_call(
            functools.partial(weight_kernel, 4),
            [shape(width, part)] * 2 + [shape(width, part, F32)] * 2
            + [shape(features, LATE), shape(features, others)],
            [IN_VMEM] * 10, [IN_VMEM] * 6,
        )(meta, *lates, *rests, act_moved, act_kept)

    def weight_again(meta, base, act_moved, act_kept, count):
        rows = features // 2 // count
        return kernel_call(
            functools.partial(again_kernel, base),
            [shape(rows, part)] * count + [shape(rows, part, F32)] * count,
            [IN_VMEM] * 4, [IN_VMEM] * (2 * count),
        )(meta, *lhs, act_moved, act_kept)

    def grads(meta, pieces, first_row, first_slope, rows, base, slopes, cuts):
        return kernel_call(
            functools.partial(grad_kernel, first_row, first_slope, base, len(slopes), 256),
            [shape(rows, c) for c in cuts], [IN_VMEM] * (5 + len(slopes)), [IN_VMEM] * len(cuts),
            [vmem((rows, features), BF)],
        )(meta, *pieces, down_weight, *slopes)

    def near_step(meta, keeps, gots):
        count = len(keeps)
        return kernel_call(
            functools.partial(near_kernel, count),
            [shape(width, part), shape(width, part, F32)], [IN_VMEM] * (2 * count), [IN_VMEM] * 2,
        )(meta, *keeps, *gots)

    def far_step(meta, mine, got):
        return kernel_call(
            far_kernel, [shape(half, part), shape(half, part, F32)], [IN_VMEM] * 2, [IN_VMEM] * 2
        )(meta, mine, got)

    late, rest, early, late_pick, rest_pick, pre = kernel_call(
        first_kernel,
        [shape(LATE, width), shape(others, width), shape(EARLY, width + ff),
         shape(LATE, home), shape(others, home), shape(home, ff)],
        [IN_HBM] * 3, [IN_VMEM] * 6,
        [vmem((home, width), BF), vmem((features,), F32), sems((3,))],
    )(meta, cotangent, layer_scale, hidden_pre)
    arrived_early = swapped(early, "dp", n // 2)

    late_c, late_y = swapped(late, "tensor", 1), swapped(late, "tensor", 2)
    rest_c, rest_y = swapped(rest, "tensor", 1), swapped(rest, "tensor", 2)
    act_la, der_la = gelu(after(meta, late), late_pick, 0, part)
    act_ra, der_ra = gelu(after(meta, act_la), rest_pick, 0, part)
    late_y = after(late_y, act_ra, late_c, rest_c, arrived_early)
    late_yc = swapped(late_y, "tensor", 1)
    lates = (late, late_c, late_y, late_yc)

    (moving_a,) = grads(after(meta, late_y), lates, 0, 0, LATE, 0, (der_la,), (part,))
    arrived_a = swapped(moving_a, "dp", n // 2)

    rest_y = after(rest_y, moving_a)
    rest_yc = swapped(rest_y, "tensor", 1)
    rests = (rest, rest_c, rest_y, rest_yc)
    *sends_a, keep_01, keep_23, lhs_moved, lhs_kept = weight_first(after(meta, moving_a), act_la, act_ra)
    lhs = (lhs_moved, lhs_kept)
    gots_a = [swapped(send, "dp", 1) for send in sends_a]

    act_l, der_l = gelu(after(meta, keep_01), late_pick, part, 2 * part)
    moving_b, moving_c = grads(after(meta, act_l), lates, 0, 0, LATE, part, (der_l,), (part, part))
    act_rb, der_rb = gelu(after(meta, moving_b, gots_a[0]), rest_pick, part, part)
    send_b, keep_b = weight_again(after(meta, act_rb, arrived_a), 0, act_l, act_rb, 1)
    got_b = swapped(send_b, "dp", 1)
    arrived_b = swapped(after(moving_b, send_b), "dp", n // 2)

    out_na, mine_a = near_step(after(meta, send_b), (keep_01, keep_23), gots_a)
    got_na = swapped(out_na, "dp", 2)
    early_sent = after(arrived_early[:, :width], out_na)
    early_c, early_y = swapped(early_sent, "tensor", 1), swapped(early_sent, "tensor", 2)
    act_rc, der_rc = gelu(after(meta, out_na), rest_pick, 2 * part, part)
    early_y = after(early_y, early_c, act_rc)
    early_yc = swapped(early_y, "tensor", 1)
    *sends_c, keep_c01, keep_c23 = weight_again(after(meta, early_yc), part, act_l, act_rc, 2)
    gots_c = [swapped(send, "dp", 1) for send in sends_c]

    out_nb, mine_b = near_step(after(meta, keep_c01, arrived_b, got_na), (keep_b,), (got_b,))
    got_nb = swapped(out_nb, "dp", 2)
    arrived_c = swapped(after(moving_c, out_nb), "dp", n // 2)
    (kept_grad,) = grads(after(meta, out_nb), rests, EARLY, EARLY, KEEP, 0, (der_ra, der_rb, der_rc), (ff,))
    early_grad = kernel_call(
        functools.partial(early_kernel, 256), shape(EARLY, ff), [IN_VMEM] * 5, IN_VMEM,
        [vmem((EARLY, features), BF), vmem((EARLY, 256), F32)],
    )(after(meta, kept_grad), arrived_early, early_c, early_y, early_yc, down_weight)

    out_fa, own_a = far_step(after(meta, early_grad), mine_a, got_na)
    got_fa = swapped(out_fa, "dp", 4)
    out_nc, mine_c = near_step(after(meta, out_fa), (keep_c01, keep_c23), gots_c)
    got_nc = swapped(out_nc, "dp", 2)
    out_fb, own_b = far_step(after(meta, out_nc), mine_b, got_nb)
    got_fb = swapped(out_fb, "dp", 4)
    out_fc, own_c = far_step(after(meta, out_fb, got_fa, arrived_c), mine_c, got_nc)
    got_fc = swapped(out_fc, "dp", 4)
    total = [a + b.astype(F32) for a, b in ((own_a, got_fa), (own_b, got_fb), (own_c, got_fc))]
    down_grad = jnp.concatenate(total, axis=1) / math.sqrt(n * home)

    hidden_grad = kernel_call(
        functools.partial(place_kernel, (part,) * 3), shape(BAL, ff), [IN_VMEM] * 5,
        pl.BlockSpec((BAL, 256), lambda i, *_: (0, i)), grid=(ff // 256,),
    )(after(meta, out_fc), kept_grad, early_grad, arrived_a, arrived_b, arrived_c)
    return (hidden_grad, down_grad)


def solution(mesh):
    pairs_and_fours = (mesh.shape["dp"], mesh.shape["tensor"]) == (8, 4)
    return jax.shard_map(
        shards if pairs_and_fours else general_shards,
        mesh=mesh,
        in_specs=(P("dp", "tensor"), P("dp", "tensor"), P(None, "tensor"), P(), P(), P()),
        out_specs=(P("dp", "tensor"), P("dp", "tensor")),
        check_vma=False,
    )


def shifted(block, axis, distance):
    devices = range(lax.axis_size(axis))
    route = [((i - distance) % len(devices), i) for i in devices]
    return lax.ppermute(block, axis, route)


def crop_rows(row_total, crop_sizes, crop_starts):
    crop_ends = jnp.cumsum(crop_sizes)
    crop_begins = crop_ends - crop_sizes
    target_rows = jnp.arange(row_total, dtype=jnp.int32)[:, None]
    inside_crop = (target_rows >= crop_begins[None, :]) & (target_rows < crop_ends[None, :])
    source_rows = jnp.sum(
        jnp.where(inside_crop, crop_starts[None, :] + target_rows - crop_begins[None, :], 0), axis=1
    )
    return (source_rows, jnp.any(inside_crop, axis=1))


def select_rows(row_block, source_rows, valid_rows):
    taken = jnp.take(row_block, source_rows, axis=0)
    return jnp.where(valid_rows[:, None], taken, jnp.zeros((), row_block.dtype))


def gelu_parts(pre_act):
    cumulative = 0.5 * (1.0 + jax.scipy.special.erf(pre_act * inv_root_two))
    activated = pre_act * cumulative
    derivative = cumulative + pre_act * jnp.exp(-0.5 * pre_act * pre_act) * inv_root_tau
    return (activated, derivative)


def local_grads(pre_rows, cot_part, live_rows, layer_scale, down_weight, home_rows):
    cot_full = lax.all_gather(cot_part, "tensor", axis=1, tiled=True)
    scaled = (cot_full.astype(F32) * layer_scale[None, :]).astype(BF)
    activated, derivative = gelu_parts(pre_rows.astype(F32))
    activation = jnp.where(live_rows[:, None], activated, 0.0).astype(BF)
    backward = jnp.dot(scaled, down_weight, preferred_element_type=F32) * derivative
    gradient_rows = jnp.where(live_rows[:, None], backward, 0.0).astype(BF)
    weight_grad = lax.psum_scatter(
        lax.dot_general(scaled, activation, (((0,), (0,)), ((), ())), preferred_element_type=F32),
        "dp",
        scatter_dimension=0,
        tiled=True,
    )
    return (gradient_rows, weight_grad / math.sqrt(lax.axis_size("dp") * home_rows))


def general_shards(hidden_pre, cotangent, down_weight, layer_scale, crop_lengths, crop_moves):
    devices = lax.axis_size("dp")
    half_axis = devices // 2
    device_index = lax.axis_index("dp")
    partner_index = (device_index + half_axis) % devices
    own_lengths = lax.dynamic_index_in_dim(crop_lengths, device_index, 0, keepdims=False)
    own_moves = lax.dynamic_index_in_dim(crop_moves, device_index, 0, keepdims=False)
    partner_lengths = lax.dynamic_index_in_dim(crop_lengths, partner_index, 0, keepdims=False)
    partner_moves = lax.dynamic_index_in_dim(crop_moves, partner_index, 0, keepdims=False)
    home_rows = hidden_pre.shape[0]
    own_starts = jnp.cumsum(own_lengths) - own_lengths
    sent_sizes = own_lengths * own_moves
    kept_sizes = own_lengths * (1 - own_moves)
    arrived = jnp.sum(partner_lengths * partner_moves)
    send_source, send_valid = crop_rows(SEND, sent_sizes, own_starts)
    keep_sizes = jnp.concatenate([kept_sizes, arrived[None]])
    keep_starts = jnp.concatenate([own_starts, jnp.full((1,), home_rows, jnp.int32)])
    keep_source, keep_valid = crop_rows(BAL, keep_sizes, keep_starts)
    live_home = jnp.arange(home_rows, dtype=jnp.int32) < jnp.sum(own_lengths)
    gradient_rows, weight_grad = local_grads(
        hidden_pre, cotangent, live_home, layer_scale, down_weight, home_rows
    )
    outgoing = select_rows(gradient_rows, send_source, send_valid)
    incoming = shifted(outgoing, "dp", half_axis)
    balanced = select_rows(jnp.concatenate([gradient_rows, incoming], 0), keep_source, keep_valid)
    return (balanced, weight_grad)
```

```python
import functools
import math

import jax
import jax.numpy as jnp
from jax import lax
from jax.experimental import pallas as pl
from jax.experimental.pallas import tpu as pltpu
from jax.sharding import PartitionSpec as P

SEND = 528
KEEP = 528
TILE = 16
EARLY = 48
LATE = SEND - EARLY
SLOTS = 4
BAL = 720
BF = jnp.bfloat16
F32 = jnp.float32

inv_root_two = 0.7071067811865476
inv_root_tau = 0.3989422804014327


def kernel_call(kernel, out_shape, in_specs, out_specs, scratch=(), grid=(1,)):
    return pl.pallas_call(
        kernel,
        grid_spec=pltpu.PrefetchScalarGridSpec(
            num_scalar_prefetch=1,
            grid=grid,
            in_specs=in_specs,
            out_specs=out_specs,
            scratch_shapes=list(scratch),
        ),
        out_shape=out_shape,
        cost_estimate=pl.CostEstimate(flops=1, bytes_accessed=1, transcendentals=0),
        compiler_params=pltpu.CompilerParams(vmem_limit_bytes=16 * 1024 * 1024),
    )


IN_VMEM = pl.BlockSpec(memory_space=pltpu.VMEM)
IN_HBM = pl.BlockSpec(memory_space=pltpu.HBM)


def shape(a, b, dtype=BF):
    return jax.ShapeDtypeStruct((a, b), dtype)


def lengths_of(meta, d):
    return [meta[j, d] for j in range(SLOTS)]


def moves_of(meta, d):
    return [meta[SLOTS + j, d] for j in range(SLOTS)]


def dp_at(meta):
    return meta[2 * SLOTS, 0]


def tensor_at(meta):
    return meta[2 * SLOTS, 1]


def kept_total(meta, d):
    return sum(a * (1 - b) for a, b in zip(lengths_of(meta, d), moves_of(meta, d)))


def picks(meta, moved, first, rows, home):
    d = dp_at(meta)
    at = lax.broadcasted_iota(jnp.int32, (rows, 1), 0) - first
    source = jnp.full((rows, 1), -1, jnp.int32)
    begin = jnp.int32(0)
    start = jnp.int32(0)
    for length, move in zip(lengths_of(meta, d), moves_of(meta, d)):
        size = length * (move if moved else 1 - move)
        inside = (at >= begin) & (at < begin + size)
        source = jnp.where(inside, at + (start - begin), source)
        begin = begin + size
        start = start + length
    columns = lax.broadcasted_iota(jnp.int32, (rows, home), 1)
    return jnp.where(columns == source, 1.0, 0.0).astype(BF)


def sent_first(meta):
    n = meta.shape[1]
    partner = lax.rem(dp_at(meta) + n // 2, n)
    return lax.rem(kept_total(meta, partner), TILE)


def early_picks(meta, home):
    return picks(meta, True, sent_first(meta), EARLY, home)


def late_picks(meta, home):
    return picks(meta, True, sent_first(meta) - EARLY, LATE, home)


def kept_picks(meta, home):
    return picks(meta, False, 0, KEEP, home)


def scaled_rows(meta, pick, cot, scale):
    width = cot.shape[1]
    rows = jnp.dot(pick, cot[...], preferred_element_type=F32)
    own = scale[pl.ds(pl.multiple_of(tensor_at(meta) * width, 128), width)]
    return (rows * own[None, :]).astype(BF)


def first_kernel(
    meta, cot_hbm, scale_hbm, pre_hbm, late_out, rest_out, early_out, late_pick, rest_pick, pre, cot, scale, sems
):
    home, width = cot.shape
    pairs = ((cot_hbm, cot), (scale_hbm, scale), (pre_hbm, pre))
    copies = [pltpu.make_async_copy(a, b, sems.at[i]) for i, (a, b) in enumerate(pairs)]
    for copy in copies:
        copy.start()
    early = early_picks(meta, home)
    late = late_picks(meta, home)
    kept = kept_picks(meta, home)
    late_pick[...] = late
    rest_pick[0:EARLY, :] = early
    rest_pick[EARLY:, :] = kept
    copies[0].wait()
    copies[1].wait()
    early_rows = scaled_rows(meta, early, cot, scale)
    early_out[:, :width] = early_rows
    late_out[...] = scaled_rows(meta, late, cot, scale)
    rest_out[0:EARLY, :] = early_rows
    rest_out[EARLY:, :] = scaled_rows(meta, kept, cot, scale)
    copies[2].wait()
    early_out[:, width:] = jnp.dot(early, pre[...], preferred_element_type=F32).astype(BF)


def gelu_and_slope(x):
    cumulative = 0.5 * (1.0 + lax.erf(x * inv_root_two))
    return x * cumulative, cumulative + x * jnp.exp(-0.5 * x * x) * inv_root_tau


def cut_at(widths, block):
    return [
        (i, c, min(block, width - c)) for i, width in enumerate(widths) for c in range(0, width, block)
    ]


def gelu_kernel(base, block, meta, pick, pre, act_out, der_out, rows_f32):
    rows = pick.shape[0]
    step = next(TILE * k for k in (3, 4, 2, 1) if rows % (TILE * k) == 0)
    for at in range(0, act_out.shape[1], block):
        source = slice(base + at, base + at + block)
        rows_f32[...] = jnp.dot(pick[...], pre[:, source], preferred_element_type=F32)
        columns = slice(at, at + block)

        def body(k, _):
            part = pl.ds(pl.multiple_of(k * step, step), step)
            value, slope = gelu_and_slope(rows_f32[part, :])
            act_out[part, columns] = value.astype(BF)
            der_out[part, columns] = slope
            return 0

        lax.fori_loop(0, rows // step, body, 0)


def assemble(meta, pieces, first_row, lhs):
    rows = lhs.shape[0]
    width = pieces[1].shape[1]
    for j, piece in enumerate(pieces):
        columns = pl.ds(pl.multiple_of((tensor_at(meta) ^ j) * width, 128), width)
        lhs[:, columns] = piece[first_row : first_row + rows, 0:width]


def grad_kernel(first_row, first_slope, base, slope_count, block, meta, p0, p1, p2, p3, weight, *rest):
    slopes, outs, lhs = rest[:slope_count], rest[slope_count:-1], rest[-1]
    rows = lhs.shape[0]
    assemble(meta, (p0, p1, p2, p3), first_row, lhs)
    parts = slopes if slope_count > len(outs) else outs
    starts = [sum(part.shape[1] for part in parts[:i]) for i in range(len(parts))]
    slope_rows = slice(first_slope, first_slope + rows)
    for i, c, wide in cut_at([part.shape[1] for part in parts], block):
        at = starts[i] + c
        inside, whole_at = slice(c, c + wide), slice(at, at + wide)
        slope = slopes[i][slope_rows, inside] if slope_count == len(parts) else slopes[0][slope_rows, whole_at]
        columns = slice(base + at, base + at + wide)
        value = (jnp.dot(lhs[...], weight[:, columns], preferred_element_type=F32) * slope).astype(BF)
        if len(outs) == len(parts):
            outs[i][:, inside] = value
        else:
            outs[0][:, whole_at] = value


def early_kernel(block, meta, own, p1, p2, p3, weight, out, lhs, acc):
    width = p1.shape[1]
    assemble(meta, (own, p1, p2, p3), 0, lhs)
    for at in range(0, out.shape[1], block):
        columns = slice(at, at + block)
        acc[...] = jnp.dot(lhs[...], weight[:, columns], preferred_element_type=F32)

        def body(k, _):
            rows = pl.ds(pl.multiple_of(k * TILE, TILE), TILE)
            _, slope = gelu_and_slope(own[rows, width + at : width + at + block].astype(F32))
            out[rows, columns] = (acc[rows, :] * slope).astype(BF)
            return 0

        lax.fori_loop(0, EARLY // TILE, body, 0)


def weight_kernel(count, meta, *refs):
    moved, kept = refs[:count], refs[count : 2 * count]
    act_moved, act_kept, *outs, lhs_moved, lhs_kept = refs[2 * count :]
    half = moved[0].shape[1] // 2
    mine = dp_at(meta) % 2 == 0
    for i in range(count):
        for piece, lhs in ((moved[i], lhs_moved), (kept[i], lhs_kept)):
            both = piece[...].T
            lo, hi = both[:half], both[half:]
            lhs[i * half : (i + 1) * half, :] = jnp.where(mine, hi, lo)
            lhs[(count + i) * half : (count + i + 1) * half, :] = jnp.where(mine, lo, hi)
    again_kernel(0, meta, lhs_moved, lhs_kept, act_moved, act_kept, *outs)


def again_kernel(base, meta, lhs_moved, lhs_kept, act_moved, act_kept, *outs):
    columns = slice(base, base + act_kept.shape[1])
    step = lhs_moved.shape[0] // 4
    at = 0
    for out in outs:
        for i in range(0, out.shape[0], step):
            part = slice(at, at + step)
            value = jnp.dot(lhs_moved[part, :], act_moved[:, columns], preferred_element_type=F32)
            value += jnp.dot(lhs_kept[part, :], act_kept[...], preferred_element_type=F32)
            out[i : i + step, :] = value.astype(out.dtype)
            at += step


def near_kernel(count, meta, *refs):
    keeps, gots, (out, mine) = refs[:count], refs[count : 2 * count], refs[2 * count :]
    half = out.shape[0] // 2
    parts = [(k, g, at) for k, g in zip(keeps, gots) for at in range(0, k.shape[0], half)]
    keeps_even = (dp_at(meta) // 2 + tensor_at(meta)) % 2 == 0
    step = 2 * TILE

    for pair in range(2):
        (k0, g0, a0), (k1, g1, a1) = parts[2 * pair], parts[2 * pair + 1]

        def body(i, _):
            def rows(at):
                return pl.ds(pl.multiple_of(at + i * step, TILE), step)

            even = k0[rows(a0), :] + g0[rows(a0), :].astype(F32)
            odd = k1[rows(a1), :] + g1[rows(a1), :].astype(F32)
            out[rows(pair * half), :] = jnp.where(keeps_even, odd, even).astype(BF)
            mine[rows(pair * half), :] = jnp.where(keeps_even, even, odd)
            return 0

        lax.fori_loop(0, half // step, body, 0)


def far_kernel(meta, held, got, out, mine):
    half = out.shape[0]
    keeps_first = (dp_at(meta) // 4 + tensor_at(meta) // 2) % 2 == 0
    step = 2 * TILE

    def body(i, _):
        first = pl.ds(pl.multiple_of(i * step, TILE), step)
        second = pl.ds(pl.multiple_of(half + i * step, TILE), step)
        a = held[first, :] + got[first, :].astype(F32)
        b = held[second, :] + got[second, :].astype(F32)
        out[first, :] = jnp.where(keeps_first, b, a).astype(BF)
        mine[first, :] = jnp.where(keeps_first, a, b)
        return 0

    lax.fori_loop(0, half // step, body, 0)


def place_kernel(cuts, meta, kept, early, *rest):
    lates, out = rest[:-1], rest[-1]
    count = kept_total(meta, dp_at(meta))
    first = jnp.minimum(count - lax.rem(count, TILE), BAL - SEND)
    first = pl.multiple_of(first, TILE)
    wide = out.shape[1]
    step = pl.program_id(0)
    columns = pl.ds(pl.multiple_of(step * wide, wide), wide)
    out[0:KEEP, :] = kept[:, columns]
    out[KEEP:, :] = jnp.zeros((out.shape[0] - KEEP, wide), BF)

    def put(block, at):
        rows = lax.broadcasted_iota(jnp.int32, (block.shape[0], 1), 0) + at
        window = pl.ds(at, block.shape[0])
        out[window, :] = jnp.where(rows < count, out[window, :], block)

    put(early[:, columns], first)
    sources = [(late, c) for late, cut in zip(lates, cuts) for c in range(0, cut, wide)]
    for i, (late, c) in enumerate(sources):

        @pl.when(step == i)
        def _():
            put(late[:, c : c + wide], pl.multiple_of(first + EARLY, TILE))


def swapped(block, axis, distance):
    n = lax.axis_size(axis)
    return lax.ppermute(block, axis, [(i, i ^ distance) for i in range(n)])


def after(value, *others):
    return lax.optimization_barrier((value, *others))[0]


def shards(hidden_pre, cotangent, down_weight, layer_scale, crop_lengths, crop_moves):
    hidden_pre, cotangent, layer_scale = (
        pltpu.with_memory_space_constraint(x, pltpu.HBM) for x in (hidden_pre, cotangent, layer_scale)
    )
    home, ff = hidden_pre.shape
    width = cotangent.shape[1]
    features = down_weight.shape[0]
    half = width // 2
    part = ff // 3
    others = EARLY + KEEP
    n = lax.axis_size("dp")
    d = lax.axis_index("dp").astype(jnp.int32)
    t = lax.axis_index("tensor").astype(jnp.int32)
    column = lax.broadcasted_iota(jnp.int32, (1, n), 1)
    own = jnp.where(column == 0, d, jnp.where(column == 1, t, 0))
    meta = jnp.concatenate([crop_lengths.T, crop_moves.T, own])
    vmem = pltpu.VMEM
    sems = pltpu.SemaphoreType.DMA

    def gelu(meta, pick, base, columns):
        rows, block = pick.shape[0], 256
        return kernel_call(
            functools.partial(gelu_kernel, base, block),
            [shape(rows, columns), shape(rows, columns, F32)],
            [IN_VMEM] * 2, [IN_VMEM] * 2, [vmem((rows, block), F32)],
        )(meta, pick, pre)

    def weight_first(meta, act_moved, act_kept):
        return kernel_call(
            functools.partial(weight_kernel, 4),
            [shape(width, part)] * 2 + [shape(width, part, F32)] * 2
            + [shape(features, LATE), shape(features, others)],
            [IN_VMEM] * 10, [IN_VMEM] * 6,
        )(meta, *lates, *rests, act_moved, act_kept)

    def weight_again(meta, base, act_moved, act_kept, count):
        rows = features // 2 // count
        return kernel_call(
            functools.partial(again_kernel, base),
            [shape(rows, part)] * count + [shape(rows, part, F32)] * count,
            [IN_VMEM] * 4, [IN_VMEM] * (2 * count),
        )(meta, *lhs, act_moved, act_kept)

    def grads(meta, pieces, first_row, first_slope, rows, base, slopes, cuts):
        return kernel_call(
            functools.partial(grad_kernel, first_row, first_slope, base, len(slopes), 256),
            [shape(rows, c) for c in cuts], [IN_VMEM] * (5 + len(slopes)), [IN_VMEM] * len(cuts),
            [vmem((rows, features), BF)],
        )(meta, *pieces, down_weight, *slopes)

    def near_step(meta, keeps, gots):
        count = len(keeps)
        return kernel_call(
            functools.partial(near_kernel, count),
            [shape(width, part), shape(width, part, F32)], [IN_VMEM] * (2 * count), [IN_VMEM] * 2,
        )(meta, *keeps, *gots)

    def far_step(meta, mine, got):
        return kernel_call(
            far_kernel, [shape(half, part), shape(half, part, F32)], [IN_VMEM] * 2, [IN_VMEM] * 2
        )(meta, mine, got)

    late, rest, early, late_pick, rest_pick, pre = kernel_call(
        first_kernel,
        [shape(LATE, width), shape(others, width), shape(EARLY, width + ff),
         shape(LATE, home), shape(others, home), shape(home, ff)],
        [IN_HBM] * 3, [IN_VMEM] * 6,
        [vmem((home, width), BF), vmem((features,), F32), sems((3,))],
    )(meta, cotangent, layer_scale, hidden_pre)
    arrived_early = swapped(early, "dp", n // 2)

    late_c, late_y = swapped(late, "tensor", 1), swapped(late, "tensor", 2)
    rest_c, rest_y = swapped(rest, "tensor", 1), swapped(rest, "tensor", 2)
    act_la, der_la = gelu(after(meta, late), late_pick, 0, part)
    act_ra, der_ra = gelu(after(meta, act_la), rest_pick, 0, part)
    late_y = after(late_y, act_ra, late_c, rest_c, arrived_early)
    late_yc = swapped(late_y, "tensor", 1)
    lates = (late, late_c, late_y, late_yc)

    (moving_a,) = grads(after(meta, late_y), lates, 0, 0, LATE, 0, (der_la,), (part,))
    arrived_a = swapped(moving_a, "dp", n // 2)

    rest_y = after(rest_y, moving_a)
    rest_yc = swapped(rest_y, "tensor", 1)
    rests = (rest, rest_c, rest_y, rest_yc)
    *sends_a, keep_01, keep_23, lhs_moved, lhs_kept = weight_first(after(meta, moving_a), act_la, act_ra)
    lhs = (lhs_moved, lhs_kept)
    gots_a = [swapped(send, "dp", 1) for send in sends_a]

    act_l, der_l = gelu(after(meta, keep_01), late_pick, part, 2 * part)
    moving_b, moving_c = grads(after(meta, act_l), lates, 0, 0, LATE, part, (der_l,), (part, part))
    act_rb, der_rb = gelu(after(meta, moving_b, gots_a[0]), rest_pick, part, part)
    send_b, keep_b = weight_again(after(meta, act_rb, arrived_a), 0, act_l, act_rb, 1)
    got_b = swapped(send_b, "dp", 1)
    arrived_b = swapped(after(moving_b, send_b), "dp", n // 2)

    out_na, mine_a = near_step(after(meta, send_b), (keep_01, keep_23), gots_a)
    got_na = swapped(out_na, "dp", 2)
    early_sent = after(arrived_early[:, :width], out_na)
    early_c, early_y = swapped(early_sent, "tensor", 1), swapped(early_sent, "tensor", 2)
    act_rc, der_rc = gelu(after(meta, out_na), rest_pick, 2 * part, part)
    early_y = after(early_y, early_c, act_rc)
    early_yc = swapped(early_y, "tensor", 1)
    *sends_c, keep_c01, keep_c23 = weight_again(after(meta, early_yc), part, act_l, act_rc, 2)
    gots_c = [swapped(send, "dp", 1) for send in sends_c]

    out_nb, mine_b = near_step(after(meta, keep_c01, arrived_b, got_na), (keep_b,), (got_b,))
    got_nb = swapped(out_nb, "dp", 2)
    arrived_c = swapped(after(moving_c, out_nb), "dp", n // 2)
    out_fa, own_a = far_step(after(meta, out_nb), mine_a, got_na)
    got_fa = swapped(out_fa, "dp", 4)
    (kept_grad,) = grads(after(meta, out_fa), rests, EARLY, EARLY, KEEP, 0, (der_ra, der_rb, der_rc), (ff,))
    early_grad = kernel_call(
        functools.partial(early_kernel, 256), shape(EARLY, ff), [IN_VMEM] * 5, IN_VMEM,
        [vmem((EARLY, features), BF), vmem((EARLY, 256), F32)],
    )(after(meta, kept_grad), arrived_early, early_c, early_y, early_yc, down_weight)

    out_nc, mine_c = near_step(after(meta, early_grad), (keep_c01, keep_c23), gots_c)
    got_nc = swapped(out_nc, "dp", 2)
    out_fb, own_b = far_step(after(meta, out_nc), mine_b, got_nb)
    got_fb = swapped(out_fb, "dp", 4)
    out_fc, own_c = far_step(after(meta, out_fb, got_fa, arrived_c), mine_c, got_nc)
    got_fc = swapped(out_fc, "dp", 4)
    total = [a + b.astype(F32) for a, b in ((own_a, got_fa), (own_b, got_fb), (own_c, got_fc))]
    down_grad = jnp.concatenate(total, axis=1) / math.sqrt(n * home)

    hidden_grad = kernel_call(
        functools.partial(place_kernel, (part,) * 3), shape(BAL, ff), [IN_VMEM] * 5,
        pl.BlockSpec((BAL, 256), lambda i, *_: (0, i)), grid=(ff // 256,),
    )(after(meta, out_fc), kept_grad, early_grad, arrived_a, arrived_b, arrived_c)
    return (hidden_grad, down_grad)


def solution(mesh):
    pairs_and_fours = (mesh.shape["dp"], mesh.shape["tensor"]) == (8, 4)
    return jax.shard_map(
        shards if pairs_and_fours else general_shards,
        mesh=mesh,
        in_specs=(P("dp", "tensor"), P("dp", "tensor"), P(None, "tensor"), P(), P(), P()),
        out_specs=(P("dp", "tensor"), P("dp", "tensor")),
        check_vma=False,
    )


def shifted(block, axis, distance):
    devices = range(lax.axis_size(axis))
    route = [((i - distance) % len(devices), i) for i in devices]
    return lax.ppermute(block, axis, route)


def crop_rows(row_total, crop_sizes, crop_starts):
    crop_ends = jnp.cumsum(crop_sizes)
    crop_begins = crop_ends - crop_sizes
    target_rows = jnp.arange(row_total, dtype=jnp.int32)[:, None]
    inside_crop = (target_rows >= crop_begins[None, :]) & (target_rows < crop_ends[None, :])
    source_rows = jnp.sum(
        jnp.where(inside_crop, crop_starts[None, :] + target_rows - crop_begins[None, :], 0), axis=1
    )
    return (source_rows, jnp.any(inside_crop, axis=1))


def select_rows(row_block, source_rows, valid_rows):
    taken = jnp.take(row_block, source_rows, axis=0)
    return jnp.where(valid_rows[:, None], taken, jnp.zeros((), row_block.dtype))


def gelu_parts(pre_act):
    cumulative = 0.5 * (1.0 + jax.scipy.special.erf(pre_act * inv_root_two))
    activated = pre_act * cumulative
    derivative = cumulative + pre_act * jnp.exp(-0.5 * pre_act * pre_act) * inv_root_tau
    return (activated, derivative)


def local_grads(pre_rows, cot_part, live_rows, layer_scale, down_weight, home_rows):
    cot_full = lax.all_gather(cot_part, "tensor", axis=1, tiled=True)
    scaled = (cot_full.astype(F32) * layer_scale[None, :]).astype(BF)
    activated, derivative = gelu_parts(pre_rows.astype(F32))
    activation = jnp.where(live_rows[:, None], activated, 0.0).astype(BF)
    backward = jnp.dot(scaled, down_weight, preferred_element_type=F32) * derivative
    gradient_rows = jnp.where(live_rows[:, None], backward, 0.0).astype(BF)
    weight_grad = lax.psum_scatter(
        lax.dot_general(scaled, activation, (((0,), (0,)), ((), ())), preferred_element_type=F32),
        "dp",
        scatter_dimension=0,
        tiled=True,
    )
    return (gradient_rows, weight_grad / math.sqrt(lax.axis_size("dp") * home_rows))


def general_shards(hidden_pre, cotangent, down_weight, layer_scale, crop_lengths, crop_moves):
    devices = lax.axis_size("dp")
    half_axis = devices // 2
    device_index = lax.axis_index("dp")
    partner_index = (device_index + half_axis) % devices
    own_lengths = lax.dynamic_index_in_dim(crop_lengths, device_index, 0, keepdims=False)
    own_moves = lax.dynamic_index_in_dim(crop_moves, device_index, 0, keepdims=False)
    partner_lengths = lax.dynamic_index_in_dim(crop_lengths, partner_index, 0, keepdims=False)
    partner_moves = lax.dynamic_index_in_dim(crop_moves, partner_index, 0, keepdims=False)
    home_rows = hidden_pre.shape[0]
    own_starts = jnp.cumsum(own_lengths) - own_lengths
    sent_sizes = own_lengths * own_moves
    kept_sizes = own_lengths * (1 - own_moves)
    arrived = jnp.sum(partner_lengths * partner_moves)
    send_source, send_valid = crop_rows(SEND, sent_sizes, own_starts)
    keep_sizes = jnp.concatenate([kept_sizes, arrived[None]])
    keep_starts = jnp.concatenate([own_starts, jnp.full((1,), home_rows, jnp.int32)])
    keep_source, keep_valid = crop_rows(BAL, keep_sizes, keep_starts)
    live_home = jnp.arange(home_rows, dtype=jnp.int32) < jnp.sum(own_lengths)
    gradient_rows, weight_grad = local_grads(
        hidden_pre, cotangent, live_home, layer_scale, down_weight, home_rows
    )
    outgoing = select_rows(gradient_rows, send_source, send_valid)
    incoming = shifted(outgoing, "dp", half_axis)
    balanced = select_rows(jnp.concatenate([gradient_rows, incoming], 0), keep_source, keep_valid)
    return (balanced, weight_grad)
```

```python
import functools
import math

import jax
import jax.numpy as jnp
from jax import lax
from jax.experimental import pallas as pl
from jax.experimental.pallas import tpu as pltpu
from jax.sharding import PartitionSpec as P

SEND = 528
KEEP = 528
TILE = 16
EARLY = 48
LATE = SEND - EARLY
SLOTS = 4
BAL = 720
BF = jnp.bfloat16
F32 = jnp.float32

inv_root_two = 0.7071067811865476
inv_root_tau = 0.3989422804014327


def kernel_call(kernel, out_shape, in_specs, out_specs, scratch=(), grid=(1,)):
    return pl.pallas_call(
        kernel,
        grid_spec=pltpu.PrefetchScalarGridSpec(
            num_scalar_prefetch=1,
            grid=grid,
            in_specs=in_specs,
            out_specs=out_specs,
            scratch_shapes=list(scratch),
        ),
        out_shape=out_shape,
        cost_estimate=pl.CostEstimate(flops=1, bytes_accessed=1, transcendentals=0),
        compiler_params=pltpu.CompilerParams(vmem_limit_bytes=16 * 1024 * 1024),
    )


IN_VMEM = pl.BlockSpec(memory_space=pltpu.VMEM)
IN_HBM = pl.BlockSpec(memory_space=pltpu.HBM)


def shape(a, b, dtype=BF):
    return jax.ShapeDtypeStruct((a, b), dtype)


def lengths_of(meta, d):
    return [meta[j, d] for j in range(SLOTS)]


def moves_of(meta, d):
    return [meta[SLOTS + j, d] for j in range(SLOTS)]


def dp_at(meta):
    return meta[2 * SLOTS, 0]


def tensor_at(meta):
    return meta[2 * SLOTS, 1]


def kept_total(meta, d):
    return sum(a * (1 - b) for a, b in zip(lengths_of(meta, d), moves_of(meta, d)))


def picks(meta, moved, first, rows, home):
    d = dp_at(meta)
    at = lax.broadcasted_iota(jnp.int32, (rows, 1), 0) - first
    source = jnp.full((rows, 1), -1, jnp.int32)
    begin = jnp.int32(0)
    start = jnp.int32(0)
    for length, move in zip(lengths_of(meta, d), moves_of(meta, d)):
        size = length * (move if moved else 1 - move)
        inside = (at >= begin) & (at < begin + size)
        source = jnp.where(inside, at + (start - begin), source)
        begin = begin + size
        start = start + length
    columns = lax.broadcasted_iota(jnp.int32, (rows, home), 1)
    return jnp.where(columns == source, 1.0, 0.0).astype(BF)


def sent_first(meta):
    n = meta.shape[1]
    partner = lax.rem(dp_at(meta) + n // 2, n)
    return lax.rem(kept_total(meta, partner), TILE)


def early_picks(meta, home):
    return picks(meta, True, sent_first(meta), EARLY, home)


def late_picks(meta, home):
    return picks(meta, True, sent_first(meta) - EARLY, LATE, home)


def kept_picks(meta, home):
    return picks(meta, False, 0, KEEP, home)


def scaled_rows(meta, pick, cot, scale):
    width = cot.shape[1]
    rows = jnp.dot(pick, cot[...], preferred_element_type=F32)
    own = scale[pl.ds(pl.multiple_of(tensor_at(meta) * width, 128), width)]
    return (rows * own[None, :]).astype(BF)


def first_kernel(
    meta, cot_hbm, scale_hbm, pre_hbm, late_out, rest_out, early_out, late_pick, rest_pick, pre, cot, scale, sems
):
    home, width = cot.shape
    pairs = ((cot_hbm, cot), (scale_hbm, scale), (pre_hbm, pre))
    copies = [pltpu.make_async_copy(a, b, sems.at[i]) for i, (a, b) in enumerate(pairs)]
    for copy in copies:
        copy.start()
    early = early_picks(meta, home)
    late = late_picks(meta, home)
    kept = kept_picks(meta, home)
    late_pick[...] = late
    rest_pick[0:EARLY, :] = early
    rest_pick[EARLY:, :] = kept
    copies[0].wait()
    copies[1].wait()
    early_rows = scaled_rows(meta, early, cot, scale)
    early_out[:, :width] = early_rows
    late_out[...] = scaled_rows(meta, late, cot, scale)
    rest_out[0:EARLY, :] = early_rows
    rest_out[EARLY:, :] = scaled_rows(meta, kept, cot, scale)
    copies[2].wait()
    early_out[:, width:] = jnp.dot(early, pre[...], preferred_element_type=F32).astype(BF)


def gelu_and_slope(x):
    cumulative = 0.5 * (1.0 + lax.erf(x * inv_root_two))
    return x * cumulative, cumulative + x * jnp.exp(-0.5 * x * x) * inv_root_tau


def cut_at(widths, block):
    return [
        (i, c, min(block, width - c)) for i, width in enumerate(widths) for c in range(0, width, block)
    ]


def gelu_kernel(base, block, meta, pick, pre, act_out, der_out, rows_f32):
    rows = pick.shape[0]
    step = next(TILE * k for k in (3, 4, 2, 1) if rows % (TILE * k) == 0)
    for at in range(0, act_out.shape[1], block):
        source = slice(base + at, base + at + block)
        rows_f32[...] = jnp.dot(pick[...], pre[:, source], preferred_element_type=F32)
        columns = slice(at, at + block)

        def body(k, _):
            part = pl.ds(pl.multiple_of(k * step, step), step)
            value, slope = gelu_and_slope(rows_f32[part, :])
            act_out[part, columns] = value.astype(BF)
            der_out[part, columns] = slope
            return 0

        lax.fori_loop(0, rows // step, body, 0)


def assemble(meta, pieces, first_row, lhs):
    rows = lhs.shape[0]
    width = pieces[1].shape[1]
    for j, piece in enumerate(pieces):
        columns = pl.ds(pl.multiple_of((tensor_at(meta) ^ j) * width, 128), width)
        lhs[:, columns] = piece[first_row : first_row + rows, 0:width]


def grad_kernel(first_row, first_slope, base, slope_count, block, meta, p0, p1, p2, p3, weight, *rest):
    slopes, outs, lhs = rest[:slope_count], rest[slope_count:-1], rest[-1]
    rows = lhs.shape[0]
    assemble(meta, (p0, p1, p2, p3), first_row, lhs)
    parts = slopes if slope_count > len(outs) else outs
    starts = [sum(part.shape[1] for part in parts[:i]) for i in range(len(parts))]
    slope_rows = slice(first_slope, first_slope + rows)
    for i, c, wide in cut_at([part.shape[1] for part in parts], block):
        at = starts[i] + c
        inside, whole_at = slice(c, c + wide), slice(at, at + wide)
        slope = slopes[i][slope_rows, inside] if slope_count == len(parts) else slopes[0][slope_rows, whole_at]
        columns = slice(base + at, base + at + wide)
        value = (jnp.dot(lhs[...], weight[:, columns], preferred_element_type=F32) * slope).astype(BF)
        if len(outs) == len(parts):
            outs[i][:, inside] = value
        else:
            outs[0][:, whole_at] = value


def early_kernel(block, meta, own, p1, p2, p3, weight, out, lhs, acc):
    width = p1.shape[1]
    assemble(meta, (own, p1, p2, p3), 0, lhs)
    for at in range(0, out.shape[1], block):
        columns = slice(at, at + block)
        acc[...] = jnp.dot(lhs[...], weight[:, columns], preferred_element_type=F32)

        def body(k, _):
            rows = pl.ds(pl.multiple_of(k * TILE, TILE), TILE)
            _, slope = gelu_and_slope(own[rows, width + at : width + at + block].astype(F32))
            out[rows, columns] = (acc[rows, :] * slope).astype(BF)
            return 0

        lax.fori_loop(0, EARLY // TILE, body, 0)


def weight_kernel(count, meta, *refs):
    moved, kept = refs[:count], refs[count : 2 * count]
    act_moved, act_kept, *outs, lhs_moved, lhs_kept = refs[2 * count :]
    half = moved[0].shape[1] // 2
    mine = dp_at(meta) % 2 == 0
    for i in range(count):
        for piece, lhs in ((moved[i], lhs_moved), (kept[i], lhs_kept)):
            both = piece[...].T
            lo, hi = both[:half], both[half:]
            lhs[i * half : (i + 1) * half, :] = jnp.where(mine, hi, lo)
            lhs[(count + i) * half : (count + i + 1) * half, :] = jnp.where(mine, lo, hi)
    again_kernel(0, meta, lhs_moved, lhs_kept, act_moved, act_kept, *outs)


def again_kernel(base, meta, lhs_moved, lhs_kept, act_moved, act_kept, *outs):
    columns = slice(base, base + act_kept.shape[1])
    step = lhs_moved.shape[0] // 4
    at = 0
    for out in outs:
        for i in range(0, out.shape[0], step):
            part = slice(at, at + step)
            value = jnp.dot(lhs_moved[part, :], act_moved[:, columns], preferred_element_type=F32)
            value += jnp.dot(lhs_kept[part, :], act_kept[...], preferred_element_type=F32)
            out[i : i + step, :] = value.astype(out.dtype)
            at += step


def near_kernel(count, meta, *refs):
    keeps, gots, (out, mine) = refs[:count], refs[count : 2 * count], refs[2 * count :]
    half = out.shape[0] // 2
    parts = [(k, g, at) for k, g in zip(keeps, gots) for at in range(0, k.shape[0], half)]
    keeps_even = (dp_at(meta) // 2 + tensor_at(meta)) % 2 == 0
    step = 2 * TILE

    for pair in range(2):
        (k0, g0, a0), (k1, g1, a1) = parts[2 * pair], parts[2 * pair + 1]

        def body(i, _):
            def rows(at):
                return pl.ds(pl.multiple_of(at + i * step, TILE), step)

            even = k0[rows(a0), :] + g0[rows(a0), :].astype(F32)
            odd = k1[rows(a1), :] + g1[rows(a1), :].astype(F32)
            out[rows(pair * half), :] = jnp.where(keeps_even, odd, even).astype(BF)
            mine[rows(pair * half), :] = jnp.where(keeps_even, even, odd)
            return 0

        lax.fori_loop(0, half // step, body, 0)


def far_kernel(meta, held, got, out, mine):
    half = out.shape[0]
    keeps_first = (dp_at(meta) // 4 + tensor_at(meta) // 2) % 2 == 0
    step = 2 * TILE

    def body(i, _):
        first = pl.ds(pl.multiple_of(i * step, TILE), step)
        second = pl.ds(pl.multiple_of(half + i * step, TILE), step)
        a = held[first, :] + got[first, :].astype(F32)
        b = held[second, :] + got[second, :].astype(F32)
        out[first, :] = jnp.where(keeps_first, b, a).astype(BF)
        mine[first, :] = jnp.where(keeps_first, a, b)
        return 0

    lax.fori_loop(0, half // step, body, 0)


def place_kernel(cuts, meta, kept, early, *rest):
    lates, out = rest[:-1], rest[-1]
    count = kept_total(meta, dp_at(meta))
    first = jnp.minimum(count - lax.rem(count, TILE), BAL - SEND)
    first = pl.multiple_of(first, TILE)
    wide = out.shape[1]
    step = pl.program_id(0)
    columns = pl.ds(pl.multiple_of(step * wide, wide), wide)
    out[0:KEEP, :] = kept[:, columns]
    out[KEEP:, :] = jnp.zeros((out.shape[0] - KEEP, wide), BF)

    def put(block, at):
        rows = lax.broadcasted_iota(jnp.int32, (block.shape[0], 1), 0) + at
        window = pl.ds(at, block.shape[0])
        out[window, :] = jnp.where(rows < count, out[window, :], block)

    put(early[:, columns], first)
    sources = [(late, c) for late, cut in zip(lates, cuts) for c in range(0, cut, wide)]
    for i, (late, c) in enumerate(sources):

        @pl.when(step == i)
        def _():
            put(late[:, c : c + wide], pl.multiple_of(first + EARLY, TILE))


def swapped(block, axis, distance):
    n = lax.axis_size(axis)
    return lax.ppermute(block, axis, [(i, i ^ distance) for i in range(n)])


def after(value, *others):
    return lax.optimization_barrier((value, *others))[0]


def shards(hidden_pre, cotangent, down_weight, layer_scale, crop_lengths, crop_moves):
    hidden_pre, cotangent, layer_scale = (
        pltpu.with_memory_space_constraint(x, pltpu.HBM) for x in (hidden_pre, cotangent, layer_scale)
    )
    home, ff = hidden_pre.shape
    width = cotangent.shape[1]
    features = down_weight.shape[0]
    half = width // 2
    part = ff // 3
    others = EARLY + KEEP
    n = lax.axis_size("dp")
    d = lax.axis_index("dp").astype(jnp.int32)
    t = lax.axis_index("tensor").astype(jnp.int32)
    column = lax.broadcasted_iota(jnp.int32, (1, n), 1)
    own = jnp.where(column == 0, d, jnp.where(column == 1, t, 0))
    meta = jnp.concatenate([crop_lengths.T, crop_moves.T, own])
    vmem = pltpu.VMEM
    sems = pltpu.SemaphoreType.DMA

    def gelu(meta, pick, base, columns):
        rows, block = pick.shape[0], 256
        return kernel_call(
            functools.partial(gelu_kernel, base, block),
            [shape(rows, columns), shape(rows, columns, F32)],
            [IN_VMEM] * 2, [IN_VMEM] * 2, [vmem((rows, block), F32)],
        )(meta, pick, pre)

    def weight_first(meta, act_moved, act_kept):
        return kernel_call(
            functools.partial(weight_kernel, 4),
            [shape(width, part)] * 2 + [shape(width, part, F32)] * 2
            + [shape(features, LATE), shape(features, others)],
            [IN_VMEM] * 10, [IN_VMEM] * 6,
        )(meta, *lates, *rests, act_moved, act_kept)

    def weight_again(meta, base, act_moved, act_kept, count):
        rows = features // 2 // count
        return kernel_call(
            functools.partial(again_kernel, base),
            [shape(rows, part)] * count + [shape(rows, part, F32)] * count,
            [IN_VMEM] * 4, [IN_VMEM] * (2 * count),
        )(meta, *lhs, act_moved, act_kept)

    def grads(meta, pieces, first_row, first_slope, rows, base, slopes, cuts):
        return kernel_call(
            functools.partial(grad_kernel, first_row, first_slope, base, len(slopes), 256),
            [shape(rows, c) for c in cuts], [IN_VMEM] * (5 + len(slopes)), [IN_VMEM] * len(cuts),
            [vmem((rows, features), BF)],
        )(meta, *pieces, down_weight, *slopes)

    def near_step(meta, keeps, gots):
        count = len(keeps)
        return kernel_call(
            functools.partial(near_kernel, count),
            [shape(width, part), shape(width, part, F32)], [IN_VMEM] * (2 * count), [IN_VMEM] * 2,
        )(meta, *keeps, *gots)

    def far_step(meta, mine, got):
        return kernel_call(
            far_kernel, [shape(half, part), shape(half, part, F32)], [IN_VMEM] * 2, [IN_VMEM] * 2
        )(meta, mine, got)

    late, rest, early, late_pick, rest_pick, pre = kernel_call(
        first_kernel,
        [shape(LATE, width), shape(others, width), shape(EARLY, width + ff),
         shape(LATE, home), shape(others, home), shape(home, ff)],
        [IN_HBM] * 3, [IN_VMEM] * 6,
        [vmem((home, width), BF), vmem((features,), F32), sems((3,))],
    )(meta, cotangent, layer_scale, hidden_pre)
    arrived_early = swapped(early, "dp", n // 2)

    late_c, late_y = swapped(late, "tensor", 1), swapped(late, "tensor", 2)
    rest_c, rest_y = swapped(rest, "tensor", 1), swapped(rest, "tensor", 2)
    act_la, der_la = gelu(after(meta, late), late_pick, 0, part)
    act_ra, der_ra = gelu(after(meta, act_la), rest_pick, 0, part)
    late_y = after(late_y, act_ra, late_c, rest_c, arrived_early)
    late_yc = swapped(late_y, "tensor", 1)
    lates = (late, late_c, late_y, late_yc)

    (moving_a,) = grads(after(meta, late_y), lates, 0, 0, LATE, 0, (der_la,), (part,))
    arrived_a = swapped(moving_a, "dp", n // 2)

    rest_y = after(rest_y, moving_a)
    rest_yc = swapped(rest_y, "tensor", 1)
    rests = (rest, rest_c, rest_y, rest_yc)
    *sends_a, keep_01, keep_23, lhs_moved, lhs_kept = weight_first(after(meta, moving_a), act_la, act_ra)
    lhs = (lhs_moved, lhs_kept)
    gots_a = [swapped(send, "dp", 1) for send in sends_a]

    act_l, der_l = gelu(after(meta, keep_01), late_pick, part, 2 * part)
    moving_b, moving_c = grads(after(meta, act_l), lates, 0, 0, LATE, part, (der_l,), (part, part))
    act_rb, der_rb = gelu(after(meta, moving_b, gots_a[0]), rest_pick, part, part)
    send_b, keep_b = weight_again(after(meta, act_rb, arrived_a), 0, act_l, act_rb, 1)
    got_b = swapped(send_b, "dp", 1)
    arrived_b = swapped(after(moving_b, send_b), "dp", n // 2)

    out_na, mine_a = near_step(after(meta, send_b), (keep_01, keep_23), gots_a)
    got_na = swapped(out_na, "dp", 2)
    early_sent = after(arrived_early[:, :width], out_na)
    early_c, early_y = swapped(early_sent, "tensor", 1), swapped(early_sent, "tensor", 2)
    act_rc, der_rc = gelu(after(meta, out_na), rest_pick, 2 * part, part)
    early_y = after(early_y, early_c, act_rc)
    early_yc = swapped(early_y, "tensor", 1)
    *sends_c, keep_c01, keep_c23 = weight_again(after(meta, early_yc), part, act_l, act_rc, 2)
    gots_c = [swapped(send, "dp", 1) for send in sends_c]

    out_nb, mine_b = near_step(after(meta, keep_c01, arrived_b, got_na), (keep_b,), (got_b,))
    got_nb = swapped(out_nb, "dp", 2)
    arrived_c = swapped(after(moving_c, out_nb), "dp", n // 2)
    out_fa, own_a = far_step(after(meta, out_nb), mine_a, got_na)
    got_fa = swapped(out_fa, "dp", 4)
    (kept_grad,) = grads(after(meta, out_fa), rests, EARLY, EARLY, KEEP, 0, (der_ra, der_rb, der_rc), (ff,))
    early_grad = kernel_call(
        functools.partial(early_kernel, 256), shape(EARLY, ff), [IN_VMEM] * 5, IN_VMEM,
        [vmem((EARLY, features), BF), vmem((EARLY, 256), F32)],
    )(after(meta, kept_grad), arrived_early, early_c, early_y, early_yc, down_weight)

    out_nc, mine_c = near_step(after(meta, early_grad), (keep_c01, keep_c23), gots_c)
    got_nc = swapped(out_nc, "dp", 2)
    out_fb, own_b = far_step(after(meta, out_nc), mine_b, got_nb)
    got_fb = swapped(out_fb, "dp", 4)
    out_fc, own_c = far_step(after(meta, out_fb), mine_c, got_nc)
    got_fc = swapped(out_fc, "dp", 4)
    got_fa, got_fb = after(got_fa, out_fc), after(got_fb, out_fc)
    total = [a + b.astype(F32) for a, b in ((own_a, got_fa), (own_b, got_fb), (own_c, got_fc))]
    down_grad = jnp.concatenate(total, axis=1) / math.sqrt(n * home)

    hidden_grad = kernel_call(
        functools.partial(place_kernel, (part,) * 3), shape(BAL, ff), [IN_VMEM] * 5,
        pl.BlockSpec((BAL, 256), lambda i, *_: (0, i)), grid=(ff // 256,),
    )(after(meta, out_fc), kept_grad, early_grad, arrived_a, arrived_b, arrived_c)
    return (hidden_grad, down_grad)


def solution(mesh):
    pairs_and_fours = (mesh.shape["dp"], mesh.shape["tensor"]) == (8, 4)
    return jax.shard_map(
        shards if pairs_and_fours else general_shards,
        mesh=mesh,
        in_specs=(P("dp", "tensor"), P("dp", "tensor"), P(None, "tensor"), P(), P(), P()),
        out_specs=(P("dp", "tensor"), P("dp", "tensor")),
        check_vma=False,
    )


def shifted(block, axis, distance):
    devices = range(lax.axis_size(axis))
    route = [((i - distance) % len(devices), i) for i in devices]
    return lax.ppermute(block, axis, route)


def crop_rows(row_total, crop_sizes, crop_starts):
    crop_ends = jnp.cumsum(crop_sizes)
    crop_begins = crop_ends - crop_sizes
    target_rows = jnp.arange(row_total, dtype=jnp.int32)[:, None]
    inside_crop = (target_rows >= crop_begins[None, :]) & (target_rows < crop_ends[None, :])
    source_rows = jnp.sum(
        jnp.where(inside_crop, crop_starts[None, :] + target_rows - crop_begins[None, :], 0), axis=1
    )
    return (source_rows, jnp.any(inside_crop, axis=1))


def select_rows(row_block, source_rows, valid_rows):
    taken = jnp.take(row_block, source_rows, axis=0)
    return jnp.where(valid_rows[:, None], taken, jnp.zeros((), row_block.dtype))


def gelu_parts(pre_act):
    cumulative = 0.5 * (1.0 + jax.scipy.special.erf(pre_act * inv_root_two))
    activated = pre_act * cumulative
    derivative = cumulative + pre_act * jnp.exp(-0.5 * pre_act * pre_act) * inv_root_tau
    return (activated, derivative)


def local_grads(pre_rows, cot_part, live_rows, layer_scale, down_weight, home_rows):
    cot_full = lax.all_gather(cot_part, "tensor", axis=1, tiled=True)
    scaled = (cot_full.astype(F32) * layer_scale[None, :]).astype(BF)
    activated, derivative = gelu_parts(pre_rows.astype(F32))
    activation = jnp.where(live_rows[:, None], activated, 0.0).astype(BF)
    backward = jnp.dot(scaled, down_weight, preferred_element_type=F32) * derivative
    gradient_rows = jnp.where(live_rows[:, None], backward, 0.0).astype(BF)
    weight_grad = lax.psum_scatter(
        lax.dot_general(scaled, activation, (((0,), (0,)), ((), ())), preferred_element_type=F32),
        "dp",
        scatter_dimension=0,
        tiled=True,
    )
    return (gradient_rows, weight_grad / math.sqrt(lax.axis_size("dp") * home_rows))


def general_shards(hidden_pre, cotangent, down_weight, layer_scale, crop_lengths, crop_moves):
    devices = lax.axis_size("dp")
    half_axis = devices // 2
    device_index = lax.axis_index("dp")
    partner_index = (device_index + half_axis) % devices
    own_lengths = lax.dynamic_index_in_dim(crop_lengths, device_index, 0, keepdims=False)
    own_moves = lax.dynamic_index_in_dim(crop_moves, device_index, 0, keepdims=False)
    partner_lengths = lax.dynamic_index_in_dim(crop_lengths, partner_index, 0, keepdims=False)
    partner_moves = lax.dynamic_index_in_dim(crop_moves, partner_index, 0, keepdims=False)
    home_rows = hidden_pre.shape[0]
    own_starts = jnp.cumsum(own_lengths) - own_lengths
    sent_sizes = own_lengths * own_moves
    kept_sizes = own_lengths * (1 - own_moves)
    arrived = jnp.sum(partner_lengths * partner_moves)
    send_source, send_valid = crop_rows(SEND, sent_sizes, own_starts)
    keep_sizes = jnp.concatenate([kept_sizes, arrived[None]])
    keep_starts = jnp.concatenate([own_starts, jnp.full((1,), home_rows, jnp.int32)])
    keep_source, keep_valid = crop_rows(BAL, keep_sizes, keep_starts)
    live_home = jnp.arange(home_rows, dtype=jnp.int32) < jnp.sum(own_lengths)
    gradient_rows, weight_grad = local_grads(
        hidden_pre, cotangent, live_home, layer_scale, down_weight, home_rows
    )
    outgoing = select_rows(gradient_rows, send_source, send_valid)
    incoming = shifted(outgoing, "dp", half_axis)
    balanced = select_rows(jnp.concatenate([gradient_rows, incoming], 0), keep_source, keep_valid)
    return (balanced, weight_grad)
```

```python
import functools
import math

import jax
import jax.numpy as jnp
from jax import lax
from jax.experimental import pallas as pl
from jax.experimental.pallas import tpu as pltpu
from jax.sharding import PartitionSpec as P

SEND = 528
KEEP = 528
TILE = 16
EARLY = 96
LATE = SEND - EARLY
SLOTS = 4
BAL = 720
BF = jnp.bfloat16
F32 = jnp.float32

inv_root_two = 0.7071067811865476
inv_root_tau = 0.3989422804014327


def kernel_call(kernel, out_shape, in_specs, out_specs, scratch=(), grid=(1,)):
    return pl.pallas_call(
        kernel,
        grid_spec=pltpu.PrefetchScalarGridSpec(
            num_scalar_prefetch=1,
            grid=grid,
            in_specs=in_specs,
            out_specs=out_specs,
            scratch_shapes=list(scratch),
        ),
        out_shape=out_shape,
        cost_estimate=pl.CostEstimate(flops=1, bytes_accessed=1, transcendentals=0),
        compiler_params=pltpu.CompilerParams(vmem_limit_bytes=16 * 1024 * 1024),
    )


IN_VMEM = pl.BlockSpec(memory_space=pltpu.VMEM)
IN_HBM = pl.BlockSpec(memory_space=pltpu.HBM)


def shape(a, b, dtype=BF):
    return jax.ShapeDtypeStruct((a, b), dtype)


def lengths_of(meta, d):
    return [meta[j, d] for j in range(SLOTS)]


def moves_of(meta, d):
    return [meta[SLOTS + j, d] for j in range(SLOTS)]


def dp_at(meta):
    return meta[2 * SLOTS, 0]


def tensor_at(meta):
    return meta[2 * SLOTS, 1]


def kept_total(meta, d):
    return sum(a * (1 - b) for a, b in zip(lengths_of(meta, d), moves_of(meta, d)))


def picks(meta, moved, first, rows, home):
    d = dp_at(meta)
    at = lax.broadcasted_iota(jnp.int32, (rows, 1), 0) - first
    source = jnp.full((rows, 1), -1, jnp.int32)
    begin = jnp.int32(0)
    start = jnp.int32(0)
    for length, move in zip(lengths_of(meta, d), moves_of(meta, d)):
        size = length * (move if moved else 1 - move)
        inside = (at >= begin) & (at < begin + size)
        source = jnp.where(inside, at + (start - begin), source)
        begin = begin + size
        start = start + length
    columns = lax.broadcasted_iota(jnp.int32, (rows, home), 1)
    return jnp.where(columns == source, 1.0, 0.0).astype(BF)


def sent_first(meta):
    n = meta.shape[1]
    partner = lax.rem(dp_at(meta) + n // 2, n)
    return lax.rem(kept_total(meta, partner), TILE)


def early_picks(meta, home):
    return picks(meta, True, sent_first(meta), EARLY, home)


def late_picks(meta, home):
    return picks(meta, True, sent_first(meta) - EARLY, LATE, home)


def kept_picks(meta, home):
    return picks(meta, False, 0, KEEP, home)


def scaled_rows(meta, pick, cot, scale):
    width = cot.shape[1]
    rows = jnp.dot(pick, cot[...], preferred_element_type=F32)
    own = scale[pl.ds(pl.multiple_of(tensor_at(meta) * width, 128), width)]
    return (rows * own[None, :]).astype(BF)


def first_kernel(
    meta, cot_hbm, scale_hbm, pre_hbm, late_out, rest_out, early_out, late_pick, rest_pick, pre, cot, scale, sems
):
    home, width = cot.shape
    pairs = ((cot_hbm, cot), (scale_hbm, scale), (pre_hbm, pre))
    copies = [pltpu.make_async_copy(a, b, sems.at[i]) for i, (a, b) in enumerate(pairs)]
    for copy in copies:
        copy.start()
    early = early_picks(meta, home)
    late = late_picks(meta, home)
    kept = kept_picks(meta, home)
    late_pick[...] = late
    rest_pick[0:EARLY, :] = early
    rest_pick[EARLY:, :] = kept
    copies[0].wait()
    copies[1].wait()
    early_rows = scaled_rows(meta, early, cot, scale)
    early_out[:, :width] = early_rows
    late_out[...] = scaled_rows(meta, late, cot, scale)
    rest_out[0:EARLY, :] = early_rows
    rest_out[EARLY:, :] = scaled_rows(meta, kept, cot, scale)
    copies[2].wait()
    early_out[:, width:] = jnp.dot(early, pre[...], preferred_element_type=F32).astype(BF)


def gelu_and_slope(x):
    cumulative = 0.5 * (1.0 + lax.erf(x * inv_root_two))
    return x * cumulative, cumulative + x * jnp.exp(-0.5 * x * x) * inv_root_tau


def cut_at(widths, block):
    return [
        (i, c, min(block, width - c)) for i, width in enumerate(widths) for c in range(0, width, block)
    ]


def gelu_kernel(base, block, meta, pick, pre, act_out, der_out, rows_f32):
    rows = pick.shape[0]
    step = next(TILE * k for k in (3, 4, 2, 1) if rows % (TILE * k) == 0)
    for at in range(0, act_out.shape[1], block):
        source = slice(base + at, base + at + block)
        rows_f32[...] = jnp.dot(pick[...], pre[:, source], preferred_element_type=F32)
        columns = slice(at, at + block)

        def body(k, _):
            part = pl.ds(pl.multiple_of(k * step, step), step)
            value, slope = gelu_and_slope(rows_f32[part, :])
            act_out[part, columns] = value.astype(BF)
            der_out[part, columns] = slope
            return 0

        lax.fori_loop(0, rows // step, body, 0)


def assemble(meta, pieces, first_row, lhs):
    rows = lhs.shape[0]
    width = pieces[1].shape[1]
    for j, piece in enumerate(pieces):
        columns = pl.ds(pl.multiple_of((tensor_at(meta) ^ j) * width, 128), width)
        lhs[:, columns] = piece[first_row : first_row + rows, 0:width]


def grad_kernel(first_row, first_slope, base, slope_count, block, meta, p0, p1, p2, p3, weight, *rest):
    slopes, outs, lhs = rest[:slope_count], rest[slope_count:-1], rest[-1]
    rows = lhs.shape[0]
    assemble(meta, (p0, p1, p2, p3), first_row, lhs)
    parts = slopes if slope_count > len(outs) else outs
    starts = [sum(part.shape[1] for part in parts[:i]) for i in range(len(parts))]
    slope_rows = slice(first_slope, first_slope + rows)
    for i, c, wide in cut_at([part.shape[1] for part in parts], block):
        at = starts[i] + c
        inside, whole_at = slice(c, c + wide), slice(at, at + wide)
        slope = slopes[i][slope_rows, inside] if slope_count == len(parts) else slopes[0][slope_rows, whole_at]
        columns = slice(base + at, base + at + wide)
        value = (jnp.dot(lhs[...], weight[:, columns], preferred_element_type=F32) * slope).astype(BF)
        if len(outs) == len(parts):
            outs[i][:, inside] = value
        else:
            outs[0][:, whole_at] = value


def early_kernel(block, meta, own, p1, p2, p3, weight, out, lhs, acc):
    width = p1.shape[1]
    assemble(meta, (own, p1, p2, p3), 0, lhs)
    for at in range(0, out.shape[1], block):
        columns = slice(at, at + block)
        acc[...] = jnp.dot(lhs[...], weight[:, columns], preferred_element_type=F32)

        def body(k, _):
            rows = pl.ds(pl.multiple_of(k * TILE, TILE), TILE)
            _, slope = gelu_and_slope(own[rows, width + at : width + at + block].astype(F32))
            out[rows, columns] = (acc[rows, :] * slope).astype(BF)
            return 0

        lax.fori_loop(0, EARLY // TILE, body, 0)


def weight_kernel(count, meta, *refs):
    moved, kept = refs[:count], refs[count : 2 * count]
    act_moved, act_kept, *outs, lhs_moved, lhs_kept = refs[2 * count :]
    half = moved[0].shape[1] // 2
    mine = dp_at(meta) % 2 == 0
    for i in range(count):
        for piece, lhs in ((moved[i], lhs_moved), (kept[i], lhs_kept)):
            both = piece[...].T
            lo, hi = both[:half], both[half:]
            lhs[i * half : (i + 1) * half, :] = jnp.where(mine, hi, lo)
            lhs[(count + i) * half : (count + i + 1) * half, :] = jnp.where(mine, lo, hi)
    again_kernel(0, meta, lhs_moved, lhs_kept, act_moved, act_kept, *outs)


def again_kernel(base, meta, lhs_moved, lhs_kept, act_moved, act_kept, *outs):
    columns = slice(base, base + act_kept.shape[1])
    step = lhs_moved.shape[0] // 4
    at = 0
    for out in outs:
        for i in range(0, out.shape[0], step):
            part = slice(at, at + step)
            value = jnp.dot(lhs_moved[part, :], act_moved[:, columns], preferred_element_type=F32)
            value += jnp.dot(lhs_kept[part, :], act_kept[...], preferred_element_type=F32)
            out[i : i + step, :] = value.astype(out.dtype)
            at += step


def near_kernel(count, meta, *refs):
    keeps, gots, (out, mine) = refs[:count], refs[count : 2 * count], refs[2 * count :]
    half = out.shape[0] // 2
    parts = [(k, g, at) for k, g in zip(keeps, gots) for at in range(0, k.shape[0], half)]
    keeps_even = (dp_at(meta) // 2 + tensor_at(meta)) % 2 == 0
    step = 2 * TILE

    for pair in range(2):
        (k0, g0, a0), (k1, g1, a1) = parts[2 * pair], parts[2 * pair + 1]

        def body(i, _):
            def rows(at):
                return pl.ds(pl.multiple_of(at + i * step, TILE), step)

            even = k0[rows(a0), :] + g0[rows(a0), :].astype(F32)
            odd = k1[rows(a1), :] + g1[rows(a1), :].astype(F32)
            out[rows(pair * half), :] = jnp.where(keeps_even, odd, even).astype(BF)
            mine[rows(pair * half), :] = jnp.where(keeps_even, even, odd)
            return 0

        lax.fori_loop(0, half // step, body, 0)


def far_kernel(meta, held, got, out, mine):
    half = out.shape[0]
    keeps_first = (dp_at(meta) // 4 + tensor_at(meta) // 2) % 2 == 0
    step = 2 * TILE

    def body(i, _):
        first = pl.ds(pl.multiple_of(i * step, TILE), step)
        second = pl.ds(pl.multiple_of(half + i * step, TILE), step)
        a = held[first, :] + got[first, :].astype(F32)
        b = held[second, :] + got[second, :].astype(F32)
        out[first, :] = jnp.where(keeps_first, b, a).astype(BF)
        mine[first, :] = jnp.where(keeps_first, a, b)
        return 0

    lax.fori_loop(0, half // step, body, 0)


def place_kernel(cuts, meta, kept, early, *rest):
    lates, out = rest[:-1], rest[-1]
    count = kept_total(meta, dp_at(meta))
    first = jnp.minimum(count - lax.rem(count, TILE), BAL - SEND)
    first = pl.multiple_of(first, TILE)
    wide = out.shape[1]
    step = pl.program_id(0)
    columns = pl.ds(pl.multiple_of(step * wide, wide), wide)
    out[0:KEEP, :] = kept[:, columns]
    out[KEEP:, :] = jnp.zeros((out.shape[0] - KEEP, wide), BF)

    def put(block, at):
        rows = lax.broadcasted_iota(jnp.int32, (block.shape[0], 1), 0) + at
        window = pl.ds(at, block.shape[0])
        out[window, :] = jnp.where(rows < count, out[window, :], block)

    put(early[:, columns], first)
    sources = [(late, c) for late, cut in zip(lates, cuts) for c in range(0, cut, wide)]
    for i, (late, c) in enumerate(sources):

        @pl.when(step == i)
        def _():
            put(late[:, c : c + wide], pl.multiple_of(first + EARLY, TILE))


def swapped(block, axis, distance):
    n = lax.axis_size(axis)
    return lax.ppermute(block, axis, [(i, i ^ distance) for i in range(n)])


def after(value, *others):
    return lax.optimization_barrier((value, *others))[0]


def shards(hidden_pre, cotangent, down_weight, layer_scale, crop_lengths, crop_moves):
    hidden_pre, cotangent, layer_scale = (
        pltpu.with_memory_space_constraint(x, pltpu.HBM) for x in (hidden_pre, cotangent, layer_scale)
    )
    home, ff = hidden_pre.shape
    width = cotangent.shape[1]
    features = down_weight.shape[0]
    half = width // 2
    part = ff // 3
    others = EARLY + KEEP
    n = lax.axis_size("dp")
    d = lax.axis_index("dp").astype(jnp.int32)
    t = lax.axis_index("tensor").astype(jnp.int32)
    column = lax.broadcasted_iota(jnp.int32, (1, n), 1)
    own = jnp.where(column == 0, d, jnp.where(column == 1, t, 0))
    meta = jnp.concatenate([crop_lengths.T, crop_moves.T, own])
    vmem = pltpu.VMEM
    sems = pltpu.SemaphoreType.DMA

    def gelu(meta, pick, base, columns):
        rows, block = pick.shape[0], 256
        return kernel_call(
            functools.partial(gelu_kernel, base, block),
            [shape(rows, columns), shape(rows, columns, F32)],
            [IN_VMEM] * 2, [IN_VMEM] * 2, [vmem((rows, block), F32)],
        )(meta, pick, pre)

    def weight_first(meta, act_moved, act_kept):
        return kernel_call(
            functools.partial(weight_kernel, 4),
            [shape(width, part)] * 2 + [shape(width, part, F32)] * 2
            + [shape(features, LATE), shape(features, others)],
            [IN_VMEM] * 10, [IN_VMEM] * 6,
        )(meta, *lates, *rests, act_moved, act_kept)

    def weight_again(meta, base, act_moved, act_kept, count):
        rows = features // 2 // count
        return kernel_call(
            functools.partial(again_kernel, base),
            [shape(rows, part)] * count + [shape(rows, part, F32)] * count,
            [IN_VMEM] * 4, [IN_VMEM] * (2 * count),
        )(meta, *lhs, act_moved, act_kept)

    def grads(meta, pieces, first_row, first_slope, rows, base, slopes, cuts):
        return kernel_call(
            functools.partial(grad_kernel, first_row, first_slope, base, len(slopes), 256),
            [shape(rows, c) for c in cuts], [IN_VMEM] * (5 + len(slopes)), [IN_VMEM] * len(cuts),
            [vmem((rows, features), BF)],
        )(meta, *pieces, down_weight, *slopes)

    def near_step(meta, keeps, gots):
        count = len(keeps)
        return kernel_call(
            functools.partial(near_kernel, count),
            [shape(width, part), shape(width, part, F32)], [IN_VMEM] * (2 * count), [IN_VMEM] * 2,
        )(meta, *keeps, *gots)

    def far_step(meta, mine, got):
        return kernel_call(
            far_kernel, [shape(half, part), shape(half, part, F32)], [IN_VMEM] * 2, [IN_VMEM] * 2
        )(meta, mine, got)

    late, rest, early, late_pick, rest_pick, pre = kernel_call(
        first_kernel,
        [shape(LATE, width), shape(others, width), shape(EARLY, width + ff),
         shape(LATE, home), shape(others, home), shape(home, ff)],
        [IN_HBM] * 3, [IN_VMEM] * 6,
        [vmem((home, width), BF), vmem((features,), F32), sems((3,))],
    )(meta, cotangent, layer_scale, hidden_pre)
    arrived_early = swapped(early, "dp", n // 2)

    late_c, late_y = swapped(late, "tensor", 1), swapped(late, "tensor", 2)
    rest_c, rest_y = swapped(rest, "tensor", 1), swapped(rest, "tensor", 2)
    act_la, der_la = gelu(after(meta, late), late_pick, 0, part)
    act_ra, der_ra = gelu(after(meta, act_la), rest_pick, 0, part)
    late_y = after(late_y, act_ra, late_c, rest_c, arrived_early)
    late_yc = swapped(late_y, "tensor", 1)
    lates = (late, late_c, late_y, late_yc)

    (moving_a,) = grads(after(meta, late_y), lates, 0, 0, LATE, 0, (der_la,), (part,))
    arrived_a = swapped(moving_a, "dp", n // 2)

    rest_y = after(rest_y, moving_a)
    rest_yc = swapped(rest_y, "tensor", 1)
    rests = (rest, rest_c, rest_y, rest_yc)
    *sends_a, keep_01, keep_23, lhs_moved, lhs_kept = weight_first(after(meta, moving_a), act_la, act_ra)
    lhs = (lhs_moved, lhs_kept)
    gots_a = [swapped(send, "dp", 1) for send in sends_a]

    act_l, der_l = gelu(after(meta, keep_01), late_pick, part, 2 * part)
    moving_b, moving_c = grads(after(meta, act_l), lates, 0, 0, LATE, part, (der_l,), (part, part))
    act_rb, der_rb = gelu(after(meta, moving_b, gots_a[0]), rest_pick, part, part)
    send_b, keep_b = weight_again(after(meta, act_rb, arrived_a), 0, act_l, act_rb, 1)
    got_b = swapped(send_b, "dp", 1)
    arrived_b = swapped(after(moving_b, send_b), "dp", n // 2)

    out_na, mine_a = near_step(after(meta, send_b), (keep_01, keep_23), gots_a)
    got_na = swapped(out_na, "dp", 2)
    early_sent = after(arrived_early[:, :width], out_na)
    early_c, early_y = swapped(early_sent, "tensor", 1), swapped(early_sent, "tensor", 2)
    act_rc, der_rc = gelu(after(meta, out_na), rest_pick, 2 * part, part)
    early_y = after(early_y, early_c, act_rc)
    early_yc = swapped(early_y, "tensor", 1)
    *sends_c, keep_c01, keep_c23 = weight_again(after(meta, early_yc), part, act_l, act_rc, 2)
    gots_c = [swapped(send, "dp", 1) for send in sends_c]

    out_nb, mine_b = near_step(after(meta, keep_c01, arrived_b, got_na), (keep_b,), (got_b,))
    got_nb = swapped(out_nb, "dp", 2)
    arrived_c = swapped(after(moving_c, out_nb), "dp", n // 2)
    out_fa, own_a = far_step(after(meta, out_nb), mine_a, got_na)
    got_fa = swapped(out_fa, "dp", 4)
    (kept_grad,) = grads(after(meta, out_fa), rests, EARLY, EARLY, KEEP, 0, (der_ra, der_rb, der_rc), (ff,))
    early_grad = kernel_call(
        functools.partial(early_kernel, 256), shape(EARLY, ff), [IN_VMEM] * 5, IN_VMEM,
        [vmem((EARLY, features), BF), vmem((EARLY, 256), F32)],
    )(after(meta, kept_grad), arrived_early, early_c, early_y, early_yc, down_weight)

    out_nc, mine_c = near_step(after(meta, early_grad), (keep_c01, keep_c23), gots_c)
    got_nc = swapped(out_nc, "dp", 2)
    out_fb, own_b = far_step(after(meta, out_nc), mine_b, got_nb)
    got_fb = swapped(out_fb, "dp", 4)
    out_fc, own_c = far_step(after(meta, out_fb), mine_c, got_nc)
    got_fc = swapped(out_fc, "dp", 4)
    got_fa, got_fb = after(got_fa, out_fc), after(got_fb, out_fc)
    total = [a + b.astype(F32) for a, b in ((own_a, got_fa), (own_b, got_fb), (own_c, got_fc))]
    down_grad = jnp.concatenate(total, axis=1) / math.sqrt(n * home)

    hidden_grad = kernel_call(
        functools.partial(place_kernel, (part,) * 3), shape(BAL, ff), [IN_VMEM] * 5,
        pl.BlockSpec((BAL, 256), lambda i, *_: (0, i)), grid=(ff // 256,),
    )(after(meta, out_fc), kept_grad, early_grad, arrived_a, arrived_b, arrived_c)
    return (hidden_grad, down_grad)


def solution(mesh):
    pairs_and_fours = (mesh.shape["dp"], mesh.shape["tensor"]) == (8, 4)
    return jax.shard_map(
        shards if pairs_and_fours else general_shards,
        mesh=mesh,
        in_specs=(P("dp", "tensor"), P("dp", "tensor"), P(None, "tensor"), P(), P(), P()),
        out_specs=(P("dp", "tensor"), P("dp", "tensor")),
        check_vma=False,
    )


def shifted(block, axis, distance):
    devices = range(lax.axis_size(axis))
    route = [((i - distance) % len(devices), i) for i in devices]
    return lax.ppermute(block, axis, route)


def crop_rows(row_total, crop_sizes, crop_starts):
    crop_ends = jnp.cumsum(crop_sizes)
    crop_begins = crop_ends - crop_sizes
    target_rows = jnp.arange(row_total, dtype=jnp.int32)[:, None]
    inside_crop = (target_rows >= crop_begins[None, :]) & (target_rows < crop_ends[None, :])
    source_rows = jnp.sum(
        jnp.where(inside_crop, crop_starts[None, :] + target_rows - crop_begins[None, :], 0), axis=1
    )
    return (source_rows, jnp.any(inside_crop, axis=1))


def select_rows(row_block, source_rows, valid_rows):
    taken = jnp.take(row_block, source_rows, axis=0)
    return jnp.where(valid_rows[:, None], taken, jnp.zeros((), row_block.dtype))


def gelu_parts(pre_act):
    cumulative = 0.5 * (1.0 + jax.scipy.special.erf(pre_act * inv_root_two))
    activated = pre_act * cumulative
    derivative = cumulative + pre_act * jnp.exp(-0.5 * pre_act * pre_act) * inv_root_tau
    return (activated, derivative)


def local_grads(pre_rows, cot_part, live_rows, layer_scale, down_weight, home_rows):
    cot_full = lax.all_gather(cot_part, "tensor", axis=1, tiled=True)
    scaled = (cot_full.astype(F32) * layer_scale[None, :]).astype(BF)
    activated, derivative = gelu_parts(pre_rows.astype(F32))
    activation = jnp.where(live_rows[:, None], activated, 0.0).astype(BF)
    backward = jnp.dot(scaled, down_weight, preferred_element_type=F32) * derivative
    gradient_rows = jnp.where(live_rows[:, None], backward, 0.0).astype(BF)
    weight_grad = lax.psum_scatter(
        lax.dot_general(scaled, activation, (((0,), (0,)), ((), ())), preferred_element_type=F32),
        "dp",
        scatter_dimension=0,
        tiled=True,
    )
    return (gradient_rows, weight_grad / math.sqrt(lax.axis_size("dp") * home_rows))


def general_shards(hidden_pre, cotangent, down_weight, layer_scale, crop_lengths, crop_moves):
    devices = lax.axis_size("dp")
    half_axis = devices // 2
    device_index = lax.axis_index("dp")
    partner_index = (device_index + half_axis) % devices
    own_lengths = lax.dynamic_index_in_dim(crop_lengths, device_index, 0, keepdims=False)
    own_moves = lax.dynamic_index_in_dim(crop_moves, device_index, 0, keepdims=False)
    partner_lengths = lax.dynamic_index_in_dim(crop_lengths, partner_index, 0, keepdims=False)
    partner_moves = lax.dynamic_index_in_dim(crop_moves, partner_index, 0, keepdims=False)
    home_rows = hidden_pre.shape[0]
    own_starts = jnp.cumsum(own_lengths) - own_lengths
    sent_sizes = own_lengths * own_moves
    kept_sizes = own_lengths * (1 - own_moves)
    arrived = jnp.sum(partner_lengths * partner_moves)
    send_source, send_valid = crop_rows(SEND, sent_sizes, own_starts)
    keep_sizes = jnp.concatenate([kept_sizes, arrived[None]])
    keep_starts = jnp.concatenate([own_starts, jnp.full((1,), home_rows, jnp.int32)])
    keep_source, keep_valid = crop_rows(BAL, keep_sizes, keep_starts)
    live_home = jnp.arange(home_rows, dtype=jnp.int32) < jnp.sum(own_lengths)
    gradient_rows, weight_grad = local_grads(
        hidden_pre, cotangent, live_home, layer_scale, down_weight, home_rows
    )
    outgoing = select_rows(gradient_rows, send_source, send_valid)
    incoming = shifted(outgoing, "dp", half_axis)
    balanced = select_rows(jnp.concatenate([gradient_rows, incoming], 0), keep_source, keep_valid)
    return (balanced, weight_grad)
```

```python
import functools
import math

import jax
import jax.numpy as jnp
from jax import lax
from jax.experimental import pallas as pl
from jax.experimental.pallas import tpu as pltpu
from jax.sharding import PartitionSpec as P

SEND = 528
KEEP = 528
TILE = 16
EARLY = 96
LATE = SEND - EARLY
SLOTS = 4
BAL = 720
BF = jnp.bfloat16
F32 = jnp.float32

inv_root_two = 0.7071067811865476
inv_root_tau = 0.3989422804014327


def kernel_call(kernel, out_shape, in_specs, out_specs, scratch=(), grid=(1,)):
    return pl.pallas_call(
        kernel,
        grid_spec=pltpu.PrefetchScalarGridSpec(
            num_scalar_prefetch=1,
            grid=grid,
            in_specs=in_specs,
            out_specs=out_specs,
            scratch_shapes=list(scratch),
        ),
        out_shape=out_shape,
        cost_estimate=pl.CostEstimate(flops=1, bytes_accessed=1, transcendentals=0),
        compiler_params=pltpu.CompilerParams(vmem_limit_bytes=16 * 1024 * 1024),
    )


IN_VMEM = pl.BlockSpec(memory_space=pltpu.VMEM)
IN_HBM = pl.BlockSpec(memory_space=pltpu.HBM)


def shape(a, b, dtype=BF):
    return jax.ShapeDtypeStruct((a, b), dtype)


def lengths_of(meta, d):
    return [meta[j, d] for j in range(SLOTS)]


def moves_of(meta, d):
    return [meta[SLOTS + j, d] for j in range(SLOTS)]


def dp_at(meta):
    return meta[2 * SLOTS, 0]


def tensor_at(meta):
    return meta[2 * SLOTS, 1]


def kept_total(meta, d):
    return sum(a * (1 - b) for a, b in zip(lengths_of(meta, d), moves_of(meta, d)))


def picks(meta, moved, first, rows, home):
    d = dp_at(meta)
    at = lax.broadcasted_iota(jnp.int32, (rows, 1), 0) - first
    source = jnp.full((rows, 1), -1, jnp.int32)
    begin = jnp.int32(0)
    start = jnp.int32(0)
    for length, move in zip(lengths_of(meta, d), moves_of(meta, d)):
        size = length * (move if moved else 1 - move)
        inside = (at >= begin) & (at < begin + size)
        source = jnp.where(inside, at + (start - begin), source)
        begin = begin + size
        start = start + length
    columns = lax.broadcasted_iota(jnp.int32, (rows, home), 1)
    return jnp.where(columns == source, 1.0, 0.0).astype(BF)


def sent_first(meta):
    n = meta.shape[1]
    partner = lax.rem(dp_at(meta) + n // 2, n)
    return lax.rem(kept_total(meta, partner), TILE)


def early_picks(meta, home):
    return picks(meta, True, sent_first(meta), EARLY, home)


def late_picks(meta, home):
    return picks(meta, True, sent_first(meta) - EARLY, LATE, home)


def kept_picks(meta, home):
    return picks(meta, False, 0, KEEP, home)


def scaled_rows(meta, pick, cot, scale):
    width = cot.shape[1]
    rows = jnp.dot(pick, cot[...], preferred_element_type=F32)
    own = scale[pl.ds(pl.multiple_of(tensor_at(meta) * width, 128), width)]
    return (rows * own[None, :]).astype(BF)


def first_kernel(
    meta, cot_hbm, scale_hbm, pre_hbm, late_out, rest_out, early_out, late_pick, rest_pick, pre, cot, scale, sems
):
    home, width = cot.shape
    pairs = ((cot_hbm, cot), (scale_hbm, scale), (pre_hbm, pre))
    copies = [pltpu.make_async_copy(a, b, sems.at[i]) for i, (a, b) in enumerate(pairs)]
    for copy in copies:
        copy.start()
    early = early_picks(meta, home)
    late = late_picks(meta, home)
    kept = kept_picks(meta, home)
    late_pick[...] = late
    rest_pick[0:EARLY, :] = early
    rest_pick[EARLY:, :] = kept
    copies[0].wait()
    copies[1].wait()
    early_rows = scaled_rows(meta, early, cot, scale)
    early_out[:, :width] = early_rows
    late_out[...] = scaled_rows(meta, late, cot, scale)
    rest_out[0:EARLY, :] = early_rows
    rest_out[EARLY:, :] = scaled_rows(meta, kept, cot, scale)
    copies[2].wait()
    early_out[:, width:] = jnp.dot(early, pre[...], preferred_element_type=F32).astype(BF)


def gelu_and_slope(x):
    cumulative = 0.5 * (1.0 + lax.erf(x * inv_root_two))
    return x * cumulative, cumulative + x * jnp.exp(-0.5 * x * x) * inv_root_tau


def cut_at(widths, block):
    return [
        (i, c, min(block, width - c)) for i, width in enumerate(widths) for c in range(0, width, block)
    ]


def gelu_kernel(base, block, meta, pick, pre, act_out, der_out, rows_f32):
    rows = pick.shape[0]
    step = next(TILE * k for k in (3, 4, 2, 1) if rows % (TILE * k) == 0)
    for at in range(0, act_out.shape[1], block):
        source = slice(base + at, base + at + block)
        rows_f32[...] = jnp.dot(pick[...], pre[:, source], preferred_element_type=F32)
        columns = slice(at, at + block)

        def body(k, _):
            part = pl.ds(pl.multiple_of(k * step, step), step)
            value, slope = gelu_and_slope(rows_f32[part, :])
            act_out[part, columns] = value.astype(BF)
            der_out[part, columns] = slope
            return 0

        lax.fori_loop(0, rows // step, body, 0)


def assemble(meta, pieces, first_row, lhs):
    rows = lhs.shape[0]
    width = pieces[1].shape[1]
    for j, piece in enumerate(pieces):
        columns = pl.ds(pl.multiple_of((tensor_at(meta) ^ j) * width, 128), width)
        lhs[:, columns] = piece[first_row : first_row + rows, 0:width]


def grad_kernel(first_row, first_slope, base, slope_count, block, meta, p0, p1, p2, p3, weight, *rest):
    slopes, outs, lhs = rest[:slope_count], rest[slope_count:-1], rest[-1]
    rows = lhs.shape[0]
    assemble(meta, (p0, p1, p2, p3), first_row, lhs)
    parts = slopes if slope_count > len(outs) else outs
    starts = [sum(part.shape[1] for part in parts[:i]) for i in range(len(parts))]
    slope_rows = slice(first_slope, first_slope + rows)
    for i, c, wide in cut_at([part.shape[1] for part in parts], block):
        at = starts[i] + c
        inside, whole_at = slice(c, c + wide), slice(at, at + wide)
        slope = slopes[i][slope_rows, inside] if slope_count == len(parts) else slopes[0][slope_rows, whole_at]
        columns = slice(base + at, base + at + wide)
        value = (jnp.dot(lhs[...], weight[:, columns], preferred_element_type=F32) * slope).astype(BF)
        if len(outs) == len(parts):
            outs[i][:, inside] = value
        else:
            outs[0][:, whole_at] = value


def early_kernel(block, meta, own, p1, p2, p3, weight, out, lhs, acc):
    width = p1.shape[1]
    assemble(meta, (own, p1, p2, p3), 0, lhs)
    for at in range(0, out.shape[1], block):
        columns = slice(at, at + block)
        acc[...] = jnp.dot(lhs[...], weight[:, columns], preferred_element_type=F32)

        def body(k, _):
            rows = pl.ds(pl.multiple_of(k * TILE, TILE), TILE)
            _, slope = gelu_and_slope(own[rows, width + at : width + at + block].astype(F32))
            out[rows, columns] = (acc[rows, :] * slope).astype(BF)
            return 0

        lax.fori_loop(0, EARLY // TILE, body, 0)


def weight_kernel(count, meta, *refs):
    moved, kept = refs[:count], refs[count : 2 * count]
    act_moved, act_kept, *outs, lhs_moved, lhs_kept = refs[2 * count :]
    half = moved[0].shape[1] // 2
    mine = dp_at(meta) % 2 == 0
    for i in range(count):
        for piece, lhs in ((moved[i], lhs_moved), (kept[i], lhs_kept)):
            both = piece[...].T
            lo, hi = both[:half], both[half:]
            lhs[i * half : (i + 1) * half, :] = jnp.where(mine, hi, lo)
            lhs[(count + i) * half : (count + i + 1) * half, :] = jnp.where(mine, lo, hi)
    again_kernel(0, meta, lhs_moved, lhs_kept, act_moved, act_kept, *outs)


def again_kernel(base, meta, lhs_moved, lhs_kept, act_moved, act_kept, *outs):
    columns = slice(base, base + act_kept.shape[1])
    step = lhs_moved.shape[0] // 4
    at = 0
    for out in outs:
        for i in range(0, out.shape[0], step):
            part = slice(at, at + step)
            value = jnp.dot(lhs_moved[part, :], act_moved[:, columns], preferred_element_type=F32)
            value += jnp.dot(lhs_kept[part, :], act_kept[...], preferred_element_type=F32)
            out[i : i + step, :] = value.astype(out.dtype)
            at += step


def near_kernel(count, meta, *refs):
    keeps, gots, (out, mine) = refs[:count], refs[count : 2 * count], refs[2 * count :]
    half = out.shape[0] // 2
    parts = [(k, g, at) for k, g in zip(keeps, gots) for at in range(0, k.shape[0], half)]
    keeps_even = (dp_at(meta) // 2 + tensor_at(meta)) % 2 == 0
    step = 2 * TILE

    for pair in range(2):
        (k0, g0, a0), (k1, g1, a1) = parts[2 * pair], parts[2 * pair + 1]

        def body(i, _):
            def rows(at):
                return pl.ds(pl.multiple_of(at + i * step, TILE), step)

            even = k0[rows(a0), :] + g0[rows(a0), :].astype(F32)
            odd = k1[rows(a1), :] + g1[rows(a1), :].astype(F32)
            out[rows(pair * half), :] = jnp.where(keeps_even, odd, even).astype(BF)
            mine[rows(pair * half), :] = jnp.where(keeps_even, even, odd)
            return 0

        lax.fori_loop(0, half // step, body, 0)


def far_kernel(meta, held, got, out, mine):
    half = out.shape[0]
    keeps_first = (dp_at(meta) // 4 + tensor_at(meta) // 2) % 2 == 0
    step = 2 * TILE

    def body(i, _):
        first = pl.ds(pl.multiple_of(i * step, TILE), step)
        second = pl.ds(pl.multiple_of(half + i * step, TILE), step)
        a = held[first, :] + got[first, :].astype(F32)
        b = held[second, :] + got[second, :].astype(F32)
        out[first, :] = jnp.where(keeps_first, b, a).astype(BF)
        mine[first, :] = jnp.where(keeps_first, a, b)
        return 0

    lax.fori_loop(0, half // step, body, 0)


def place_kernel(cuts, meta, kept, early, *rest):
    lates, out = rest[:-1], rest[-1]
    count = kept_total(meta, dp_at(meta))
    first = jnp.minimum(count - lax.rem(count, TILE), BAL - SEND)
    first = pl.multiple_of(first, TILE)
    wide = out.shape[1]
    step = pl.program_id(0)
    columns = pl.ds(pl.multiple_of(step * wide, wide), wide)
    out[0:KEEP, :] = kept[:, columns]
    out[KEEP:, :] = jnp.zeros((out.shape[0] - KEEP, wide), BF)

    def put(block, at):
        rows = lax.broadcasted_iota(jnp.int32, (block.shape[0], 1), 0) + at
        window = pl.ds(at, block.shape[0])
        out[window, :] = jnp.where(rows < count, out[window, :], block)

    put(early[:, columns], first)
    sources = [(late, c) for late, cut in zip(lates, cuts) for c in range(0, cut, wide)]
    for i, (late, c) in enumerate(sources):

        @pl.when(step == i)
        def _():
            put(late[:, c : c + wide], pl.multiple_of(first + EARLY, TILE))


def swapped(block, axis, distance):
    n = lax.axis_size(axis)
    return lax.ppermute(block, axis, [(i, i ^ distance) for i in range(n)])


def after(value, *others):
    return lax.optimization_barrier((value, *others))[0]


def shards(hidden_pre, cotangent, down_weight, layer_scale, crop_lengths, crop_moves):
    hidden_pre, cotangent, layer_scale = (
        pltpu.with_memory_space_constraint(x, pltpu.HBM) for x in (hidden_pre, cotangent, layer_scale)
    )
    home, ff = hidden_pre.shape
    width = cotangent.shape[1]
    features = down_weight.shape[0]
    half = width // 2
    part = ff // 3
    others = EARLY + KEEP
    n = lax.axis_size("dp")
    d = lax.axis_index("dp").astype(jnp.int32)
    t = lax.axis_index("tensor").astype(jnp.int32)
    column = lax.broadcasted_iota(jnp.int32, (1, n), 1)
    own = jnp.where(column == 0, d, jnp.where(column == 1, t, 0))
    meta = jnp.concatenate([crop_lengths.T, crop_moves.T, own])
    vmem = pltpu.VMEM
    sems = pltpu.SemaphoreType.DMA

    def gelu(meta, pick, base, columns):
        rows, block = pick.shape[0], 256
        return kernel_call(
            functools.partial(gelu_kernel, base, block),
            [shape(rows, columns), shape(rows, columns, F32)],
            [IN_VMEM] * 2, [IN_VMEM] * 2, [vmem((rows, block), F32)],
        )(meta, pick, pre)

    def weight_first(meta, act_moved, act_kept):
        return kernel_call(
            functools.partial(weight_kernel, 4),
            [shape(width, part)] * 2 + [shape(width, part, F32)] * 2
            + [shape(features, LATE), shape(features, others)],
            [IN_VMEM] * 10, [IN_VMEM] * 6,
        )(meta, *lates, *rests, act_moved, act_kept)

    def weight_again(meta, base, act_moved, act_kept, count):
        rows = features // 2 // count
        return kernel_call(
            functools.partial(again_kernel, base),
            [shape(rows, part)] * count + [shape(rows, part, F32)] * count,
            [IN_VMEM] * 4, [IN_VMEM] * (2 * count),
        )(meta, *lhs, act_moved, act_kept)

    def grads(meta, pieces, first_row, first_slope, rows, base, slopes, cuts):
        return kernel_call(
            functools.partial(grad_kernel, first_row, first_slope, base, len(slopes), 256),
            [shape(rows, c) for c in cuts], [IN_VMEM] * (5 + len(slopes)), [IN_VMEM] * len(cuts),
            [vmem((rows, features), BF)],
        )(meta, *pieces, down_weight, *slopes)

    def near_step(meta, keeps, gots):
        count = len(keeps)
        return kernel_call(
            functools.partial(near_kernel, count),
            [shape(width, part), shape(width, part, F32)], [IN_VMEM] * (2 * count), [IN_VMEM] * 2,
        )(meta, *keeps, *gots)

    def far_step(meta, mine, got):
        return kernel_call(
            far_kernel, [shape(half, part), shape(half, part, F32)], [IN_VMEM] * 2, [IN_VMEM] * 2
        )(meta, mine, got)

    late, rest, early, late_pick, rest_pick, pre = kernel_call(
        first_kernel,
        [shape(LATE, width), shape(others, width), shape(EARLY, width + ff),
         shape(LATE, home), shape(others, home), shape(home, ff)],
        [IN_HBM] * 3, [IN_VMEM] * 6,
        [vmem((home, width), BF), vmem((features,), F32), sems((3,))],
    )(meta, cotangent, layer_scale, hidden_pre)
    arrived_early = swapped(early, "dp", n // 2)

    late_c, late_y = swapped(late, "tensor", 1), swapped(late, "tensor", 2)
    rest_c, rest_y = swapped(rest, "tensor", 1), swapped(rest, "tensor", 2)
    act_la, der_la = gelu(after(meta, late), late_pick, 0, part)
    act_ra, der_ra = gelu(after(meta, act_la), rest_pick, 0, part)
    late_y = after(late_y, act_ra, late_c, rest_c, arrived_early)
    late_yc = swapped(late_y, "tensor", 1)
    lates = (late, late_c, late_y, late_yc)

    (moving_a,) = grads(after(meta, late_y), lates, 0, 0, LATE, 0, (der_la,), (part,))
    arrived_a = swapped(moving_a, "dp", n // 2)

    rest_y = after(rest_y, moving_a)
    rest_yc = swapped(rest_y, "tensor", 1)
    rests = (rest, rest_c, rest_y, rest_yc)
    *sends_a, keep_01, keep_23, lhs_moved, lhs_kept = weight_first(after(meta, moving_a), act_la, act_ra)
    lhs = (lhs_moved, lhs_kept)
    gots_a = [swapped(send, "dp", 1) for send in sends_a]

    act_l, der_l = gelu(after(meta, keep_01), late_pick, part, 2 * part)
    moving_b, moving_c = grads(after(meta, act_l), lates, 0, 0, LATE, part, (der_l,), (part, part))
    act_rb, der_rb = gelu(after(meta, moving_b, gots_a[0]), rest_pick, part, part)
    arrived_b = swapped(moving_b, "dp", n // 2)
    *sends_b, keep_b01, keep_b23 = weight_again(after(meta, act_rb, arrived_a), 0, act_l, act_rb, 2)
    gots_b = [swapped(send, "dp", 1) for send in sends_b]

    out_na, mine_a = near_step(after(meta, keep_b01), (keep_01, keep_23), gots_a)
    got_na = swapped(out_na, "dp", 2)
    early_sent = after(arrived_early[:, :width], out_na)
    early_c, early_y = swapped(early_sent, "tensor", 1), swapped(early_sent, "tensor", 2)
    act_rc, der_rc = gelu(after(meta, out_na), rest_pick, 2 * part, part)
    early_y = after(early_y, early_c, act_rc)
    early_yc = swapped(early_y, "tensor", 1)
    *sends_c, keep_c01, keep_c23 = weight_again(after(meta, early_yc), part, act_l, act_rc, 2)
    gots_c = [swapped(send, "dp", 1) for send in sends_c]

    out_nb, mine_b = near_step(after(meta, keep_c01, arrived_b, got_na), (keep_b01, keep_b23), gots_b)
    got_nb = swapped(out_nb, "dp", 2)
    arrived_c = swapped(after(moving_c, out_nb), "dp", n // 2)
    out_fa, own_a = far_step(after(meta, out_nb), mine_a, got_na)
    got_fa = swapped(out_fa, "dp", 4)
    (kept_grad,) = grads(after(meta, out_fa), rests, EARLY, EARLY, KEEP, 0, (der_ra, der_rb, der_rc), (ff,))
    early_grad = kernel_call(
        functools.partial(early_kernel, 256), shape(EARLY, ff), [IN_VMEM] * 5, IN_VMEM,
        [vmem((EARLY, features), BF), vmem((EARLY, 256), F32)],
    )(after(meta, kept_grad), arrived_early, early_c, early_y, early_yc, down_weight)

    out_nc, mine_c = near_step(after(meta, early_grad), (keep_c01, keep_c23), gots_c)
    got_nc = swapped(out_nc, "dp", 2)
    out_fb, own_b = far_step(after(meta, out_nc), mine_b, got_nb)
    got_fb = swapped(out_fb, "dp", 4)
    out_fc, own_c = far_step(after(meta, out_fb), mine_c, got_nc)
    got_fc = swapped(out_fc, "dp", 4)
    got_fa, got_fb = after(got_fa, out_fc), after(got_fb, out_fc)
    total = [a + b.astype(F32) for a, b in ((own_a, got_fa), (own_b, got_fb), (own_c, got_fc))]
    down_grad = jnp.concatenate(total, axis=1) / math.sqrt(n * home)

    hidden_grad = kernel_call(
        functools.partial(place_kernel, (part,) * 3), shape(BAL, ff), [IN_VMEM] * 5,
        pl.BlockSpec((BAL, 256), lambda i, *_: (0, i)), grid=(ff // 256,),
    )(after(meta, out_fc), kept_grad, early_grad, arrived_a, arrived_b, arrived_c)
    return (hidden_grad, down_grad)


def solution(mesh):
    pairs_and_fours = (mesh.shape["dp"], mesh.shape["tensor"]) == (8, 4)
    return jax.shard_map(
        shards if pairs_and_fours else general_shards,
        mesh=mesh,
        in_specs=(P("dp", "tensor"), P("dp", "tensor"), P(None, "tensor"), P(), P(), P()),
        out_specs=(P("dp", "tensor"), P("dp", "tensor")),
        check_vma=False,
    )


def shifted(block, axis, distance):
    devices = range(lax.axis_size(axis))
    route = [((i - distance) % len(devices), i) for i in devices]
    return lax.ppermute(block, axis, route)


def crop_rows(row_total, crop_sizes, crop_starts):
    crop_ends = jnp.cumsum(crop_sizes)
    crop_begins = crop_ends - crop_sizes
    target_rows = jnp.arange(row_total, dtype=jnp.int32)[:, None]
    inside_crop = (target_rows >= crop_begins[None, :]) & (target_rows < crop_ends[None, :])
    source_rows = jnp.sum(
        jnp.where(inside_crop, crop_starts[None, :] + target_rows - crop_begins[None, :], 0), axis=1
    )
    return (source_rows, jnp.any(inside_crop, axis=1))


def select_rows(row_block, source_rows, valid_rows):
    taken = jnp.take(row_block, source_rows, axis=0)
    return jnp.where(valid_rows[:, None], taken, jnp.zeros((), row_block.dtype))


def gelu_parts(pre_act):
    cumulative = 0.5 * (1.0 + jax.scipy.special.erf(pre_act * inv_root_two))
    activated = pre_act * cumulative
    derivative = cumulative + pre_act * jnp.exp(-0.5 * pre_act * pre_act) * inv_root_tau
    return (activated, derivative)


def local_grads(pre_rows, cot_part, live_rows, layer_scale, down_weight, home_rows):
    cot_full = lax.all_gather(cot_part, "tensor", axis=1, tiled=True)
    scaled = (cot_full.astype(F32) * layer_scale[None, :]).astype(BF)
    activated, derivative = gelu_parts(pre_rows.astype(F32))
    activation = jnp.where(live_rows[:, None], activated, 0.0).astype(BF)
    backward = jnp.dot(scaled, down_weight, preferred_element_type=F32) * derivative
    gradient_rows = jnp.where(live_rows[:, None], backward, 0.0).astype(BF)
    weight_grad = lax.psum_scatter(
        lax.dot_general(scaled, activation, (((0,), (0,)), ((), ())), preferred_element_type=F32),
        "dp",
        scatter_dimension=0,
        tiled=True,
    )
    return (gradient_rows, weight_grad / math.sqrt(lax.axis_size("dp") * home_rows))


def general_shards(hidden_pre, cotangent, down_weight, layer_scale, crop_lengths, crop_moves):
    devices = lax.axis_size("dp")
    half_axis = devices // 2
    device_index = lax.axis_index("dp")
    partner_index = (device_index + half_axis) % devices
    own_lengths = lax.dynamic_index_in_dim(crop_lengths, device_index, 0, keepdims=False)
    own_moves = lax.dynamic_index_in_dim(crop_moves, device_index, 0, keepdims=False)
    partner_lengths = lax.dynamic_index_in_dim(crop_lengths, partner_index, 0, keepdims=False)
    partner_moves = lax.dynamic_index_in_dim(crop_moves, partner_index, 0, keepdims=False)
    home_rows = hidden_pre.shape[0]
    own_starts = jnp.cumsum(own_lengths) - own_lengths
    sent_sizes = own_lengths * own_moves
    kept_sizes = own_lengths * (1 - own_moves)
    arrived = jnp.sum(partner_lengths * partner_moves)
    send_source, send_valid = crop_rows(SEND, sent_sizes, own_starts)
    keep_sizes = jnp.concatenate([kept_sizes, arrived[None]])
    keep_starts = jnp.concatenate([own_starts, jnp.full((1,), home_rows, jnp.int32)])
    keep_source, keep_valid = crop_rows(BAL, keep_sizes, keep_starts)
    live_home = jnp.arange(home_rows, dtype=jnp.int32) < jnp.sum(own_lengths)
    gradient_rows, weight_grad = local_grads(
        hidden_pre, cotangent, live_home, layer_scale, down_weight, home_rows
    )
    outgoing = select_rows(gradient_rows, send_source, send_valid)
    incoming = shifted(outgoing, "dp", half_axis)
    balanced = select_rows(jnp.concatenate([gradient_rows, incoming], 0), keep_source, keep_valid)
    return (balanced, weight_grad)
```
